256 devices in a mesh: grp: 8 (over x_lo, y), ctx: 32 (over z, x_hi, core).
Axes of the slice: x: 4 (x_hi: 2, x_lo: 2; x = x_hi * 2 + x_lo), y: 4, z: 8, core: 2. Of those that a mesh axis runs over, the one named last changes fastest.
Arguments:
- prompt_k: bfloat16 [512, 2048], P(('grp', 'ctx')), may hold values from -7 to 7
- prompt_v: bfloat16 [512, 2048], P(('grp', 'ctx')), may hold values from -6 to 6
- comp_q: bfloat16 [8, 32, 128, 2048], P('grp', 'ctx'), may hold values from -120 to 120
- comp_k: bfloat16 [8, 32, 128, 2048], P('grp', 'ctx'), may hold values from -6 to 6
- comp_v: bfloat16 [8, 32, 128, 2048], P('grp', 'ctx'), may hold values from -6 to 6
- grad_out: bfloat16 [8, 32, 64, 2048], P('grp', 'ctx'), may hold values from -24 to 24
- rewards: float32 [8, 32], P('grp', 'ctx'), may hold values from -4 to 4
- mask_pos: int32 [8, 32, 64], P('grp', 'ctx'), may hold values from 0 to 128, as said below
Outputs:
- grad_query: bfloat16 [8, 32, 64, 2048], P('grp', 'ctx')
- grad_comp_k: bfloat16 [8, 32, 128, 2048], P('grp', 'ctx')
- grad_comp_v: bfloat16 [8, 32, 128, 2048], P('grp', 'ctx')
- grad_prompt_k: bfloat16 [512, 2048], P(('grp', 'ctx'))
- grad_prompt_v: bfloat16 [512, 2048], P(('grp', 'ctx'))
The draws below stay inside these ranges and needn't reach their ends.
Inputs may be any that keep to these rules, and one draw needn't show every extreme that they name: `mask_pos`: each completion lists its masked positions in increasing order, each once, then 128 in every unused slot; every completion has 16 or more masked positions, and in every group some completion has exactly 64.
All inputs are finite; a program needn't handle non-finite values.
Results may differ from the reference program's by a relative error of at most 0.015.
Values may be sent and summed in bfloat16 or wider, within the bound.
A program may use at most 128 MiB of HBM per device.

```python
import jax
import jax.numpy as jnp
from jax import lax

HEADS = 16
HEAD_DIM = 128
WIDTH = 2048
COMP_LEN = 128
MASK_SLOTS = 64
GROUPS = 8
MEMBERS = 32
PROMPT = 512


def paired_draw(key):
    splits = jax.random.split(key, 3)
    key_table = jax.random.truncated_normal(splits[0], -6.0, 6.0, (PROMPT, WIDTH), jnp.float32)
    odd_rows = (jnp.arange(PROMPT) % 2 == 1)[:, None]
    key_table = jnp.where(odd_rows, key_table, key_table)
    query_table = jax.random.truncated_normal(splits[2], -6.0, 6.0, (GROUPS, MEMBERS, COMP_LEN, WIDTH), jnp.float32)
    current = query_table[:, :, ::16, :]
    query_table = query_table.at[:, :, ::16, :].set(current)
    return (key_table, query_table)


def draw_prompt_k(key, part):
    key_table, query_table = paired_draw(key)
    return key_table.astype(jnp.bfloat16)


def draw_comp_q(key, part):
    key_table, query_table = paired_draw(key)
    return query_table.astype(jnp.bfloat16)


def draw_mask_pos(key, part):
    key = jax.random.fold_in(key, 7)
    splits = jax.random.split(key, 3)
    counts = jax.random.randint(splits[0], (GROUPS, MEMBERS), MASK_SLOTS // 4, MASK_SLOTS + 1)
    fullest = jax.random.randint(splits[1], (GROUPS,), 0, MEMBERS)
    counts = jnp.where(jnp.arange(MEMBERS)[None, :] == fullest[:, None], MASK_SLOTS, counts)
    spots = jnp.arange(COMP_LEN, dtype=jnp.int32)
    scores = jax.random.randint(splits[2], (GROUPS, MEMBERS, COMP_LEN), 0, COMP_LEN) * COMP_LEN + spots
    ranks = jnp.argsort(jnp.argsort(scores, axis=-1), axis=-1)
    picked = ranks < counts[..., None]
    order_key = jnp.where(picked, 0, COMP_LEN) + spots
    ordered = jnp.argsort(order_key, axis=-1)[..., :MASK_SLOTS].astype(jnp.int32)
    slot_index = jnp.arange(MASK_SLOTS)[None, None, :]
    return jnp.where(slot_index < counts[..., None], ordered, COMP_LEN).astype(jnp.int32)


def level_of(key, shape, cuts, smallest, top_value):
    def one(position, blocks):
        draws = jax.random.uniform(jax.random.fold_in(jax.random.fold_in(key, 6), position), (blocks,), jnp.float32, smallest / len(cuts), top_value / len(cuts))
        return jnp.repeat(jnp.exp(draws), shape[position] // blocks).reshape((-1,) + (1,) * (len(shape) - position - 1))

    factor_of = one(*cuts[0])
    for cut in cuts[1:]:
        factor_of = factor_of * one(*cut)
    return factor_of


def centred(key, dims, deviation, reach, cuts=(), kind=jnp.bfloat16):
    values = jax.random.normal(key, dims, jnp.float32) * deviation
    if len(cuts) > 0:
        values = level_of(key, dims, cuts, -0.22, 0.18) * values
    return jnp.clip(values, min=-reach, max=reach).astype(kind)


def setup_inputs(seed: int = 0) -> dict:
    arg_keys = jax.random.split(jax.random.key(seed), 9)
    return {
        "prompt_k": draw_prompt_k(jax.random.fold_in(arg_keys[8], 71), 0),
        "prompt_v": centred(arg_keys[1], (PROMPT, WIDTH), 1.0, 6.0, ((0, 256),)),
        "comp_q": draw_comp_q(jax.random.fold_in(arg_keys[8], 71), 0),
        "comp_k": centred(arg_keys[3], (GROUPS, MEMBERS, COMP_LEN, WIDTH), 1.0, 6.0, ((0, 8), (1, 32))),
        "comp_v": centred(arg_keys[4], (GROUPS, MEMBERS, COMP_LEN, WIDTH), 1.0, 6.0, ((0, 8), (1, 32))),
        "grad_out": centred(arg_keys[5], (GROUPS, MEMBERS, MASK_SLOTS, WIDTH), 4.0, 24.0, ((0, 8), (1, 32))),
        "rewards": centred(arg_keys[6], (GROUPS, MEMBERS), 1.0, 4.0, ((0, 8), (1, 32)), jnp.float32),
        "mask_pos": draw_mask_pos(jax.random.fold_in(arg_keys[8], 71), 0),
    }


def output_products(form, left, right):
    return jnp.einsum(form, left.astype(jnp.float32), right.astype(jnp.float32), precision=lax.Precision.HIGHEST)


def attention_grads(query_rows, weighted, prompt_keys, prompt_values, own_keys, own_values):
    slot_count = query_rows.shape[0]
    features = query_rows.shape[1]
    logit_scale_factor = HEAD_DIM ** -0.5
    query_head_rows = query_rows.reshape(slot_count, HEADS, HEAD_DIM)
    gradient_heads = weighted.reshape(slot_count, HEADS, HEAD_DIM)
    context_key_heads = prompt_keys.reshape(-1, HEADS, HEAD_DIM)
    context_value_heads = prompt_values.reshape(-1, HEADS, HEAD_DIM)
    self_key_heads = own_keys.reshape(-1, HEADS, HEAD_DIM)
    self_value_heads = own_values.reshape(-1, HEADS, HEAD_DIM)
    context_scores = output_products("eon,con->oec", query_head_rows, context_key_heads) * logit_scale_factor
    self_scores = output_products("skf,gkf->ksg", query_head_rows, self_key_heads) * logit_scale_factor
    row_max = jnp.maximum(jnp.max(context_scores, axis=-1), jnp.max(self_scores, axis=-1))[..., None]
    exp_prompt = jnp.exp(context_scores - row_max)
    exp_own = jnp.exp(self_scores - row_max)
    denom = jnp.sum(exp_prompt, axis=-1, keepdims=True) + jnp.sum(exp_own, axis=-1, keepdims=True)
    prob_prompt = exp_prompt / denom
    prob_own = exp_own / denom
    rounded_context_probs = prob_prompt.astype(jnp.bfloat16)
    rounded_self_probs = prob_own.astype(jnp.bfloat16)
    attended_output = output_products("uls,suo->luo", rounded_context_probs, context_value_heads) + output_products("xwz,zxn->wxn", rounded_self_probs, self_value_heads)
    inner_sums = jnp.transpose(jnp.sum(gradient_heads.astype(jnp.float32) * attended_output, axis=-1))[..., None]
    probability_grad_context = output_products("eon,con->oec", gradient_heads, context_value_heads)
    probability_grad_self = output_products("skf,gkf->ksg", gradient_heads, self_value_heads)
    score_grad_context = (prob_prompt * (probability_grad_context - inner_sums)).astype(jnp.bfloat16)
    score_grad_self = (prob_own * (probability_grad_self - inner_sums)).astype(jnp.bfloat16)
    gradient_query_rows = (output_products("uls,suo->luo", score_grad_context, context_key_heads) + output_products("xwz,zxn->wxn", score_grad_self, self_key_heads)) * logit_scale_factor
    gradient_context_key = output_products("uvt,vus->tus", score_grad_context, query_head_rows) * logit_scale_factor
    gradient_context_value = output_products("uvt,vus->tus", rounded_context_probs, gradient_heads)
    gradient_self_key = output_products("iou,oig->uig", score_grad_self, query_head_rows) * logit_scale_factor
    gradient_self_value = output_products("iou,oig->uig", rounded_self_probs, gradient_heads)
    return (gradient_query_rows.reshape(slot_count, features), gradient_context_key.reshape(-1, features), gradient_context_value.reshape(-1, features),
            gradient_self_key.reshape(-1, features), gradient_self_value.reshape(-1, features))


def reference(prompt_k, prompt_v, comp_q, comp_k, comp_v, grad_out, rewards, mask_pos):
    is_masked = mask_pos < COMP_LEN
    masked_count = jnp.sum(is_masked.astype(jnp.float32), axis=(1, 2))
    advantage = rewards - (jnp.sum(rewards, axis=1) / MEMBERS)[:, None]
    token_weight = advantage * (MASK_SLOTS * MEMBERS) / masked_count[:, None]
    features = prompt_k.shape[1]
    total_comps = GROUPS * MEMBERS
    inputs = (comp_q.reshape(total_comps, COMP_LEN, features), comp_k.reshape(total_comps, COMP_LEN, features),
              comp_v.reshape(total_comps, COMP_LEN, features), grad_out.reshape(total_comps, MASK_SLOTS, features),
              mask_pos.reshape(total_comps, MASK_SLOTS).astype(jnp.int32), token_weight.reshape(total_comps))

    def advance(running, pieces):
        queries, own_keys, own_values, upstream, positions, weight_one = pieces
        live = positions < COMP_LEN
        slot_rows = jnp.clip(positions, 0, COMP_LEN - 1).astype(jnp.int32)
        query_rows = jnp.take(queries, slot_rows, axis=0)
        weighted = (upstream.astype(jnp.float32) * jnp.where(live, weight_one, jnp.float32(0.0))[:, None]).astype(jnp.bfloat16)
        gradient_query_rows, gradient_context_key, gradient_context_value, gradient_self_key, gradient_self_value = attention_grads(query_rows, weighted, prompt_k, prompt_v, own_keys, own_values)
        updated = (running[0] + gradient_context_key, running[1] + gradient_context_value)
        return updated, (gradient_query_rows.astype(jnp.bfloat16), gradient_self_key.astype(jnp.bfloat16), gradient_self_value.astype(jnp.bfloat16))

    start = (jnp.zeros(prompt_k.shape, jnp.float32), jnp.zeros(prompt_k.shape, jnp.float32))
    sums, outputs = lax.scan(advance, start, inputs)
    grad_query = outputs[0].reshape(GROUPS, MEMBERS, MASK_SLOTS, features)
    grad_comp_k = outputs[1].reshape(GROUPS, MEMBERS, COMP_LEN, features)
    grad_comp_v = outputs[2].reshape(GROUPS, MEMBERS, COMP_LEN, features)
    return (grad_query, grad_comp_k, grad_comp_v, sums[0].astype(jnp.bfloat16), sums[1].astype(jnp.bfloat16))
```

```python
import jax
import jax.numpy as jnp
from jax import lax
from jax.experimental import pallas as pl
from jax.experimental.pallas import tpu as pltpu
from jax.sharding import PartitionSpec as P

HEADS = 16
DIM = 128
SLOTS = 64
ROWS = 128
WIDTH = 2048
PROMPT = 512
F32 = jnp.float32
BF16 = jnp.bfloat16
SCALE = DIM ** -0.5
SCALE2 = SCALE * 1.4426950408889634
MESH = pl.DeviceIdType.MESH

KV, QG, ZKV, ZSUM, YKV, OWN, FIN, DQ, RS1, RS2, RS3, KINDS = range(12)


def dot_nt(a, b):
    return lax.dot_general(a, b, (((1,), (1,)), ((), ())), preferred_element_type=F32)


def dot_nn(a, b):
    return lax.dot_general(a, b, (((1,), (0,)), ((), ())), preferred_element_type=F32)


def dot_tn(a, b):
    return lax.dot_general(a, b, (((0,), (0,)), ((), ())), preferred_element_type=F32)


def kernel(
    pk_hbm, pv_hbm, rw_hbm, mp_hbm, cq_hbm, ck_hbm, cv_hbm, go_hbm,
    dq_hbm, dk_hbm, dv_hbm, gk_hbm, gv_hbm,
    pk, pv, rw, mp, cq, ck, cv, go, xb, xbr, kvs, kvr, kvb, gsum, gsumr, own_e, own_d, st, str_,
    fs, fr, pw, ds, sb1, r1, sum1, sb2, r2, t3, r3, dqs, dqr, dqo, dko, dvo, gko, gvo,
    in_sem, out_sem, ss, rs,
):
    grp = lax.axis_index("grp")
    ctx = lax.axis_index("ctx")
    x_lo, y = lax.div(grp, 4), lax.rem(grp, 4)
    z = lax.div(ctx, 4)
    z_hi, z_lo, low = lax.div(z, 2), lax.rem(z, 2), lax.rem(ctx, 4)
    a = x_lo * 8 + z_lo * 4 + low

    def a_peer(b):
        return {
            "grp": lax.div(b, 8) * 4 + y,
            "ctx": (z_hi * 2 + lax.rem(lax.div(b, 4), 2)) * 4 + lax.rem(b, 4),
        }

    def z_peer(b):
        return {"grp": grp, "ctx": (b * 2 + z_lo) * 4 + low}

    def y_peer(b):
        return {"grp": x_lo * 4 + b, "ctx": ctx}

    a_others = [lax.rem(a + k, 16) for k in range(1, 16)]
    z_others = [lax.rem(z_hi + k, 4) for k in range(1, 4)]
    y_others = [lax.rem(y + k, 4) for k in range(1, 4)]

    def remote(kind, src, dst, device):
        return pltpu.make_async_remote_copy(
            src_ref=src, dst_ref=dst, send_sem=ss.at[kind], recv_sem=rs.at[kind],
            device_id=device, device_id_type=MESH,
        )

    def arrived(kind, dst):
        remote(kind, dst, dst, y_peer(y_others[0])).wait_recv()

    def sent(kind, src):
        remote(kind, src, src, y_peer(y_others[0])).wait_send()

    loads = [
        pltpu.make_async_copy(src, dst, in_sem.at[n])
        for n, (src, dst) in enumerate(
            (
                (pk_hbm, pk), (pv_hbm, pv), (rw_hbm, rw), (mp_hbm, mp),
                (cq_hbm, cq), (go_hbm, go), (ck_hbm, ck), (cv_hbm, cv),
            )
        )
    ]
    for load in loads:
        load.start()

    barrier = pltpu.get_barrier_semaphore()
    for b in a_others:
        pl.semaphore_signal(barrier, inc=1, device_id=a_peer(b), device_id_type=MESH)
    for b in z_others:
        pl.semaphore_signal(barrier, inc=1, device_id=z_peer(b), device_id_type=MESH)
    for b in y_others:
        pl.semaphore_signal(barrier, inc=1, device_id=y_peer(b), device_id_type=MESH)

    for load in loads[:4]:
        load.wait()
    pos = mp[...]
    pos2 = jnp.concatenate([pos, pos], axis=1)
    live = pos < ROWS
    count = jnp.sum(jnp.where(live, 1.0, 0.0), axis=1, keepdims=True)
    reward = rw[...]
    lines = jnp.concatenate(
        [
            pk[...].astype(F32),
            pv[...].astype(F32),
            jnp.broadcast_to(count, (1, WIDTH)),
            jnp.broadcast_to(reward, (1, WIDTH)),
            jnp.zeros((2, WIDTH), F32),
        ],
        axis=0,
    )
    for h in range(HEADS):
        kvs[h] = lines[:, h * DIM : (h + 1) * DIM]

    pl.semaphore_wait(barrier, 21)

    for b in a_others:
        remote(KV, kvs.at[b], kvr.at[a], a_peer(b)).start()
    kvr[a] = kvs[a]

    row = lax.broadcasted_iota(jnp.int32, (ROWS, 2 * SLOTS), 0)
    pick = jnp.where(row == jnp.minimum(pos2, ROWS - 1), 1.0, 0.0).astype(BF16)
    loads[4].wait()
    picked = dot_tn(pick, cq[...])[:SLOTS].astype(BF16)
    loads[5].wait()
    for h in range(HEADS):
        xb[h, 0:SLOTS, :] = picked[:, h * DIM : (h + 1) * DIM]
        xb[h, SLOTS : 2 * SLOTS, :] = go[:, h * DIM : (h + 1) * DIM]

    arrived(KV, kvr.at[pl.ds(0, 15)])
    blocks = kvr[...]
    kvb[y, z_hi, 0, 0:16, :] = blocks[:, 0, :].astype(BF16)
    kvb[y, z_hi, 0, 16:32, :] = blocks[:, 1, :].astype(BF16)
    kvb[y, z_hi, 1, 0:16, :] = blocks[:, 2, :].astype(BF16)
    kvb[y, z_hi, 1, 16:32, :] = blocks[:, 3, :].astype(BF16)
    for b in z_others:
        remote(ZKV, kvb.at[y, z_hi], kvb.at[y, z_hi], z_peer(b)).start()
    mine = lax.broadcasted_iota(jnp.int32, (16, DIM), 0) // 8 == x_lo
    count16 = jnp.sum(jnp.where(mine, blocks[:, 4, :], 0.0), axis=0, keepdims=True)
    reward16 = jnp.sum(jnp.where(mine, blocks[:, 5, :], 0.0), axis=0, keepdims=True)
    gsum[...] = jnp.concatenate([count16, reward16, jnp.zeros((6, DIM), F32)], axis=0)
    for b in z_others:
        remote(ZSUM, gsum, gsumr.at[z_hi], z_peer(b)).start()

    for b in a_others:
        remote(QG, xb.at[b], xbr.at[a], a_peer(b)).start()
    xbr[a] = xb[a]

    def own_scores(h):
        q = xb[h, 0:SLOTS, :]
        g = xb[h, SLOTS : 2 * SLOTS, :]
        s = dot_nt(ck[:, h * DIM : (h + 1) * DIM], jnp.concatenate([q, q], axis=0)) * SCALE2
        d = dot_nt(cv[:, h * DIM : (h + 1) * DIM], jnp.concatenate([g, g], axis=0))
        m = jnp.max(s, axis=0, keepdims=True)
        e = jnp.exp2(s - m)
        own_e[h] = e
        own_d[h] = d
        st[h] = jnp.concatenate(
            [
                m,
                jnp.sum(e, axis=0, keepdims=True),
                jnp.sum(e * d, axis=0, keepdims=True),
                jnp.zeros((5, DIM), F32),
            ],
            axis=0,
        )

    loads[6].wait()
    loads[7].wait()
    for h in range(HEADS // 2):
        own_scores(h)

    arrived(ZKV, kvb.at[0, pl.ds(0, 3)])
    for b in y_others:
        remote(YKV, kvb.at[y], kvb.at[y], y_peer(b)).start()
    for h in range(HEADS // 2, HEADS):
        own_scores(h)
    arrived(ZSUM, gsumr.at[pl.ds(0, 3)])
    total = gsum[...]
    for b in z_others:
        total = total + gsumr[b]
    weight = (reward - total[1:2] / 32.0) * (SLOTS * 32) / total[0:1]
    weight = jnp.where(pos2 < ROWS, weight, 0.0)
    for h in range(HEADS):
        st[h, 3:4, :] = weight
    for b in a_others:
        remote(OWN, st.at[b], str_.at[a], a_peer(b)).start()
    str_[a] = st[a]

    arrived(QG, xbr.at[pl.ds(0, 15)])
    arrived(YKV, kvb.at[pl.ds(0, 3)])
    arrived(OWN, str_.at[pl.ds(0, 15)])
    keys = kvb[:, :, 0].reshape(PROMPT, DIM)
    values = kvb[:, :, 1].reshape(PROMPT, DIM)
    left = lax.broadcasted_iota(jnp.int32, (8, DIM), 1) < SLOTS
    def pair(t, _):
        q = xbr[pl.ds(2 * t, 2), 0:SLOTS, :].reshape(2 * SLOTS, DIM)
        g = xbr[pl.ds(2 * t, 2), SLOTS : 2 * SLOTS, :].reshape(2 * SLOTS, DIM)
        s = dot_nt(keys, q) * SCALE2
        d = dot_nt(values, g)
        mp_ = jnp.max(s, axis=0, keepdims=True)
        e = jnp.exp2(s - mp_)
        lp = jnp.sum(e, axis=0, keepdims=True)
        ip = jnp.sum(e * d, axis=0, keepdims=True)
        stats = jnp.where(left, str_[2 * t], str_[2 * t + 1])
        mo, lo, io, w = stats[0:1], stats[1:2], stats[2:3], stats[3:4]
        m = jnp.maximum(mp_, mo)
        fp = jnp.exp2(mp_ - m)
        fo = jnp.exp2(mo - m)
        inv = 1.0 / (lp * fp + lo * fo)
        inner = (ip * fp + io * fo) * inv
        coef = fp * inv * w
        cols = pl.ds(pl.multiple_of(t * 128, 128), 128)
        p = (e * coef).astype(BF16)
        dsc = (e * (d - inner) * (coef * SCALE)).astype(BF16)
        pw[:, :, cols] = p.reshape(4, 128, 128)
        ds[:, :, cols] = dsc.reshape(4, 128, 128)
        final = jnp.concatenate([m, inv, inner, jnp.zeros((5, DIM), F32)], axis=0)
        fs[2 * t] = final
        fs[2 * t + 1] = final
        return 0

    lax.fori_loop(0, 8, pair, 0, unroll=2)

    q_all = xbr[:, 0:SLOTS, :].reshape(16 * SLOTS, DIM)
    g_all = xbr[:, SLOTS : 2 * SLOTS, :].reshape(16 * SLOTS, DIM)
    for b in y_others + [y]:
        grad_k = dot_nn(ds[b], q_all)
        grad_v = dot_nn(pw[b], g_all)
        if b is not y:
            sb1[b, 0] = grad_k.astype(BF16)
            sb1[b, 1] = grad_v.astype(BF16)
            remote(RS1, sb1.at[b], r1.at[y], y_peer(b)).start()
    for b in a_others:
        remote(FIN, fs.at[b], fr.at[a], a_peer(b)).start()
    fr[a] = fs[a]
    for t in range(8):
        grad_q = dot_tn(ds[:, :, t * 128 : (t + 1) * 128].reshape(PROMPT, 2 * SLOTS), keys)
        dqs[2 * t] = grad_q[:SLOTS].astype(BF16)
        dqs[2 * t + 1] = grad_q[SLOTS:].astype(BF16)
    for b in a_others:
        remote(DQ, dqs.at[b], dqr.at[a], a_peer(b)).start()
    dqr[a] = dqs[a]

    arrived(RS1, r1.at[pl.ds(0, 3)])
    for b in y_others:
        grad_k = grad_k + r1[b, 0].astype(F32)
        grad_v = grad_v + r1[b, 1].astype(F32)
    for b in range(4):
        sum1[b, 0] = grad_k[b * 32 : (b + 1) * 32]
        sum1[b, 1] = grad_v[b * 32 : (b + 1) * 32]
        sb2[b, 0] = grad_k[b * 32 : (b + 1) * 32].astype(BF16)
        sb2[b, 1] = grad_v[b * 32 : (b + 1) * 32].astype(BF16)
    for b in z_others:
        remote(RS2, sb2.at[b], r2.at[z_hi], z_peer(b)).start()

    arrived(FIN, fr.at[pl.ds(0, 15)])
    arrived(DQ, dqr.at[pl.ds(0, 15)])
    here = left == (lax.rem(a, 2) == 0)
    nothing = jnp.zeros((SLOTS, DIM), BF16)
    for h in range(HEADS):
        cols = slice(h * DIM, (h + 1) * DIM)
        fin = fr[h]
        fin = jnp.where(here, fin, jnp.concatenate([fin[:, SLOTS:], fin[:, :SLOTS]], axis=1))
        m, inv, inner = fin[0:1], fin[1:2], fin[2:3]
        coef = jnp.exp2(st[h, 0:1, :] - m) * inv * weight
        e = own_e[h]
        p = (e * coef).astype(BF16)
        dsc = (e * (own_d[h] - inner) * (coef * SCALE)).astype(BF16)
        dvo[:, cols] = dot_nn(p, jnp.concatenate([xb[h, SLOTS:, :], nothing], axis=0)).astype(BF16)
        dko[:, cols] = dot_nn(dsc, jnp.concatenate([xb[h, :SLOTS, :], nothing], axis=0)).astype(BF16)
        dqo[:, cols] = (dot_tn(dsc, ck[:, cols])[:SLOTS] + dqr[h].astype(F32)).astype(BF16)
    stores = [
        pltpu.make_async_copy(src, dst, out_sem.at[n])
        for n, (src, dst) in enumerate(
            ((dqo, dq_hbm), (dko, dk_hbm), (dvo, dv_hbm), (gko, gk_hbm), (gvo, gv_hbm))
        )
    ]
    for store in stores[:3]:
        store.start()

    arrived(RS2, r2.at[pl.ds(0, 3)])
    line = lax.broadcasted_iota(jnp.int32, (16, 8, DIM), 1)
    lines = jnp.zeros((16, 8, DIM), F32)
    for kv in range(2):
        part = sum1[z_hi, kv]
        for b in z_others:
            part = part + r2[b, kv].astype(F32)
        for r in range(2):
            lines = jnp.where(line == kv * 2 + r, part[r * 16 : (r + 1) * 16][:, None, :], lines)
    t3[...] = lines
    for b in a_others:
        remote(RS3, t3.at[b], r3.at[a], a_peer(b)).start()
    r3[a] = t3[a]
    arrived(RS3, r3.at[pl.ds(0, 15)])
    for h in range(HEADS):
        cols = slice(h * DIM, (h + 1) * DIM)
        gko[:, cols] = r3[h, 0:2, :].astype(BF16)
        gvo[:, cols] = r3[h, 2:4, :].astype(BF16)

    for store in stores[3:]:
        store.start()

    sent(KV, kvs.at[pl.ds(0, 15)])
    sent(QG, xb.at[pl.ds(0, 15)])
    sent(ZKV, kvb.at[0, pl.ds(0, 3)])
    sent(ZSUM, gsumr.at[pl.ds(0, 3)])
    sent(YKV, kvb.at[pl.ds(0, 3)])
    sent(OWN, st.at[pl.ds(0, 15)])
    sent(FIN, fs.at[pl.ds(0, 15)])
    sent(DQ, dqs.at[pl.ds(0, 15)])
    sent(RS1, sb1.at[pl.ds(0, 3)])
    sent(RS2, sb2.at[pl.ds(0, 3)])
    sent(RS3, t3.at[pl.ds(0, 15)])
    for store in stores:
        store.wait()


def store_all(*refs):
    sources, targets, held, sem = refs[:5], refs[5:10], refs[10:15], refs[15]
    parts = []
    for n in range(5):
        rows = sources[n].shape[0]
        step = min(rows, SLOTS)
        for first in range(0, rows, step):
            parts.append((n, pl.ds(first, step)))
    loads = [
        pltpu.make_async_copy(sources[n].at[span], held[n].at[span], sem.at[0, p])
        for p, (n, span) in enumerate(parts)
    ]
    stores = [
        pltpu.make_async_copy(held[n].at[span], targets[n].at[span], sem.at[1, p])
        for p, (n, span) in enumerate(parts)
    ]
    for load in loads:
        load.start()
    for load, store in zip(loads, stores):
        load.wait()
        store.start()
    for store in stores:
        store.wait()


def shards(prompt_k, prompt_v, comp_q, comp_k, comp_v, grad_out, rewards, mask_pos):
    hbm = pl.BlockSpec(memory_space=pltpu.HBM)
    V = pltpu.VMEM
    grads = pl.pallas_call(
        kernel,
        out_shape=(
            jax.ShapeDtypeStruct((SLOTS, WIDTH), BF16),
            jax.ShapeDtypeStruct((ROWS, WIDTH), BF16),
            jax.ShapeDtypeStruct((ROWS, WIDTH), BF16),
            jax.ShapeDtypeStruct((2, WIDTH), BF16),
            jax.ShapeDtypeStruct((2, WIDTH), BF16),
        ),
        in_specs=[hbm] * 8,
        out_specs=(hbm,) * 5,
        scratch_shapes=[
            V((2, WIDTH), BF16),
            V((2, WIDTH), BF16),
            V((1, 1), F32),
            V((1, SLOTS), jnp.int32),
            V((ROWS, WIDTH), BF16),
            V((ROWS, WIDTH), BF16),
            V((ROWS, WIDTH), BF16),
            V((SLOTS, WIDTH), BF16),
            V((16, 128, DIM), BF16),
            V((16, 128, DIM), BF16),
            V((16, 8, DIM), F32),
            V((16, 8, DIM), F32),
            V((4, 4, 2, 32, DIM), BF16),
            V((8, DIM), F32),
            V((4, 8, DIM), F32),
            V((16, 128, DIM), F32),
            V((16, 128, DIM), F32),
            V((16, 8, DIM), F32),
            V((16, 8, DIM), F32),
            V((16, 8, DIM), F32),
            V((16, 8, DIM), F32),
            V((4, 128, 16 * SLOTS), BF16),
            V((4, 128, 16 * SLOTS), BF16),
            V((4, 2, 128, DIM), BF16),
            V((4, 2, 128, DIM), BF16),
            V((4, 2, 32, DIM), F32),
            V((4, 2, 32, DIM), BF16),
            V((4, 2, 32, DIM), BF16),
            V((16, 8, DIM), F32),
            V((16, 8, DIM), F32),
            V((16, SLOTS, DIM), BF16),
            V((16, SLOTS, DIM), BF16),
            V((SLOTS, WIDTH), BF16),
            V((ROWS, WIDTH), BF16),
            V((ROWS, WIDTH), BF16),
            V((2, WIDTH), BF16),
            V((2, WIDTH), BF16),
            pltpu.SemaphoreType.DMA((8,)),
            pltpu.SemaphoreType.DMA((5,)),
            pltpu.SemaphoreType.DMA((KINDS,)),
            pltpu.SemaphoreType.DMA((KINDS,)),
        ],
        compiler_params=pltpu.CompilerParams(
            collective_id=0, has_side_effects=True, vmem_limit_bytes=60 * 1024 * 1024
        ),
    )(
        prompt_k, prompt_v, rewards, mask_pos[0], comp_q[0, 0], comp_k[0, 0], comp_v[0, 0],
        grad_out[0, 0],
    )
    dq, dk, dv, gk, gv = pl.pallas_call(
        store_all,
        out_shape=[jax.ShapeDtypeStruct(grad.shape, BF16) for grad in grads],
        in_specs=[hbm] * 5,
        out_specs=[hbm] * 5,
        scratch_shapes=[V(grad.shape, BF16) for grad in grads] + [pltpu.SemaphoreType.DMA((2, 7))],
        compiler_params=pltpu.CompilerParams(vmem_limit_bytes=60 * 1024 * 1024),
    )(*grads)
    return dq[None, None], dk[None, None], dv[None, None], gk, gv


def solution(mesh):
    wide = P("grp", "ctx", None, None)
    rows = P(("grp", "ctx"), None)
    return jax.shard_map(
        shards,
        mesh=mesh,
        in_specs=(rows, rows, wide, wide, wide, wide, P("grp", "ctx"), P("grp", "ctx", None)),
        out_specs=(wide, wide, wide, rows, rows),
        check_vma=False,
    )
```

```python
import jax
import jax.numpy as jnp
from jax import lax
from jax.experimental import pallas as pl
from jax.experimental.pallas import tpu as pltpu
from jax.sharding import PartitionSpec as P

HEADS = 16
DIM = 128
SLOTS = 64
ROWS = 128
WIDTH = 2048
PROMPT = 512
F32 = jnp.float32
BF16 = jnp.bfloat16
SCALE = DIM ** -0.5
SCALE2 = SCALE * 1.4426950408889634
MESH = pl.DeviceIdType.MESH

KV, QG, ZKV, ZSUM, XSUM, YKV, OWN, FIN, DQ, RS1, RS2, RS3, KINDS = range(13)


def dot_nt(a, b):
    return lax.dot_general(a, b, (((1,), (1,)), ((), ())), preferred_element_type=F32)


def dot_nn(a, b):
    return lax.dot_general(a, b, (((1,), (0,)), ((), ())), preferred_element_type=F32)


def dot_tn(a, b):
    return lax.dot_general(a, b, (((0,), (0,)), ((), ())), preferred_element_type=F32)


def kernel(
    pk_hbm, pv_hbm, rw_hbm, mp_hbm, cq_hbm, ck_hbm, cv_hbm, go_hbm,
    dq_hbm, dk_hbm, dv_hbm, gk_hbm, gv_hbm,
    pk, pv, rw, mp, cq, ck, cv, go, xb, xbr, kvs, kvr, kvb, gsum, gsumr, gsum2, gsumx, own_e, own_d, st, str_,
    fs, fr, pw, ds, sb1, r1, sum1, sb2, r2, t3, r3, dqs, dqr, dqo, dko, dvo, gko, gvo,
    in_sem, out_sem, ss, rs,
):
    grp = lax.axis_index("grp")
    ctx = lax.axis_index("ctx")
    x_lo, y_hi, y_lo = lax.div(grp, 4), lax.rem(lax.div(grp, 2), 2), lax.rem(grp, 2)
    z_hi, z_lo = lax.div(ctx, 8), lax.rem(lax.div(ctx, 4), 2)
    x_hi, core = lax.rem(lax.div(ctx, 2), 2), lax.rem(ctx, 2)
    a = x_lo * 8 + y_lo * 4 + z_lo * 2 + core
    w = x_hi * 2 + y_hi

    def device(x_lo, x_hi, y_lo, y_hi, z_lo, z_hi, core):
        return {
            "grp": x_lo * 4 + y_hi * 2 + y_lo,
            "ctx": (z_hi * 2 + z_lo) * 4 + x_hi * 2 + core,
        }

    def a_peer(i):
        return device(
            lax.div(i, 8), x_hi, lax.rem(lax.div(i, 4), 2), y_hi,
            lax.rem(lax.div(i, 2), 2), z_hi, lax.rem(i, 2),
        )

    def z_peer(i):
        return device(x_lo, x_hi, y_lo, y_hi, z_lo, i, core)

    def w_peer(i):
        return device(x_lo, lax.div(i, 2), y_lo, lax.rem(i, 2), z_lo, z_hi, core)

    x_peer = device(x_lo, 1 - x_hi, y_lo, y_hi, z_lo, z_hi, core)
    a_others = [lax.rem(a + k, 16) for k in range(1, 16)]
    z_others = [lax.rem(z_hi + k, 4) for k in range(1, 4)]
    w_others = [lax.rem(w + k, 4) for k in range(1, 4)]

    def remote(kind, src, dst, device):
        return pltpu.make_async_remote_copy(
            src_ref=src, dst_ref=dst, send_sem=ss.at[kind], recv_sem=rs.at[kind],
            device_id=device, device_id_type=MESH,
        )

    def arrived(kind, dst):
        remote(kind, dst, dst, w_peer(w_others[0])).wait_recv()

    def sent(kind, src):
        remote(kind, src, src, w_peer(w_others[0])).wait_send()

    loads = [
        pltpu.make_async_copy(src, dst, in_sem.at[n])
        for n, (src, dst) in enumerate(
            (
                (pk_hbm, pk), (pv_hbm, pv), (rw_hbm, rw), (mp_hbm, mp),
                (cq_hbm, cq), (go_hbm, go), (ck_hbm, ck), (cv_hbm, cv),
            )
        )
    ]
    for load in loads:
        load.start()

    barrier = pltpu.get_barrier_semaphore()
    for b in a_others:
        pl.semaphore_signal(barrier, inc=1, device_id=a_peer(b), device_id_type=MESH)
    for b in z_others:
        pl.semaphore_signal(barrier, inc=1, device_id=z_peer(b), device_id_type=MESH)
    for b in w_others:
        pl.semaphore_signal(barrier, inc=1, device_id=w_peer(b), device_id_type=MESH)

    for load in loads[:4]:
        load.wait()
    pos = mp[...]
    pos2 = jnp.concatenate([pos, pos], axis=1)
    live = pos < ROWS
    count = jnp.sum(jnp.where(live, 1.0, 0.0), axis=1, keepdims=True)
    reward = rw[...]
    lines = jnp.concatenate(
        [
            pk[...].astype(F32),
            pv[...].astype(F32),
            jnp.broadcast_to(count, (1, WIDTH)),
            jnp.broadcast_to(reward, (1, WIDTH)),
            jnp.zeros((2, WIDTH), F32),
        ],
        axis=0,
    )
    for h in range(HEADS):
        kvs[h] = lines[:, h * DIM : (h + 1) * DIM]

    pl.semaphore_wait(barrier, 21)

    for b in a_others:
        remote(KV, kvs.at[b], kvr.at[a], a_peer(b)).start()
    kvr[a] = kvs[a]

    row = lax.broadcasted_iota(jnp.int32, (ROWS, 2 * SLOTS), 0)
    pick = jnp.where(row == jnp.minimum(pos2, ROWS - 1), 1.0, 0.0).astype(BF16)
    loads[4].wait()
    picked = dot_tn(pick, cq[...])[:SLOTS].astype(BF16)
    loads[5].wait()
    for h in range(HEADS):
        xb[h, 0:SLOTS, :] = picked[:, h * DIM : (h + 1) * DIM]
        xb[h, SLOTS : 2 * SLOTS, :] = go[:, h * DIM : (h + 1) * DIM]

    arrived(KV, kvr.at[pl.ds(0, 15)])
    blocks = kvr[...]
    kvb[w, z_hi, 0, 0:16, :] = blocks[:, 0, :].astype(BF16)
    kvb[w, z_hi, 0, 16:32, :] = blocks[:, 1, :].astype(BF16)
    kvb[w, z_hi, 1, 0:16, :] = blocks[:, 2, :].astype(BF16)
    kvb[w, z_hi, 1, 16:32, :] = blocks[:, 3, :].astype(BF16)
    for b in z_others:
        remote(ZKV, kvb.at[w, z_hi], kvb.at[w, z_hi], z_peer(b)).start()
    mine = lax.broadcasted_iota(jnp.int32, (16, DIM), 0) // 4 == lax.div(a, 4)
    count16 = jnp.sum(jnp.where(mine, blocks[:, 4, :], 0.0), axis=0, keepdims=True)
    reward16 = jnp.sum(jnp.where(mine, blocks[:, 5, :], 0.0), axis=0, keepdims=True)
    gsum[...] = jnp.concatenate([count16, reward16, jnp.zeros((6, DIM), F32)], axis=0)
    for b in z_others:
        remote(ZSUM, gsum, gsumr.at[z_hi], z_peer(b)).start()

    for b in a_others:
        remote(QG, xb.at[b], xbr.at[a], a_peer(b)).start()
    xbr[a] = xb[a]

    def own_scores(h):
        q = xb[h, 0:SLOTS, :]
        g = xb[h, SLOTS : 2 * SLOTS, :]
        s = dot_nt(ck[:, h * DIM : (h + 1) * DIM], jnp.concatenate([q, q], axis=0)) * SCALE2
        d = dot_nt(cv[:, h * DIM : (h + 1) * DIM], jnp.concatenate([g, g], axis=0))
        m = jnp.max(s, axis=0, keepdims=True)
        e = jnp.exp2(s - m)
        own_e[h] = e
        own_d[h] = d
        st[h] = jnp.concatenate(
            [
                m,
                jnp.sum(e, axis=0, keepdims=True),
                jnp.sum(e * d, axis=0, keepdims=True),
                jnp.zeros((5, DIM), F32),
            ],
            axis=0,
        )

    loads[6].wait()
    loads[7].wait()
    for h in range(HEADS // 2):
        own_scores(h)

    arrived(ZKV, kvb.at[0, pl.ds(0, 3)])
    for b in w_others:
        remote(YKV, kvb.at[w], kvb.at[w], w_peer(b)).start()
    arrived(ZSUM, gsumr.at[pl.ds(0, 3)])
    total = gsum[...]
    for b in z_others:
        total = total + gsumr[b]
    gsum2[...] = total
    remote(XSUM, gsum2, gsumx, x_peer).start()
    for h in range(HEADS // 2, HEADS):
        own_scores(h)
    arrived(XSUM, gsumx)
    total = total + gsumx[...]
    weight = (reward - total[1:2] / 32.0) * (SLOTS * 32) / total[0:1]
    weight = jnp.where(pos2 < ROWS, weight, 0.0)
    for h in range(HEADS):
        st[h, 3:4, :] = weight
    for b in a_others:
        remote(OWN, st.at[b], str_.at[a], a_peer(b)).start()
    str_[a] = st[a]

    arrived(QG, xbr.at[pl.ds(0, 15)])
    arrived(YKV, kvb.at[pl.ds(0, 3)])
    arrived(OWN, str_.at[pl.ds(0, 15)])
    keys = kvb[:, :, 0].reshape(PROMPT, DIM)
    values = kvb[:, :, 1].reshape(PROMPT, DIM)
    left = lax.broadcasted_iota(jnp.int32, (8, DIM), 1) < SLOTS
    def pair(t, _):
        q = xbr[pl.ds(2 * t, 2), 0:SLOTS, :].reshape(2 * SLOTS, DIM)
        g = xbr[pl.ds(2 * t, 2), SLOTS : 2 * SLOTS, :].reshape(2 * SLOTS, DIM)
        s = dot_nt(keys, q) * SCALE2
        d = dot_nt(values, g)
        mp_ = jnp.max(s, axis=0, keepdims=True)
        e = jnp.exp2(s - mp_)
        lp = jnp.sum(e, axis=0, keepdims=True)
        ip = jnp.sum(e * d, axis=0, keepdims=True)
        stats = jnp.where(left, str_[2 * t], str_[2 * t + 1])
        mo, lo, io, tw = stats[0:1], stats[1:2], stats[2:3], stats[3:4]
        m = jnp.maximum(mp_, mo)
        fp = jnp.exp2(mp_ - m)
        fo = jnp.exp2(mo - m)
        inv = 1.0 / (lp * fp + lo * fo)
        inner = (ip * fp + io * fo) * inv
        coef = fp * inv * tw
        cols = pl.ds(pl.multiple_of(t * 128, 128), 128)
        p = (e * coef).astype(BF16)
        dsc = (e * (d - inner) * (coef * SCALE)).astype(BF16)
        pw[:, :, cols] = p.reshape(4, 128, 128)
        ds[:, :, cols] = dsc.reshape(4, 128, 128)
        final = jnp.concatenate([m, inv, inner, jnp.zeros((5, DIM), F32)], axis=0)
        fs[2 * t] = final
        fs[2 * t + 1] = final
        return 0

    lax.fori_loop(0, 8, pair, 0, unroll=2)

    q_all = xbr[:, 0:SLOTS, :].reshape(16 * SLOTS, DIM)
    g_all = xbr[:, SLOTS : 2 * SLOTS, :].reshape(16 * SLOTS, DIM)
    for b in w_others + [w]:
        grad_k = dot_nn(ds[b], q_all)
        grad_v = dot_nn(pw[b], g_all)
        if b is not w:
            sb1[b, 0] = grad_k.astype(BF16)
            sb1[b, 1] = grad_v.astype(BF16)
            remote(RS1, sb1.at[b], r1.at[w], w_peer(b)).start()
    for b in a_others:
        remote(FIN, fs.at[b], fr.at[a], a_peer(b)).start()
    fr[a] = fs[a]
    for t in range(8):
        grad_q = dot_tn(ds[:, :, t * 128 : (t + 1) * 128].reshape(PROMPT, 2 * SLOTS), keys)
        dqs[2 * t] = grad_q[:SLOTS].astype(BF16)
        dqs[2 * t + 1] = grad_q[SLOTS:].astype(BF16)
    for b in a_others:
        remote(DQ, dqs.at[b], dqr.at[a], a_peer(b)).start()
    dqr[a] = dqs[a]

    arrived(RS1, r1.at[pl.ds(0, 3)])
    for b in w_others:
        grad_k = grad_k + r1[b, 0].astype(F32)
        grad_v = grad_v + r1[b, 1].astype(F32)
    for b in range(4):
        sum1[b, 0] = grad_k[b * 32 : (b + 1) * 32]
        sum1[b, 1] = grad_v[b * 32 : (b + 1) * 32]
        sb2[b, 0] = grad_k[b * 32 : (b + 1) * 32].astype(BF16)
        sb2[b, 1] = grad_v[b * 32 : (b + 1) * 32].astype(BF16)
    for b in z_others:
        remote(RS2, sb2.at[b], r2.at[z_hi], z_peer(b)).start()

    arrived(FIN, fr.at[pl.ds(0, 15)])
    arrived(DQ, dqr.at[pl.ds(0, 15)])
    here = left == (lax.rem(a, 2) == 0)
    nothing = jnp.zeros((SLOTS, DIM), BF16)
    for h in range(HEADS):
        cols = slice(h * DIM, (h + 1) * DIM)
        fin = fr[h]
        fin = jnp.where(here, fin, jnp.concatenate([fin[:, SLOTS:], fin[:, :SLOTS]], axis=1))
        m, inv, inner = fin[0:1], fin[1:2], fin[2:3]
        coef = jnp.exp2(st[h, 0:1, :] - m) * inv * weight
        e = own_e[h]
        p = (e * coef).astype(BF16)
        dsc = (e * (own_d[h] - inner) * (coef * SCALE)).astype(BF16)
        dvo[:, cols] = dot_nn(p, jnp.concatenate([xb[h, SLOTS:, :], nothing], axis=0)).astype(BF16)
        dko[:, cols] = dot_nn(dsc, jnp.concatenate([xb[h, :SLOTS, :], nothing], axis=0)).astype(BF16)
        dqo[:, cols] = (dot_tn(dsc, ck[:, cols])[:SLOTS] + dqr[h].astype(F32)).astype(BF16)
    stores = [
        pltpu.make_async_copy(src, dst, out_sem.at[n])
        for n, (src, dst) in enumerate(
            ((dqo, dq_hbm), (dko, dk_hbm), (dvo, dv_hbm), (gko, gk_hbm), (gvo, gv_hbm))
        )
    ]
    for store in stores[:3]:
        store.start()

    arrived(RS2, r2.at[pl.ds(0, 3)])
    line = lax.broadcasted_iota(jnp.int32, (16, 8, DIM), 1)
    lines = jnp.zeros((16, 8, DIM), F32)
    for kv in range(2):
        part = sum1[z_hi, kv]
        for b in z_others:
            part = part + r2[b, kv].astype(F32)
        for r in range(2):
            lines = jnp.where(line == kv * 2 + r, part[r * 16 : (r + 1) * 16][:, None, :], lines)
    t3[...] = lines
    for b in a_others:
        remote(RS3, t3.at[b], r3.at[a], a_peer(b)).start()
    r3[a] = t3[a]
    arrived(RS3, r3.at[pl.ds(0, 15)])
    for h in range(HEADS):
        cols = slice(h * DIM, (h + 1) * DIM)
        gko[:, cols] = r3[h, 0:2, :].astype(BF16)
        gvo[:, cols] = r3[h, 2:4, :].astype(BF16)

    for store in stores[3:]:
        store.start()

    sent(KV, kvs.at[pl.ds(0, 15)])
    sent(QG, xb.at[pl.ds(0, 15)])
    sent(ZKV, kvb.at[0, pl.ds(0, 3)])
    sent(ZSUM, gsumr.at[pl.ds(0, 3)])
    sent(XSUM, gsum2)
    sent(YKV, kvb.at[pl.ds(0, 3)])
    sent(OWN, st.at[pl.ds(0, 15)])
    sent(FIN, fs.at[pl.ds(0, 15)])
    sent(DQ, dqs.at[pl.ds(0, 15)])
    sent(RS1, sb1.at[pl.ds(0, 3)])
    sent(RS2, sb2.at[pl.ds(0, 3)])
    sent(RS3, t3.at[pl.ds(0, 15)])
    for store in stores:
        store.wait()


def store_all(*refs):
    sources, targets, held, sem = refs[:5], refs[5:10], refs[10:15], refs[15]
    parts = []
    for n in range(5):
        rows = sources[n].shape[0]
        step = min(rows, SLOTS)
        for first in range(0, rows, step):
            parts.append((n, pl.ds(first, step)))
    loads = [
        pltpu.make_async_copy(sources[n].at[span], held[n].at[span], sem.at[0, p])
        for p, (n, span) in enumerate(parts)
    ]
    stores = [
        pltpu.make_async_copy(held[n].at[span], targets[n].at[span], sem.at[1, p])
        for p, (n, span) in enumerate(parts)
    ]
    for load in loads:
        load.start()
    for load, store in zip(loads, stores):
        load.wait()
        store.start()
    for store in stores:
        store.wait()


def shards(prompt_k, prompt_v, comp_q, comp_k, comp_v, grad_out, rewards, mask_pos):
    hbm = pl.BlockSpec(memory_space=pltpu.HBM)
    V = pltpu.VMEM
    grads = pl.pallas_call(
        kernel,
        out_shape=(
            jax.ShapeDtypeStruct((SLOTS, WIDTH), BF16),
            jax.ShapeDtypeStruct((ROWS, WIDTH), BF16),
            jax.ShapeDtypeStruct((ROWS, WIDTH), BF16),
            jax.ShapeDtypeStruct((2, WIDTH), BF16),
            jax.ShapeDtypeStruct((2, WIDTH), BF16),
        ),
        in_specs=[hbm] * 8,
        out_specs=(hbm,) * 5,
        scratch_shapes=[
            V((2, WIDTH), BF16),
            V((2, WIDTH), BF16),
            V((1, 1), F32),
            V((1, SLOTS), jnp.int32),
            V((ROWS, WIDTH), BF16),
            V((ROWS, WIDTH), BF16),
            V((ROWS, WIDTH), BF16),
            V((SLOTS, WIDTH), BF16),
            V((16, 128, DIM), BF16),
            V((16, 128, DIM), BF16),
            V((16, 8, DIM), F32),
            V((16, 8, DIM), F32),
            V((4, 4, 2, 32, DIM), BF16),
            V((8, DIM), F32),
            V((4, 8, DIM), F32),
            V((8, DIM), F32),
            V((8, DIM), F32),
            V((16, 128, DIM), F32),
            V((16, 128, DIM), F32),
            V((16, 8, DIM), F32),
            V((16, 8, DIM), F32),
            V((16, 8, DIM), F32),
            V((16, 8, DIM), F32),
            V((4, 128, 16 * SLOTS), BF16),
            V((4, 128, 16 * SLOTS), BF16),
            V((4, 2, 128, DIM), BF16),
            V((4, 2, 128, DIM), BF16),
            V((4, 2, 32, DIM), F32),
            V((4, 2, 32, DIM), BF16),
            V((4, 2, 32, DIM), BF16),
            V((16, 8, DIM), F32),
            V((16, 8, DIM), F32),
            V((16, SLOTS, DIM), BF16),
            V((16, SLOTS, DIM), BF16),
            V((SLOTS, WIDTH), BF16),
            V((ROWS, WIDTH), BF16),
            V((ROWS, WIDTH), BF16),
            V((2, WIDTH), BF16),
            V((2, WIDTH), BF16),
            pltpu.SemaphoreType.DMA((8,)),
            pltpu.SemaphoreType.DMA((5,)),
            pltpu.SemaphoreType.DMA((KINDS,)),
            pltpu.SemaphoreType.DMA((KINDS,)),
        ],
        compiler_params=pltpu.CompilerParams(
            collective_id=0, has_side_effects=True, vmem_limit_bytes=60 * 1024 * 1024
        ),
    )(
        prompt_k, prompt_v, rewards, mask_pos[0], comp_q[0, 0], comp_k[0, 0], comp_v[0, 0],
        grad_out[0, 0],
    )
    dq, dk, dv, gk, gv = pl.pallas_call(
        store_all,
        out_shape=[jax.ShapeDtypeStruct(grad.shape, BF16) for grad in grads],
        in_specs=[hbm] * 5,
        out_specs=[hbm] * 5,
        scratch_shapes=[V(grad.shape, BF16) for grad in grads] + [pltpu.SemaphoreType.DMA((2, 7))],
        compiler_params=pltpu.CompilerParams(vmem_limit_bytes=60 * 1024 * 1024),
    )(*grads)
    return dq[None, None], dk[None, None], dv[None, None], gk, gv


def solution(mesh):
    wide = P("grp", "ctx", None, None)
    rows = P(("grp", "ctx"), None)
    return jax.shard_map(
        shards,
        mesh=mesh,
        in_specs=(rows, rows, wide, wide, wide, wide, P("grp", "ctx"), P("grp", "ctx", None)),
        out_specs=(wide, wide, wide, rows, rows),
        check_vma=False,
    )
```

```python
import jax
import jax.numpy as jnp
from jax import lax
from jax.experimental import pallas as pl
from jax.experimental.pallas import tpu as pltpu
from jax.sharding import PartitionSpec as P

HEADS = 16
DIM = 128
SLOTS = 64
ROWS = 128
WIDTH = 2048
PROMPT = 512
F32 = jnp.float32
BF16 = jnp.bfloat16
SCALE = DIM ** -0.5
SCALE2 = SCALE * 1.4426950408889634
MESH = pl.DeviceIdType.MESH

(
    KV, QUERY, GRAD, ZK, ZV, ZSUM, YK, YV, OWN, FIN, DQ, YSUM_K, YSUM_V, ZSUM_K, ZSUM_V, OUT, KINDS
) = range(17)


def dot_nt(a, b):
    return lax.dot_general(a, b, (((1,), (1,)), ((), ())), preferred_element_type=F32)


def dot_nn(a, b):
    return lax.dot_general(a, b, (((1,), (0,)), ((), ())), preferred_element_type=F32)


def dot_tn(a, b):
    return lax.dot_general(a, b, (((0,), (0,)), ((), ())), preferred_element_type=F32)


def kernel(
    pk_hbm, pv_hbm, rw_hbm, mp_hbm, cq_hbm, ck_hbm, cv_hbm, go_hbm,
    dq_hbm, dk_hbm, dv_hbm, gk_hbm, gv_hbm,
    pk, pv, rw, mp, cq, ck, cv, go, xq, xqr, xg, xgr, kvs, kvr, kb, vb, gsum, gsumr, own_e, own_d, st, str_,
    fs, fr, exps, prods, part, pw, ds,
    sbk, sbv, rk, rv, hk, hv, szk, szv, rzk, rzv, t3, r3, dqs, dqr, dqo, dko, dvo, gko, gvo,
    in_sem, out_sem, ss, rs, ry,
):
    grp = lax.axis_index("grp")
    ctx = lax.axis_index("ctx")
    x_lo, y = lax.div(grp, 4), lax.rem(grp, 4)
    z = lax.div(ctx, 4)
    z_hi, z_lo, low = lax.div(z, 2), lax.rem(z, 2), lax.rem(ctx, 4)
    a = z_lo * 8 + x_lo * 4 + low

    def a_peer(b):
        return {
            "grp": lax.rem(lax.div(b, 4), 2) * 4 + y,
            "ctx": (z_hi * 2 + lax.div(b, 8)) * 4 + lax.rem(b, 4),
        }

    def z_peer(b):
        return {"grp": grp, "ctx": (b * 2 + z_lo) * 4 + low}

    def y_peer(b):
        return {"grp": x_lo * 4 + b, "ctx": ctx}

    a_others = [z_lo * 8 + lax.rem(a + k, 8) for k in range(1, 8)]
    a_others += [(1 - z_lo) * 8 + lax.rem(a + k, 8) for k in range(8)]
    z_others = [lax.rem(z_hi + k, 4) for k in range(1, 4)]
    y_others = [lax.rem(y + k, 4) for k in range(1, 4)]

    def remote(kind, src, dst, device):
        return pltpu.make_async_remote_copy(
            src_ref=src, dst_ref=dst, send_sem=ss.at[kind], recv_sem=rs.at[kind],
            device_id=device, device_id_type=MESH,
        )

    def along_y(kv, ref, row, b):
        return pltpu.make_async_remote_copy(
            src_ref=ref.at[row], dst_ref=ref.at[row], send_sem=ss.at[YK + kv],
            recv_sem=ry.at[kv, row], device_id=y_peer(b), device_id_type=MESH,
        )

    def arrived(kind, dst):
        remote(kind, dst, dst, y_peer(y_others[0])).wait_recv()

    def sent(kind, src):
        remote(kind, src, src, y_peer(y_others[0])).wait_send()

    loads = [
        pltpu.make_async_copy(src, dst, in_sem.at[n])
        for n, (src, dst) in enumerate(
            (
                (pk_hbm, pk), (pv_hbm, pv), (rw_hbm, rw), (mp_hbm, mp),
                (cq_hbm, cq), (go_hbm, go), (ck_hbm, ck), (cv_hbm, cv),
            )
        )
    ]
    for load in loads:
        load.start()

    barrier = pltpu.get_barrier_semaphore()
    for b in a_others:
        pl.semaphore_signal(barrier, inc=1, device_id=a_peer(b), device_id_type=MESH)
    for b in z_others:
        pl.semaphore_signal(barrier, inc=1, device_id=z_peer(b), device_id_type=MESH)
    for b in y_others:
        pl.semaphore_signal(barrier, inc=1, device_id=y_peer(b), device_id_type=MESH)

    for load in loads[:4]:
        load.wait()
    pos = mp[...]
    pos2 = jnp.concatenate([pos, pos], axis=1)
    live = pos < ROWS
    count = jnp.sum(jnp.where(live, 1.0, 0.0), axis=1, keepdims=True)
    reward = rw[...]
    lines = jnp.concatenate(
        [
            pk[...].astype(F32),
            pv[...].astype(F32),
            jnp.broadcast_to(count, (1, WIDTH)),
            jnp.broadcast_to(reward, (1, WIDTH)),
            jnp.zeros((2, WIDTH), F32),
        ],
        axis=0,
    )
    for h in range(HEADS):
        kvs[h] = lines[:, h * DIM : (h + 1) * DIM]

    pl.semaphore_wait(barrier, 21)

    for b in a_others:
        remote(KV, kvs.at[b], kvr.at[a], a_peer(b)).start()
    kvr[a] = kvs[a]

    row = lax.broadcasted_iota(jnp.int32, (ROWS, 2 * SLOTS), 0)
    pick = jnp.where(row == jnp.minimum(pos2, ROWS - 1), 1.0, 0.0).astype(BF16)
    loads[4].wait()
    picked = dot_tn(pick, cq[...])[:SLOTS].astype(BF16)
    for h in range(HEADS):
        xq[h] = picked[:, h * DIM : (h + 1) * DIM]
    for b in a_others:
        remote(QUERY, xq.at[b], xqr.at[a], a_peer(b)).start()
    xqr[a] = xq[a]
    loads[5].wait()
    for h in range(HEADS):
        xg[h] = go[:, h * DIM : (h + 1) * DIM]

    arrived(KV, kvr.at[pl.ds(0, 15)])
    blocks = kvr[...]
    kb[y, z_hi, 0:16, :] = blocks[:, 0, :].astype(BF16)
    kb[y, z_hi, 16:32, :] = blocks[:, 1, :].astype(BF16)
    for b in z_others:
        remote(ZK, kb.at[y, z_hi], kb.at[y, z_hi], z_peer(b)).start()
    vb[y, z_hi, 0:16, :] = blocks[:, 2, :].astype(BF16)
    vb[y, z_hi, 16:32, :] = blocks[:, 3, :].astype(BF16)
    for b in z_others:
        remote(ZV, vb.at[y, z_hi], vb.at[y, z_hi], z_peer(b)).start()
    mine = lax.broadcasted_iota(jnp.int32, (16, DIM), 0) // 4 % 2 == x_lo
    count16 = jnp.sum(jnp.where(mine, blocks[:, 4, :], 0.0), axis=0, keepdims=True)
    reward16 = jnp.sum(jnp.where(mine, blocks[:, 5, :], 0.0), axis=0, keepdims=True)
    gsum[...] = jnp.concatenate([count16, reward16, jnp.zeros((6, DIM), F32)], axis=0)
    for b in z_others:
        remote(ZSUM, gsum, gsumr.at[z_hi], z_peer(b)).start()
    for b in a_others:
        remote(GRAD, xg.at[b], xgr.at[a], a_peer(b)).start()
    xgr[a] = xg[a]

    def own_scores(h):
        q = xq[h]
        g = xg[h]
        s = dot_nt(ck[:, h * DIM : (h + 1) * DIM], jnp.concatenate([q, q], axis=0)) * SCALE2
        d = dot_nt(cv[:, h * DIM : (h + 1) * DIM], jnp.concatenate([g, g], axis=0))
        m = jnp.max(s, axis=0, keepdims=True)
        e = jnp.exp2(s - m)
        own_e[h] = e
        own_d[h] = d
        st[h] = jnp.concatenate(
            [
                m,
                jnp.sum(e, axis=0, keepdims=True),
                jnp.sum(e * d, axis=0, keepdims=True),
                jnp.zeros((5, DIM), F32),
            ],
            axis=0,
        )

    loads[6].wait()
    loads[7].wait()
    for h in range(4):
        own_scores(h)

    arrived(ZK, kb.at[0, pl.ds(0, 3)])
    for b in y_others:
        along_y(0, kb, y, b).start()
    arrived(ZV, vb.at[0, pl.ds(0, 3)])
    for b in y_others:
        along_y(1, vb, y, b).start()
    for h in range(4, HEADS):
        own_scores(h)
    arrived(ZSUM, gsumr.at[pl.ds(0, 3)])
    total = gsum[...]
    for b in z_others:
        total = total + gsumr[b]
    weight = (reward - total[1:2] / 32.0) * (SLOTS * 32) / total[0:1]
    weight = jnp.where(pos2 < ROWS, weight, 0.0)
    for h in range(HEADS):
        st[h, 3:4, :] = weight
    for b in a_others:
        remote(OWN, st.at[b], str_.at[a], a_peer(b)).start()
    str_[a] = st[a]

    def key_block(b):
        block = kb[b].reshape(128, DIM)
        for n in range(4):
            cols = slice(n * 256, (n + 1) * 256)
            s = dot_nt(block, xqr[4 * n : 4 * n + 4].reshape(256, DIM)) * SCALE2
            m = jnp.max(s, axis=0, keepdims=True)
            e = jnp.exp2(s - m)
            exps[b, :, cols] = e
            part[b, 0:1, cols] = m
            part[b, 1:2, cols] = jnp.sum(e, axis=0, keepdims=True)

    def value_block(b):
        block = vb[b].reshape(128, DIM)
        for n in range(4):
            cols = slice(n * 256, (n + 1) * 256)
            d = dot_nt(block, xgr[4 * n : 4 * n + 4].reshape(256, DIM)) * SCALE
            prods[b, :, cols] = d
            part[b, 2:3, cols] = jnp.sum(exps[b, :, cols] * d, axis=0, keepdims=True)

    near_first = [y_others[0], y_others[2], y_others[1]]
    far_first = [y_others[1], y_others[0], y_others[2]]
    arrived(QUERY, xqr.at[pl.ds(0, 15)])
    key_block(y)
    for b in near_first:
        along_y(0, kb, b, b).wait_recv()
        key_block(b)
    arrived(GRAD, xgr.at[pl.ds(0, 15)])
    value_block(y)
    for b in near_first:
        along_y(1, vb, b, b).wait_recv()
        value_block(b)

    arrived(OWN, str_.at[pl.ds(0, 15)])
    left = lax.broadcasted_iota(jnp.int32, (8, DIM), 1) < SLOTS
    stats = jnp.concatenate(
        [jnp.where(left, str_[2 * t], str_[2 * t + 1]) for t in range(8)], axis=1
    )
    m = stats[0:1]
    for b in range(4):
        m = jnp.maximum(m, part[b, 0:1, :])
    fo = jnp.exp2(stats[0:1] - m)
    total = stats[1:2] * fo
    inner = stats[2:3] * (fo * SCALE)
    for b in range(4):
        f = jnp.exp2(part[b, 0:1, :] - m)
        total = total + part[b, 1:2, :] * f
        inner = inner + part[b, 2:3, :] * f
        part[b, 3:4, :] = f
    inv = 1.0 / total
    inner = inner * inv
    weights = inv * stats[3:4]

    def finish(b):
        coef = part[b, 3:4, :] * weights
        for n in range(4):
            cols = slice(n * 256, (n + 1) * 256)
            p = exps[b, :, cols] * coef[:, cols]
            pw[b, :, cols] = p.astype(BF16)
            ds[b, :, cols] = (p * (prods[b, :, cols] - inner[:, cols])).astype(BF16)

    q_all = xqr[...].reshape(16 * SLOTS, DIM)
    g_all = xgr[...].reshape(16 * SLOTS, DIM)
    for b in far_first:
        finish(b)
        sbv[b] = dot_nn(pw[b], g_all).astype(BF16)
        remote(YSUM_V, sbv.at[b], rv.at[y], y_peer(b)).start()
    for b in far_first:
        sbk[b] = dot_nn(ds[b], q_all).astype(BF16)
        remote(YSUM_K, sbk.at[b], rk.at[y], y_peer(b)).start()
    finish(y)
    final = jnp.concatenate(
        [m, inv, inner * (1.0 / SCALE), jnp.zeros((5, 16 * SLOTS), F32)], axis=0
    )
    for t in range(8):
        fs[2 * t] = final[:, t * DIM : (t + 1) * DIM]
        fs[2 * t + 1] = final[:, t * DIM : (t + 1) * DIM]
    keys = kb[...].reshape(PROMPT, DIM)
    grad_v = dot_nn(pw[y], g_all)
    grad_k = dot_nn(ds[y], q_all)
    for b in a_others:
        remote(FIN, fs.at[b], fr.at[a], a_peer(b)).start()
    fr[a] = fs[a]
    for t in range(8):
        grad_q = dot_tn(ds[:, :, t * 128 : (t + 1) * 128].reshape(PROMPT, 2 * SLOTS), keys)
        dqs[2 * t] = grad_q[:SLOTS].astype(BF16)
        dqs[2 * t + 1] = grad_q[SLOTS:].astype(BF16)
    for b in a_others:
        remote(DQ, dqs.at[b], dqr.at[a], a_peer(b)).start()
    dqr[a] = dqs[a]

    def next_sum(total, kind_y, received, held, send, kind_z, target):
        arrived(kind_y, received.at[pl.ds(0, 3)])
        for b in y_others:
            total = total + received[b].astype(F32)
        held[...] = total.reshape(4, 32, DIM)
        send[...] = total.astype(BF16).reshape(4, 32, DIM)
        for b in z_others:
            remote(kind_z, send.at[b], target.at[z_hi], z_peer(b)).start()

    next_sum(grad_v, YSUM_V, rv, hv, szv, ZSUM_V, rzv)
    next_sum(grad_k, YSUM_K, rk, hk, szk, ZSUM_K, rzk)

    arrived(FIN, fr.at[pl.ds(0, 15)])
    arrived(DQ, dqr.at[pl.ds(0, 15)])
    here = left == (lax.rem(a, 2) == 0)
    nothing = jnp.zeros((SLOTS, DIM), BF16)
    for h in range(HEADS):
        cols = slice(h * DIM, (h + 1) * DIM)
        fin = fr[h]
        fin = jnp.where(here, fin, jnp.concatenate([fin[:, SLOTS:], fin[:, :SLOTS]], axis=1))
        m, inv, inner = fin[0:1], fin[1:2], fin[2:3]
        coef = jnp.exp2(st[h, 0:1, :] - m) * inv * weight
        e = own_e[h]
        p = (e * coef).astype(BF16)
        dsc = (e * (own_d[h] - inner) * (coef * SCALE)).astype(BF16)
        dvo[:, cols] = dot_nn(p, jnp.concatenate([xg[h], nothing], axis=0)).astype(BF16)
        dko[:, cols] = dot_nn(dsc, jnp.concatenate([xq[h], nothing], axis=0)).astype(BF16)
        dqo[:, cols] = (dot_tn(dsc, ck[:, cols])[:SLOTS] + dqr[h].astype(F32)).astype(BF16)
    stores = [
        pltpu.make_async_copy(src, dst, out_sem.at[n])
        for n, (src, dst) in enumerate(
            ((dqo, dq_hbm), (dko, dk_hbm), (dvo, dv_hbm), (gko, gk_hbm), (gvo, gv_hbm))
        )
    ]
    for store in stores[:3]:
        store.start()

    arrived(ZSUM_V, rzv.at[pl.ds(0, 3)])
    arrived(ZSUM_K, rzk.at[pl.ds(0, 3)])
    line = lax.broadcasted_iota(jnp.int32, (16, 8, DIM), 1)
    lines = jnp.zeros((16, 8, DIM), F32)
    for kv, (held, received) in enumerate(((hk, rzk), (hv, rzv))):
        part = held[z_hi]
        for b in z_others:
            part = part + received[b].astype(F32)
        for r in range(2):
            lines = jnp.where(line == kv * 2 + r, part[r * 16 : (r + 1) * 16][:, None, :], lines)
    t3[...] = lines
    for b in a_others:
        remote(OUT, t3.at[b], r3.at[a], a_peer(b)).start()
    r3[a] = t3[a]
    arrived(OUT, r3.at[pl.ds(0, 15)])
    for h in range(HEADS):
        cols = slice(h * DIM, (h + 1) * DIM)
        gko[:, cols] = r3[h, 0:2, :].astype(BF16)
        gvo[:, cols] = r3[h, 2:4, :].astype(BF16)

    for store in stores[3:]:
        store.start()

    sent(KV, kvs.at[pl.ds(0, 15)])
    sent(QUERY, xq.at[pl.ds(0, 15)])
    sent(GRAD, xg.at[pl.ds(0, 15)])
    sent(ZK, kb.at[0, pl.ds(0, 3)])
    sent(ZV, vb.at[0, pl.ds(0, 3)])
    sent(ZSUM, gsumr.at[pl.ds(0, 3)])
    sent(YK, kb.at[pl.ds(0, 3)])
    sent(YV, vb.at[pl.ds(0, 3)])
    sent(OWN, st.at[pl.ds(0, 15)])
    sent(FIN, fs.at[pl.ds(0, 15)])
    sent(DQ, dqs.at[pl.ds(0, 15)])
    sent(YSUM_V, sbv.at[pl.ds(0, 3)])
    sent(YSUM_K, sbk.at[pl.ds(0, 3)])
    sent(ZSUM_V, szv.at[pl.ds(0, 3)])
    sent(ZSUM_K, szk.at[pl.ds(0, 3)])
    sent(OUT, t3.at[pl.ds(0, 15)])
    for store in stores:
        store.wait()


def store_all(*refs):
    sources, targets, held, sem = refs[:5], refs[5:10], refs[10:15], refs[15]
    parts = []
    for n in range(5):
        rows = sources[n].shape[0]
        step = min(rows, SLOTS)
        for first in range(0, rows, step):
            parts.append((n, pl.ds(first, step)))
    loads = [
        pltpu.make_async_copy(sources[n].at[span], held[n].at[span], sem.at[0, p])
        for p, (n, span) in enumerate(parts)
    ]
    stores = [
        pltpu.make_async_copy(held[n].at[span], targets[n].at[span], sem.at[1, p])
        for p, (n, span) in enumerate(parts)
    ]
    for load in loads:
        load.start()
    for load, store in zip(loads, stores):
        load.wait()
        store.start()
    for store in stores:
        store.wait()


def shards(prompt_k, prompt_v, comp_q, comp_k, comp_v, grad_out, rewards, mask_pos):
    hbm = pl.BlockSpec(memory_space=pltpu.HBM)
    V = pltpu.VMEM
    grads = pl.pallas_call(
        kernel,
        out_shape=(
            jax.ShapeDtypeStruct((SLOTS, WIDTH), BF16),
            jax.ShapeDtypeStruct((ROWS, WIDTH), BF16),
            jax.ShapeDtypeStruct((ROWS, WIDTH), BF16),
            jax.ShapeDtypeStruct((2, WIDTH), BF16),
            jax.ShapeDtypeStruct((2, WIDTH), BF16),
        ),
        in_specs=[hbm] * 8,
        out_specs=(hbm,) * 5,
        scratch_shapes=[
            V((2, WIDTH), BF16),
            V((2, WIDTH), BF16),
            V((1, 1), F32),
            V((1, SLOTS), jnp.int32),
            V((ROWS, WIDTH), BF16),
            V((ROWS, WIDTH), BF16),
            V((ROWS, WIDTH), BF16),
            V((SLOTS, WIDTH), BF16),
            V((16, SLOTS, DIM), BF16),
            V((16, SLOTS, DIM), BF16),
            V((16, SLOTS, DIM), BF16),
            V((16, SLOTS, DIM), BF16),
            V((16, 8, DIM), F32),
            V((16, 8, DIM), F32),
            V((4, 4, 32, DIM), BF16),
            V((4, 4, 32, DIM), BF16),
            V((8, DIM), F32),
            V((4, 8, DIM), F32),
            V((16, 128, DIM), F32),
            V((16, 128, DIM), F32),
            V((16, 8, DIM), F32),
            V((16, 8, DIM), F32),
            V((16, 8, DIM), F32),
            V((16, 8, DIM), F32),
            V((4, 128, 16 * SLOTS), F32),
            V((4, 128, 16 * SLOTS), F32),
            V((4, 8, 16 * SLOTS), F32),
            V((4, 128, 16 * SLOTS), BF16),
            V((4, 128, 16 * SLOTS), BF16),
            V((4, 128, DIM), BF16),
            V((4, 128, DIM), BF16),
            V((4, 128, DIM), BF16),
            V((4, 128, DIM), BF16),
            V((4, 32, DIM), F32),
            V((4, 32, DIM), F32),
            V((4, 32, DIM), BF16),
            V((4, 32, DIM), BF16),
            V((4, 32, DIM), BF16),
            V((4, 32, DIM), BF16),
            V((16, 8, DIM), F32),
            V((16, 8, DIM), F32),
            V((16, SLOTS, DIM), BF16),
            V((16, SLOTS, DIM), BF16),
            V((SLOTS, WIDTH), BF16),
            V((ROWS, WIDTH), BF16),
            V((ROWS, WIDTH), BF16),
            V((2, WIDTH), BF16),
            V((2, WIDTH), BF16),
            pltpu.SemaphoreType.DMA((8,)),
            pltpu.SemaphoreType.DMA((5,)),
            pltpu.SemaphoreType.DMA((KINDS,)),
            pltpu.SemaphoreType.DMA((KINDS,)),
            pltpu.SemaphoreType.DMA((2, 4)),
        ],
        compiler_params=pltpu.CompilerParams(
            collective_id=0, has_side_effects=True, vmem_limit_bytes=60 * 1024 * 1024
        ),
    )(
        prompt_k, prompt_v, rewards, mask_pos[0], comp_q[0, 0], comp_k[0, 0], comp_v[0, 0],
        grad_out[0, 0],
    )
    dq, dk, dv, gk, gv = pl.pallas_call(
        store_all,
        out_shape=[jax.ShapeDtypeStruct(grad.shape, BF16) for grad in grads],
        in_specs=[hbm] * 5,
        out_specs=[hbm] * 5,
        scratch_shapes=[V(grad.shape, BF16) for grad in grads] + [pltpu.SemaphoreType.DMA((2, 7))],
        compiler_params=pltpu.CompilerParams(vmem_limit_bytes=60 * 1024 * 1024),
    )(*grads)
    return dq[None, None], dk[None, None], dv[None, None], gk, gv


def solution(mesh):
    wide = P("grp", "ctx", None, None)
    rows = P(("grp", "ctx"), None)
    return jax.shard_map(
        shards,
        mesh=mesh,
        in_specs=(rows, rows, wide, wide, wide, wide, P("grp", "ctx"), P("grp", "ctx", None)),
        out_specs=(wide, wide, wide, rows, rows),
        check_vma=False,
    )
```

```python
import jax
import jax.numpy as jnp
from jax import lax
from jax.experimental import pallas as pl
from jax.experimental.pallas import tpu as pltpu
from jax.sharding import PartitionSpec as P

HEADS = 16
DIM = 128
SLOTS = 64
ROWS = 128
WIDTH = 2048
PROMPT = 512
F32 = jnp.float32
BF16 = jnp.bfloat16
SCALE = DIM ** -0.5
SCALE2 = SCALE * 1.4426950408889634
MESH = pl.DeviceIdType.MESH

(
    KV, QUERY, GRAD, ZK, ZV, ZSUM, YK, YV, OWN, FIN, DQ, YSUM_K, YSUM_V, ZSUM_K, ZSUM_V, OUT, KINDS
) = range(17)


def dot_nt(a, b):
    return lax.dot_general(a, b, (((1,), (1,)), ((), ())), preferred_element_type=F32)


def dot_nn(a, b):
    return lax.dot_general(a, b, (((1,), (0,)), ((), ())), preferred_element_type=F32)


def dot_tn(a, b):
    return lax.dot_general(a, b, (((0,), (0,)), ((), ())), preferred_element_type=F32)


def kernel(
    pk_hbm, pv_hbm, rw_hbm, mp_hbm, cq_hbm, ck_hbm, cv_hbm, go_hbm,
    dq_hbm, dk_hbm, dv_hbm, gk_hbm, gv_hbm,
    pk, pv, rw, mp, cq, ck, cv, go, xq, xqr, xg, xgr, kvs, kvr, kb, vb, gsum, gsumr, own_e, own_d, st, str_,
    fs, fr, exps, prods, part, pw, ds,
    sbk, sbv, rk, rv, hk, hv, szk, szv, rzk, rzv, t3, r3, dqs, dqr, own_q, dqo, dko, dvo, gko, gvo,
    in_sem, out_sem, ss, rs, ry,
):
    grp = lax.axis_index("grp")
    ctx = lax.axis_index("ctx")
    x_lo, y = lax.div(grp, 4), lax.rem(grp, 4)
    z = lax.div(ctx, 4)
    z_hi, z_lo, low = lax.div(z, 2), lax.rem(z, 2), lax.rem(ctx, 4)
    a = z_lo * 8 + x_lo * 4 + low

    def a_peer(b):
        return {
            "grp": lax.rem(lax.div(b, 4), 2) * 4 + y,
            "ctx": (z_hi * 2 + lax.div(b, 8)) * 4 + lax.rem(b, 4),
        }

    def z_peer(b):
        return {"grp": grp, "ctx": (b * 2 + z_lo) * 4 + low}

    def y_peer(b):
        return {"grp": x_lo * 4 + b, "ctx": ctx}

    a_others = [z_lo * 8 + lax.rem(a + k, 8) for k in range(1, 8)]
    a_others += [(1 - z_lo) * 8 + lax.rem(a + k, 8) for k in range(8)]
    z_others = [lax.rem(z_hi + k, 4) for k in range(1, 4)]
    y_others = [lax.rem(y + k, 4) for k in range(1, 4)]

    def remote(kind, src, dst, device):
        return pltpu.make_async_remote_copy(
            src_ref=src, dst_ref=dst, send_sem=ss.at[kind], recv_sem=rs.at[kind],
            device_id=device, device_id_type=MESH,
        )

    def along_y(kv, ref, row, b):
        return pltpu.make_async_remote_copy(
            src_ref=ref.at[row], dst_ref=ref.at[row], send_sem=ss.at[YK + kv],
            recv_sem=ry.at[kv, row], device_id=y_peer(b), device_id_type=MESH,
        )

    def arrived(kind, dst):
        remote(kind, dst, dst, y_peer(y_others[0])).wait_recv()

    def sent(kind, src):
        remote(kind, src, src, y_peer(y_others[0])).wait_send()

    loads = [
        pltpu.make_async_copy(src, dst, in_sem.at[n])
        for n, (src, dst) in enumerate(
            (
                (pk_hbm, pk), (pv_hbm, pv), (rw_hbm, rw), (mp_hbm, mp),
                (cq_hbm, cq), (go_hbm, go), (ck_hbm, ck), (cv_hbm, cv),
            )
        )
    ]
    for load in loads:
        load.start()

    barrier = pltpu.get_barrier_semaphore()
    for b in a_others:
        pl.semaphore_signal(barrier, inc=1, device_id=a_peer(b), device_id_type=MESH)
    for b in z_others:
        pl.semaphore_signal(barrier, inc=1, device_id=z_peer(b), device_id_type=MESH)
    for b in y_others:
        pl.semaphore_signal(barrier, inc=1, device_id=y_peer(b), device_id_type=MESH)

    for load in loads[:4]:
        load.wait()
    pos = mp[...]
    pos2 = jnp.concatenate([pos, pos], axis=1)
    live = pos < ROWS
    count = jnp.sum(jnp.where(live, 1.0, 0.0), axis=1, keepdims=True)
    reward = rw[...]
    lines = jnp.concatenate(
        [
            pk[...].astype(F32),
            pv[...].astype(F32),
            jnp.broadcast_to(count, (1, WIDTH)),
            jnp.broadcast_to(reward, (1, WIDTH)),
            jnp.zeros((2, WIDTH), F32),
        ],
        axis=0,
    )
    for h in range(HEADS):
        kvs[h] = lines[:, h * DIM : (h + 1) * DIM]

    pl.semaphore_wait(barrier, 21)

    for b in a_others:
        remote(KV, kvs.at[b], kvr.at[a], a_peer(b)).start()
    kvr[a] = kvs[a]

    row = lax.broadcasted_iota(jnp.int32, (ROWS, 2 * SLOTS), 0)
    pick = jnp.where(row == jnp.minimum(pos2, ROWS - 1), 1.0, 0.0).astype(BF16)
    loads[4].wait()
    picked = dot_tn(pick, cq[...])[:SLOTS].astype(BF16)
    for h in range(HEADS):
        xq[h] = picked[:, h * DIM : (h + 1) * DIM]
    for b in a_others:
        remote(QUERY, xq.at[b], xqr.at[a], a_peer(b)).start()
    xqr[a] = xq[a]
    loads[5].wait()
    for h in range(HEADS):
        xg[h] = go[:, h * DIM : (h + 1) * DIM]

    arrived(KV, kvr.at[pl.ds(0, 15)])
    blocks = kvr[...]
    kb[y, z_hi, 0:16, :] = blocks[:, 0, :].astype(BF16)
    kb[y, z_hi, 16:32, :] = blocks[:, 1, :].astype(BF16)
    for b in z_others:
        remote(ZK, kb.at[y, z_hi], kb.at[y, z_hi], z_peer(b)).start()
    vb[y, z_hi, 0:16, :] = blocks[:, 2, :].astype(BF16)
    vb[y, z_hi, 16:32, :] = blocks[:, 3, :].astype(BF16)
    for b in z_others:
        remote(ZV, vb.at[y, z_hi], vb.at[y, z_hi], z_peer(b)).start()
    mine = lax.broadcasted_iota(jnp.int32, (16, DIM), 0) // 4 % 2 == x_lo
    count16 = jnp.sum(jnp.where(mine, blocks[:, 4, :], 0.0), axis=0, keepdims=True)
    reward16 = jnp.sum(jnp.where(mine, blocks[:, 5, :], 0.0), axis=0, keepdims=True)
    gsum[...] = jnp.concatenate([count16, reward16, jnp.zeros((6, DIM), F32)], axis=0)
    for b in z_others:
        remote(ZSUM, gsum, gsumr.at[z_hi], z_peer(b)).start()
    for b in a_others:
        remote(GRAD, xg.at[b], xgr.at[a], a_peer(b)).start()
    xgr[a] = xg[a]

    def own_scores(h):
        q = xq[h]
        g = xg[h]
        s = dot_nt(ck[:, h * DIM : (h + 1) * DIM], jnp.concatenate([q, q], axis=0)) * SCALE2
        d = dot_nt(cv[:, h * DIM : (h + 1) * DIM], jnp.concatenate([g, g], axis=0))
        m = jnp.max(s, axis=0, keepdims=True)
        e = jnp.exp2(s - m)
        own_e[h] = e
        own_d[h] = d
        st[h] = jnp.concatenate(
            [
                m,
                jnp.sum(e, axis=0, keepdims=True),
                jnp.sum(e * d, axis=0, keepdims=True),
                jnp.zeros((5, DIM), F32),
            ],
            axis=0,
        )

    loads[6].wait()
    loads[7].wait()
    for h in range(4):
        own_scores(h)

    arrived(ZK, kb.at[0, pl.ds(0, 3)])
    for b in y_others:
        along_y(0, kb, y, b).start()
    arrived(ZV, vb.at[0, pl.ds(0, 3)])
    for b in y_others:
        along_y(1, vb, y, b).start()
    for h in range(4, HEADS):
        own_scores(h)
    arrived(ZSUM, gsumr.at[pl.ds(0, 3)])
    total = gsum[...]
    for b in z_others:
        total = total + gsumr[b]
    weight = (reward - total[1:2] / 32.0) * (SLOTS * 32) / total[0:1]
    weight = jnp.where(pos2 < ROWS, weight, 0.0)
    for h in range(HEADS):
        st[h, 3:4, :] = weight
    for b in a_others:
        remote(OWN, st.at[b], str_.at[a], a_peer(b)).start()
    str_[a] = st[a]

    def key_block(b):
        block = kb[b].reshape(128, DIM)
        for n in range(4):
            cols = slice(n * 256, (n + 1) * 256)
            s = dot_nt(block, xqr[4 * n : 4 * n + 4].reshape(256, DIM)) * SCALE2
            m = jnp.max(s, axis=0, keepdims=True)
            e = jnp.exp2(s - m)
            exps[b, :, cols] = e
            part[b, 0:1, cols] = m
            part[b, 1:2, cols] = jnp.sum(e, axis=0, keepdims=True)

    def value_block(b):
        block = vb[b].reshape(128, DIM)
        for n in range(4):
            cols = slice(n * 256, (n + 1) * 256)
            d = dot_nt(block, xgr[4 * n : 4 * n + 4].reshape(256, DIM)) * SCALE
            prods[b, :, cols] = d
            part[b, 2:3, cols] = jnp.sum(exps[b, :, cols] * d, axis=0, keepdims=True)

    near_first = [y_others[0], y_others[2], y_others[1]]
    far_first = [y_others[1], y_others[0], y_others[2]]
    arrived(QUERY, xqr.at[pl.ds(0, 15)])
    key_block(y)
    for b in near_first:
        along_y(0, kb, b, b).wait_recv()
        key_block(b)
    arrived(GRAD, xgr.at[pl.ds(0, 15)])
    value_block(y)
    for b in near_first:
        along_y(1, vb, b, b).wait_recv()
        value_block(b)

    arrived(OWN, str_.at[pl.ds(0, 15)])
    left = lax.broadcasted_iota(jnp.int32, (8, DIM), 1) < SLOTS
    stats = jnp.concatenate(
        [jnp.where(left, str_[2 * t], str_[2 * t + 1]) for t in range(8)], axis=1
    )
    m = stats[0:1]
    for b in range(4):
        m = jnp.maximum(m, part[b, 0:1, :])
    fo = jnp.exp2(stats[0:1] - m)
    total = stats[1:2] * fo
    inner = stats[2:3] * (fo * SCALE)
    for b in range(4):
        f = jnp.exp2(part[b, 0:1, :] - m)
        total = total + part[b, 1:2, :] * f
        inner = inner + part[b, 2:3, :] * f
        part[b, 3:4, :] = f
    inv = 1.0 / total
    inner = inner * inv
    weights = inv * stats[3:4]

    def finish(b):
        coef = part[b, 3:4, :] * weights
        for n in range(4):
            cols = slice(n * 256, (n + 1) * 256)
            p = exps[b, :, cols] * coef[:, cols]
            pw[b, :, cols] = p.astype(BF16)
            ds[b, :, cols] = (p * (prods[b, :, cols] - inner[:, cols])).astype(BF16)

    q_all = xqr[...].reshape(16 * SLOTS, DIM)
    g_all = xgr[...].reshape(16 * SLOTS, DIM)
    for b in far_first:
        finish(b)
        sbv[b] = dot_nn(pw[b], g_all).astype(BF16)
        remote(YSUM_V, sbv.at[b], rv.at[y], y_peer(b)).start()
    for b in far_first:
        sbk[b] = dot_nn(ds[b], q_all).astype(BF16)
        remote(YSUM_K, sbk.at[b], rk.at[y], y_peer(b)).start()
    finish(y)
    final = jnp.concatenate(
        [m, inv, inner * (1.0 / SCALE), jnp.zeros((5, 16 * SLOTS), F32)], axis=0
    )
    for t in range(8):
        fs[2 * t] = final[:, t * DIM : (t + 1) * DIM]
        fs[2 * t + 1] = final[:, t * DIM : (t + 1) * DIM]
    keys = kb[...].reshape(PROMPT, DIM)
    grad_v = dot_nn(pw[y], g_all)
    grad_k = dot_nn(ds[y], q_all)
    for b in a_others:
        remote(FIN, fs.at[b], fr.at[a], a_peer(b)).start()
    fr[a] = fs[a]
    for t in range(8):
        grad_q = dot_tn(ds[:, :, t * 128 : (t + 1) * 128].reshape(PROMPT, 2 * SLOTS), keys)
        dqs[2 * t] = grad_q[:SLOTS].astype(BF16)
        dqs[2 * t + 1] = grad_q[SLOTS:].astype(BF16)
    for b in a_others:
        remote(DQ, dqs.at[b], dqr.at[a], a_peer(b)).start()
    dqr[a] = dqs[a]

    def next_sum(total, kind_y, received, held, send, kind_z, target):
        arrived(kind_y, received.at[pl.ds(0, 3)])
        for b in y_others:
            total = total + received[b].astype(F32)
        held[...] = total.reshape(4, 32, DIM)
        send[...] = total.astype(BF16).reshape(4, 32, DIM)
        for b in z_others:
            remote(kind_z, send.at[b], target.at[z_hi], z_peer(b)).start()

    next_sum(grad_v, YSUM_V, rv, hv, szv, ZSUM_V, rzv)
    next_sum(grad_k, YSUM_K, rk, hk, szk, ZSUM_K, rzk)

    arrived(FIN, fr.at[pl.ds(0, 15)])
    here = left == (lax.rem(a, 2) == 0)
    nothing = jnp.zeros((SLOTS, DIM), BF16)
    for h in range(HEADS):
        cols = slice(h * DIM, (h + 1) * DIM)
        fin = fr[h]
        fin = jnp.where(here, fin, jnp.concatenate([fin[:, SLOTS:], fin[:, :SLOTS]], axis=1))
        m, inv, inner = fin[0:1], fin[1:2], fin[2:3]
        coef = jnp.exp2(st[h, 0:1, :] - m) * inv * weight
        e = own_e[h]
        p = (e * coef).astype(BF16)
        dsc = (e * (own_d[h] - inner) * (coef * SCALE)).astype(BF16)
        dvo[:, cols] = dot_nn(p, jnp.concatenate([xg[h], nothing], axis=0)).astype(BF16)
        dko[:, cols] = dot_nn(dsc, jnp.concatenate([xq[h], nothing], axis=0)).astype(BF16)
        own_q[h] = dot_tn(dsc, ck[:, cols])[:SLOTS]
    stores = [
        pltpu.make_async_copy(src, dst, out_sem.at[n])
        for n, (src, dst) in enumerate(
            ((dqo, dq_hbm), (dko, dk_hbm), (dvo, dv_hbm), (gko, gk_hbm), (gvo, gv_hbm))
        )
    ]
    for store in stores[1:3]:
        store.start()

    arrived(ZSUM_V, rzv.at[pl.ds(0, 3)])
    arrived(ZSUM_K, rzk.at[pl.ds(0, 3)])
    line = lax.broadcasted_iota(jnp.int32, (16, 8, DIM), 1)
    lines = jnp.zeros((16, 8, DIM), F32)
    for kv, (held, received) in enumerate(((hk, rzk), (hv, rzv))):
        part = held[z_hi]
        for b in z_others:
            part = part + received[b].astype(F32)
        for r in range(2):
            lines = jnp.where(line == kv * 2 + r, part[r * 16 : (r + 1) * 16][:, None, :], lines)
    t3[...] = lines
    for b in a_others:
        remote(OUT, t3.at[b], r3.at[a], a_peer(b)).start()
    r3[a] = t3[a]
    arrived(DQ, dqr.at[pl.ds(0, 15)])
    for h in range(HEADS):
        dqo[:, h * DIM : (h + 1) * DIM] = (own_q[h] + dqr[h].astype(F32)).astype(BF16)
    stores[0].start()
    arrived(OUT, r3.at[pl.ds(0, 15)])
    for h in range(HEADS):
        cols = slice(h * DIM, (h + 1) * DIM)
        gko[:, cols] = r3[h, 0:2, :].astype(BF16)
        gvo[:, cols] = r3[h, 2:4, :].astype(BF16)

    for store in stores[3:]:
        store.start()

    sent(KV, kvs.at[pl.ds(0, 15)])
    sent(QUERY, xq.at[pl.ds(0, 15)])
    sent(GRAD, xg.at[pl.ds(0, 15)])
    sent(ZK, kb.at[0, pl.ds(0, 3)])
    sent(ZV, vb.at[0, pl.ds(0, 3)])
    sent(ZSUM, gsumr.at[pl.ds(0, 3)])
    sent(YK, kb.at[pl.ds(0, 3)])
    sent(YV, vb.at[pl.ds(0, 3)])
    sent(OWN, st.at[pl.ds(0, 15)])
    sent(FIN, fs.at[pl.ds(0, 15)])
    sent(DQ, dqs.at[pl.ds(0, 15)])
    sent(YSUM_V, sbv.at[pl.ds(0, 3)])
    sent(YSUM_K, sbk.at[pl.ds(0, 3)])
    sent(ZSUM_V, szv.at[pl.ds(0, 3)])
    sent(ZSUM_K, szk.at[pl.ds(0, 3)])
    sent(OUT, t3.at[pl.ds(0, 15)])
    for store in stores:
        store.wait()


def store_all(*refs):
    sources, targets, held, sem = refs[:5], refs[5:10], refs[10:15], refs[15]
    parts = []
    for n in range(5):
        rows = sources[n].shape[0]
        step = min(rows, 32)
        for first in range(0, rows, step):
            parts.append((n, pl.ds(first, step)))
    loads = [
        pltpu.make_async_copy(sources[n].at[span], held[n].at[span], sem.at[0, p])
        for p, (n, span) in enumerate(parts)
    ]
    stores = [
        pltpu.make_async_copy(held[n].at[span], targets[n].at[span], sem.at[1, p])
        for p, (n, span) in enumerate(parts)
    ]
    for load in loads:
        load.start()
    for load, store in zip(loads, stores):
        load.wait()
        store.start()
    for store in stores:
        store.wait()


def shards(prompt_k, prompt_v, comp_q, comp_k, comp_v, grad_out, rewards, mask_pos):
    hbm = pl.BlockSpec(memory_space=pltpu.HBM)
    V = pltpu.VMEM
    grads = pl.pallas_call(
        kernel,
        out_shape=(
            jax.ShapeDtypeStruct((SLOTS, WIDTH), BF16),
            jax.ShapeDtypeStruct((ROWS, WIDTH), BF16),
            jax.ShapeDtypeStruct((ROWS, WIDTH), BF16),
            jax.ShapeDtypeStruct((2, WIDTH), BF16),
            jax.ShapeDtypeStruct((2, WIDTH), BF16),
        ),
        in_specs=[hbm] * 8,
        out_specs=(hbm,) * 5,
        scratch_shapes=[
            V((2, WIDTH), BF16),
            V((2, WIDTH), BF16),
            V((1, 1), F32),
            V((1, SLOTS), jnp.int32),
            V((ROWS, WIDTH), BF16),
            V((ROWS, WIDTH), BF16),
            V((ROWS, WIDTH), BF16),
            V((SLOTS, WIDTH), BF16),
            V((16, SLOTS, DIM), BF16),
            V((16, SLOTS, DIM), BF16),
            V((16, SLOTS, DIM), BF16),
            V((16, SLOTS, DIM), BF16),
            V((16, 8, DIM), F32),
            V((16, 8, DIM), F32),
            V((4, 4, 32, DIM), BF16),
            V((4, 4, 32, DIM), BF16),
            V((8, DIM), F32),
            V((4, 8, DIM), F32),
            V((16, 128, DIM), F32),
            V((16, 128, DIM), F32),
            V((16, 8, DIM), F32),
            V((16, 8, DIM), F32),
            V((16, 8, DIM), F32),
            V((16, 8, DIM), F32),
            V((4, 128, 16 * SLOTS), F32),
            V((4, 128, 16 * SLOTS), F32),
            V((4, 8, 16 * SLOTS), F32),
            V((4, 128, 16 * SLOTS), BF16),
            V((4, 128, 16 * SLOTS), BF16),
            V((4, 128, DIM), BF16),
            V((4, 128, DIM), BF16),
            V((4, 128, DIM), BF16),
            V((4, 128, DIM), BF16),
            V((4, 32, DIM), F32),
            V((4, 32, DIM), F32),
            V((4, 32, DIM), BF16),
            V((4, 32, DIM), BF16),
            V((4, 32, DIM), BF16),
            V((4, 32, DIM), BF16),
            V((16, 8, DIM), F32),
            V((16, 8, DIM), F32),
            V((16, SLOTS, DIM), BF16),
            V((16, SLOTS, DIM), BF16),
            V((16, SLOTS, DIM), F32),
            V((SLOTS, WIDTH), BF16),
            V((ROWS, WIDTH), BF16),
            V((ROWS, WIDTH), BF16),
            V((2, WIDTH), BF16),
            V((2, WIDTH), BF16),
            pltpu.SemaphoreType.DMA((8,)),
            pltpu.SemaphoreType.DMA((5,)),
            pltpu.SemaphoreType.DMA((KINDS,)),
            pltpu.SemaphoreType.DMA((KINDS,)),
            pltpu.SemaphoreType.DMA((2, 4)),
        ],
        compiler_params=pltpu.CompilerParams(
            collective_id=0, has_side_effects=True, vmem_limit_bytes=60 * 1024 * 1024
        ),
    )(
        prompt_k, prompt_v, rewards, mask_pos[0], comp_q[0, 0], comp_k[0, 0], comp_v[0, 0],
        grad_out[0, 0],
    )
    dq, dk, dv, gk, gv = pl.pallas_call(
        store_all,
        out_shape=[jax.ShapeDtypeStruct(grad.shape, BF16) for grad in grads],
        in_specs=[hbm] * 5,
        out_specs=[hbm] * 5,
        scratch_shapes=[V(grad.shape, BF16) for grad in grads] + [pltpu.SemaphoreType.DMA((2, 12))],
        compiler_params=pltpu.CompilerParams(vmem_limit_bytes=60 * 1024 * 1024),
    )(*grads)
    return dq[None, None], dk[None, None], dv[None, None], gk, gv


def solution(mesh):
    wide = P("grp", "ctx", None, None)
    rows = P(("grp", "ctx"), None)
    return jax.shard_map(
        shards,
        mesh=mesh,
        in_specs=(rows, rows, wide, wide, wide, wide, P("grp", "ctx"), P("grp", "ctx", None)),
        out_specs=(wide, wide, wide, rows, rows),
        check_vma=False,
    )
```

```python
import jax
import jax.numpy as jnp
from jax import lax
from jax.experimental import pallas as pl
from jax.experimental.pallas import tpu as pltpu
from jax.sharding import PartitionSpec as P

HEADS = 16
DIM = 128
SLOTS = 64
ROWS = 128
WIDTH = 2048
PROMPT = 512
F32 = jnp.float32
BF16 = jnp.bfloat16
SCALE = DIM ** -0.5
SCALE2 = SCALE * 1.4426950408889634
MESH = pl.DeviceIdType.MESH

(
    KV, QUERY, GRAD, ZK, ZV, ZSUM, YK, YV, OWN, FIN, DQ, YSUM_K, YSUM_V, ZSUM_K, ZSUM_V, OUT, KINDS
) = range(17)


def dot_nt(a, b):
    return lax.dot_general(a, b, (((1,), (1,)), ((), ())), preferred_element_type=F32)


def dot_nn(a, b):
    return lax.dot_general(a, b, (((1,), (0,)), ((), ())), preferred_element_type=F32)


def dot_tn(a, b):
    return lax.dot_general(a, b, (((0,), (0,)), ((), ())), preferred_element_type=F32)


def kernel(
    pk_hbm, pv_hbm, rw_hbm, mp_hbm, cq_hbm, ck_hbm, cv_hbm, go_hbm,
    dq_hbm, dk_hbm, dv_hbm, gk_hbm, gv_hbm,
    pk, pv, rw, mp, cq, ck, cv, go, xq, xqr, xg, xgr, kvs, kvr, kb, vb, gsum, gsumr, own_e, own_d, st, str_,
    fs, fr, exps, prods, part, pw, ds,
    sbk, sbv, rk, rv, hk, hv, szk, szv, rzk, rzv, t3, r3, dqs, dqr, own_q, dqo, dko, dvo, gko, gvo,
    in_sem, out_sem, ss, rs, ry,
):
    grp = lax.axis_index("grp")
    ctx = lax.axis_index("ctx")
    x_lo, y = lax.div(grp, 4), lax.rem(grp, 4)
    z = lax.div(ctx, 4)
    z_hi, z_lo, low = lax.div(z, 2), lax.rem(z, 2), lax.rem(ctx, 4)
    a = z_lo * 8 + x_lo * 4 + low

    def a_peer(b):
        return {
            "grp": lax.rem(lax.div(b, 4), 2) * 4 + y,
            "ctx": (z_hi * 2 + lax.div(b, 8)) * 4 + lax.rem(b, 4),
        }

    def z_peer(b):
        return {"grp": grp, "ctx": (b * 2 + z_lo) * 4 + low}

    def y_peer(b):
        return {"grp": x_lo * 4 + b, "ctx": ctx}

    a_same_z = [z_lo * 8 + lax.rem(a + k, 8) for k in range(1, 8)]
    a_other_z = [(1 - z_lo) * 8 + lax.rem(a + k, 8) for k in range(8)]
    a_others = a_same_z + a_other_z
    z_others = [lax.rem(z_hi + k, 4) for k in range(1, 4)]
    y_others = [lax.rem(y + k, 4) for k in range(1, 4)]

    def remote(kind, src, dst, device):
        return pltpu.make_async_remote_copy(
            src_ref=src, dst_ref=dst, send_sem=ss.at[kind], recv_sem=rs.at[kind],
            device_id=device, device_id_type=MESH,
        )

    def along_y(kv, ref, row, b):
        return pltpu.make_async_remote_copy(
            src_ref=ref.at[row], dst_ref=ref.at[row], send_sem=ss.at[YK + kv],
            recv_sem=ry.at[kv, row], device_id=y_peer(b), device_id_type=MESH,
        )

    def arrived(kind, dst):
        remote(kind, dst, dst, y_peer(y_others[0])).wait_recv()

    def sent(kind, src):
        remote(kind, src, src, y_peer(y_others[0])).wait_send()

    loads = [
        pltpu.make_async_copy(src, dst, in_sem.at[n])
        for n, (src, dst) in enumerate(
            (
                (pk_hbm, pk), (pv_hbm, pv), (rw_hbm, rw), (mp_hbm, mp),
                (cq_hbm, cq), (go_hbm, go), (ck_hbm, ck), (cv_hbm, cv),
            )
        )
    ]
    for load in loads:
        load.start()

    barrier = pltpu.get_barrier_semaphore()
    for b in a_others:
        pl.semaphore_signal(barrier, inc=1, device_id=a_peer(b), device_id_type=MESH)
    for b in z_others:
        pl.semaphore_signal(barrier, inc=1, device_id=z_peer(b), device_id_type=MESH)
    for b in y_others:
        pl.semaphore_signal(barrier, inc=1, device_id=y_peer(b), device_id_type=MESH)

    for load in loads[:4]:
        load.wait()
    pos = mp[...]
    pos2 = jnp.concatenate([pos, pos], axis=1)
    live = pos < ROWS
    count = jnp.sum(jnp.where(live, 1.0, 0.0), axis=1, keepdims=True)
    reward = rw[...]
    lines = jnp.concatenate(
        [
            pk[...].astype(F32),
            pv[...].astype(F32),
            jnp.broadcast_to(count, (1, WIDTH)),
            jnp.broadcast_to(reward, (1, WIDTH)),
            jnp.zeros((2, WIDTH), F32),
        ],
        axis=0,
    )
    for h in range(HEADS):
        kvs[h] = lines[:, h * DIM : (h + 1) * DIM]

    pl.semaphore_wait(barrier, 21)

    for b in a_others:
        remote(KV, kvs.at[b], kvr.at[a], a_peer(b)).start()
    kvr[a] = kvs[a]

    row = lax.broadcasted_iota(jnp.int32, (ROWS, 2 * SLOTS), 0)
    pick = jnp.where(row == jnp.minimum(pos2, ROWS - 1), 1.0, 0.0).astype(BF16)
    loads[4].wait()
    picked = dot_tn(pick, cq[...])[:SLOTS].astype(BF16)
    for h in range(HEADS):
        xq[h] = picked[:, h * DIM : (h + 1) * DIM]
    for b in a_same_z:
        remote(QUERY, xq.at[b], xqr.at[a], a_peer(b)).start()
    xqr[a] = xq[a]
    loads[5].wait()
    for h in range(HEADS):
        xg[h] = go[:, h * DIM : (h + 1) * DIM]
    for b in a_same_z:
        remote(GRAD, xg.at[b], xgr.at[a], a_peer(b)).start()
    xgr[a] = xg[a]

    arrived(KV, kvr.at[pl.ds(0, 15)])
    blocks = kvr[...]
    kb[y, z_hi, 0:16, :] = blocks[:, 0, :].astype(BF16)
    kb[y, z_hi, 16:32, :] = blocks[:, 1, :].astype(BF16)
    for b in z_others:
        remote(ZK, kb.at[y, z_hi], kb.at[y, z_hi], z_peer(b)).start()
    vb[y, z_hi, 0:16, :] = blocks[:, 2, :].astype(BF16)
    vb[y, z_hi, 16:32, :] = blocks[:, 3, :].astype(BF16)
    for b in z_others:
        remote(ZV, vb.at[y, z_hi], vb.at[y, z_hi], z_peer(b)).start()
    mine = lax.broadcasted_iota(jnp.int32, (16, DIM), 0) // 4 % 2 == x_lo
    count16 = jnp.sum(jnp.where(mine, blocks[:, 4, :], 0.0), axis=0, keepdims=True)
    reward16 = jnp.sum(jnp.where(mine, blocks[:, 5, :], 0.0), axis=0, keepdims=True)
    gsum[...] = jnp.concatenate([count16, reward16, jnp.zeros((6, DIM), F32)], axis=0)
    for b in z_others:
        remote(ZSUM, gsum, gsumr.at[z_hi], z_peer(b)).start()
    for b in a_other_z:
        remote(QUERY, xq.at[b], xqr.at[a], a_peer(b)).start()
    for b in a_other_z:
        remote(GRAD, xg.at[b], xgr.at[a], a_peer(b)).start()

    def own_scores(h):
        q = xq[h]
        g = xg[h]
        s = dot_nt(ck[:, h * DIM : (h + 1) * DIM], jnp.concatenate([q, q], axis=0)) * SCALE2
        d = dot_nt(cv[:, h * DIM : (h + 1) * DIM], jnp.concatenate([g, g], axis=0))
        m = jnp.max(s, axis=0, keepdims=True)
        e = jnp.exp2(s - m)
        own_e[h] = e
        own_d[h] = d
        st[h] = jnp.concatenate(
            [
                m,
                jnp.sum(e, axis=0, keepdims=True),
                jnp.sum(e * d, axis=0, keepdims=True),
                jnp.zeros((5, DIM), F32),
            ],
            axis=0,
        )

    loads[6].wait()
    loads[7].wait()
    for h in range(4):
        own_scores(h)

    arrived(ZK, kb.at[0, pl.ds(0, 3)])
    for b in y_others:
        along_y(0, kb, y, b).start()
    arrived(ZV, vb.at[0, pl.ds(0, 3)])
    for b in y_others:
        along_y(1, vb, y, b).start()
    for h in range(4, HEADS):
        own_scores(h)
    arrived(ZSUM, gsumr.at[pl.ds(0, 3)])
    total = gsum[...]
    for b in z_others:
        total = total + gsumr[b]
    weight = (reward - total[1:2] / 32.0) * (SLOTS * 32) / total[0:1]
    weight = jnp.where(pos2 < ROWS, weight, 0.0)
    for h in range(HEADS):
        st[h, 3:4, :] = weight
    for b in a_others:
        remote(OWN, st.at[b], str_.at[a], a_peer(b)).start()
    str_[a] = st[a]

    def key_block(b):
        block = kb[b].reshape(128, DIM)
        for n in range(4):
            cols = slice(n * 256, (n + 1) * 256)
            s = dot_nt(block, xqr[4 * n : 4 * n + 4].reshape(256, DIM)) * SCALE2
            m = jnp.max(s, axis=0, keepdims=True)
            e = jnp.exp2(s - m)
            exps[b, :, cols] = e
            part[b, 0:1, cols] = m
            part[b, 1:2, cols] = jnp.sum(e, axis=0, keepdims=True)

    def value_block(b):
        block = vb[b].reshape(128, DIM)
        for n in range(4):
            cols = slice(n * 256, (n + 1) * 256)
            d = dot_nt(block, xgr[4 * n : 4 * n + 4].reshape(256, DIM)) * SCALE
            prods[b, :, cols] = d
            part[b, 2:3, cols] = jnp.sum(exps[b, :, cols] * d, axis=0, keepdims=True)

    near_first = [y_others[0], y_others[2], y_others[1]]
    far_first = [y_others[1], y_others[0], y_others[2]]
    arrived(QUERY, xqr.at[pl.ds(0, 15)])
    key_block(y)
    for b in near_first:
        along_y(0, kb, b, b).wait_recv()
        key_block(b)
    arrived(GRAD, xgr.at[pl.ds(0, 15)])
    value_block(y)
    for b in near_first:
        along_y(1, vb, b, b).wait_recv()
        value_block(b)

    arrived(OWN, str_.at[pl.ds(0, 15)])
    left = lax.broadcasted_iota(jnp.int32, (8, DIM), 1) < SLOTS
    stats = jnp.concatenate(
        [jnp.where(left, str_[2 * t], str_[2 * t + 1]) for t in range(8)], axis=1
    )
    m = stats[0:1]
    for b in range(4):
        m = jnp.maximum(m, part[b, 0:1, :])
    fo = jnp.exp2(stats[0:1] - m)
    total = stats[1:2] * fo
    inner = stats[2:3] * (fo * SCALE)
    for b in range(4):
        f = jnp.exp2(part[b, 0:1, :] - m)
        total = total + part[b, 1:2, :] * f
        inner = inner + part[b, 2:3, :] * f
        part[b, 3:4, :] = f
    inv = 1.0 / total
    inner = inner * inv
    weights = inv * stats[3:4]

    def finish(b):
        coef = part[b, 3:4, :] * weights
        for n in range(4):
            cols = slice(n * 256, (n + 1) * 256)
            p = exps[b, :, cols] * coef[:, cols]
            pw[b, :, cols] = p.astype(BF16)
            ds[b, :, cols] = (p * (prods[b, :, cols] - inner[:, cols])).astype(BF16)

    q_all = xqr[...].reshape(16 * SLOTS, DIM)
    g_all = xgr[...].reshape(16 * SLOTS, DIM)
    for b in far_first:
        finish(b)
        sbv[b] = dot_nn(pw[b], g_all).astype(BF16)
        remote(YSUM_V, sbv.at[b], rv.at[y], y_peer(b)).start()
    for b in far_first:
        sbk[b] = dot_nn(ds[b], q_all).astype(BF16)
        remote(YSUM_K, sbk.at[b], rk.at[y], y_peer(b)).start()
    finish(y)
    final = jnp.concatenate(
        [m, inv, inner * (1.0 / SCALE), jnp.zeros((5, 16 * SLOTS), F32)], axis=0
    )
    for t in range(8):
        fs[2 * t] = final[:, t * DIM : (t + 1) * DIM]
        fs[2 * t + 1] = final[:, t * DIM : (t + 1) * DIM]
    keys = kb[...].reshape(PROMPT, DIM)
    grad_v = dot_nn(pw[y], g_all)
    grad_k = dot_nn(ds[y], q_all)
    for b in a_others:
        remote(FIN, fs.at[b], fr.at[a], a_peer(b)).start()
    fr[a] = fs[a]
    for t in range(8):
        grad_q = dot_tn(ds[:, :, t * 128 : (t + 1) * 128].reshape(PROMPT, 2 * SLOTS), keys)
        dqs[2 * t] = grad_q[:SLOTS].astype(BF16)
        dqs[2 * t + 1] = grad_q[SLOTS:].astype(BF16)
    for b in a_other_z + a_same_z:
        remote(DQ, dqs.at[b], dqr.at[a], a_peer(b)).start()
    dqr[a] = dqs[a]

    def next_sum(total, kind_y, received, held, send, kind_z, target):
        arrived(kind_y, received.at[pl.ds(0, 3)])
        for b in y_others:
            total = total + received[b].astype(F32)
        held[...] = total.reshape(4, 32, DIM)
        send[...] = total.astype(BF16).reshape(4, 32, DIM)
        for b in z_others:
            remote(kind_z, send.at[b], target.at[z_hi], z_peer(b)).start()

    next_sum(grad_v, YSUM_V, rv, hv, szv, ZSUM_V, rzv)
    next_sum(grad_k, YSUM_K, rk, hk, szk, ZSUM_K, rzk)

    arrived(FIN, fr.at[pl.ds(0, 15)])
    here = left == (lax.rem(a, 2) == 0)
    nothing = jnp.zeros((SLOTS, DIM), BF16)
    for h in range(HEADS):
        cols = slice(h * DIM, (h + 1) * DIM)
        fin = fr[h]
        fin = jnp.where(here, fin, jnp.concatenate([fin[:, SLOTS:], fin[:, :SLOTS]], axis=1))
        m, inv, inner = fin[0:1], fin[1:2], fin[2:3]
        coef = jnp.exp2(st[h, 0:1, :] - m) * inv * weight
        e = own_e[h]
        p = (e * coef).astype(BF16)
        dsc = (e * (own_d[h] - inner) * (coef * SCALE)).astype(BF16)
        dvo[:, cols] = dot_nn(p, jnp.concatenate([xg[h], nothing], axis=0)).astype(BF16)
        dko[:, cols] = dot_nn(dsc, jnp.concatenate([xq[h], nothing], axis=0)).astype(BF16)
        own_q[h] = dot_tn(dsc, ck[:, cols])[:SLOTS]
    stores = [
        pltpu.make_async_copy(src, dst, out_sem.at[n])
        for n, (src, dst) in enumerate(
            ((dqo, dq_hbm), (dko, dk_hbm), (dvo, dv_hbm), (gko, gk_hbm), (gvo, gv_hbm))
        )
    ]
    for store in stores[1:3]:
        store.start()

    arrived(ZSUM_V, rzv.at[pl.ds(0, 3)])
    arrived(ZSUM_K, rzk.at[pl.ds(0, 3)])
    line = lax.broadcasted_iota(jnp.int32, (16, 8, DIM), 1)
    lines = jnp.zeros((16, 8, DIM), F32)
    for kv, (held, received) in enumerate(((hk, rzk), (hv, rzv))):
        part = held[z_hi]
        for b in z_others:
            part = part + received[b].astype(F32)
        for r in range(2):
            lines = jnp.where(line == kv * 2 + r, part[r * 16 : (r + 1) * 16][:, None, :], lines)
    t3[...] = lines
    for b in a_others:
        remote(OUT, t3.at[b], r3.at[a], a_peer(b)).start()
    r3[a] = t3[a]
    arrived(DQ, dqr.at[pl.ds(0, 15)])
    for h in range(HEADS):
        dqo[:, h * DIM : (h + 1) * DIM] = (own_q[h] + dqr[h].astype(F32)).astype(BF16)
    stores[0].start()
    arrived(OUT, r3.at[pl.ds(0, 15)])
    for h in range(HEADS):
        cols = slice(h * DIM, (h + 1) * DIM)
        gko[:, cols] = r3[h, 0:2, :].astype(BF16)
        gvo[:, cols] = r3[h, 2:4, :].astype(BF16)

    for store in stores[3:]:
        store.start()

    sent(KV, kvs.at[pl.ds(0, 15)])
    sent(QUERY, xq.at[pl.ds(0, 15)])
    sent(GRAD, xg.at[pl.ds(0, 15)])
    sent(ZK, kb.at[0, pl.ds(0, 3)])
    sent(ZV, vb.at[0, pl.ds(0, 3)])
    sent(ZSUM, gsumr.at[pl.ds(0, 3)])
    sent(YK, kb.at[pl.ds(0, 3)])
    sent(YV, vb.at[pl.ds(0, 3)])
    sent(OWN, st.at[pl.ds(0, 15)])
    sent(FIN, fs.at[pl.ds(0, 15)])
    sent(DQ, dqs.at[pl.ds(0, 15)])
    sent(YSUM_V, sbv.at[pl.ds(0, 3)])
    sent(YSUM_K, sbk.at[pl.ds(0, 3)])
    sent(ZSUM_V, szv.at[pl.ds(0, 3)])
    sent(ZSUM_K, szk.at[pl.ds(0, 3)])
    sent(OUT, t3.at[pl.ds(0, 15)])
    for store in stores:
        store.wait()


def store_all(*refs):
    sources, targets, held, sem = refs[:5], refs[5:10], refs[10:15], refs[15]
    parts = []
    for n in range(5):
        rows = sources[n].shape[0]
        step = min(rows, 64)
        for first in range(0, rows, step):
            parts.append((n, pl.ds(first, step)))
    loads = [
        pltpu.make_async_copy(sources[n].at[span], held[n].at[span], sem.at[0, p])
        for p, (n, span) in enumerate(parts)
    ]
    stores = [
        pltpu.make_async_copy(held[n].at[span], targets[n].at[span], sem.at[1, p])
        for p, (n, span) in enumerate(parts)
    ]
    for load in loads:
        load.start()
    for load, store in zip(loads, stores):
        load.wait()
        store.start()
    for store in stores:
        store.wait()


def shards(prompt_k, prompt_v, comp_q, comp_k, comp_v, grad_out, rewards, mask_pos):
    hbm = pl.BlockSpec(memory_space=pltpu.HBM)
    V = pltpu.VMEM
    grads = pl.pallas_call(
        kernel,
        out_shape=(
            jax.ShapeDtypeStruct((SLOTS, WIDTH), BF16),
            jax.ShapeDtypeStruct((ROWS, WIDTH), BF16),
            jax.ShapeDtypeStruct((ROWS, WIDTH), BF16),
            jax.ShapeDtypeStruct((2, WIDTH), BF16),
            jax.ShapeDtypeStruct((2, WIDTH), BF16),
        ),
        in_specs=[hbm] * 8,
        out_specs=(hbm,) * 5,
        scratch_shapes=[
            V((2, WIDTH), BF16),
            V((2, WIDTH), BF16),
            V((1, 1), F32),
            V((1, SLOTS), jnp.int32),
            V((ROWS, WIDTH), BF16),
            V((ROWS, WIDTH), BF16),
            V((ROWS, WIDTH), BF16),
            V((SLOTS, WIDTH), BF16),
            V((16, SLOTS, DIM), BF16),
            V((16, SLOTS, DIM), BF16),
            V((16, SLOTS, DIM), BF16),
            V((16, SLOTS, DIM), BF16),
            V((16, 8, DIM), F32),
            V((16, 8, DIM), F32),
            V((4, 4, 32, DIM), BF16),
            V((4, 4, 32, DIM), BF16),
            V((8, DIM), F32),
            V((4, 8, DIM), F32),
            V((16, 128, DIM), F32),
            V((16, 128, DIM), F32),
            V((16, 8, DIM), F32),
            V((16, 8, DIM), F32),
            V((16, 8, DIM), F32),
            V((16, 8, DIM), F32),
            V((4, 128, 16 * SLOTS), F32),
            V((4, 128, 16 * SLOTS), F32),
            V((4, 8, 16 * SLOTS), F32),
            V((4, 128, 16 * SLOTS), BF16),
            V((4, 128, 16 * SLOTS), BF16),
            V((4, 128, DIM), BF16),
            V((4, 128, DIM), BF16),
            V((4, 128, DIM), BF16),
            V((4, 128, DIM), BF16),
            V((4, 32, DIM), F32),
            V((4, 32, DIM), F32),
            V((4, 32, DIM), BF16),
            V((4, 32, DIM), BF16),
            V((4, 32, DIM), BF16),
            V((4, 32, DIM), BF16),
            V((16, 8, DIM), F32),
            V((16, 8, DIM), F32),
            V((16, SLOTS, DIM), BF16),
            V((16, SLOTS, DIM), BF16),
            V((16, SLOTS, DIM), F32),
            V((SLOTS, WIDTH), BF16),
            V((ROWS, WIDTH), BF16),
            V((ROWS, WIDTH), BF16),
            V((2, WIDTH), BF16),
            V((2, WIDTH), BF16),
            pltpu.SemaphoreType.DMA((8,)),
            pltpu.SemaphoreType.DMA((5,)),
            pltpu.SemaphoreType.DMA((KINDS,)),
            pltpu.SemaphoreType.DMA((KINDS,)),
            pltpu.SemaphoreType.DMA((2, 4)),
        ],
        compiler_params=pltpu.CompilerParams(
            collective_id=0, has_side_effects=True, vmem_limit_bytes=60 * 1024 * 1024
        ),
    )(
        prompt_k, prompt_v, rewards, mask_pos[0], comp_q[0, 0], comp_k[0, 0], comp_v[0, 0],
        grad_out[0, 0],
    )
    dq, dk, dv, gk, gv = pl.pallas_call(
        store_all,
        out_shape=[jax.ShapeDtypeStruct(grad.shape, BF16) for grad in grads],
        in_specs=[hbm] * 5,
        out_specs=[hbm] * 5,
        scratch_shapes=[V(grad.shape, BF16) for grad in grads] + [pltpu.SemaphoreType.DMA((2, 12))],
        compiler_params=pltpu.CompilerParams(vmem_limit_bytes=60 * 1024 * 1024),
    )(*grads)
    return dq[None, None], dk[None, None], dv[None, None], gk, gv


def solution(mesh):
    wide = P("grp", "ctx", None, None)
    rows = P(("grp", "ctx"), None)
    return jax.shard_map(
        shards,
        mesh=mesh,
        in_specs=(rows, rows, wide, wide, wide, wide, P("grp", "ctx"), P("grp", "ctx", None)),
        out_specs=(wide, wide, wide, rows, rows),
        check_vma=False,
    )
```

```python
import jax
import jax.numpy as jnp
from jax import lax
from jax.experimental import pallas as pl
from jax.experimental.pallas import tpu as pltpu
from jax.sharding import PartitionSpec as P

HEADS = 16
DIM = 128
SLOTS = 64
ROWS = 128
WIDTH = 2048
PROMPT = 512
F32 = jnp.float32
BF16 = jnp.bfloat16
SCALE = DIM ** -0.5
SCALE2 = SCALE * 1.4426950408889634
MESH = pl.DeviceIdType.MESH

(
    KV, QUERY, GRAD, ZK, ZV, ZSUM, YK, YV, OWN, FIN, DQ, YSUM_K, YSUM_V, ZSUM_K, ZSUM_V, OUT, KINDS
) = range(17)


def dot_nt(a, b):
    return lax.dot_general(a, b, (((1,), (1,)), ((), ())), preferred_element_type=F32)


def dot_nn(a, b):
    return lax.dot_general(a, b, (((1,), (0,)), ((), ())), preferred_element_type=F32)


def dot_tn(a, b):
    return lax.dot_general(a, b, (((0,), (0,)), ((), ())), preferred_element_type=F32)


def kernel(
    pk_hbm, pv_hbm, rw_hbm, mp_hbm, cq_hbm, ck_hbm, cv_hbm, go_hbm,
    dq_hbm, dk_hbm, dv_hbm, gk_hbm, gv_hbm,
    pk, pv, rw, mp, cq, ck, cv, go, xq, xqr, xg, xgr, kvs, kvr, kb, vb, gsum, gsumr, own_e, own_d, st, str_,
    fs, fr, exps, prods, part, pw, ds,
    sbk, sbv, rk, rv, hk, hv, szk, szv, rzk, rzv, t3, r3, dqs, dqr, own_q, dqo, dko, dvo, gko, gvo,
    in_sem, out_sem, ss, rs, ry,
):
    grp = lax.axis_index("grp")
    ctx = lax.axis_index("ctx")
    x_lo, y = lax.div(grp, 4), lax.rem(grp, 4)
    z = lax.div(ctx, 4)
    z_hi, z_lo, low = lax.div(z, 2), lax.rem(z, 2), lax.rem(ctx, 4)
    a = z_lo * 8 + x_lo * 4 + low

    def a_peer(b):
        return {
            "grp": lax.rem(lax.div(b, 4), 2) * 4 + y,
            "ctx": (z_hi * 2 + lax.div(b, 8)) * 4 + lax.rem(b, 4),
        }

    def z_peer(b):
        return {"grp": grp, "ctx": (b * 2 + z_lo) * 4 + low}

    def y_peer(b):
        return {"grp": x_lo * 4 + b, "ctx": ctx}

    a_others = [z_lo * 8 + lax.rem(a + k, 8) for k in range(1, 8)]
    a_others += [(1 - z_lo) * 8 + lax.rem(a + k, 8) for k in range(8)]
    z_others = [lax.rem(z_hi + k, 4) for k in range(1, 4)]
    y_others = [lax.rem(y + k, 4) for k in range(1, 4)]

    def remote(kind, src, dst, device):
        return pltpu.make_async_remote_copy(
            src_ref=src, dst_ref=dst, send_sem=ss.at[kind], recv_sem=rs.at[kind],
            device_id=device, device_id_type=MESH,
        )

    def along_y(kv, ref, row, b):
        return pltpu.make_async_remote_copy(
            src_ref=ref.at[row], dst_ref=ref.at[row], send_sem=ss.at[YK + kv],
            recv_sem=ry.at[kv, row], device_id=y_peer(b), device_id_type=MESH,
        )

    def arrived(kind, dst):
        remote(kind, dst, dst, y_peer(y_others[0])).wait_recv()

    def sent(kind, src):
        remote(kind, src, src, y_peer(y_others[0])).wait_send()

    loads = [
        pltpu.make_async_copy(src, dst, in_sem.at[n])
        for n, (src, dst) in enumerate(
            (
                (pk_hbm, pk), (pv_hbm, pv), (rw_hbm, rw), (mp_hbm, mp),
                (cq_hbm, cq), (go_hbm, go), (ck_hbm, ck), (cv_hbm, cv),
            )
        )
    ]
    for load in loads:
        load.start()

    barrier = pltpu.get_barrier_semaphore()
    for b in a_others:
        pl.semaphore_signal(barrier, inc=1, device_id=a_peer(b), device_id_type=MESH)
    for b in z_others:
        pl.semaphore_signal(barrier, inc=1, device_id=z_peer(b), device_id_type=MESH)
    for b in y_others:
        pl.semaphore_signal(barrier, inc=1, device_id=y_peer(b), device_id_type=MESH)

    for load in loads[:4]:
        load.wait()
    pos = mp[...]
    pos2 = jnp.concatenate([pos, pos], axis=1)
    live = pos < ROWS
    count = jnp.sum(jnp.where(live, 1.0, 0.0), axis=1, keepdims=True)
    reward = rw[...]
    lines = jnp.concatenate(
        [
            pk[...].astype(F32),
            pv[...].astype(F32),
            jnp.broadcast_to(count, (1, WIDTH)),
            jnp.broadcast_to(reward, (1, WIDTH)),
            jnp.zeros((2, WIDTH), F32),
        ],
        axis=0,
    )
    for h in range(HEADS):
        kvs[h] = lines[:, h * DIM : (h + 1) * DIM]

    pl.semaphore_wait(barrier, 21)

    for b in a_others:
        remote(KV, kvs.at[b], kvr.at[a], a_peer(b)).start()
    kvr[a] = kvs[a]

    row = lax.broadcasted_iota(jnp.int32, (ROWS, 2 * SLOTS), 0)
    pick = jnp.where(row == jnp.minimum(pos2, ROWS - 1), 1.0, 0.0).astype(BF16)
    loads[4].wait()
    picked = dot_tn(pick, cq[...])[:SLOTS].astype(BF16)
    for h in range(HEADS):
        xq[h] = picked[:, h * DIM : (h + 1) * DIM]
    loads[5].wait()
    for h in range(HEADS):
        xg[h] = go[:, h * DIM : (h + 1) * DIM]

    arrived(KV, kvr.at[pl.ds(0, 15)])
    blocks = kvr[...]
    kb[y, z_hi, 0:16, :] = blocks[:, 0, :].astype(BF16)
    kb[y, z_hi, 16:32, :] = blocks[:, 1, :].astype(BF16)
    for b in z_others:
        remote(ZK, kb.at[y, z_hi], kb.at[y, z_hi], z_peer(b)).start()
    vb[y, z_hi, 0:16, :] = blocks[:, 2, :].astype(BF16)
    vb[y, z_hi, 16:32, :] = blocks[:, 3, :].astype(BF16)
    for b in z_others:
        remote(ZV, vb.at[y, z_hi], vb.at[y, z_hi], z_peer(b)).start()
    mine = lax.broadcasted_iota(jnp.int32, (16, DIM), 0) // 4 % 2 == x_lo
    count16 = jnp.sum(jnp.where(mine, blocks[:, 4, :], 0.0), axis=0, keepdims=True)
    reward16 = jnp.sum(jnp.where(mine, blocks[:, 5, :], 0.0), axis=0, keepdims=True)
    gsum[...] = jnp.concatenate([count16, reward16, jnp.zeros((6, DIM), F32)], axis=0)
    for b in z_others:
        remote(ZSUM, gsum, gsumr.at[z_hi], z_peer(b)).start()
    for b in a_others:
        remote(QUERY, xq.at[b], xqr.at[a], a_peer(b)).start()
    xqr[a] = xq[a]

    def own_scores(h):
        q = xq[h]
        g = xg[h]
        s = dot_nt(ck[:, h * DIM : (h + 1) * DIM], jnp.concatenate([q, q], axis=0)) * SCALE2
        d = dot_nt(cv[:, h * DIM : (h + 1) * DIM], jnp.concatenate([g, g], axis=0))
        m = jnp.max(s, axis=0, keepdims=True)
        e = jnp.exp2(s - m)
        own_e[h] = e
        own_d[h] = d
        st[h] = jnp.concatenate(
            [
                m,
                jnp.sum(e, axis=0, keepdims=True),
                jnp.sum(e * d, axis=0, keepdims=True),
                jnp.zeros((5, DIM), F32),
            ],
            axis=0,
        )

    loads[6].wait()
    loads[7].wait()
    for h in range(2):
        own_scores(h)

    arrived(ZK, kb.at[0, pl.ds(0, 3)])
    for b in y_others:
        along_y(0, kb, y, b).start()
    arrived(ZV, vb.at[0, pl.ds(0, 3)])
    for b in y_others:
        along_y(1, vb, y, b).start()
    for b in a_others:
        remote(GRAD, xg.at[b], xgr.at[a], a_peer(b)).start()
    xgr[a] = xg[a]
    for h in range(2, HEADS):
        own_scores(h)
    arrived(ZSUM, gsumr.at[pl.ds(0, 3)])
    total = gsum[...]
    for b in z_others:
        total = total + gsumr[b]
    weight = (reward - total[1:2] / 32.0) * (SLOTS * 32) / total[0:1]
    weight = jnp.where(pos2 < ROWS, weight, 0.0)
    for h in range(HEADS):
        st[h, 3:4, :] = weight
    for b in a_others:
        remote(OWN, st.at[b], str_.at[a], a_peer(b)).start()
    str_[a] = st[a]

    def key_block(b):
        block = kb[b].reshape(128, DIM)
        for n in range(4):
            cols = slice(n * 256, (n + 1) * 256)
            s = dot_nt(block, xqr[4 * n : 4 * n + 4].reshape(256, DIM)) * SCALE2
            m = jnp.max(s, axis=0, keepdims=True)
            e = jnp.exp2(s - m)
            exps[b, :, cols] = e
            part[b, 0:1, cols] = m
            part[b, 1:2, cols] = jnp.sum(e, axis=0, keepdims=True)

    def value_block(b):
        block = vb[b].reshape(128, DIM)
        for n in range(4):
            cols = slice(n * 256, (n + 1) * 256)
            d = dot_nt(block, xgr[4 * n : 4 * n + 4].reshape(256, DIM)) * SCALE
            prods[b, :, cols] = d
            part[b, 2:3, cols] = jnp.sum(exps[b, :, cols] * d, axis=0, keepdims=True)

    near_first = [y_others[0], y_others[2], y_others[1]]
    far_first = [y_others[1], y_others[0], y_others[2]]
    arrived(QUERY, xqr.at[pl.ds(0, 15)])
    key_block(y)
    for b in near_first:
        along_y(0, kb, b, b).wait_recv()
        key_block(b)
    arrived(GRAD, xgr.at[pl.ds(0, 15)])
    value_block(y)
    for b in near_first:
        along_y(1, vb, b, b).wait_recv()
        value_block(b)

    arrived(OWN, str_.at[pl.ds(0, 15)])
    left = lax.broadcasted_iota(jnp.int32, (8, DIM), 1) < SLOTS
    stats = jnp.concatenate(
        [jnp.where(left, str_[2 * t], str_[2 * t + 1]) for t in range(8)], axis=1
    )
    m = stats[0:1]
    for b in range(4):
        m = jnp.maximum(m, part[b, 0:1, :])
    fo = jnp.exp2(stats[0:1] - m)
    total = stats[1:2] * fo
    inner = stats[2:3] * (fo * SCALE)
    for b in range(4):
        f = jnp.exp2(part[b, 0:1, :] - m)
        total = total + part[b, 1:2, :] * f
        inner = inner + part[b, 2:3, :] * f
        part[b, 3:4, :] = f
    inv = 1.0 / total
    inner = inner * inv
    weights = inv * stats[3:4]

    def finish(b):
        coef = part[b, 3:4, :] * weights
        for n in range(4):
            cols = slice(n * 256, (n + 1) * 256)
            p = exps[b, :, cols] * coef[:, cols]
            pw[b, :, cols] = p.astype(BF16)
            ds[b, :, cols] = (p * (prods[b, :, cols] - inner[:, cols])).astype(BF16)

    q_all = xqr[...].reshape(16 * SLOTS, DIM)
    g_all = xgr[...].reshape(16 * SLOTS, DIM)
    for b in far_first:
        finish(b)
        sbv[b] = dot_nn(pw[b], g_all).astype(BF16)
        remote(YSUM_V, sbv.at[b], rv.at[y], y_peer(b)).start()
    for b in far_first:
        sbk[b] = dot_nn(ds[b], q_all).astype(BF16)
        remote(YSUM_K, sbk.at[b], rk.at[y], y_peer(b)).start()
    finish(y)
    final = jnp.concatenate(
        [m, inv, inner * (1.0 / SCALE), jnp.zeros((5, 16 * SLOTS), F32)], axis=0
    )
    for t in range(8):
        fs[2 * t] = final[:, t * DIM : (t + 1) * DIM]
        fs[2 * t + 1] = final[:, t * DIM : (t + 1) * DIM]
    keys = kb[...].reshape(PROMPT, DIM)
    grad_v = dot_nn(pw[y], g_all)
    grad_k = dot_nn(ds[y], q_all)
    for b in a_others:
        remote(FIN, fs.at[b], fr.at[a], a_peer(b)).start()
    fr[a] = fs[a]
    for t in range(8):
        grad_q = dot_tn(ds[:, :, t * 128 : (t + 1) * 128].reshape(PROMPT, 2 * SLOTS), keys)
        dqs[2 * t] = grad_q[:SLOTS].astype(BF16)
        dqs[2 * t + 1] = grad_q[SLOTS:].astype(BF16)

    def next_sum(total, kind_y, received, held, send, kind_z, target):
        arrived(kind_y, received.at[pl.ds(0, 3)])
        for b in y_others:
            total = total + received[b].astype(F32)
        held[...] = total.reshape(4, 32, DIM)
        send[...] = total.astype(BF16).reshape(4, 32, DIM)
        for b in z_others:
            remote(kind_z, send.at[b], target.at[z_hi], z_peer(b)).start()

    next_sum(grad_v, YSUM_V, rv, hv, szv, ZSUM_V, rzv)
    next_sum(grad_k, YSUM_K, rk, hk, szk, ZSUM_K, rzk)
    for b in a_others:
        remote(DQ, dqs.at[b], dqr.at[a], a_peer(b)).start()
    dqr[a] = dqs[a]

    arrived(FIN, fr.at[pl.ds(0, 15)])
    here = left == (lax.rem(a, 2) == 0)
    nothing = jnp.zeros((SLOTS, DIM), BF16)
    for h in range(HEADS):
        cols = slice(h * DIM, (h + 1) * DIM)
        fin = fr[h]
        fin = jnp.where(here, fin, jnp.concatenate([fin[:, SLOTS:], fin[:, :SLOTS]], axis=1))
        m, inv, inner = fin[0:1], fin[1:2], fin[2:3]
        coef = jnp.exp2(st[h, 0:1, :] - m) * inv * weight
        e = own_e[h]
        p = (e * coef).astype(BF16)
        dsc = (e * (own_d[h] - inner) * (coef * SCALE)).astype(BF16)
        dvo[:, cols] = dot_nn(p, jnp.concatenate([xg[h], nothing], axis=0)).astype(BF16)
        dko[:, cols] = dot_nn(dsc, jnp.concatenate([xq[h], nothing], axis=0)).astype(BF16)
        own_q[h] = dot_tn(dsc, ck[:, cols])[:SLOTS]
    stores = [
        pltpu.make_async_copy(src, dst, out_sem.at[n])
        for n, (src, dst) in enumerate(
            ((dqo, dq_hbm), (dko, dk_hbm), (dvo, dv_hbm), (gko, gk_hbm), (gvo, gv_hbm))
        )
    ]
    for store in stores[1:3]:
        store.start()

    arrived(ZSUM_V, rzv.at[pl.ds(0, 3)])
    arrived(ZSUM_K, rzk.at[pl.ds(0, 3)])
    line = lax.broadcasted_iota(jnp.int32, (16, 8, DIM), 1)
    lines = jnp.zeros((16, 8, DIM), F32)
    for kv, (held, received) in enumerate(((hk, rzk), (hv, rzv))):
        part = held[z_hi]
        for b in z_others:
            part = part + received[b].astype(F32)
        for r in range(2):
            lines = jnp.where(line == kv * 2 + r, part[r * 16 : (r + 1) * 16][:, None, :], lines)
    t3[...] = lines
    for b in a_others:
        remote(OUT, t3.at[b], r3.at[a], a_peer(b)).start()
    r3[a] = t3[a]
    arrived(DQ, dqr.at[pl.ds(0, 15)])
    for h in range(HEADS):
        dqo[:, h * DIM : (h + 1) * DIM] = (own_q[h] + dqr[h].astype(F32)).astype(BF16)
    stores[0].start()
    arrived(OUT, r3.at[pl.ds(0, 15)])
    for h in range(HEADS):
        cols = slice(h * DIM, (h + 1) * DIM)
        gko[:, cols] = r3[h, 0:2, :].astype(BF16)
        gvo[:, cols] = r3[h, 2:4, :].astype(BF16)

    for store in stores[3:]:
        store.start()

    sent(KV, kvs.at[pl.ds(0, 15)])
    sent(QUERY, xq.at[pl.ds(0, 15)])
    sent(GRAD, xg.at[pl.ds(0, 15)])
    sent(ZK, kb.at[0, pl.ds(0, 3)])
    sent(ZV, vb.at[0, pl.ds(0, 3)])
    sent(ZSUM, gsumr.at[pl.ds(0, 3)])
    sent(YK, kb.at[pl.ds(0, 3)])
    sent(YV, vb.at[pl.ds(0, 3)])
    sent(OWN, st.at[pl.ds(0, 15)])
    sent(FIN, fs.at[pl.ds(0, 15)])
    sent(DQ, dqs.at[pl.ds(0, 15)])
    sent(YSUM_V, sbv.at[pl.ds(0, 3)])
    sent(YSUM_K, sbk.at[pl.ds(0, 3)])
    sent(ZSUM_V, szv.at[pl.ds(0, 3)])
    sent(ZSUM_K, szk.at[pl.ds(0, 3)])
    sent(OUT, t3.at[pl.ds(0, 15)])
    for store in stores:
        store.wait()


def store_all(*refs):
    sources, targets, held, sem = refs[:5], refs[5:10], refs[10:15], refs[15]
    parts = []
    for n in range(5):
        rows = sources[n].shape[0]
        step = min(rows, 64)
        for first in range(0, rows, step):
            parts.append((n, pl.ds(first, step)))
    loads = [
        pltpu.make_async_copy(sources[n].at[span], held[n].at[span], sem.at[0, p])
        for p, (n, span) in enumerate(parts)
    ]
    stores = [
        pltpu.make_async_copy(held[n].at[span], targets[n].at[span], sem.at[1, p])
        for p, (n, span) in enumerate(parts)
    ]
    for load in loads:
        load.start()
    for load, store in zip(loads, stores):
        load.wait()
        store.start()
    for store in stores:
        store.wait()


def shards(prompt_k, prompt_v, comp_q, comp_k, comp_v, grad_out, rewards, mask_pos):
    hbm = pl.BlockSpec(memory_space=pltpu.HBM)
    V = pltpu.VMEM
    grads = pl.pallas_call(
        kernel,
        out_shape=(
            jax.ShapeDtypeStruct((SLOTS, WIDTH), BF16),
            jax.ShapeDtypeStruct((ROWS, WIDTH), BF16),
            jax.ShapeDtypeStruct((ROWS, WIDTH), BF16),
            jax.ShapeDtypeStruct((2, WIDTH), BF16),
            jax.ShapeDtypeStruct((2, WIDTH), BF16),
        ),
        in_specs=[hbm] * 8,
        out_specs=(hbm,) * 5,
        scratch_shapes=[
            V((2, WIDTH), BF16),
            V((2, WIDTH), BF16),
            V((1, 1), F32),
            V((1, SLOTS), jnp.int32),
            V((ROWS, WIDTH), BF16),
            V((ROWS, WIDTH), BF16),
            V((ROWS, WIDTH), BF16),
            V((SLOTS, WIDTH), BF16),
            V((16, SLOTS, DIM), BF16),
            V((16, SLOTS, DIM), BF16),
            V((16, SLOTS, DIM), BF16),
            V((16, SLOTS, DIM), BF16),
            V((16, 8, DIM), F32),
            V((16, 8, DIM), F32),
            V((4, 4, 32, DIM), BF16),
            V((4, 4, 32, DIM), BF16),
            V((8, DIM), F32),
            V((4, 8, DIM), F32),
            V((16, 128, DIM), F32),
            V((16, 128, DIM), F32),
            V((16, 8, DIM), F32),
            V((16, 8, DIM), F32),
            V((16, 8, DIM), F32),
            V((16, 8, DIM), F32),
            V((4, 128, 16 * SLOTS), F32),
            V((4, 128, 16 * SLOTS), F32),
            V((4, 8, 16 * SLOTS), F32),
            V((4, 128, 16 * SLOTS), BF16),
            V((4, 128, 16 * SLOTS), BF16),
            V((4, 128, DIM), BF16),
            V((4, 128, DIM), BF16),
            V((4, 128, DIM), BF16),
            V((4, 128, DIM), BF16),
            V((4, 32, DIM), F32),
            V((4, 32, DIM), F32),
            V((4, 32, DIM), BF16),
            V((4, 32, DIM), BF16),
            V((4, 32, DIM), BF16),
            V((4, 32, DIM), BF16),
            V((16, 8, DIM), F32),
            V((16, 8, DIM), F32),
            V((16, SLOTS, DIM), BF16),
            V((16, SLOTS, DIM), BF16),
            V((16, SLOTS, DIM), F32),
            V((SLOTS, WIDTH), BF16),
            V((ROWS, WIDTH), BF16),
            V((ROWS, WIDTH), BF16),
            V((2, WIDTH), BF16),
            V((2, WIDTH), BF16),
            pltpu.SemaphoreType.DMA((8,)),
            pltpu.SemaphoreType.DMA((5,)),
            pltpu.SemaphoreType.DMA((KINDS,)),
            pltpu.SemaphoreType.DMA((KINDS,)),
            pltpu.SemaphoreType.DMA((2, 4)),
        ],
        compiler_params=pltpu.CompilerParams(
            collective_id=0, has_side_effects=True, vmem_limit_bytes=60 * 1024 * 1024
        ),
    )(
        prompt_k, prompt_v, rewards, mask_pos[0], comp_q[0, 0], comp_k[0, 0], comp_v[0, 0],
        grad_out[0, 0],
    )
    dq, dk, dv, gk, gv = pl.pallas_call(
        store_all,
        out_shape=[jax.ShapeDtypeStruct(grad.shape, BF16) for grad in grads],
        in_specs=[hbm] * 5,
        out_specs=[hbm] * 5,
        scratch_shapes=[V(grad.shape, BF16) for grad in grads] + [pltpu.SemaphoreType.DMA((2, 12))],
        compiler_params=pltpu.CompilerParams(vmem_limit_bytes=60 * 1024 * 1024),
    )(*grads)
    return dq[None, None], dk[None, None], dv[None, None], gk, gv


def solution(mesh):
    wide = P("grp", "ctx", None, None)
    rows = P(("grp", "ctx"), None)
    return jax.shard_map(
        shards,
        mesh=mesh,
        in_specs=(rows, rows, wide, wide, wide, wide, P("grp", "ctx"), P("grp", "ctx", None)),
        out_specs=(wide, wide, wide, rows, rows),
        check_vma=False,
    )
```

```python
import jax
import jax.numpy as jnp
from jax import lax
from jax.experimental import pallas as pl
from jax.experimental.pallas import tpu as pltpu
from jax.sharding import PartitionSpec as P

HEADS = 16
DIM = 128
SLOTS = 64
ROWS = 128
WIDTH = 2048
PROMPT = 512
F32 = jnp.float32
BF16 = jnp.bfloat16
SCALE = DIM ** -0.5
SCALE2 = SCALE * 1.4426950408889634
MESH = pl.DeviceIdType.MESH

(
    KV, QUERY, GRAD, ZK, ZV, ZSUM, YK, YV, OWN, FIN, DQ, YSUM_K, YSUM_V, ZSUM_K, ZSUM_V, OUT, KINDS
) = range(17)


def dot_nt(a, b):
    return lax.dot_general(a, b, (((1,), (1,)), ((), ())), preferred_element_type=F32)


def dot_nn(a, b):
    return lax.dot_general(a, b, (((1,), (0,)), ((), ())), preferred_element_type=F32)


def dot_tn(a, b):
    return lax.dot_general(a, b, (((0,), (0,)), ((), ())), preferred_element_type=F32)


def kernel(
    pk_hbm, pv_hbm, rw_hbm, mp_hbm, cq_hbm, ck_hbm, cv_hbm, go_hbm,
    dq_hbm, dk_hbm, dv_hbm, gk_hbm, gv_hbm,
    pk, pv, rw, mp, cq, ck, cv, go, xq, xqr, xg, xgr, kvs, kvr, kb, vb, gsum, gsumr, own_e, own_d, st, str_,
    fs, fr, exps, prods, part, pw, ds,
    sbk, sbv, rk, rv, hk, hv, szk, szv, rzk, rzv, t3, r3, dqs, dqr, own_q, dqo, dko, dvo, gko, gvo,
    in_sem, out_sem, ss, rs, ry,
):
    grp = lax.axis_index("grp")
    ctx = lax.axis_index("ctx")
    x_lo, y = lax.div(grp, 4), lax.rem(grp, 4)
    z = lax.div(ctx, 4)
    z_hi, z_lo, low = lax.div(z, 2), lax.rem(z, 2), lax.rem(ctx, 4)
    a = z_lo * 8 + x_lo * 4 + low

    def a_peer(b):
        return {
            "grp": lax.rem(lax.div(b, 4), 2) * 4 + y,
            "ctx": (z_hi * 2 + lax.div(b, 8)) * 4 + lax.rem(b, 4),
        }

    def z_peer(b):
        return {"grp": grp, "ctx": (b * 2 + z_lo) * 4 + low}

    def y_peer(b):
        return {"grp": x_lo * 4 + b, "ctx": ctx}

    a_others = [z_lo * 8 + lax.rem(a + k, 8) for k in range(1, 8)]
    a_others += [(1 - z_lo) * 8 + lax.rem(a + k, 8) for k in range(8)]
    z_others = [lax.rem(z_hi + k, 4) for k in range(1, 4)]
    y_others = [lax.rem(y + k, 4) for k in range(1, 4)]

    def remote(kind, src, dst, device):
        return pltpu.make_async_remote_copy(
            src_ref=src, dst_ref=dst, send_sem=ss.at[kind], recv_sem=rs.at[kind],
            device_id=device, device_id_type=MESH,
        )

    def along_y(kv, ref, row, b):
        return pltpu.make_async_remote_copy(
            src_ref=ref.at[row], dst_ref=ref.at[row], send_sem=ss.at[YK + kv],
            recv_sem=ry.at[kv, row], device_id=y_peer(b), device_id_type=MESH,
        )

    def arrived(kind, dst):
        remote(kind, dst, dst, y_peer(y_others[0])).wait_recv()

    def sent(kind, src):
        remote(kind, src, src, y_peer(y_others[0])).wait_send()

    loads = [
        pltpu.make_async_copy(src, dst, in_sem.at[n])
        for n, (src, dst) in enumerate(
            (
                (pk_hbm, pk), (pv_hbm, pv), (rw_hbm, rw), (mp_hbm, mp),
                (cq_hbm, cq), (go_hbm, go), (ck_hbm, ck), (cv_hbm, cv),
            )
        )
    ]
    for load in loads:
        load.start()

    barrier = pltpu.get_barrier_semaphore()
    for b in a_others:
        pl.semaphore_signal(barrier, inc=1, device_id=a_peer(b), device_id_type=MESH)
    for b in z_others:
        pl.semaphore_signal(barrier, inc=1, device_id=z_peer(b), device_id_type=MESH)
    for b in y_others:
        pl.semaphore_signal(barrier, inc=1, device_id=y_peer(b), device_id_type=MESH)

    for load in loads[:4]:
        load.wait()
    pos = mp[...]
    pos2 = jnp.concatenate([pos, pos], axis=1)
    live = pos < ROWS
    count = jnp.sum(jnp.where(live, 1.0, 0.0), axis=1, keepdims=True)
    reward = rw[...]
    lines = jnp.concatenate(
        [
            pk[...].astype(F32),
            pv[...].astype(F32),
            jnp.broadcast_to(count, (1, WIDTH)),
            jnp.broadcast_to(reward, (1, WIDTH)),
            jnp.zeros((2, WIDTH), F32),
        ],
        axis=0,
    )
    for h in range(HEADS):
        kvs[h] = lines[:, h * DIM : (h + 1) * DIM]

    pl.semaphore_wait(barrier, 21)

    for b in a_others:
        remote(KV, kvs.at[b], kvr.at[a], a_peer(b)).start()
    kvr[a] = kvs[a]

    row = lax.broadcasted_iota(jnp.int32, (ROWS, 2 * SLOTS), 0)
    pick = jnp.where(row == jnp.minimum(pos2, ROWS - 1), 1.0, 0.0).astype(BF16)
    loads[4].wait()
    picked = dot_tn(pick, cq[...])[:SLOTS].astype(BF16)
    for h in range(HEADS):
        xq[h] = picked[:, h * DIM : (h + 1) * DIM]
    for b in a_others:
        remote(QUERY, xq.at[b], xqr.at[a], a_peer(b)).start()
    xqr[a] = xq[a]
    loads[5].wait()
    for h in range(HEADS):
        xg[h] = go[:, h * DIM : (h + 1) * DIM]

    arrived(KV, kvr.at[pl.ds(0, 15)])
    blocks = kvr[...]
    kb[y, z_hi, 0:16, :] = blocks[:, 0, :].astype(BF16)
    kb[y, z_hi, 16:32, :] = blocks[:, 1, :].astype(BF16)
    for b in z_others:
        remote(ZK, kb.at[y, z_hi], kb.at[y, z_hi], z_peer(b)).start()
    vb[y, z_hi, 0:16, :] = blocks[:, 2, :].astype(BF16)
    vb[y, z_hi, 16:32, :] = blocks[:, 3, :].astype(BF16)
    for b in z_others:
        remote(ZV, vb.at[y, z_hi], vb.at[y, z_hi], z_peer(b)).start()
    mine = lax.broadcasted_iota(jnp.int32, (16, DIM), 0) // 4 % 2 == x_lo
    count16 = jnp.sum(jnp.where(mine, blocks[:, 4, :], 0.0), axis=0, keepdims=True)
    reward16 = jnp.sum(jnp.where(mine, blocks[:, 5, :], 0.0), axis=0, keepdims=True)
    gsum[...] = jnp.concatenate([count16, reward16, jnp.zeros((6, DIM), F32)], axis=0)
    for b in z_others:
        remote(ZSUM, gsum, gsumr.at[z_hi], z_peer(b)).start()
    for b in a_others:
        remote(GRAD, xg.at[b], xgr.at[a], a_peer(b)).start()
    xgr[a] = xg[a]

    nothing = jnp.zeros((SLOTS, DIM), BF16)

    def both(ref, t):
        return jnp.concatenate(
            [
                jnp.concatenate([ref[2 * t], nothing], axis=1),
                jnp.concatenate([nothing, ref[2 * t + 1]], axis=1),
            ],
            axis=0,
        )

    def own_scores(t):
        cols = slice(t * 256, (t + 1) * 256)
        s = dot_nt(ck[:, cols], both(xq, t)) * SCALE2
        d = dot_nt(cv[:, cols], both(xg, t))
        m = jnp.max(s, axis=0, keepdims=True)
        e = jnp.exp2(s - m)
        own_e[t] = e
        own_d[t] = d
        st[t] = jnp.concatenate(
            [
                m,
                jnp.sum(e, axis=0, keepdims=True),
                jnp.sum(e * d, axis=0, keepdims=True),
                jnp.zeros((5, DIM), F32),
            ],
            axis=0,
        )

    left = lax.broadcasted_iota(jnp.int32, (8, DIM), 1) < SLOTS
    odd = jnp.broadcast_to(lax.rem(a, 2), (8, DIM)) == 1

    def side_by_side(ref, t):
        one, two = ref[2 * t], ref[2 * t + 1]
        moved = pltpu.roll(jnp.where(odd, one, two), SLOTS, 1)
        return jnp.where(left != odd, jnp.where(left, one, two), moved)

    loads[6].wait()
    loads[7].wait()
    for t in range(2):
        own_scores(t)

    arrived(ZK, kb.at[0, pl.ds(0, 3)])
    for b in y_others:
        along_y(0, kb, y, b).start()
    arrived(ZV, vb.at[0, pl.ds(0, 3)])
    for b in y_others:
        along_y(1, vb, y, b).start()
    for t in range(2, 8):
        own_scores(t)
    arrived(ZSUM, gsumr.at[pl.ds(0, 3)])
    total = gsum[...]
    for b in z_others:
        total = total + gsumr[b]
    weight = (reward - total[1:2] / 32.0) * (SLOTS * 32) / total[0:1]
    weight = jnp.where(pos2 < ROWS, weight, 0.0)
    for t in range(8):
        st[t, 3:4, :] = weight
    for b in a_others:
        remote(OWN, st.at[lax.div(b, 2)], str_.at[a], a_peer(b)).start()
    str_[a] = st[lax.div(a, 2)]

    def key_block(b):
        block = kb[b].reshape(128, DIM)
        for n in range(4):
            cols = slice(n * 256, (n + 1) * 256)
            s = dot_nt(block, xqr[4 * n : 4 * n + 4].reshape(256, DIM)) * SCALE2
            m = jnp.max(s, axis=0, keepdims=True)
            e = jnp.exp2(s - m)
            exps[b, :, cols] = e
            part[b, 0:1, cols] = m
            part[b, 1:2, cols] = jnp.sum(e, axis=0, keepdims=True)

    def value_block(b):
        block = vb[b].reshape(128, DIM)
        for n in range(4):
            cols = slice(n * 256, (n + 1) * 256)
            d = dot_nt(block, xgr[4 * n : 4 * n + 4].reshape(256, DIM)) * SCALE
            prods[b, :, cols] = d
            part[b, 2:3, cols] = jnp.sum(exps[b, :, cols] * d, axis=0, keepdims=True)

    near_first = [y_others[0], y_others[2], y_others[1]]
    far_first = [y_others[1], y_others[0], y_others[2]]
    arrived(QUERY, xqr.at[pl.ds(0, 15)])
    key_block(y)
    for b in near_first:
        along_y(0, kb, b, b).wait_recv()
        key_block(b)
    arrived(GRAD, xgr.at[pl.ds(0, 15)])
    value_block(y)
    for b in near_first:
        along_y(1, vb, b, b).wait_recv()
        value_block(b)

    arrived(OWN, str_.at[pl.ds(0, 15)])
    stats = jnp.concatenate([side_by_side(str_, t) for t in range(8)], axis=1)
    m = stats[0:1]
    for b in range(4):
        m = jnp.maximum(m, part[b, 0:1, :])
    fo = jnp.exp2(stats[0:1] - m)
    total = stats[1:2] * fo
    inner = stats[2:3] * (fo * SCALE)
    for b in range(4):
        f = jnp.exp2(part[b, 0:1, :] - m)
        total = total + part[b, 1:2, :] * f
        inner = inner + part[b, 2:3, :] * f
        part[b, 3:4, :] = f
    inv = 1.0 / total
    inner = inner * inv
    weights = inv * stats[3:4]

    def finish(b):
        coef = part[b, 3:4, :] * weights
        for n in range(4):
            cols = slice(n * 256, (n + 1) * 256)
            p = exps[b, :, cols] * coef[:, cols]
            pw[b, :, cols] = p.astype(BF16)
            ds[b, :, cols] = (p * (prods[b, :, cols] - inner[:, cols])).astype(BF16)

    q_all = xqr[...].reshape(16 * SLOTS, DIM)
    g_all = xgr[...].reshape(16 * SLOTS, DIM)
    for b in far_first:
        finish(b)
        sbv[b] = dot_nn(pw[b], g_all).astype(BF16)
        remote(YSUM_V, sbv.at[b], rv.at[y], y_peer(b)).start()
    for b in far_first:
        sbk[b] = dot_nn(ds[b], q_all).astype(BF16)
        remote(YSUM_K, sbk.at[b], rk.at[y], y_peer(b)).start()
    finish(y)
    final = jnp.concatenate(
        [m, inv, inner * (1.0 / SCALE), jnp.zeros((5, 16 * SLOTS), F32)], axis=0
    )
    for t in range(8):
        fs[t] = final[:, t * DIM : (t + 1) * DIM]
    keys = kb[...].reshape(PROMPT, DIM)
    grad_v = dot_nn(pw[y], g_all)
    grad_k = dot_nn(ds[y], q_all)
    for b in a_others:
        remote(FIN, fs.at[lax.div(b, 2)], fr.at[a], a_peer(b)).start()
    fr[a] = fs[lax.div(a, 2)]
    for t in range(8):
        grad_q = dot_tn(ds[:, :, t * 128 : (t + 1) * 128].reshape(PROMPT, 2 * SLOTS), keys)
        dqs[2 * t] = grad_q[:SLOTS].astype(BF16)
        dqs[2 * t + 1] = grad_q[SLOTS:].astype(BF16)
    for b in a_others:
        remote(DQ, dqs.at[b], dqr.at[a], a_peer(b)).start()
    dqr[a] = dqs[a]

    def next_sum(total, kind_y, received, held, send, kind_z, target):
        arrived(kind_y, received.at[pl.ds(0, 3)])
        for b in y_others:
            total = total + received[b].astype(F32)
        held[...] = total.reshape(4, 32, DIM)
        send[...] = total.astype(BF16).reshape(4, 32, DIM)
        for b in z_others:
            remote(kind_z, send.at[b], target.at[z_hi], z_peer(b)).start()

    next_sum(grad_v, YSUM_V, rv, hv, szv, ZSUM_V, rzv)
    next_sum(grad_k, YSUM_K, rk, hk, szk, ZSUM_K, rzk)

    arrived(FIN, fr.at[pl.ds(0, 15)])
    for t in range(8):
        cols = slice(t * 256, (t + 1) * 256)
        fin = side_by_side(fr, t)
        m, inv, inner = fin[0:1], fin[1:2], fin[2:3]
        coef = jnp.exp2(st[t, 0:1, :] - m) * inv * weight
        e = own_e[t]
        p = (e * coef).astype(BF16)
        dsc = (e * (own_d[t] - inner) * (coef * SCALE)).astype(BF16)
        dvo[:, cols] = dot_nn(p, both(xg, t)).astype(BF16)
        dko[:, cols] = dot_nn(dsc, both(xq, t)).astype(BF16)
        grad_q = dot_tn(dsc, ck[:, cols])
        own_q[2 * t] = grad_q[:SLOTS, :DIM]
        own_q[2 * t + 1] = grad_q[SLOTS:, DIM:]
    stores = [
        pltpu.make_async_copy(src, dst, out_sem.at[n])
        for n, (src, dst) in enumerate(
            ((dqo, dq_hbm), (dko, dk_hbm), (dvo, dv_hbm), (gko, gk_hbm), (gvo, gv_hbm))
        )
    ]
    for store in stores[1:3]:
        store.start()

    arrived(ZSUM_V, rzv.at[pl.ds(0, 3)])
    arrived(ZSUM_K, rzk.at[pl.ds(0, 3)])
    line = lax.broadcasted_iota(jnp.int32, (16, 8, DIM), 1)
    lines = jnp.zeros((16, 8, DIM), F32)
    for kv, (held, received) in enumerate(((hk, rzk), (hv, rzv))):
        part = held[z_hi]
        for b in z_others:
            part = part + received[b].astype(F32)
        for r in range(2):
            lines = jnp.where(line == kv * 2 + r, part[r * 16 : (r + 1) * 16][:, None, :], lines)
    t3[...] = lines
    for b in a_others:
        remote(OUT, t3.at[b], r3.at[a], a_peer(b)).start()
    r3[a] = t3[a]
    arrived(DQ, dqr.at[pl.ds(0, 15)])
    for h in range(HEADS):
        dqo[:, h * DIM : (h + 1) * DIM] = (own_q[h] + dqr[h].astype(F32)).astype(BF16)
    stores[0].start()
    arrived(OUT, r3.at[pl.ds(0, 15)])
    for h in range(HEADS):
        cols = slice(h * DIM, (h + 1) * DIM)
        gko[:, cols] = r3[h, 0:2, :].astype(BF16)
        gvo[:, cols] = r3[h, 2:4, :].astype(BF16)

    for store in stores[3:]:
        store.start()

    sent(KV, kvs.at[pl.ds(0, 15)])
    sent(QUERY, xq.at[pl.ds(0, 15)])
    sent(GRAD, xg.at[pl.ds(0, 15)])
    sent(ZK, kb.at[0, pl.ds(0, 3)])
    sent(ZV, vb.at[0, pl.ds(0, 3)])
    sent(ZSUM, gsumr.at[pl.ds(0, 3)])
    sent(YK, kb.at[pl.ds(0, 3)])
    sent(YV, vb.at[pl.ds(0, 3)])
    sent(OWN, str_.at[pl.ds(0, 15)])
    sent(FIN, fr.at[pl.ds(0, 15)])
    sent(DQ, dqs.at[pl.ds(0, 15)])
    sent(YSUM_V, sbv.at[pl.ds(0, 3)])
    sent(YSUM_K, sbk.at[pl.ds(0, 3)])
    sent(ZSUM_V, szv.at[pl.ds(0, 3)])
    sent(ZSUM_K, szk.at[pl.ds(0, 3)])
    sent(OUT, t3.at[pl.ds(0, 15)])
    for store in stores:
        store.wait()


def store_all(*refs):
    sources, targets, held, sem = refs[:5], refs[5:10], refs[10:15], refs[15]
    parts = []
    for n in range(5):
        rows = sources[n].shape[0]
        step = min(rows, 64)
        for first in range(0, rows, step):
            parts.append((n, pl.ds(first, step)))
    loads = [
        pltpu.make_async_copy(sources[n].at[span], held[n].at[span], sem.at[0, p])
        for p, (n, span) in enumerate(parts)
    ]
    stores = [
        pltpu.make_async_copy(held[n].at[span], targets[n].at[span], sem.at[1, p])
        for p, (n, span) in enumerate(parts)
    ]
    for load in loads:
        load.start()
    for load, store in zip(loads, stores):
        load.wait()
        store.start()
    for store in stores:
        store.wait()


def shards(prompt_k, prompt_v, comp_q, comp_k, comp_v, grad_out, rewards, mask_pos):
    hbm = pl.BlockSpec(memory_space=pltpu.HBM)
    V = pltpu.VMEM
    grads = pl.pallas_call(
        kernel,
        out_shape=(
            jax.ShapeDtypeStruct((SLOTS, WIDTH), BF16),
            jax.ShapeDtypeStruct((ROWS, WIDTH), BF16),
            jax.ShapeDtypeStruct((ROWS, WIDTH), BF16),
            jax.ShapeDtypeStruct((2, WIDTH), BF16),
            jax.ShapeDtypeStruct((2, WIDTH), BF16),
        ),
        in_specs=[hbm] * 8,
        out_specs=(hbm,) * 5,
        scratch_shapes=[
            V((2, WIDTH), BF16),
            V((2, WIDTH), BF16),
            V((1, 1), F32),
            V((1, SLOTS), jnp.int32),
            V((ROWS, WIDTH), BF16),
            V((ROWS, WIDTH), BF16),
            V((ROWS, WIDTH), BF16),
            V((SLOTS, WIDTH), BF16),
            V((16, SLOTS, DIM), BF16),
            V((16, SLOTS, DIM), BF16),
            V((16, SLOTS, DIM), BF16),
            V((16, SLOTS, DIM), BF16),
            V((16, 8, DIM), F32),
            V((16, 8, DIM), F32),
            V((4, 4, 32, DIM), BF16),
            V((4, 4, 32, DIM), BF16),
            V((8, DIM), F32),
            V((4, 8, DIM), F32),
            V((8, 128, DIM), F32),
            V((8, 128, DIM), F32),
            V((8, 8, DIM), F32),
            V((16, 8, DIM), F32),
            V((8, 8, DIM), F32),
            V((16, 8, DIM), F32),
            V((4, 128, 16 * SLOTS), F32),
            V((4, 128, 16 * SLOTS), F32),
            V((4, 8, 16 * SLOTS), F32),
            V((4, 128, 16 * SLOTS), BF16),
            V((4, 128, 16 * SLOTS), BF16),
            V((4, 128, DIM), BF16),
            V((4, 128, DIM), BF16),
            V((4, 128, DIM), BF16),
            V((4, 128, DIM), BF16),
            V((4, 32, DIM), F32),
            V((4, 32, DIM), F32),
            V((4, 32, DIM), BF16),
            V((4, 32, DIM), BF16),
            V((4, 32, DIM), BF16),
            V((4, 32, DIM), BF16),
            V((16, 8, DIM), F32),
            V((16, 8, DIM), F32),
            V((16, SLOTS, DIM), BF16),
            V((16, SLOTS, DIM), BF16),
            V((16, SLOTS, DIM), F32),
            V((SLOTS, WIDTH), BF16),
            V((ROWS, WIDTH), BF16),
            V((ROWS, WIDTH), BF16),
            V((2, WIDTH), BF16),
            V((2, WIDTH), BF16),
            pltpu.SemaphoreType.DMA((8,)),
            pltpu.SemaphoreType.DMA((5,)),
            pltpu.SemaphoreType.DMA((KINDS,)),
            pltpu.SemaphoreType.DMA((KINDS,)),
            pltpu.SemaphoreType.DMA((2, 4)),
        ],
        compiler_params=pltpu.CompilerParams(
            collective_id=0, has_side_effects=True, vmem_limit_bytes=60 * 1024 * 1024
        ),
    )(
        prompt_k, prompt_v, rewards, mask_pos[0], comp_q[0, 0], comp_k[0, 0], comp_v[0, 0],
        grad_out[0, 0],
    )
    dq, dk, dv, gk, gv = pl.pallas_call(
        store_all,
        out_shape=[jax.ShapeDtypeStruct(grad.shape, BF16) for grad in grads],
        in_specs=[hbm] * 5,
        out_specs=[hbm] * 5,
        scratch_shapes=[V(grad.shape, BF16) for grad in grads] + [pltpu.SemaphoreType.DMA((2, 12))],
        compiler_params=pltpu.CompilerParams(vmem_limit_bytes=60 * 1024 * 1024),
    )(*grads)
    return dq[None, None], dk[None, None], dv[None, None], gk, gv


def solution(mesh):
    wide = P("grp", "ctx", None, None)
    rows = P(("grp", "ctx"), None)
    return jax.shard_map(
        shards,
        mesh=mesh,
        in_specs=(rows, rows, wide, wide, wide, wide, P("grp", "ctx"), P("grp", "ctx", None)),
        out_specs=(wide, wide, wide, rows, rows),
        check_vma=False,
    )
```

```python
import jax
import jax.numpy as jnp
from jax import lax
from jax.experimental import pallas as pl
from jax.experimental.pallas import tpu as pltpu
from jax.sharding import PartitionSpec as P

HEADS = 16
DIM = 128
SLOTS = 64
ROWS = 128
WIDTH = 2048
PROMPT = 512
F32 = jnp.float32
BF16 = jnp.bfloat16
SCALE = DIM ** -0.5
SCALE2 = SCALE * 1.4426950408889634
MESH = pl.DeviceIdType.MESH

(
    KV, QUERY, GRAD, ZK, ZV, ZSUM, YK, YV, OWN, FIN, DQ, YSUM_K, YSUM_V, ZSUM_K, ZSUM_V, OUT, KINDS
) = range(17)


def dot_nt(a, b):
    return lax.dot_general(a, b, (((1,), (1,)), ((), ())), preferred_element_type=F32)


def dot_nn(a, b):
    return lax.dot_general(a, b, (((1,), (0,)), ((), ())), preferred_element_type=F32)


def dot_tn(a, b):
    return lax.dot_general(a, b, (((0,), (0,)), ((), ())), preferred_element_type=F32)


def kernel(
    pk_hbm, pv_hbm, rw_hbm, mp_hbm, cq_hbm, ck_hbm, cv_hbm, go_hbm,
    dq_hbm, dk_hbm, dv_hbm, gp_hbm,
    pk, pv, rw, mp, cq, ck, cv, go, xq, xqr, xg, xgr, kvs, kvr, kb, vb, gsum, gsumr, own_e, own_d, st, str_,
    fs, fr, exps, prods, part, pw, ds,
    sbk, sbv, rk, rv, hk, hv, szk, szv, rzk, rzv, t3, dqs, dqr, own_q, dqo, dko, dvo,
    in_sem, out_sem, ss, rs, ry,
):
    grp = lax.axis_index("grp")
    ctx = lax.axis_index("ctx")
    x_lo, y = lax.div(grp, 4), lax.rem(grp, 4)
    z = lax.div(ctx, 4)
    z_hi, z_lo, low = lax.div(z, 2), lax.rem(z, 2), lax.rem(ctx, 4)
    a = z_lo * 8 + x_lo * 4 + low

    def a_peer(b):
        return {
            "grp": lax.rem(lax.div(b, 4), 2) * 4 + y,
            "ctx": (z_hi * 2 + lax.div(b, 8)) * 4 + lax.rem(b, 4),
        }

    def z_peer(b):
        return {"grp": grp, "ctx": (b * 2 + z_lo) * 4 + low}

    def y_peer(b):
        return {"grp": x_lo * 4 + b, "ctx": ctx}

    a_others = [z_lo * 8 + lax.rem(a + k, 8) for k in range(1, 8)]
    a_others += [(1 - z_lo) * 8 + lax.rem(a + k, 8) for k in range(8)]
    z_others = [lax.rem(z_hi + k, 4) for k in range(1, 4)]
    y_others = [lax.rem(y + k, 4) for k in range(1, 4)]

    def remote(kind, src, dst, device):
        return pltpu.make_async_remote_copy(
            src_ref=src, dst_ref=dst, send_sem=ss.at[kind], recv_sem=rs.at[kind],
            device_id=device, device_id_type=MESH,
        )

    def along_y(kv, ref, row, b):
        return pltpu.make_async_remote_copy(
            src_ref=ref.at[row], dst_ref=ref.at[row], send_sem=ss.at[YK + kv],
            recv_sem=ry.at[kv, row], device_id=y_peer(b), device_id_type=MESH,
        )

    def arrived(kind, dst):
        remote(kind, dst, dst, y_peer(y_others[0])).wait_recv()

    def sent(kind, src):
        remote(kind, src, src, y_peer(y_others[0])).wait_send()

    loads = [
        pltpu.make_async_copy(src, dst, in_sem.at[n])
        for n, (src, dst) in enumerate(
            (
                (pk_hbm, pk), (pv_hbm, pv), (rw_hbm, rw), (mp_hbm, mp),
                (cq_hbm, cq), (go_hbm, go), (ck_hbm, ck), (cv_hbm, cv),
            )
        )
    ]
    for load in loads:
        load.start()

    barrier = pltpu.get_barrier_semaphore()
    for b in a_others:
        pl.semaphore_signal(barrier, inc=1, device_id=a_peer(b), device_id_type=MESH)
    for b in z_others:
        pl.semaphore_signal(barrier, inc=1, device_id=z_peer(b), device_id_type=MESH)
    for b in y_others:
        pl.semaphore_signal(barrier, inc=1, device_id=y_peer(b), device_id_type=MESH)

    for load in loads[:4]:
        load.wait()
    pos = mp[...]
    pos2 = jnp.concatenate([pos, pos], axis=1)
    live = pos < ROWS
    count = jnp.sum(jnp.where(live, 1.0, 0.0), axis=1, keepdims=True)
    reward = rw[...]
    lines = jnp.concatenate(
        [
            pk[...].astype(F32),
            pv[...].astype(F32),
            jnp.broadcast_to(count, (1, WIDTH)),
            jnp.broadcast_to(reward, (1, WIDTH)),
            jnp.zeros((2, WIDTH), F32),
        ],
        axis=0,
    )
    for h in range(HEADS):
        kvs[h] = lines[:, h * DIM : (h + 1) * DIM]

    pl.semaphore_wait(barrier, 21)

    for b in a_others:
        remote(KV, kvs.at[b], kvr.at[a], a_peer(b)).start()
    kvr[a] = kvs[a]

    row = lax.broadcasted_iota(jnp.int32, (ROWS, 2 * SLOTS), 0)
    pick = jnp.where(row == jnp.minimum(pos2, ROWS - 1), 1.0, 0.0).astype(BF16)
    loads[4].wait()
    picked = dot_tn(pick, cq[...])[:SLOTS].astype(BF16)
    for h in range(HEADS):
        xq[h] = picked[:, h * DIM : (h + 1) * DIM]
    for b in a_others:
        remote(QUERY, xq.at[b], xqr.at[a], a_peer(b)).start()
    xqr[a] = xq[a]
    loads[5].wait()
    for h in range(HEADS):
        xg[h] = go[:, h * DIM : (h + 1) * DIM]

    nothing = jnp.zeros((SLOTS, DIM), BF16)

    def both(ref, t):
        return jnp.concatenate(
            [
                jnp.concatenate([ref[2 * t], nothing], axis=1),
                jnp.concatenate([nothing, ref[2 * t + 1]], axis=1),
            ],
            axis=0,
        )

    def own_scores(t):
        cols = slice(t * 256, (t + 1) * 256)
        s = dot_nt(ck[:, cols], both(xq, t)) * SCALE2
        d = dot_nt(cv[:, cols], both(xg, t))
        m = jnp.max(s, axis=0, keepdims=True)
        e = jnp.exp2(s - m)
        own_e[t] = e
        own_d[t] = d
        st[t] = jnp.concatenate(
            [
                m,
                jnp.sum(e, axis=0, keepdims=True),
                jnp.sum(e * d, axis=0, keepdims=True),
                jnp.zeros((5, DIM), F32),
            ],
            axis=0,
        )

    left = lax.broadcasted_iota(jnp.int32, (8, DIM), 1) < SLOTS
    odd = jnp.broadcast_to(lax.rem(a, 2), (8, DIM)) == 1

    def side_by_side(ref, t):
        one, two = ref[2 * t], ref[2 * t + 1]
        moved = pltpu.roll(jnp.where(odd, one, two), SLOTS, 1)
        return jnp.where(left != odd, jnp.where(left, one, two), moved)

    loads[6].wait()
    loads[7].wait()
    for t in range(4):
        own_scores(t)

    arrived(KV, kvr.at[pl.ds(0, 15)])
    blocks = kvr[...]
    kb[y, z_hi, 0:16, :] = blocks[:, 0, :].astype(BF16)
    kb[y, z_hi, 16:32, :] = blocks[:, 1, :].astype(BF16)
    for b in z_others:
        remote(ZK, kb.at[y, z_hi], kb.at[y, z_hi], z_peer(b)).start()
    vb[y, z_hi, 0:16, :] = blocks[:, 2, :].astype(BF16)
    vb[y, z_hi, 16:32, :] = blocks[:, 3, :].astype(BF16)
    for b in z_others:
        remote(ZV, vb.at[y, z_hi], vb.at[y, z_hi], z_peer(b)).start()
    mine = lax.broadcasted_iota(jnp.int32, (16, DIM), 0) // 4 % 2 == x_lo
    count16 = jnp.sum(jnp.where(mine, blocks[:, 4, :], 0.0), axis=0, keepdims=True)
    reward16 = jnp.sum(jnp.where(mine, blocks[:, 5, :], 0.0), axis=0, keepdims=True)
    gsum[...] = jnp.concatenate([count16, reward16, jnp.zeros((6, DIM), F32)], axis=0)
    for b in z_others:
        remote(ZSUM, gsum, gsumr.at[z_hi], z_peer(b)).start()
    for b in a_others:
        remote(GRAD, xg.at[b], xgr.at[a], a_peer(b)).start()
    xgr[a] = xg[a]

    for t in range(4, 8):
        own_scores(t)

    arrived(ZK, kb.at[0, pl.ds(0, 3)])
    for b in y_others:
        along_y(0, kb, y, b).start()
    arrived(ZV, vb.at[0, pl.ds(0, 3)])
    for b in y_others:
        along_y(1, vb, y, b).start()
    arrived(ZSUM, gsumr.at[pl.ds(0, 3)])
    total = gsum[...]
    for b in z_others:
        total = total + gsumr[b]
    weight = (reward - total[1:2] / 32.0) * (SLOTS * 32) / total[0:1]
    weight = jnp.where(pos2 < ROWS, weight, 0.0)
    for t in range(8):
        st[t, 3:4, :] = weight
    for b in a_others:
        remote(OWN, st.at[lax.div(b, 2)], str_.at[a], a_peer(b)).start()
    str_[a] = st[lax.div(a, 2)]

    def key_block(b):
        block = kb[b].reshape(128, DIM)
        for n in range(4):
            cols = slice(n * 256, (n + 1) * 256)
            s = dot_nt(block, xqr[4 * n : 4 * n + 4].reshape(256, DIM)) * SCALE2
            m = jnp.max(s, axis=0, keepdims=True)
            e = jnp.exp2(s - m)
            exps[b, :, cols] = e
            part[b, 0:1, cols] = m
            part[b, 1:2, cols] = jnp.sum(e, axis=0, keepdims=True)

    def value_block(b):
        block = vb[b].reshape(128, DIM)
        for n in range(4):
            cols = slice(n * 256, (n + 1) * 256)
            d = dot_nt(block, xgr[4 * n : 4 * n + 4].reshape(256, DIM)) * SCALE
            prods[b, :, cols] = d
            part[b, 2:3, cols] = jnp.sum(exps[b, :, cols] * d, axis=0, keepdims=True)

    near_first = [y_others[0], y_others[2], y_others[1]]
    far_first = [y_others[1], y_others[0], y_others[2]]
    arrived(QUERY, xqr.at[pl.ds(0, 15)])
    key_block(y)
    for b in near_first:
        along_y(0, kb, b, b).wait_recv()
        key_block(b)
    arrived(OWN, str_.at[pl.ds(0, 15)])
    stats = jnp.concatenate([side_by_side(str_, t) for t in range(8)], axis=1)
    m = stats[0:1]
    for b in range(4):
        m = jnp.maximum(m, part[b, 0:1, :])
    fo = jnp.exp2(stats[0:1] - m)
    total = stats[1:2] * fo
    for b in range(4):
        f = jnp.exp2(part[b, 0:1, :] - m)
        total = total + part[b, 1:2, :] * f
        part[b, 3:4, :] = f
    inv = 1.0 / total
    weights = stats[3:4]

    def probabilities(b):
        coef = part[b, 3:4, :] * inv
        for n in range(4):
            cols = slice(n * 256, (n + 1) * 256)
            p = exps[b, :, cols] * coef[:, cols]
            exps[b, :, cols] = p
            pw[b, :, cols] = (p * weights[:, cols]).astype(BF16)

    arrived(GRAD, xgr.at[pl.ds(0, 15)])
    q_all = xqr[...].reshape(16 * SLOTS, DIM)
    g_all = xgr[...].reshape(16 * SLOTS, DIM)
    for b in far_first:
        probabilities(b)
        sbv[b] = dot_nn(pw[b], g_all).astype(BF16)
        remote(YSUM_V, sbv.at[b], rv.at[y], y_peer(b)).start()
    probabilities(y)

    value_block(y)
    for b in near_first:
        along_y(1, vb, b, b).wait_recv()
        value_block(b)
    inner = stats[2:3] * (fo * inv * SCALE)
    for b in range(4):
        inner = inner + part[b, 2:3, :]

    def finish(b):
        for n in range(4):
            cols = slice(n * 256, (n + 1) * 256)
            dscore = exps[b, :, cols] * (prods[b, :, cols] - inner[:, cols])
            ds[b, :, cols] = (dscore * weights[:, cols]).astype(BF16)

    for b in far_first:
        finish(b)
        sbk[b] = dot_nn(ds[b], q_all).astype(BF16)
        remote(YSUM_K, sbk.at[b], rk.at[y], y_peer(b)).start()
    finish(y)
    final = jnp.concatenate(
        [m, inv, inner * (1.0 / SCALE), jnp.zeros((5, 16 * SLOTS), F32)], axis=0
    )
    for t in range(8):
        fs[t] = final[:, t * DIM : (t + 1) * DIM]
    keys = kb[...].reshape(PROMPT, DIM)
    grad_v = dot_nn(pw[y], g_all)
    grad_k = dot_nn(ds[y], q_all)
    for b in a_others:
        remote(FIN, fs.at[lax.div(b, 2)], fr.at[a], a_peer(b)).start()
    fr[a] = fs[lax.div(a, 2)]
    for t in range(8):
        grad_q = dot_tn(ds[:, :, t * 128 : (t + 1) * 128].reshape(PROMPT, 2 * SLOTS), keys)
        dqs[2 * t] = grad_q[:SLOTS].astype(BF16)
        dqs[2 * t + 1] = grad_q[SLOTS:].astype(BF16)
    for b in a_others:
        remote(DQ, dqs.at[b], dqr.at[a], a_peer(b)).start()
    dqr[a] = dqs[a]

    def next_sum(total, kind_y, received, held, send, kind_z, target):
        arrived(kind_y, received.at[pl.ds(0, 3)])
        for b in y_others:
            total = total + received[b].astype(F32)
        held[...] = total.reshape(4, 32, DIM)
        send[...] = total.astype(BF16).reshape(4, 32, DIM)
        for b in z_others:
            remote(kind_z, send.at[b], target.at[z_hi], z_peer(b)).start()

    next_sum(grad_v, YSUM_V, rv, hv, szv, ZSUM_V, rzv)
    next_sum(grad_k, YSUM_K, rk, hk, szk, ZSUM_K, rzk)

    arrived(FIN, fr.at[pl.ds(0, 15)])
    for t in range(8):
        cols = slice(t * 256, (t + 1) * 256)
        fin = side_by_side(fr, t)
        m, inv, inner = fin[0:1], fin[1:2], fin[2:3]
        coef = jnp.exp2(st[t, 0:1, :] - m) * inv * weight
        e = own_e[t]
        p = (e * coef).astype(BF16)
        dsc = (e * (own_d[t] - inner) * (coef * SCALE)).astype(BF16)
        dvo[:, cols] = dot_nn(p, both(xg, t)).astype(BF16)
        dko[:, cols] = dot_nn(dsc, both(xq, t)).astype(BF16)
        grad_q = dot_tn(dsc, ck[:, cols])
        own_q[2 * t] = grad_q[:SLOTS, :DIM]
        own_q[2 * t + 1] = grad_q[SLOTS:, DIM:]
    stores = [
        pltpu.make_async_copy(src, dst, out_sem.at[n])
        for n, (src, dst) in enumerate(
            ((dqo, dq_hbm), (dko, dk_hbm), (dvo, dv_hbm), (t3.at[a], gp_hbm.at[a]))
        )
    ]
    for store in stores[1:3]:
        store.start()

    arrived(ZSUM_V, rzv.at[pl.ds(0, 3)])
    arrived(ZSUM_K, rzk.at[pl.ds(0, 3)])
    line = lax.broadcasted_iota(jnp.int32, (16, 8, DIM), 1)
    lines = jnp.zeros((16, 8, DIM), F32)
    for kv, (held, received) in enumerate(((hk, rzk), (hv, rzv))):
        part = held[z_hi]
        for b in z_others:
            part = part + received[b].astype(F32)
        for r in range(2):
            lines = jnp.where(line == kv * 2 + r, part[r * 16 : (r + 1) * 16][:, None, :], lines)
    t3[...] = lines
    for b in a_others:
        remote(OUT, t3.at[b], gp_hbm.at[a], a_peer(b)).start()
    stores[3].start()
    arrived(DQ, dqr.at[pl.ds(0, 15)])
    for h in range(HEADS):
        dqo[:, h * DIM : (h + 1) * DIM] = (own_q[h] + dqr[h].astype(F32)).astype(BF16)
    stores[0].start()
    arrived(OUT, gp_hbm.at[pl.ds(0, 15)])

    sent(KV, kvs.at[pl.ds(0, 15)])
    sent(QUERY, xq.at[pl.ds(0, 15)])
    sent(GRAD, xg.at[pl.ds(0, 15)])
    sent(ZK, kb.at[0, pl.ds(0, 3)])
    sent(ZV, vb.at[0, pl.ds(0, 3)])
    sent(ZSUM, gsumr.at[pl.ds(0, 3)])
    sent(YK, kb.at[pl.ds(0, 3)])
    sent(YV, vb.at[pl.ds(0, 3)])
    sent(OWN, str_.at[pl.ds(0, 15)])
    sent(FIN, fr.at[pl.ds(0, 15)])
    sent(DQ, dqs.at[pl.ds(0, 15)])
    sent(YSUM_V, sbv.at[pl.ds(0, 3)])
    sent(YSUM_K, sbk.at[pl.ds(0, 3)])
    sent(ZSUM_V, szv.at[pl.ds(0, 3)])
    sent(ZSUM_K, szk.at[pl.ds(0, 3)])
    sent(OUT, t3.at[pl.ds(0, 15)])
    for store in stores:
        store.wait()


def store_all(dq, dk, dv, gp, dq_out, dk_out, dv_out, gk_out, gv_out, *scratch):
    dq_held, dk_held, dv_held, gp_held, gk_held, gv_held, in_sem, out_sem = scratch
    parts = [(gp, gp_held)]
    stores = []
    for source, held, target in ((dq, dq_held, dq_out), (dk, dk_held, dk_out), (dv, dv_held, dv_out)):
        for first in range(0, source.shape[0], SLOTS):
            span = pl.ds(first, SLOTS)
            parts.append((source.at[span], held.at[span]))
            stores.append((held.at[span], target.at[span]))
    stores += [(gk_held, gk_out), (gv_held, gv_out)]
    loads = [pltpu.make_async_copy(*pair, in_sem.at[n]) for n, pair in enumerate(parts)]
    stores = [pltpu.make_async_copy(*pair, out_sem.at[n]) for n, pair in enumerate(stores)]
    for load in loads[1:] + loads[:1]:
        load.start()
    for load, store in zip(loads[1:], stores):
        load.wait()
        store.start()
    loads[0].wait()
    for h in range(HEADS):
        cols = slice(h * DIM, (h + 1) * DIM)
        gk_held[:, cols] = gp_held[h, 0:2, :].astype(BF16)
        gv_held[:, cols] = gp_held[h, 2:4, :].astype(BF16)
    for store in stores[-2:]:
        store.start()
    for store in stores:
        store.wait()


def shards(prompt_k, prompt_v, comp_q, comp_k, comp_v, grad_out, rewards, mask_pos):
    hbm = pl.BlockSpec(memory_space=pltpu.HBM)
    V = pltpu.VMEM
    grads = pl.pallas_call(
        kernel,
        out_shape=(
            jax.ShapeDtypeStruct((SLOTS, WIDTH), BF16),
            jax.ShapeDtypeStruct((ROWS, WIDTH), BF16),
            jax.ShapeDtypeStruct((ROWS, WIDTH), BF16),
            jax.ShapeDtypeStruct((16, 8, DIM), F32),
        ),
        in_specs=[hbm] * 8,
        out_specs=(hbm,) * 4,
        scratch_shapes=[
            V((2, WIDTH), BF16),
            V((2, WIDTH), BF16),
            V((1, 1), F32),
            V((1, SLOTS), jnp.int32),
            V((ROWS, WIDTH), BF16),
            V((ROWS, WIDTH), BF16),
            V((ROWS, WIDTH), BF16),
            V((SLOTS, WIDTH), BF16),
            V((16, SLOTS, DIM), BF16),
            V((16, SLOTS, DIM), BF16),
            V((16, SLOTS, DIM), BF16),
            V((16, SLOTS, DIM), BF16),
            V((16, 8, DIM), F32),
            V((16, 8, DIM), F32),
            V((4, 4, 32, DIM), BF16),
            V((4, 4, 32, DIM), BF16),
            V((8, DIM), F32),
            V((4, 8, DIM), F32),
            V((8, 128, DIM), F32),
            V((8, 128, DIM), F32),
            V((8, 8, DIM), F32),
            V((16, 8, DIM), F32),
            V((8, 8, DIM), F32),
            V((16, 8, DIM), F32),
            V((4, 128, 16 * SLOTS), F32),
            V((4, 128, 16 * SLOTS), F32),
            V((4, 8, 16 * SLOTS), F32),
            V((4, 128, 16 * SLOTS), BF16),
            V((4, 128, 16 * SLOTS), BF16),
            V((4, 128, DIM), BF16),
            V((4, 128, DIM), BF16),
            V((4, 128, DIM), BF16),
            V((4, 128, DIM), BF16),
            V((4, 32, DIM), F32),
            V((4, 32, DIM), F32),
            V((4, 32, DIM), BF16),
            V((4, 32, DIM), BF16),
            V((4, 32, DIM), BF16),
            V((4, 32, DIM), BF16),
            V((16, 8, DIM), F32),
            V((16, SLOTS, DIM), BF16),
            V((16, SLOTS, DIM), BF16),
            V((16, SLOTS, DIM), F32),
            V((SLOTS, WIDTH), BF16),
            V((ROWS, WIDTH), BF16),
            V((ROWS, WIDTH), BF16),
            pltpu.SemaphoreType.DMA((8,)),
            pltpu.SemaphoreType.DMA((4,)),
            pltpu.SemaphoreType.DMA((KINDS,)),
            pltpu.SemaphoreType.DMA((KINDS,)),
            pltpu.SemaphoreType.DMA((2, 4)),
        ],
        compiler_params=pltpu.CompilerParams(
            collective_id=0, has_side_effects=True, vmem_limit_bytes=60 * 1024 * 1024
        ),
    )(
        prompt_k, prompt_v, rewards, mask_pos[0], comp_q[0, 0], comp_k[0, 0], comp_v[0, 0],
        grad_out[0, 0],
    )
    wide = [jax.ShapeDtypeStruct(grad.shape, BF16) for grad in grads[:3]]
    thin = [jax.ShapeDtypeStruct((2, WIDTH), BF16)] * 2
    dq, dk, dv, gk, gv = pl.pallas_call(
        store_all,
        out_shape=wide + thin,
        in_specs=[hbm] * 4,
        out_specs=[hbm] * 5,
        scratch_shapes=[V(grad.shape, BF16) for grad in grads[:3]]
        + [
            V((16, 8, DIM), F32),
            V((2, WIDTH), BF16),
            V((2, WIDTH), BF16),
            pltpu.SemaphoreType.DMA((6,)),
            pltpu.SemaphoreType.DMA((7,)),
        ],
        compiler_params=pltpu.CompilerParams(vmem_limit_bytes=60 * 1024 * 1024),
    )(*grads)
    return dq[None, None], dk[None, None], dv[None, None], gk, gv


def solution(mesh):
    wide = P("grp", "ctx", None, None)
    rows = P(("grp", "ctx"), None)
    return jax.shard_map(
        shards,
        mesh=mesh,
        in_specs=(rows, rows, wide, wide, wide, wide, P("grp", "ctx"), P("grp", "ctx", None)),
        out_specs=(wide, wide, wide, rows, rows),
        check_vma=False,
    )
```

```python
import jax
import jax.numpy as jnp
from jax import lax
from jax.experimental import pallas as pl
from jax.experimental.pallas import tpu as pltpu
from jax.sharding import PartitionSpec as P

HEADS = 16
DIM = 128
SLOTS = 64
ROWS = 128
WIDTH = 2048
PROMPT = 512
F32 = jnp.float32
BF16 = jnp.bfloat16
SCALE = DIM ** -0.5
SCALE2 = SCALE * 1.4426950408889634
MESH = pl.DeviceIdType.MESH

(
    KV, QUERY, GRAD, ZK, ZV, ZSUM, YK, YV, OWN, FIN, DQ, YSUM_K, YSUM_V, ZSUM_K, ZSUM_V, OUT, KINDS
) = range(17)


def dot_nt(a, b):
    return lax.dot_general(a, b, (((1,), (1,)), ((), ())), preferred_element_type=F32)


def dot_nn(a, b):
    return lax.dot_general(a, b, (((1,), (0,)), ((), ())), preferred_element_type=F32)


def dot_tn(a, b):
    return lax.dot_general(a, b, (((0,), (0,)), ((), ())), preferred_element_type=F32)


def kernel(
    pk_hbm, pv_hbm, rw_hbm, mp_hbm, cq_hbm, ck_hbm, cv_hbm, go_hbm,
    dq_hbm, dk_hbm, dv_hbm, gp_hbm,
    pk, pv, rw, mp, cq, ck, cv, go, xq, xqr, xg, xgr, kvs, kvr, kb, vb, gsum, gsumr, own_e, own_d, st, str_,
    fs, fr, exps, prods, part, pw, ds,
    sbk, sbv, rk, rv, hk, hv, szk, szv, rzk, rzv, t3, dqs, dqr, own_q, dqo, dko, dvo,
    in_sem, out_sem, ss, rs, ry,
):
    grp = lax.axis_index("grp")
    ctx = lax.axis_index("ctx")
    x_lo, y = lax.div(grp, 4), lax.rem(grp, 4)
    z = lax.div(ctx, 4)
    z_hi, z_lo, low = lax.div(z, 2), lax.rem(z, 2), lax.rem(ctx, 4)
    a = z_lo * 8 + x_lo * 4 + low

    def a_peer(b):
        return {
            "grp": lax.rem(lax.div(b, 4), 2) * 4 + y,
            "ctx": (z_hi * 2 + lax.div(b, 8)) * 4 + lax.rem(b, 4),
        }

    def z_peer(b):
        return {"grp": grp, "ctx": (b * 2 + z_lo) * 4 + low}

    def y_peer(b):
        return {"grp": x_lo * 4 + b, "ctx": ctx}

    a_others = [z_lo * 8 + lax.rem(a + k, 8) for k in range(1, 8)]
    a_others += [(1 - z_lo) * 8 + lax.rem(a + k, 8) for k in range(8)]
    z_others = [lax.rem(z_hi + k, 4) for k in range(1, 4)]
    y_others = [lax.rem(y + k, 4) for k in range(1, 4)]

    def remote(kind, src, dst, device):
        return pltpu.make_async_remote_copy(
            src_ref=src, dst_ref=dst, send_sem=ss.at[kind], recv_sem=rs.at[kind],
            device_id=device, device_id_type=MESH,
        )

    def along_y(kv, ref, row, b):
        return pltpu.make_async_remote_copy(
            src_ref=ref.at[row], dst_ref=ref.at[row], send_sem=ss.at[YK + kv],
            recv_sem=ry.at[kv, row], device_id=y_peer(b), device_id_type=MESH,
        )

    def arrived(kind, dst):
        remote(kind, dst, dst, y_peer(y_others[0])).wait_recv()

    def sent(kind, src):
        remote(kind, src, src, y_peer(y_others[0])).wait_send()

    loads = [
        pltpu.make_async_copy(src, dst, in_sem.at[n])
        for n, (src, dst) in enumerate(
            (
                (pk_hbm, pk), (pv_hbm, pv), (rw_hbm, rw), (mp_hbm, mp),
                (cq_hbm, cq), (go_hbm, go), (ck_hbm, ck), (cv_hbm, cv),
            )
        )
    ]
    for load in loads:
        load.start()

    barrier = pltpu.get_barrier_semaphore()
    for b in a_others:
        pl.semaphore_signal(barrier, inc=1, device_id=a_peer(b), device_id_type=MESH)
    for b in z_others:
        pl.semaphore_signal(barrier, inc=1, device_id=z_peer(b), device_id_type=MESH)
    for b in y_others:
        pl.semaphore_signal(barrier, inc=1, device_id=y_peer(b), device_id_type=MESH)

    for load in loads[:4]:
        load.wait()
    pos = mp[...]
    pos2 = jnp.concatenate([pos, pos], axis=1)
    live = pos < ROWS
    count = jnp.sum(jnp.where(live, 1.0, 0.0), axis=1, keepdims=True)
    reward = rw[...]
    lines = jnp.concatenate(
        [
            pk[...].astype(F32),
            pv[...].astype(F32),
            jnp.broadcast_to(count, (1, WIDTH)),
            jnp.broadcast_to(reward, (1, WIDTH)),
            jnp.zeros((2, WIDTH), F32),
        ],
        axis=0,
    )
    for h in range(HEADS):
        kvs[h] = lines[:, h * DIM : (h + 1) * DIM]

    pl.semaphore_wait(barrier, 21)

    for b in a_others:
        remote(KV, kvs.at[b], kvr.at[a], a_peer(b)).start()
    kvr[a] = kvs[a]

    row = lax.broadcasted_iota(jnp.int32, (ROWS, 2 * SLOTS), 0)
    pick = jnp.where(row == jnp.minimum(pos2, ROWS - 1), 1.0, 0.0).astype(BF16)
    loads[4].wait()
    picked = dot_tn(pick, cq[...])[:SLOTS].astype(BF16)
    for h in range(HEADS):
        xq[h] = picked[:, h * DIM : (h + 1) * DIM]
    loads[5].wait()
    for h in range(HEADS):
        xg[h] = go[:, h * DIM : (h + 1) * DIM]

    nothing = jnp.zeros((SLOTS, DIM), BF16)

    def both(ref, t):
        return jnp.concatenate(
            [
                jnp.concatenate([ref[2 * t], nothing], axis=1),
                jnp.concatenate([nothing, ref[2 * t + 1]], axis=1),
            ],
            axis=0,
        )

    def own_scores(t):
        cols = slice(t * 256, (t + 1) * 256)
        s = dot_nt(ck[:, cols], both(xq, t)) * SCALE2
        d = dot_nt(cv[:, cols], both(xg, t))
        m = jnp.max(s, axis=0, keepdims=True)
        e = jnp.exp2(s - m)
        own_e[t] = e
        own_d[t] = d
        st[t] = jnp.concatenate(
            [
                m,
                jnp.sum(e, axis=0, keepdims=True),
                jnp.sum(e * d, axis=0, keepdims=True),
                jnp.zeros((5, DIM), F32),
            ],
            axis=0,
        )

    left = lax.broadcasted_iota(jnp.int32, (8, DIM), 1) < SLOTS
    odd = jnp.broadcast_to(lax.rem(a, 2), (8, DIM)) == 1

    def side_by_side(ref, t):
        one, two = ref[2 * t], ref[2 * t + 1]
        moved = pltpu.roll(jnp.where(odd, one, two), SLOTS, 1)
        return jnp.where(left != odd, jnp.where(left, one, two), moved)

    loads[6].wait()
    loads[7].wait()
    for t in range(4):
        own_scores(t)

    arrived(KV, kvr.at[pl.ds(0, 15)])
    blocks = kvr[...]
    kb[y, z_hi, 0:16, :] = blocks[:, 0, :].astype(BF16)
    kb[y, z_hi, 16:32, :] = blocks[:, 1, :].astype(BF16)
    for b in z_others:
        remote(ZK, kb.at[y, z_hi], kb.at[y, z_hi], z_peer(b)).start()
    vb[y, z_hi, 0:16, :] = blocks[:, 2, :].astype(BF16)
    vb[y, z_hi, 16:32, :] = blocks[:, 3, :].astype(BF16)
    for b in z_others:
        remote(ZV, vb.at[y, z_hi], vb.at[y, z_hi], z_peer(b)).start()
    mine = lax.broadcasted_iota(jnp.int32, (16, DIM), 0) // 4 % 2 == x_lo
    count16 = jnp.sum(jnp.where(mine, blocks[:, 4, :], 0.0), axis=0, keepdims=True)
    reward16 = jnp.sum(jnp.where(mine, blocks[:, 5, :], 0.0), axis=0, keepdims=True)
    gsum[...] = jnp.concatenate([count16, reward16, jnp.zeros((6, DIM), F32)], axis=0)
    for b in z_others:
        remote(ZSUM, gsum, gsumr.at[z_hi], z_peer(b)).start()
    for b in a_others:
        remote(QUERY, xq.at[b], xqr.at[a], a_peer(b)).start()
    xqr[a] = xq[a]
    for b in a_others:
        remote(GRAD, xg.at[b], xgr.at[a], a_peer(b)).start()
    xgr[a] = xg[a]

    for t in range(4, 8):
        own_scores(t)

    arrived(ZK, kb.at[0, pl.ds(0, 3)])
    for b in y_others:
        along_y(0, kb, y, b).start()
    arrived(ZV, vb.at[0, pl.ds(0, 3)])
    for b in y_others:
        along_y(1, vb, y, b).start()
    arrived(ZSUM, gsumr.at[pl.ds(0, 3)])
    total = gsum[...]
    for b in z_others:
        total = total + gsumr[b]
    weight = (reward - total[1:2] / 32.0) * (SLOTS * 32) / total[0:1]
    weight = jnp.where(pos2 < ROWS, weight, 0.0)
    for t in range(8):
        st[t, 3:4, :] = weight
    for b in a_others:
        remote(OWN, st.at[lax.div(b, 2)], str_.at[a], a_peer(b)).start()
    str_[a] = st[lax.div(a, 2)]

    def key_block(b):
        block = kb[b].reshape(128, DIM)
        for n in range(4):
            cols = slice(n * 256, (n + 1) * 256)
            s = dot_nt(block, xqr[4 * n : 4 * n + 4].reshape(256, DIM)) * SCALE2
            m = jnp.max(s, axis=0, keepdims=True)
            e = jnp.exp2(s - m)
            exps[b, :, cols] = e
            part[b, 0:1, cols] = m
            part[b, 1:2, cols] = jnp.sum(e, axis=0, keepdims=True)

    def value_block(b):
        block = vb[b].reshape(128, DIM)
        for n in range(4):
            cols = slice(n * 256, (n + 1) * 256)
            d = dot_nt(block, xgr[4 * n : 4 * n + 4].reshape(256, DIM)) * SCALE
            prods[b, :, cols] = d
            part[b, 2:3, cols] = jnp.sum(exps[b, :, cols] * d, axis=0, keepdims=True)

    near_first = [y_others[0], y_others[2], y_others[1]]
    far_first = [y_others[1], y_others[0], y_others[2]]
    arrived(QUERY, xqr.at[pl.ds(0, 15)])
    key_block(y)
    for b in near_first:
        along_y(0, kb, b, b).wait_recv()
        key_block(b)
    arrived(OWN, str_.at[pl.ds(0, 15)])
    stats = jnp.concatenate([side_by_side(str_, t) for t in range(8)], axis=1)
    m = stats[0:1]
    for b in range(4):
        m = jnp.maximum(m, part[b, 0:1, :])
    fo = jnp.exp2(stats[0:1] - m)
    total = stats[1:2] * fo
    for b in range(4):
        f = jnp.exp2(part[b, 0:1, :] - m)
        total = total + part[b, 1:2, :] * f
        part[b, 3:4, :] = f
    inv = 1.0 / total
    weights = stats[3:4]

    def probabilities(b):
        coef = part[b, 3:4, :] * inv
        for n in range(4):
            cols = slice(n * 256, (n + 1) * 256)
            p = exps[b, :, cols] * coef[:, cols]
            exps[b, :, cols] = p
            pw[b, :, cols] = (p * weights[:, cols]).astype(BF16)

    arrived(GRAD, xgr.at[pl.ds(0, 15)])
    q_all = xqr[...].reshape(16 * SLOTS, DIM)
    g_all = xgr[...].reshape(16 * SLOTS, DIM)
    for b in far_first:
        probabilities(b)
        sbv[b] = dot_nn(pw[b], g_all).astype(BF16)
        remote(YSUM_V, sbv.at[b], rv.at[y], y_peer(b)).start()
    probabilities(y)

    value_block(y)
    for b in near_first:
        along_y(1, vb, b, b).wait_recv()
        value_block(b)
    inner = stats[2:3] * (fo * inv * SCALE)
    for b in range(4):
        inner = inner + part[b, 2:3, :]

    def finish(b):
        for n in range(4):
            cols = slice(n * 256, (n + 1) * 256)
            dscore = exps[b, :, cols] * (prods[b, :, cols] - inner[:, cols])
            ds[b, :, cols] = (dscore * weights[:, cols]).astype(BF16)

    for b in far_first:
        finish(b)
        sbk[b] = dot_nn(ds[b], q_all).astype(BF16)
        remote(YSUM_K, sbk.at[b], rk.at[y], y_peer(b)).start()
    finish(y)
    final = jnp.concatenate(
        [m, inv, inner * (1.0 / SCALE), jnp.zeros((5, 16 * SLOTS), F32)], axis=0
    )
    for t in range(8):
        fs[t] = final[:, t * DIM : (t + 1) * DIM]
    keys = kb[...].reshape(PROMPT, DIM)
    grad_v = dot_nn(pw[y], g_all)
    grad_k = dot_nn(ds[y], q_all)
    for b in a_others:
        remote(FIN, fs.at[lax.div(b, 2)], fr.at[a], a_peer(b)).start()
    fr[a] = fs[lax.div(a, 2)]
    for t in range(8):
        grad_q = dot_tn(ds[:, :, t * 128 : (t + 1) * 128].reshape(PROMPT, 2 * SLOTS), keys)
        dqs[2 * t] = grad_q[:SLOTS].astype(BF16)
        dqs[2 * t + 1] = grad_q[SLOTS:].astype(BF16)
    for b in a_others:
        remote(DQ, dqs.at[b], dqr.at[a], a_peer(b)).start()
    dqr[a] = dqs[a]

    def next_sum(total, kind_y, received, held, send, kind_z, target):
        arrived(kind_y, received.at[pl.ds(0, 3)])
        for b in y_others:
            total = total + received[b].astype(F32)
        held[...] = total.reshape(4, 32, DIM)
        send[...] = total.astype(BF16).reshape(4, 32, DIM)
        for b in z_others:
            remote(kind_z, send.at[b], target.at[z_hi], z_peer(b)).start()

    next_sum(grad_v, YSUM_V, rv, hv, szv, ZSUM_V, rzv)
    next_sum(grad_k, YSUM_K, rk, hk, szk, ZSUM_K, rzk)

    arrived(FIN, fr.at[pl.ds(0, 15)])
    for t in range(8):
        cols = slice(t * 256, (t + 1) * 256)
        fin = side_by_side(fr, t)
        m, inv, inner = fin[0:1], fin[1:2], fin[2:3]
        coef = jnp.exp2(st[t, 0:1, :] - m) * inv * weight
        e = own_e[t]
        p = (e * coef).astype(BF16)
        dsc = (e * (own_d[t] - inner) * (coef * SCALE)).astype(BF16)
        dvo[:, cols] = dot_nn(p, both(xg, t)).astype(BF16)
        dko[:, cols] = dot_nn(dsc, both(xq, t)).astype(BF16)
        grad_q = dot_tn(dsc, ck[:, cols])
        own_q[2 * t] = grad_q[:SLOTS, :DIM]
        own_q[2 * t + 1] = grad_q[SLOTS:, DIM:]
    stores = [
        pltpu.make_async_copy(src, dst, out_sem.at[n])
        for n, (src, dst) in enumerate(
            ((dqo, dq_hbm), (dko, dk_hbm), (dvo, dv_hbm), (t3.at[a], gp_hbm.at[a]))
        )
    ]
    for store in stores[1:3]:
        store.start()

    arrived(ZSUM_V, rzv.at[pl.ds(0, 3)])
    arrived(ZSUM_K, rzk.at[pl.ds(0, 3)])
    line = lax.broadcasted_iota(jnp.int32, (16, 8, DIM), 1)
    lines = jnp.zeros((16, 8, DIM), F32)
    for kv, (held, received) in enumerate(((hk, rzk), (hv, rzv))):
        part = held[z_hi]
        for b in z_others:
            part = part + received[b].astype(F32)
        for r in range(2):
            lines = jnp.where(line == kv * 2 + r, part[r * 16 : (r + 1) * 16][:, None, :], lines)
    t3[...] = lines
    for b in a_others:
        remote(OUT, t3.at[b], gp_hbm.at[a], a_peer(b)).start()
    stores[3].start()
    arrived(DQ, dqr.at[pl.ds(0, 15)])
    for h in range(HEADS):
        dqo[:, h * DIM : (h + 1) * DIM] = (own_q[h] + dqr[h].astype(F32)).astype(BF16)
    stores[0].start()
    arrived(OUT, gp_hbm.at[pl.ds(0, 15)])

    sent(KV, kvs.at[pl.ds(0, 15)])
    sent(QUERY, xq.at[pl.ds(0, 15)])
    sent(GRAD, xg.at[pl.ds(0, 15)])
    sent(ZK, kb.at[0, pl.ds(0, 3)])
    sent(ZV, vb.at[0, pl.ds(0, 3)])
    sent(ZSUM, gsumr.at[pl.ds(0, 3)])
    sent(YK, kb.at[pl.ds(0, 3)])
    sent(YV, vb.at[pl.ds(0, 3)])
    sent(OWN, str_.at[pl.ds(0, 15)])
    sent(FIN, fr.at[pl.ds(0, 15)])
    sent(DQ, dqs.at[pl.ds(0, 15)])
    sent(YSUM_V, sbv.at[pl.ds(0, 3)])
    sent(YSUM_K, sbk.at[pl.ds(0, 3)])
    sent(ZSUM_V, szv.at[pl.ds(0, 3)])
    sent(ZSUM_K, szk.at[pl.ds(0, 3)])
    sent(OUT, t3.at[pl.ds(0, 15)])
    for store in stores:
        store.wait()


def store_all(dq, dk, dv, gp, dq_out, dk_out, dv_out, gk_out, gv_out, *scratch):
    dq_held, dk_held, dv_held, gp_held, gk_held, gv_held, in_sem, out_sem = scratch
    parts = [(gp, gp_held)]
    stores = []
    for source, held, target in ((dq, dq_held, dq_out), (dk, dk_held, dk_out), (dv, dv_held, dv_out)):
        for first in range(0, source.shape[0], SLOTS):
            span = pl.ds(first, SLOTS)
            parts.append((source.at[span], held.at[span]))
            stores.append((held.at[span], target.at[span]))
    stores += [(gk_held, gk_out), (gv_held, gv_out)]
    loads = [pltpu.make_async_copy(*pair, in_sem.at[n]) for n, pair in enumerate(parts)]
    stores = [pltpu.make_async_copy(*pair, out_sem.at[n]) for n, pair in enumerate(stores)]
    for load in loads[1:] + loads[:1]:
        load.start()
    for load, store in zip(loads[1:], stores):
        load.wait()
        store.start()
    loads[0].wait()
    for h in range(HEADS):
        cols = slice(h * DIM, (h + 1) * DIM)
        gk_held[:, cols] = gp_held[h, 0:2, :].astype(BF16)
        gv_held[:, cols] = gp_held[h, 2:4, :].astype(BF16)
    for store in stores[-2:]:
        store.start()
    for store in stores:
        store.wait()


def shards(prompt_k, prompt_v, comp_q, comp_k, comp_v, grad_out, rewards, mask_pos):
    hbm = pl.BlockSpec(memory_space=pltpu.HBM)
    V = pltpu.VMEM
    grads = pl.pallas_call(
        kernel,
        out_shape=(
            jax.ShapeDtypeStruct((SLOTS, WIDTH), BF16),
            jax.ShapeDtypeStruct((ROWS, WIDTH), BF16),
            jax.ShapeDtypeStruct((ROWS, WIDTH), BF16),
            jax.ShapeDtypeStruct((16, 8, DIM), F32),
        ),
        in_specs=[hbm] * 8,
        out_specs=(hbm,) * 4,
        scratch_shapes=[
            V((2, WIDTH), BF16),
            V((2, WIDTH), BF16),
            V((1, 1), F32),
            V((1, SLOTS), jnp.int32),
            V((ROWS, WIDTH), BF16),
            V((ROWS, WIDTH), BF16),
            V((ROWS, WIDTH), BF16),
            V((SLOTS, WIDTH), BF16),
            V((16, SLOTS, DIM), BF16),
            V((16, SLOTS, DIM), BF16),
            V((16, SLOTS, DIM), BF16),
            V((16, SLOTS, DIM), BF16),
            V((16, 8, DIM), F32),
            V((16, 8, DIM), F32),
            V((4, 4, 32, DIM), BF16),
            V((4, 4, 32, DIM), BF16),
            V((8, DIM), F32),
            V((4, 8, DIM), F32),
            V((8, 128, DIM), F32),
            V((8, 128, DIM), F32),
            V((8, 8, DIM), F32),
            V((16, 8, DIM), F32),
            V((8, 8, DIM), F32),
            V((16, 8, DIM), F32),
            V((4, 128, 16 * SLOTS), F32),
            V((4, 128, 16 * SLOTS), F32),
            V((4, 8, 16 * SLOTS), F32),
            V((4, 128, 16 * SLOTS), BF16),
            V((4, 128, 16 * SLOTS), BF16),
            V((4, 128, DIM), BF16),
            V((4, 128, DIM), BF16),
            V((4, 128, DIM), BF16),
            V((4, 128, DIM), BF16),
            V((4, 32, DIM), F32),
            V((4, 32, DIM), F32),
            V((4, 32, DIM), BF16),
            V((4, 32, DIM), BF16),
            V((4, 32, DIM), BF16),
            V((4, 32, DIM), BF16),
            V((16, 8, DIM), F32),
            V((16, SLOTS, DIM), BF16),
            V((16, SLOTS, DIM), BF16),
            V((16, SLOTS, DIM), F32),
            V((SLOTS, WIDTH), BF16),
            V((ROWS, WIDTH), BF16),
            V((ROWS, WIDTH), BF16),
            pltpu.SemaphoreType.DMA((8,)),
            pltpu.SemaphoreType.DMA((4,)),
            pltpu.SemaphoreType.DMA((KINDS,)),
            pltpu.SemaphoreType.DMA((KINDS,)),
            pltpu.SemaphoreType.DMA((2, 4)),
        ],
        compiler_params=pltpu.CompilerParams(
            collective_id=0, has_side_effects=True, vmem_limit_bytes=60 * 1024 * 1024
        ),
    )(
        prompt_k, prompt_v, rewards, mask_pos[0], comp_q[0, 0], comp_k[0, 0], comp_v[0, 0],
        grad_out[0, 0],
    )
    wide = [jax.ShapeDtypeStruct(grad.shape, BF16) for grad in grads[:3]]
    thin = [jax.ShapeDtypeStruct((2, WIDTH), BF16)] * 2
    dq, dk, dv, gk, gv = pl.pallas_call(
        store_all,
        out_shape=wide + thin,
        in_specs=[hbm] * 4,
        out_specs=[hbm] * 5,
        scratch_shapes=[V(grad.shape, BF16) for grad in grads[:3]]
        + [
            V((16, 8, DIM), F32),
            V((2, WIDTH), BF16),
            V((2, WIDTH), BF16),
            pltpu.SemaphoreType.DMA((6,)),
            pltpu.SemaphoreType.DMA((7,)),
        ],
        compiler_params=pltpu.CompilerParams(vmem_limit_bytes=60 * 1024 * 1024),
    )(*grads)
    return dq[None, None], dk[None, None], dv[None, None], gk, gv


def solution(mesh):
    wide = P("grp", "ctx", None, None)
    rows = P(("grp", "ctx"), None)
    return jax.shard_map(
        shards,
        mesh=mesh,
        in_specs=(rows, rows, wide, wide, wide, wide, P("grp", "ctx"), P("grp", "ctx", None)),
        out_specs=(wide, wide, wide, rows, rows),
        check_vma=False,
    )
```

```python
import jax
import jax.numpy as jnp
from jax import lax
from jax.experimental import pallas as pl
from jax.experimental.pallas import tpu as pltpu
from jax.sharding import PartitionSpec as P

HEADS = 16
DIM = 128
SLOTS = 64
ROWS = 128
WIDTH = 2048
PROMPT = 512
F32 = jnp.float32
BF16 = jnp.bfloat16
SCALE = DIM ** -0.5
SCALE2 = SCALE * 1.4426950408889634
MESH = pl.DeviceIdType.MESH

(
    KV, QUERY, GRAD, ZK, ZV, ZSUM, YK, YV, OWN, FIN, DQ, YSUM_K, YSUM_V, ZSUM_K, ZSUM_V, OUT, KINDS
) = range(17)


def dot_nt(a, b):
    return lax.dot_general(a, b, (((1,), (1,)), ((), ())), preferred_element_type=F32)


def dot_nn(a, b):
    return lax.dot_general(a, b, (((1,), (0,)), ((), ())), preferred_element_type=F32)


def dot_tn(a, b):
    return lax.dot_general(a, b, (((0,), (0,)), ((), ())), preferred_element_type=F32)


def kernel(
    pk_hbm, pv_hbm, rw_hbm, mp_hbm, cq_hbm, ck_hbm, cv_hbm, go_hbm,
    dq_hbm, dk_hbm, dv_hbm, gp_hbm,
    pk, pv, rw, mp, cq, ck, cv, go, xq, xqr, xg, xgr, kvs, kvr, kb, vb, gsum, gsumr, own_e, own_d, st, str_,
    fs, fr, exps, prods, part, pw, ds, kt,
    sbk, sbv, rk, rv, hk, hv, szk, szv, rzk, rzv, t3, dqs, dqr, own_q, dqo, dko, dvo,
    in_sem, out_sem, ss, rs, ry,
):
    grp = lax.axis_index("grp")
    ctx = lax.axis_index("ctx")
    x_lo, y = lax.div(grp, 4), lax.rem(grp, 4)
    z = lax.div(ctx, 4)
    z_hi, z_lo, low = lax.div(z, 2), lax.rem(z, 2), lax.rem(ctx, 4)
    a = z_lo * 8 + x_lo * 4 + low

    def a_peer(b):
        return {
            "grp": lax.rem(lax.div(b, 4), 2) * 4 + y,
            "ctx": (z_hi * 2 + lax.div(b, 8)) * 4 + lax.rem(b, 4),
        }

    def z_peer(b):
        return {"grp": grp, "ctx": (b * 2 + z_lo) * 4 + low}

    def y_peer(b):
        return {"grp": x_lo * 4 + b, "ctx": ctx}

    a_others = [z_lo * 8 + lax.rem(a + k, 8) for k in range(1, 8)]
    a_others += [(1 - z_lo) * 8 + lax.rem(a + k, 8) for k in range(8)]
    z_others = [lax.rem(z_hi + k, 4) for k in range(1, 4)]
    y_others = [lax.rem(y + k, 4) for k in range(1, 4)]

    def remote(kind, src, dst, device):
        return pltpu.make_async_remote_copy(
            src_ref=src, dst_ref=dst, send_sem=ss.at[kind], recv_sem=rs.at[kind],
            device_id=device, device_id_type=MESH,
        )

    def along_y(kv, ref, row, b):
        return pltpu.make_async_remote_copy(
            src_ref=ref.at[row], dst_ref=ref.at[row], send_sem=ss.at[YK + kv],
            recv_sem=ry.at[kv, row], device_id=y_peer(b), device_id_type=MESH,
        )

    def arrived(kind, dst):
        remote(kind, dst, dst, y_peer(y_others[0])).wait_recv()

    def sent(kind, src):
        remote(kind, src, src, y_peer(y_others[0])).wait_send()

    loads = [
        pltpu.make_async_copy(src, dst, in_sem.at[n])
        for n, (src, dst) in enumerate(
            (
                (pk_hbm, pk), (pv_hbm, pv), (rw_hbm, rw), (mp_hbm, mp),
                (cq_hbm, cq), (go_hbm, go), (ck_hbm, ck), (cv_hbm, cv),
            )
        )
    ]
    for load in loads:
        load.start()

    barrier = pltpu.get_barrier_semaphore()
    for b in a_others:
        pl.semaphore_signal(barrier, inc=1, device_id=a_peer(b), device_id_type=MESH)
    for b in z_others:
        pl.semaphore_signal(barrier, inc=1, device_id=z_peer(b), device_id_type=MESH)
    for b in y_others:
        pl.semaphore_signal(barrier, inc=1, device_id=y_peer(b), device_id_type=MESH)

    for load in loads[:4]:
        load.wait()
    pos = mp[...]
    pos2 = jnp.concatenate([pos, pos], axis=1)
    live = pos < ROWS
    count = jnp.sum(jnp.where(live, 1.0, 0.0), axis=1, keepdims=True)
    reward = rw[...]
    lines = jnp.concatenate(
        [
            pk[...].astype(F32),
            pv[...].astype(F32),
            jnp.broadcast_to(count, (1, WIDTH)),
            jnp.broadcast_to(reward, (1, WIDTH)),
            jnp.zeros((2, WIDTH), F32),
        ],
        axis=0,
    )
    for h in range(HEADS):
        kvs[h] = lines[:, h * DIM : (h + 1) * DIM]

    pl.semaphore_wait(barrier, 21)

    for b in a_others:
        remote(KV, kvs.at[b], kvr.at[a], a_peer(b)).start()
    kvr[a] = kvs[a]

    row = lax.broadcasted_iota(jnp.int32, (ROWS, 2 * SLOTS), 0)
    pick = jnp.where(row == jnp.minimum(pos2, ROWS - 1), 1.0, 0.0).astype(BF16)
    loads[4].wait()
    picked = dot_tn(pick, cq[...])[:SLOTS].astype(BF16)
    for h in range(HEADS):
        xq[h] = picked[:, h * DIM : (h + 1) * DIM]
    loads[5].wait()
    for h in range(HEADS):
        xg[h] = go[:, h * DIM : (h + 1) * DIM]

    nothing = jnp.zeros((SLOTS, DIM), BF16)

    def both(ref, t):
        return jnp.concatenate(
            [
                jnp.concatenate([ref[2 * t], nothing], axis=1),
                jnp.concatenate([nothing, ref[2 * t + 1]], axis=1),
            ],
            axis=0,
        )

    def own_scores(t):
        cols = slice(t * 256, (t + 1) * 256)
        s = dot_nt(ck[:, cols], both(xq, t)) * SCALE2
        d = dot_nt(cv[:, cols], both(xg, t))
        m = jnp.max(s, axis=0, keepdims=True)
        e = jnp.exp2(s - m)
        own_e[t] = e
        own_d[t] = d
        st[t] = jnp.concatenate(
            [
                m,
                jnp.sum(e, axis=0, keepdims=True),
                jnp.sum(e * d, axis=0, keepdims=True),
                jnp.zeros((5, DIM), F32),
            ],
            axis=0,
        )

    left = lax.broadcasted_iota(jnp.int32, (8, DIM), 1) < SLOTS
    odd = jnp.broadcast_to(lax.rem(a, 2), (8, DIM)) == 1

    def side_by_side(ref, t):
        one, two = ref[2 * t], ref[2 * t + 1]
        moved = pltpu.roll(jnp.where(odd, one, two), SLOTS, 1)
        return jnp.where(left != odd, jnp.where(left, one, two), moved)

    loads[6].wait()
    loads[7].wait()
    for t in range(4):
        own_scores(t)

    arrived(KV, kvr.at[pl.ds(0, 15)])
    blocks = kvr[...]
    kb[y, z_hi, 0:16, :] = blocks[:, 0, :].astype(BF16)
    kb[y, z_hi, 16:32, :] = blocks[:, 1, :].astype(BF16)
    for b in z_others:
        remote(ZK, kb.at[y, z_hi], kb.at[y, z_hi], z_peer(b)).start()
    vb[y, z_hi, 0:16, :] = blocks[:, 2, :].astype(BF16)
    vb[y, z_hi, 16:32, :] = blocks[:, 3, :].astype(BF16)
    for b in z_others:
        remote(ZV, vb.at[y, z_hi], vb.at[y, z_hi], z_peer(b)).start()
    mine = lax.broadcasted_iota(jnp.int32, (16, DIM), 0) // 4 % 2 == x_lo
    count16 = jnp.sum(jnp.where(mine, blocks[:, 4, :], 0.0), axis=0, keepdims=True)
    reward16 = jnp.sum(jnp.where(mine, blocks[:, 5, :], 0.0), axis=0, keepdims=True)
    gsum[...] = jnp.concatenate([count16, reward16, jnp.zeros((6, DIM), F32)], axis=0)
    for b in z_others:
        remote(ZSUM, gsum, gsumr.at[z_hi], z_peer(b)).start()
    for b in a_others:
        remote(QUERY, xq.at[b], xqr.at[a], a_peer(b)).start()
    xqr[a] = xq[a]
    for b in a_others:
        remote(GRAD, xg.at[b], xgr.at[a], a_peer(b)).start()
    xgr[a] = xg[a]

    for t in range(4, 8):
        own_scores(t)

    arrived(ZK, kb.at[0, pl.ds(0, 3)])
    for b in y_others:
        along_y(0, kb, y, b).start()
    arrived(ZV, vb.at[0, pl.ds(0, 3)])
    for b in y_others:
        along_y(1, vb, y, b).start()
    arrived(ZSUM, gsumr.at[pl.ds(0, 3)])
    total = gsum[...]
    for b in z_others:
        total = total + gsumr[b]
    weight = (reward - total[1:2] / 32.0) * (SLOTS * 32) / total[0:1]
    weight = jnp.where(pos2 < ROWS, weight, 0.0)
    for t in range(8):
        st[t, 3:4, :] = weight
    for b in a_others:
        remote(OWN, st.at[lax.div(b, 2)], str_.at[a], a_peer(b)).start()
    str_[a] = st[lax.div(a, 2)]

    def key_block(b):
        block = kb[b].reshape(128, DIM)
        for n in range(4):
            cols = slice(n * 256, (n + 1) * 256)
            s = dot_nt(block, xqr[4 * n : 4 * n + 4].reshape(256, DIM)) * SCALE2
            m = jnp.max(s, axis=0, keepdims=True)
            e = jnp.exp2(s - m)
            exps[b, :, cols] = e
            part[b, 0:1, cols] = m
            part[b, 1:2, cols] = jnp.sum(e, axis=0, keepdims=True)

    def value_block(b):
        block = vb[b].reshape(128, DIM)
        for n in range(4):
            cols = slice(n * 256, (n + 1) * 256)
            d = dot_nt(block, xgr[4 * n : 4 * n + 4].reshape(256, DIM)) * SCALE
            prods[b, :, cols] = d
            part[b, 2:3, cols] = jnp.sum(exps[b, :, cols] * d, axis=0, keepdims=True)

    near_first = [y_others[0], y_others[2], y_others[1]]
    far_first = [y_others[1], y_others[0], y_others[2]]
    arrived(QUERY, xqr.at[pl.ds(0, 15)])
    key_block(y)
    for b in near_first:
        along_y(0, kb, b, b).wait_recv()
        key_block(b)
    arrived(OWN, str_.at[pl.ds(0, 15)])
    stats = jnp.concatenate([side_by_side(str_, t) for t in range(8)], axis=1)
    m = stats[0:1]
    for b in range(4):
        m = jnp.maximum(m, part[b, 0:1, :])
    fo = jnp.exp2(stats[0:1] - m)
    total = stats[1:2] * fo
    for b in range(4):
        f = jnp.exp2(part[b, 0:1, :] - m)
        total = total + part[b, 1:2, :] * f
        part[b, 3:4, :] = f
    inv = 1.0 / total
    weights = stats[3:4]

    def probabilities(b):
        coef = part[b, 3:4, :] * inv
        for n in range(4):
            cols = slice(n * 256, (n + 1) * 256)
            p = exps[b, :, cols] * coef[:, cols]
            exps[b, :, cols] = p
            pw[b, :, cols] = (p * weights[:, cols]).astype(BF16)

    arrived(GRAD, xgr.at[pl.ds(0, 15)])
    q_all = xqr[...].reshape(16 * SLOTS, DIM)
    g_all = xgr[...].reshape(16 * SLOTS, DIM)
    for b in far_first:
        probabilities(b)
        sbv[b] = dot_nn(pw[b], g_all).astype(BF16)
        remote(YSUM_V, sbv.at[b], rv.at[y], y_peer(b)).start()
    probabilities(y)
    for b in range(4):
        kt[:, b * 128 : (b + 1) * 128] = jnp.transpose(
            kb[b].reshape(128, DIM).astype(F32)
        ).astype(BF16)

    value_block(y)
    for b in near_first:
        along_y(1, vb, b, b).wait_recv()
        value_block(b)
    inner = stats[2:3] * (fo * inv * SCALE)
    for b in range(4):
        inner = inner + part[b, 2:3, :]

    def finish(b):
        for n in range(4):
            cols = slice(n * 256, (n + 1) * 256)
            dscore = exps[b, :, cols] * (prods[b, :, cols] - inner[:, cols])
            ds[b, :, cols] = (dscore * weights[:, cols]).astype(BF16)

    for b in far_first:
        finish(b)
        sbk[b] = dot_nn(ds[b], q_all).astype(BF16)
        remote(YSUM_K, sbk.at[b], rk.at[y], y_peer(b)).start()
    finish(y)
    final = jnp.concatenate(
        [m, inv, inner * (1.0 / SCALE), jnp.zeros((5, 16 * SLOTS), F32)], axis=0
    )
    for t in range(8):
        fs[t] = final[:, t * DIM : (t + 1) * DIM]
    grad_v = dot_nn(pw[y], g_all)
    grad_k = dot_nn(ds[y], q_all)
    for b in a_others:
        remote(FIN, fs.at[lax.div(b, 2)], fr.at[a], a_peer(b)).start()
    fr[a] = fs[lax.div(a, 2)]
    for t in range(4):
        cols = slice(t * 256, (t + 1) * 256)
        grad_q = dot_nn(kt[...], ds[:, :, cols].reshape(PROMPT, 256))
        for u in range(2):
            turned = jnp.transpose(grad_q[:, u * 128 : (u + 1) * 128]).astype(BF16)
            dqs[4 * t + 2 * u] = turned[:SLOTS]
            dqs[4 * t + 2 * u + 1] = turned[SLOTS:]
    for b in a_others:
        remote(DQ, dqs.at[b], dqr.at[a], a_peer(b)).start()
    dqr[a] = dqs[a]

    def next_sum(total, kind_y, received, held, send, kind_z, target):
        arrived(kind_y, received.at[pl.ds(0, 3)])
        for b in y_others:
            total = total + received[b].astype(F32)
        held[...] = total.reshape(4, 32, DIM)
        send[...] = total.astype(BF16).reshape(4, 32, DIM)
        for b in z_others:
            remote(kind_z, send.at[b], target.at[z_hi], z_peer(b)).start()

    next_sum(grad_v, YSUM_V, rv, hv, szv, ZSUM_V, rzv)
    next_sum(grad_k, YSUM_K, rk, hk, szk, ZSUM_K, rzk)

    arrived(FIN, fr.at[pl.ds(0, 15)])
    for t in range(8):
        cols = slice(t * 256, (t + 1) * 256)
        fin = side_by_side(fr, t)
        m, inv, inner = fin[0:1], fin[1:2], fin[2:3]
        coef = jnp.exp2(st[t, 0:1, :] - m) * inv * weight
        e = own_e[t]
        p = (e * coef).astype(BF16)
        dsc = (e * (own_d[t] - inner) * (coef * SCALE)).astype(BF16)
        dvo[:, cols] = dot_nn(p, both(xg, t)).astype(BF16)
        dko[:, cols] = dot_nn(dsc, both(xq, t)).astype(BF16)
        grad_q = dot_tn(dsc, ck[:, cols])
        own_q[2 * t] = grad_q[:SLOTS, :DIM]
        own_q[2 * t + 1] = grad_q[SLOTS:, DIM:]
    stores = [
        pltpu.make_async_copy(src, dst, out_sem.at[n])
        for n, (src, dst) in enumerate(
            ((dqo, dq_hbm), (dko, dk_hbm), (dvo, dv_hbm), (t3.at[a], gp_hbm.at[a]))
        )
    ]
    for store in stores[1:3]:
        store.start()

    arrived(ZSUM_V, rzv.at[pl.ds(0, 3)])
    arrived(ZSUM_K, rzk.at[pl.ds(0, 3)])
    line = lax.broadcasted_iota(jnp.int32, (16, 8, DIM), 1)
    lines = jnp.zeros((16, 8, DIM), F32)
    for kv, (held, received) in enumerate(((hk, rzk), (hv, rzv))):
        part = held[z_hi]
        for b in z_others:
            part = part + received[b].astype(F32)
        for r in range(2):
            lines = jnp.where(line == kv * 2 + r, part[r * 16 : (r + 1) * 16][:, None, :], lines)
    t3[...] = lines
    for b in a_others:
        remote(OUT, t3.at[b], gp_hbm.at[a], a_peer(b)).start()
    stores[3].start()
    arrived(DQ, dqr.at[pl.ds(0, 15)])
    for h in range(HEADS):
        dqo[:, h * DIM : (h + 1) * DIM] = (own_q[h] + dqr[h].astype(F32)).astype(BF16)
    stores[0].start()
    arrived(OUT, gp_hbm.at[pl.ds(0, 15)])

    sent(KV, kvs.at[pl.ds(0, 15)])
    sent(QUERY, xq.at[pl.ds(0, 15)])
    sent(GRAD, xg.at[pl.ds(0, 15)])
    sent(ZK, kb.at[0, pl.ds(0, 3)])
    sent(ZV, vb.at[0, pl.ds(0, 3)])
    sent(ZSUM, gsumr.at[pl.ds(0, 3)])
    sent(YK, kb.at[pl.ds(0, 3)])
    sent(YV, vb.at[pl.ds(0, 3)])
    sent(OWN, str_.at[pl.ds(0, 15)])
    sent(FIN, fr.at[pl.ds(0, 15)])
    sent(DQ, dqs.at[pl.ds(0, 15)])
    sent(YSUM_V, sbv.at[pl.ds(0, 3)])
    sent(YSUM_K, sbk.at[pl.ds(0, 3)])
    sent(ZSUM_V, szv.at[pl.ds(0, 3)])
    sent(ZSUM_K, szk.at[pl.ds(0, 3)])
    sent(OUT, t3.at[pl.ds(0, 15)])
    for store in stores:
        store.wait()


def store_all(dq, dk, dv, gp, dq_out, dk_out, dv_out, gk_out, gv_out, *scratch):
    dq_held, dk_held, dv_held, gp_held, gk_held, gv_held, in_sem, out_sem = scratch
    parts = [(gp, gp_held)]
    stores = []
    for source, held, target in ((dq, dq_held, dq_out), (dk, dk_held, dk_out), (dv, dv_held, dv_out)):
        for first in range(0, source.shape[0], SLOTS):
            span = pl.ds(first, SLOTS)
            parts.append((source.at[span], held.at[span]))
            stores.append((held.at[span], target.at[span]))
    stores += [(gk_held, gk_out), (gv_held, gv_out)]
    loads = [pltpu.make_async_copy(*pair, in_sem.at[n]) for n, pair in enumerate(parts)]
    stores = [pltpu.make_async_copy(*pair, out_sem.at[n]) for n, pair in enumerate(stores)]
    for load in loads[1:] + loads[:1]:
        load.start()
    for load, store in zip(loads[1:], stores):
        load.wait()
        store.start()
    loads[0].wait()
    for h in range(HEADS):
        cols = slice(h * DIM, (h + 1) * DIM)
        gk_held[:, cols] = gp_held[h, 0:2, :].astype(BF16)
        gv_held[:, cols] = gp_held[h, 2:4, :].astype(BF16)
    for store in stores[-2:]:
        store.start()
    for store in stores:
        store.wait()


def shards(prompt_k, prompt_v, comp_q, comp_k, comp_v, grad_out, rewards, mask_pos):
    hbm = pl.BlockSpec(memory_space=pltpu.HBM)
    V = pltpu.VMEM
    grads = pl.pallas_call(
        kernel,
        out_shape=(
            jax.ShapeDtypeStruct((SLOTS, WIDTH), BF16),
            jax.ShapeDtypeStruct((ROWS, WIDTH), BF16),
            jax.ShapeDtypeStruct((ROWS, WIDTH), BF16),
            jax.ShapeDtypeStruct((16, 8, DIM), F32),
        ),
        in_specs=[hbm] * 8,
        out_specs=(hbm,) * 4,
        scratch_shapes=[
            V((2, WIDTH), BF16),
            V((2, WIDTH), BF16),
            V((1, 1), F32),
            V((1, SLOTS), jnp.int32),
            V((ROWS, WIDTH), BF16),
            V((ROWS, WIDTH), BF16),
            V((ROWS, WIDTH), BF16),
            V((SLOTS, WIDTH), BF16),
            V((16, SLOTS, DIM), BF16),
            V((16, SLOTS, DIM), BF16),
            V((16, SLOTS, DIM), BF16),
            V((16, SLOTS, DIM), BF16),
            V((16, 8, DIM), F32),
            V((16, 8, DIM), F32),
            V((4, 4, 32, DIM), BF16),
            V((4, 4, 32, DIM), BF16),
            V((8, DIM), F32),
            V((4, 8, DIM), F32),
            V((8, 128, DIM), F32),
            V((8, 128, DIM), F32),
            V((8, 8, DIM), F32),
            V((16, 8, DIM), F32),
            V((8, 8, DIM), F32),
            V((16, 8, DIM), F32),
            V((4, 128, 16 * SLOTS), F32),
            V((4, 128, 16 * SLOTS), F32),
            V((4, 8, 16 * SLOTS), F32),
            V((4, 128, 16 * SLOTS), BF16),
            V((4, 128, 16 * SLOTS), BF16),
            V((DIM, PROMPT), BF16),
            V((4, 128, DIM), BF16),
            V((4, 128, DIM), BF16),
            V((4, 128, DIM), BF16),
            V((4, 128, DIM), BF16),
            V((4, 32, DIM), F32),
            V((4, 32, DIM), F32),
            V((4, 32, DIM), BF16),
            V((4, 32, DIM), BF16),
            V((4, 32, DIM), BF16),
            V((4, 32, DIM), BF16),
            V((16, 8, DIM), F32),
            V((16, SLOTS, DIM), BF16),
            V((16, SLOTS, DIM), BF16),
            V((16, SLOTS, DIM), F32),
            V((SLOTS, WIDTH), BF16),
            V((ROWS, WIDTH), BF16),
            V((ROWS, WIDTH), BF16),
            pltpu.SemaphoreType.DMA((8,)),
            pltpu.SemaphoreType.DMA((4,)),
            pltpu.SemaphoreType.DMA((KINDS,)),
            pltpu.SemaphoreType.DMA((KINDS,)),
            pltpu.SemaphoreType.DMA((2, 4)),
        ],
        compiler_params=pltpu.CompilerParams(
            collective_id=0, has_side_effects=True, vmem_limit_bytes=60 * 1024 * 1024
        ),
    )(
        prompt_k, prompt_v, rewards, mask_pos[0], comp_q[0, 0], comp_k[0, 0], comp_v[0, 0],
        grad_out[0, 0],
    )
    wide = [jax.ShapeDtypeStruct(grad.shape, BF16) for grad in grads[:3]]
    thin = [jax.ShapeDtypeStruct((2, WIDTH), BF16)] * 2
    dq, dk, dv, gk, gv = pl.pallas_call(
        store_all,
        out_shape=wide + thin,
        in_specs=[hbm] * 4,
        out_specs=[hbm] * 5,
        scratch_shapes=[V(grad.shape, BF16) for grad in grads[:3]]
        + [
            V((16, 8, DIM), F32),
            V((2, WIDTH), BF16),
            V((2, WIDTH), BF16),
            pltpu.SemaphoreType.DMA((6,)),
            pltpu.SemaphoreType.DMA((7,)),
        ],
        compiler_params=pltpu.CompilerParams(vmem_limit_bytes=60 * 1024 * 1024),
    )(*grads)
    return dq[None, None], dk[None, None], dv[None, None], gk, gv


def solution(mesh):
    wide = P("grp", "ctx", None, None)
    rows = P(("grp", "ctx"), None)
    return jax.shard_map(
        shards,
        mesh=mesh,
        in_specs=(rows, rows, wide, wide, wide, wide, P("grp", "ctx"), P("grp", "ctx", None)),
        out_specs=(wide, wide, wide, rows, rows),
        check_vma=False,
    )
```

```python
import jax
import jax.numpy as jnp
from jax import lax
from jax.experimental import pallas as pl
from jax.experimental.pallas import tpu as pltpu
from jax.sharding import PartitionSpec as P

HEADS = 16
DIM = 128
SLOTS = 64
ROWS = 128
WIDTH = 2048
PROMPT = 512
F32 = jnp.float32
BF16 = jnp.bfloat16
SCALE = DIM ** -0.5
SCALE2 = SCALE * 1.4426950408889634
MESH = pl.DeviceIdType.MESH

(
    KV, QUERY, GRAD, ZK, ZV, ZSUM, YK, YV, OWN, FIN, DQ, YSUM_K, YSUM_V, ZSUM_K, ZSUM_V, OUT, KINDS
) = range(17)


def dot_nt(a, b):
    return lax.dot_general(a, b, (((1,), (1,)), ((), ())), preferred_element_type=F32)


def dot_nn(a, b):
    return lax.dot_general(a, b, (((1,), (0,)), ((), ())), preferred_element_type=F32)


def dot_tn(a, b):
    return lax.dot_general(a, b, (((0,), (0,)), ((), ())), preferred_element_type=F32)


def kernel(
    pk_hbm, pv_hbm, rw_hbm, mp_hbm, cq_hbm, ck_hbm, cv_hbm, go_hbm,
    own_hbm, dqr, dk_hbm, dv_hbm, gp_hbm,
    pk, pv, rw, mp, cq, ck, cv, go, xq, xqr, xg, xgr, kvs, kvr, kb, vb, gsum, gsumr, own_e, own_d, st, str_,
    fs, fr, exps, prods, part, pw, ds,
    sbk, sbv, rk, rv, hk, hv, szk, szv, rzk, rzv, t3, dqs, dqo, dko, dvo,
    in_sem, out_sem, ss, rs, ry,
):
    grp = lax.axis_index("grp")
    ctx = lax.axis_index("ctx")
    x_lo, y = lax.div(grp, 4), lax.rem(grp, 4)
    z = lax.div(ctx, 4)
    z_hi, z_lo, low = lax.div(z, 2), lax.rem(z, 2), lax.rem(ctx, 4)
    a = z_lo * 8 + x_lo * 4 + low

    def a_peer(b):
        return {
            "grp": lax.rem(lax.div(b, 4), 2) * 4 + y,
            "ctx": (z_hi * 2 + lax.div(b, 8)) * 4 + lax.rem(b, 4),
        }

    def z_peer(b):
        return {"grp": grp, "ctx": (b * 2 + z_lo) * 4 + low}

    def y_peer(b):
        return {"grp": x_lo * 4 + b, "ctx": ctx}

    flips = [(dz, 0, 1, dc) for dz in (1, 0) for dc in (1, 0)]
    flips += [(dz, 1, dx, dc) for dz in (1, 0) for dx in (1, 0) for dc in (1, 0)]
    flips += [(1, 0, 0, 1), (1, 0, 0, 0), (0, 0, 0, 1)]

    def flipped(bit, flip):
        return 1 - bit if flip else bit

    x_hi, core = lax.div(low, 2), lax.rem(low, 2)
    a_others = [
        flipped(z_lo, dz) * 8 + flipped(x_lo, dl) * 4 + flipped(x_hi, dh) * 2 + flipped(core, dc)
        for dz, dl, dh, dc in flips
    ]
    z_others = [lax.rem(z_hi + k, 4) for k in range(1, 4)]
    y_others = [lax.rem(y + k, 4) for k in range(1, 4)]

    def remote(kind, src, dst, device):
        return pltpu.make_async_remote_copy(
            src_ref=src, dst_ref=dst, send_sem=ss.at[kind], recv_sem=rs.at[kind],
            device_id=device, device_id_type=MESH,
        )

    def along_y(kv, ref, row, b):
        return pltpu.make_async_remote_copy(
            src_ref=ref.at[row], dst_ref=ref.at[row], send_sem=ss.at[YK + kv],
            recv_sem=ry.at[kv, row], device_id=y_peer(b), device_id_type=MESH,
        )

    def arrived(kind, dst):
        remote(kind, dst, dst, y_peer(y_others[0])).wait_recv()

    def sent(kind, src):
        remote(kind, src, src, y_peer(y_others[0])).wait_send()

    loads = [
        pltpu.make_async_copy(src, dst, in_sem.at[n])
        for n, (src, dst) in enumerate(
            (
                (pk_hbm, pk), (pv_hbm, pv), (rw_hbm, rw), (mp_hbm, mp),
                (cq_hbm, cq), (go_hbm, go), (ck_hbm, ck), (cv_hbm, cv),
            )
        )
    ]
    for load in loads:
        load.start()

    barrier = pltpu.get_barrier_semaphore()
    for b in a_others:
        pl.semaphore_signal(barrier, inc=1, device_id=a_peer(b), device_id_type=MESH)
    for b in z_others:
        pl.semaphore_signal(barrier, inc=1, device_id=z_peer(b), device_id_type=MESH)
    for b in y_others:
        pl.semaphore_signal(barrier, inc=1, device_id=y_peer(b), device_id_type=MESH)

    for load in loads[:4]:
        load.wait()
    pos = mp[...]
    pos2 = jnp.concatenate([pos, pos], axis=1)
    live = pos < ROWS
    count = jnp.sum(jnp.where(live, 1.0, 0.0), axis=1, keepdims=True)
    reward = rw[...]
    lines = jnp.concatenate(
        [
            pk[...].astype(F32),
            pv[...].astype(F32),
            jnp.broadcast_to(count, (1, WIDTH)),
            jnp.broadcast_to(reward, (1, WIDTH)),
            jnp.zeros((2, WIDTH), F32),
        ],
        axis=0,
    )
    for h in range(HEADS):
        kvs[h] = lines[:, h * DIM : (h + 1) * DIM]

    pl.semaphore_wait(barrier, 21)

    for b in a_others:
        remote(KV, kvs.at[b], kvr.at[a], a_peer(b)).start()
    kvr[a] = kvs[a]

    row = lax.broadcasted_iota(jnp.int32, (ROWS, 2 * SLOTS), 0)
    pick = jnp.where(row == jnp.minimum(pos2, ROWS - 1), 1.0, 0.0).astype(BF16)
    loads[4].wait()
    picked = dot_tn(pick, cq[...])[:SLOTS].astype(BF16)
    for h in range(HEADS):
        xq[h] = picked[:, h * DIM : (h + 1) * DIM]
    loads[5].wait()
    for h in range(HEADS):
        xg[h] = go[:, h * DIM : (h + 1) * DIM]

    nothing = jnp.zeros((SLOTS, DIM), BF16)

    def both(ref, t):
        return jnp.concatenate(
            [
                jnp.concatenate([ref[2 * t], nothing], axis=1),
                jnp.concatenate([nothing, ref[2 * t + 1]], axis=1),
            ],
            axis=0,
        )

    def own_scores(t):
        cols = slice(t * 256, (t + 1) * 256)
        s = dot_nt(ck[:, cols], both(xq, t)) * SCALE2
        d = dot_nt(cv[:, cols], both(xg, t))
        m = jnp.max(s, axis=0, keepdims=True)
        e = jnp.exp2(s - m)
        own_e[t] = e
        own_d[t] = d
        st[t] = jnp.concatenate(
            [
                m,
                jnp.sum(e, axis=0, keepdims=True),
                jnp.sum(e * d, axis=0, keepdims=True),
                jnp.zeros((5, DIM), F32),
            ],
            axis=0,
        )

    left = lax.broadcasted_iota(jnp.int32, (8, DIM), 1) < SLOTS
    odd = jnp.broadcast_to(lax.rem(a, 2), (8, DIM)) == 1

    def side_by_side(ref, t):
        one, two = ref[2 * t], ref[2 * t + 1]
        moved = pltpu.roll(jnp.where(odd, one, two), SLOTS, 1)
        return jnp.where(left != odd, jnp.where(left, one, two), moved)

    loads[6].wait()
    loads[7].wait()
    for t in range(4):
        own_scores(t)

    arrived(KV, kvr.at[pl.ds(0, 15)])
    blocks = kvr[...]
    kb[y, z_hi, 0:16, :] = blocks[:, 0, :].astype(BF16)
    kb[y, z_hi, 16:32, :] = blocks[:, 1, :].astype(BF16)
    for b in z_others:
        remote(ZK, kb.at[y, z_hi], kb.at[y, z_hi], z_peer(b)).start()
    vb[y, z_hi, 0:16, :] = blocks[:, 2, :].astype(BF16)
    vb[y, z_hi, 16:32, :] = blocks[:, 3, :].astype(BF16)
    for b in z_others:
        remote(ZV, vb.at[y, z_hi], vb.at[y, z_hi], z_peer(b)).start()
    mine = lax.broadcasted_iota(jnp.int32, (16, DIM), 0) // 4 % 2 == x_lo
    count16 = jnp.sum(jnp.where(mine, blocks[:, 4, :], 0.0), axis=0, keepdims=True)
    reward16 = jnp.sum(jnp.where(mine, blocks[:, 5, :], 0.0), axis=0, keepdims=True)
    gsum[...] = jnp.concatenate([count16, reward16, jnp.zeros((6, DIM), F32)], axis=0)
    for b in z_others:
        remote(ZSUM, gsum, gsumr.at[z_hi], z_peer(b)).start()
    for b in a_others:
        remote(QUERY, xq.at[b], xqr.at[a], a_peer(b)).start()
    xqr[a] = xq[a]
    for b in a_others:
        remote(GRAD, xg.at[b], xgr.at[a], a_peer(b)).start()
    xgr[a] = xg[a]

    for t in range(4, 8):
        own_scores(t)

    arrived(ZK, kb.at[0, pl.ds(0, 3)])
    for b in y_others:
        along_y(0, kb, y, b).start()
    arrived(ZV, vb.at[0, pl.ds(0, 3)])
    for b in y_others:
        along_y(1, vb, y, b).start()
    arrived(ZSUM, gsumr.at[pl.ds(0, 3)])
    total = gsum[...]
    for b in z_others:
        total = total + gsumr[b]
    weight = (reward - total[1:2] / 32.0) * (SLOTS * 32) / total[0:1]
    weight = jnp.where(pos2 < ROWS, weight, 0.0)
    for t in range(8):
        st[t, 3:4, :] = weight
    for b in a_others:
        remote(OWN, st.at[lax.div(b, 2)], str_.at[a], a_peer(b)).start()
    str_[a] = st[lax.div(a, 2)]

    def key_block(b):
        block = kb[b].reshape(128, DIM)
        for n in range(4):
            cols = slice(n * 256, (n + 1) * 256)
            s = dot_nt(block, xqr[4 * n : 4 * n + 4].reshape(256, DIM)) * SCALE2
            m = jnp.max(s, axis=0, keepdims=True)
            e = jnp.exp2(s - m)
            exps[b, :, cols] = e
            part[b, 0:1, cols] = m
            part[b, 1:2, cols] = jnp.sum(e, axis=0, keepdims=True)

    def value_block(b):
        block = vb[b].reshape(128, DIM)
        for n in range(4):
            cols = slice(n * 256, (n + 1) * 256)
            d = dot_nt(block, xgr[4 * n : 4 * n + 4].reshape(256, DIM)) * SCALE
            prods[b, :, cols] = d
            part[b, 2:3, cols] = jnp.sum(exps[b, :, cols] * d, axis=0, keepdims=True)

    near_first = [y_others[0], y_others[2], y_others[1]]
    far_first = [y_others[1], y_others[0], y_others[2]]
    arrived(QUERY, xqr.at[pl.ds(0, 15)])
    key_block(y)
    for b in near_first:
        along_y(0, kb, b, b).wait_recv()
        key_block(b)
    arrived(OWN, str_.at[pl.ds(0, 15)])
    stats = jnp.concatenate([side_by_side(str_, t) for t in range(8)], axis=1)
    m = stats[0:1]
    for b in range(4):
        m = jnp.maximum(m, part[b, 0:1, :])
    fo = jnp.exp2(stats[0:1] - m)
    total = stats[1:2] * fo
    for b in range(4):
        f = jnp.exp2(part[b, 0:1, :] - m)
        total = total + part[b, 1:2, :] * f
        part[b, 3:4, :] = f
    inv = 1.0 / total
    weights = stats[3:4]

    def probabilities(b):
        coef = part[b, 3:4, :] * inv
        for n in range(4):
            cols = slice(n * 256, (n + 1) * 256)
            p = exps[b, :, cols] * coef[:, cols]
            exps[b, :, cols] = p
            pw[b, :, cols] = (p * weights[:, cols]).astype(BF16)

    arrived(GRAD, xgr.at[pl.ds(0, 15)])
    q_all = xqr[...].reshape(16 * SLOTS, DIM)
    g_all = xgr[...].reshape(16 * SLOTS, DIM)
    for b in far_first:
        probabilities(b)
        sbv[b] = dot_nn(pw[b], g_all).astype(BF16)
        remote(YSUM_V, sbv.at[b], rv.at[y], y_peer(b)).start()
    probabilities(y)

    value_block(y)
    for b in near_first:
        along_y(1, vb, b, b).wait_recv()
        value_block(b)
    inner = stats[2:3] * (fo * inv * SCALE)
    for b in range(4):
        inner = inner + part[b, 2:3, :]

    def finish(b):
        for n in range(4):
            cols = slice(n * 256, (n + 1) * 256)
            dscore = exps[b, :, cols] * (prods[b, :, cols] - inner[:, cols])
            ds[b, :, cols] = (dscore * weights[:, cols]).astype(BF16)

    for b in far_first:
        finish(b)
        sbk[b] = dot_nn(ds[b], q_all).astype(BF16)
        remote(YSUM_K, sbk.at[b], rk.at[y], y_peer(b)).start()
    finish(y)
    final = jnp.concatenate(
        [m, inv, inner * (1.0 / SCALE), jnp.zeros((5, 16 * SLOTS), F32)], axis=0
    )
    for t in range(8):
        fs[t] = final[:, t * DIM : (t + 1) * DIM]
    keys = kb[...].reshape(PROMPT, DIM)
    grad_v = dot_nn(pw[y], g_all)
    grad_k = dot_nn(ds[y], q_all)
    for b in a_others:
        remote(FIN, fs.at[lax.div(b, 2)], fr.at[a], a_peer(b)).start()
    fr[a] = fs[lax.div(a, 2)]
    for t in range(8):
        grad_q = dot_tn(ds[:, :, t * 128 : (t + 1) * 128].reshape(PROMPT, 2 * SLOTS), keys)
        dqs[2 * t] = grad_q[:SLOTS].astype(BF16)
        dqs[2 * t + 1] = grad_q[SLOTS:].astype(BF16)
    for b in a_others:
        remote(DQ, dqs.at[b], dqr.at[a], a_peer(b)).start()
    own_part = pltpu.make_async_copy(dqs.at[a], dqr.at[a], out_sem.at[4])
    own_part.start()

    def next_sum(total, kind_y, received, held, send, kind_z, target):
        arrived(kind_y, received.at[pl.ds(0, 3)])
        for b in y_others:
            total = total + received[b].astype(F32)
        held[...] = total.reshape(4, 32, DIM)
        send[...] = total.astype(BF16).reshape(4, 32, DIM)
        for b in z_others:
            remote(kind_z, send.at[b], target.at[z_hi], z_peer(b)).start()

    next_sum(grad_v, YSUM_V, rv, hv, szv, ZSUM_V, rzv)
    next_sum(grad_k, YSUM_K, rk, hk, szk, ZSUM_K, rzk)

    arrived(FIN, fr.at[pl.ds(0, 15)])
    for t in range(8):
        cols = slice(t * 256, (t + 1) * 256)
        fin = side_by_side(fr, t)
        m, inv, inner = fin[0:1], fin[1:2], fin[2:3]
        coef = jnp.exp2(st[t, 0:1, :] - m) * inv * weight
        e = own_e[t]
        p = (e * coef).astype(BF16)
        dsc = (e * (own_d[t] - inner) * (coef * SCALE)).astype(BF16)
        dvo[:, cols] = dot_nn(p, both(xg, t)).astype(BF16)
        dko[:, cols] = dot_nn(dsc, both(xq, t)).astype(BF16)
        grad_q = dot_tn(dsc, ck[:, cols])
        dqo[2 * t] = grad_q[:SLOTS, :DIM].astype(BF16)
        dqo[2 * t + 1] = grad_q[SLOTS:, DIM:].astype(BF16)
    stores = [
        pltpu.make_async_copy(src, dst, out_sem.at[n])
        for n, (src, dst) in enumerate(
            ((dqo, own_hbm), (dko, dk_hbm), (dvo, dv_hbm), (t3.at[a], gp_hbm.at[a]))
        )
    ]
    for store in stores[:3]:
        store.start()

    arrived(ZSUM_V, rzv.at[pl.ds(0, 3)])
    arrived(ZSUM_K, rzk.at[pl.ds(0, 3)])
    line = lax.broadcasted_iota(jnp.int32, (16, 8, DIM), 1)
    lines = jnp.zeros((16, 8, DIM), F32)
    for kv, (held, received) in enumerate(((hk, rzk), (hv, rzv))):
        part = held[z_hi]
        for b in z_others:
            part = part + received[b].astype(F32)
        for r in range(2):
            lines = jnp.where(line == kv * 2 + r, part[r * 16 : (r + 1) * 16][:, None, :], lines)
    t3[...] = lines
    for b in a_others:
        remote(OUT, t3.at[b], gp_hbm.at[a], a_peer(b)).start()
    stores[3].start()
    arrived(DQ, dqr.at[pl.ds(0, 15)])
    arrived(OUT, gp_hbm.at[pl.ds(0, 15)])

    sent(KV, kvs.at[pl.ds(0, 15)])
    sent(QUERY, xq.at[pl.ds(0, 15)])
    sent(GRAD, xg.at[pl.ds(0, 15)])
    sent(ZK, kb.at[0, pl.ds(0, 3)])
    sent(ZV, vb.at[0, pl.ds(0, 3)])
    sent(ZSUM, gsumr.at[pl.ds(0, 3)])
    sent(YK, kb.at[pl.ds(0, 3)])
    sent(YV, vb.at[pl.ds(0, 3)])
    sent(OWN, str_.at[pl.ds(0, 15)])
    sent(FIN, fr.at[pl.ds(0, 15)])
    sent(DQ, dqs.at[pl.ds(0, 15)])
    sent(YSUM_V, sbv.at[pl.ds(0, 3)])
    sent(YSUM_K, sbk.at[pl.ds(0, 3)])
    sent(ZSUM_V, szv.at[pl.ds(0, 3)])
    sent(ZSUM_K, szk.at[pl.ds(0, 3)])
    sent(OUT, t3.at[pl.ds(0, 15)])
    for store in stores + [own_part]:
        store.wait()


def store_all(own, other, dk, dv, gp, dq_out, dk_out, dv_out, gk_out, gv_out, *scratch):
    (
        own_held, other_held, dk_held, dv_held, gp_held, dq_held, gk_held, gv_held,
        in_sem, out_sem,
    ) = scratch
    pairs = [(own, own_held), (other, other_held), (gp, gp_held)]
    stores = []
    for source, held, target in ((dk, dk_held, dk_out), (dv, dv_held, dv_out)):
        for first in range(0, ROWS, SLOTS):
            span = pl.ds(first, SLOTS)
            pairs.append((source.at[span], held.at[span]))
            stores.append((held.at[span], target.at[span]))
    stores += [(dq_held, dq_out), (gk_held, gk_out), (gv_held, gv_out)]
    loads = [pltpu.make_async_copy(*pair, in_sem.at[n]) for n, pair in enumerate(pairs)]
    stores = [pltpu.make_async_copy(*pair, out_sem.at[n]) for n, pair in enumerate(stores)]
    for load in loads:
        load.start()
    loads[0].wait()
    loads[1].wait()
    for h in range(HEADS):
        cols = slice(h * DIM, (h + 1) * DIM)
        total = own_held[h].astype(F32) + other_held[h].astype(F32)
        dq_held[:, cols] = total.astype(BF16)
    stores[4].start()
    loads[2].wait()
    for h in range(HEADS):
        cols = slice(h * DIM, (h + 1) * DIM)
        gk_held[:, cols] = gp_held[h, 0:2, :].astype(BF16)
        gv_held[:, cols] = gp_held[h, 2:4, :].astype(BF16)
    stores[5].start()
    stores[6].start()
    for n in range(4):
        loads[3 + n].wait()
        stores[n].start()
    for store in stores:
        store.wait()


def shards(prompt_k, prompt_v, comp_q, comp_k, comp_v, grad_out, rewards, mask_pos):
    hbm = pl.BlockSpec(memory_space=pltpu.HBM)
    V = pltpu.VMEM
    grads = pl.pallas_call(
        kernel,
        out_shape=(
            jax.ShapeDtypeStruct((HEADS, SLOTS, DIM), BF16),
            jax.ShapeDtypeStruct((HEADS, SLOTS, DIM), BF16),
            jax.ShapeDtypeStruct((ROWS, WIDTH), BF16),
            jax.ShapeDtypeStruct((ROWS, WIDTH), BF16),
            jax.ShapeDtypeStruct((16, 8, DIM), F32),
        ),
        in_specs=[hbm] * 8,
        out_specs=(hbm,) * 5,
        scratch_shapes=[
            V((2, WIDTH), BF16),
            V((2, WIDTH), BF16),
            V((1, 1), F32),
            V((1, SLOTS), jnp.int32),
            V((ROWS, WIDTH), BF16),
            V((ROWS, WIDTH), BF16),
            V((ROWS, WIDTH), BF16),
            V((SLOTS, WIDTH), BF16),
            V((16, SLOTS, DIM), BF16),
            V((16, SLOTS, DIM), BF16),
            V((16, SLOTS, DIM), BF16),
            V((16, SLOTS, DIM), BF16),
            V((16, 8, DIM), F32),
            V((16, 8, DIM), F32),
            V((4, 4, 32, DIM), BF16),
            V((4, 4, 32, DIM), BF16),
            V((8, DIM), F32),
            V((4, 8, DIM), F32),
            V((8, 128, DIM), F32),
            V((8, 128, DIM), F32),
            V((8, 8, DIM), F32),
            V((16, 8, DIM), F32),
            V((8, 8, DIM), F32),
            V((16, 8, DIM), F32),
            V((4, 128, 16 * SLOTS), F32),
            V((4, 128, 16 * SLOTS), F32),
            V((4, 8, 16 * SLOTS), F32),
            V((4, 128, 16 * SLOTS), BF16),
            V((4, 128, 16 * SLOTS), BF16),
            V((4, 128, DIM), BF16),
            V((4, 128, DIM), BF16),
            V((4, 128, DIM), BF16),
            V((4, 128, DIM), BF16),
            V((4, 32, DIM), F32),
            V((4, 32, DIM), F32),
            V((4, 32, DIM), BF16),
            V((4, 32, DIM), BF16),
            V((4, 32, DIM), BF16),
            V((4, 32, DIM), BF16),
            V((16, 8, DIM), F32),
            V((16, SLOTS, DIM), BF16),
            V((16, SLOTS, DIM), BF16),
            V((ROWS, WIDTH), BF16),
            V((ROWS, WIDTH), BF16),
            pltpu.SemaphoreType.DMA((8,)),
            pltpu.SemaphoreType.DMA((5,)),
            pltpu.SemaphoreType.DMA((KINDS,)),
            pltpu.SemaphoreType.DMA((KINDS,)),
            pltpu.SemaphoreType.DMA((2, 4)),
        ],
        compiler_params=pltpu.CompilerParams(
            collective_id=0, has_side_effects=True, vmem_limit_bytes=60 * 1024 * 1024
        ),
    )(
        prompt_k, prompt_v, rewards, mask_pos[0], comp_q[0, 0], comp_k[0, 0], comp_v[0, 0],
        grad_out[0, 0],
    )
    shapes = [(SLOTS, WIDTH), (ROWS, WIDTH), (ROWS, WIDTH), (2, WIDTH), (2, WIDTH)]
    dq, dk, dv, gk, gv = pl.pallas_call(
        store_all,
        out_shape=[jax.ShapeDtypeStruct(shape, BF16) for shape in shapes],
        in_specs=[hbm] * 5,
        out_specs=[hbm] * 5,
        scratch_shapes=[V(grad.shape, grad.dtype) for grad in grads]
        + [
            V((SLOTS, WIDTH), BF16),
            V((2, WIDTH), BF16),
            V((2, WIDTH), BF16),
            pltpu.SemaphoreType.DMA((7,)),
            pltpu.SemaphoreType.DMA((7,)),
        ],
        compiler_params=pltpu.CompilerParams(vmem_limit_bytes=60 * 1024 * 1024),
    )(*grads)
    return dq[None, None], dk[None, None], dv[None, None], gk, gv


def solution(mesh):
    wide = P("grp", "ctx", None, None)
    rows = P(("grp", "ctx"), None)
    return jax.shard_map(
        shards,
        mesh=mesh,
        in_specs=(rows, rows, wide, wide, wide, wide, P("grp", "ctx"), P("grp", "ctx", None)),
        out_specs=(wide, wide, wide, rows, rows),
        check_vma=False,
    )
```

```python
import jax
import jax.numpy as jnp
from jax import lax
from jax.experimental import pallas as pl
from jax.experimental.pallas import tpu as pltpu
from jax.sharding import PartitionSpec as P

HEADS = 16
DIM = 128
SLOTS = 64
ROWS = 128
WIDTH = 2048
PROMPT = 512
F32 = jnp.float32
BF16 = jnp.bfloat16
SCALE = DIM ** -0.5
SCALE2 = SCALE * 1.4426950408889634
MESH = pl.DeviceIdType.MESH

(
    KV, QUERY, GRAD, ZK, ZV, ZSUM, YK, YV, OWN, FIN, DQ, YSUM_K, YSUM_V, ZSUM_K, ZSUM_V, OUT, KINDS
) = range(17)


def dot_nt(a, b):
    return lax.dot_general(a, b, (((1,), (1,)), ((), ())), preferred_element_type=F32)


def dot_nn(a, b):
    return lax.dot_general(a, b, (((1,), (0,)), ((), ())), preferred_element_type=F32)


def dot_tn(a, b):
    return lax.dot_general(a, b, (((0,), (0,)), ((), ())), preferred_element_type=F32)


def kernel(
    pk_hbm, pv_hbm, rw_hbm, mp_hbm, cq_hbm, ck_hbm, cv_hbm, go_hbm,
    own_hbm, dqr, dk_hbm, dv_hbm, gp_hbm,
    pk, pv, rw, mp, cq, ck, cv, go, xq, xqr, xg, xgr, kvs, kvr, kb, vb, gsum, gsumr, own_e, own_d, st, str_,
    fs, fr, exps, prods, part, pw, ds,
    sbk, sbv, rk, rv, hk, hv, szk, szv, rzk, rzv, t3, dqs, dqo, dko, dvo,
    in_sem, out_sem, ss, rs, ry,
):
    grp = lax.axis_index("grp")
    ctx = lax.axis_index("ctx")
    x_lo, y = lax.div(grp, 4), lax.rem(grp, 4)
    z = lax.div(ctx, 4)
    z_hi, z_lo, low = lax.div(z, 2), lax.rem(z, 2), lax.rem(ctx, 4)
    a = z_lo * 8 + x_lo * 4 + low

    def a_peer(b):
        return {
            "grp": lax.rem(lax.div(b, 4), 2) * 4 + y,
            "ctx": (z_hi * 2 + lax.div(b, 8)) * 4 + lax.rem(b, 4),
        }

    def z_peer(b):
        return {"grp": grp, "ctx": (b * 2 + z_lo) * 4 + low}

    def y_peer(b):
        return {"grp": x_lo * 4 + b, "ctx": ctx}

    flips = [(dz, 0, 1, dc) for dz in (1, 0) for dc in (1, 0)]
    flips += [(dz, 1, dx, dc) for dz in (1, 0) for dx in (1, 0) for dc in (1, 0)]
    flips += [(1, 0, 0, 1), (1, 0, 0, 0), (0, 0, 0, 1)]

    def flipped(bit, flip):
        return 1 - bit if flip else bit

    x_hi, core = lax.div(low, 2), lax.rem(low, 2)
    a_others = [
        flipped(z_lo, dz) * 8 + flipped(x_lo, dl) * 4 + flipped(x_hi, dh) * 2 + flipped(core, dc)
        for dz, dl, dh, dc in flips
    ]
    z_others = [lax.rem(z_hi + k, 4) for k in (2, 1, 3)]
    y_others = [lax.rem(y + k, 4) for k in (2, 1, 3)]

    def remote(kind, src, dst, device):
        return pltpu.make_async_remote_copy(
            src_ref=src, dst_ref=dst, send_sem=ss.at[kind], recv_sem=rs.at[kind],
            device_id=device, device_id_type=MESH,
        )

    def along_y(kv, ref, row, b):
        return pltpu.make_async_remote_copy(
            src_ref=ref.at[row], dst_ref=ref.at[row], send_sem=ss.at[YK + kv],
            recv_sem=ry.at[kv, row], device_id=y_peer(b), device_id_type=MESH,
        )

    def arrived(kind, dst):
        remote(kind, dst, dst, y_peer(y_others[0])).wait_recv()

    def sent(kind, src):
        remote(kind, src, src, y_peer(y_others[0])).wait_send()

    loads = [
        pltpu.make_async_copy(src, dst, in_sem.at[n])
        for n, (src, dst) in enumerate(
            (
                (pk_hbm, pk), (pv_hbm, pv), (rw_hbm, rw), (mp_hbm, mp),
                (cq_hbm, cq), (go_hbm, go), (ck_hbm, ck), (cv_hbm, cv),
            )
        )
    ]
    for load in loads[:4]:
        load.start()

    barrier = pltpu.get_barrier_semaphore()
    for b in z_others:
        pl.semaphore_signal(barrier, inc=1, device_id=z_peer(b), device_id_type=MESH)
    for b in y_others:
        pl.semaphore_signal(barrier, inc=1, device_id=y_peer(b), device_id_type=MESH)
    for b in a_others:
        pl.semaphore_signal(barrier, inc=1, device_id=a_peer(b), device_id_type=MESH)
    for load in loads[4:]:
        load.start()

    for load in loads[:4]:
        load.wait()
    pos = mp[...]
    pos2 = jnp.concatenate([pos, pos], axis=1)
    live = pos < ROWS
    count = jnp.sum(jnp.where(live, 1.0, 0.0), axis=1, keepdims=True)
    reward = rw[...]
    lines = jnp.concatenate(
        [
            pk[...].astype(F32),
            pv[...].astype(F32),
            jnp.broadcast_to(count, (1, WIDTH)),
            jnp.broadcast_to(reward, (1, WIDTH)),
            jnp.zeros((2, WIDTH), F32),
        ],
        axis=0,
    )
    for h in range(HEADS):
        kvs[h] = lines[:, h * DIM : (h + 1) * DIM]

    pl.semaphore_wait(barrier, 21)

    for b in a_others:
        remote(KV, kvs.at[b], kvr.at[a], a_peer(b)).start()
    kvr[a] = kvs[a]

    row = lax.broadcasted_iota(jnp.int32, (ROWS, 2 * SLOTS), 0)
    pick = jnp.where(row == jnp.minimum(pos2, ROWS - 1), 1.0, 0.0).astype(BF16)
    loads[4].wait()
    picked = dot_tn(pick, cq[...])[:SLOTS].astype(BF16)
    for h in range(HEADS):
        xq[h] = picked[:, h * DIM : (h + 1) * DIM]
    loads[5].wait()
    for h in range(HEADS):
        xg[h] = go[:, h * DIM : (h + 1) * DIM]

    nothing = jnp.zeros((SLOTS, DIM), BF16)

    def both(ref, t):
        return jnp.concatenate(
            [
                jnp.concatenate([ref[2 * t], nothing], axis=1),
                jnp.concatenate([nothing, ref[2 * t + 1]], axis=1),
            ],
            axis=0,
        )

    def own_scores(t):
        cols = slice(t * 256, (t + 1) * 256)
        s = dot_nt(ck[:, cols], both(xq, t)) * SCALE2
        d = dot_nt(cv[:, cols], both(xg, t))
        m = jnp.max(s, axis=0, keepdims=True)
        e = jnp.exp2(s - m)
        own_e[t] = e
        own_d[t] = d
        st[t] = jnp.concatenate(
            [
                m,
                jnp.sum(e, axis=0, keepdims=True),
                jnp.sum(e * d, axis=0, keepdims=True),
                jnp.zeros((5, DIM), F32),
            ],
            axis=0,
        )

    left = lax.broadcasted_iota(jnp.int32, (8, DIM), 1) < SLOTS
    odd = jnp.broadcast_to(lax.rem(a, 2), (8, DIM)) == 1

    def side_by_side(ref, t):
        one, two = ref[2 * t], ref[2 * t + 1]
        moved = pltpu.roll(jnp.where(odd, one, two), SLOTS, 1)
        return jnp.where(left != odd, jnp.where(left, one, two), moved)

    loads[6].wait()
    loads[7].wait()
    for t in range(4):
        own_scores(t)

    arrived(KV, kvr.at[pl.ds(0, 15)])
    blocks = kvr[...]
    kb[y, z_hi, 0:16, :] = blocks[:, 0, :].astype(BF16)
    kb[y, z_hi, 16:32, :] = blocks[:, 1, :].astype(BF16)
    for b in z_others:
        remote(ZK, kb.at[y, z_hi], kb.at[y, z_hi], z_peer(b)).start()
    vb[y, z_hi, 0:16, :] = blocks[:, 2, :].astype(BF16)
    vb[y, z_hi, 16:32, :] = blocks[:, 3, :].astype(BF16)
    for b in z_others:
        remote(ZV, vb.at[y, z_hi], vb.at[y, z_hi], z_peer(b)).start()
    mine = lax.broadcasted_iota(jnp.int32, (16, DIM), 0) // 4 % 2 == x_lo
    count16 = jnp.sum(jnp.where(mine, blocks[:, 4, :], 0.0), axis=0, keepdims=True)
    reward16 = jnp.sum(jnp.where(mine, blocks[:, 5, :], 0.0), axis=0, keepdims=True)
    gsum[...] = jnp.concatenate([count16, reward16, jnp.zeros((6, DIM), F32)], axis=0)
    for b in z_others:
        remote(ZSUM, gsum, gsumr.at[z_hi], z_peer(b)).start()
    for b in a_others:
        remote(QUERY, xq.at[b], xqr.at[a], a_peer(b)).start()
    xqr[a] = xq[a]
    for b in a_others:
        remote(GRAD, xg.at[b], xgr.at[a], a_peer(b)).start()
    xgr[a] = xg[a]

    for t in range(4, 8):
        own_scores(t)

    arrived(ZK, kb.at[0, pl.ds(0, 3)])
    for b in y_others:
        along_y(0, kb, y, b).start()
    arrived(ZV, vb.at[0, pl.ds(0, 3)])
    for b in y_others:
        along_y(1, vb, y, b).start()
    arrived(ZSUM, gsumr.at[pl.ds(0, 3)])
    total = gsum[...]
    for b in z_others:
        total = total + gsumr[b]
    weight = (reward - total[1:2] / 32.0) * (SLOTS * 32) / total[0:1]
    weight = jnp.where(pos2 < ROWS, weight, 0.0)
    for t in range(8):
        st[t, 3:4, :] = weight
    for b in a_others:
        remote(OWN, st.at[lax.div(b, 2)], str_.at[a], a_peer(b)).start()
    str_[a] = st[lax.div(a, 2)]

    def key_block(b):
        block = kb[b].reshape(128, DIM)
        for n in range(4):
            cols = slice(n * 256, (n + 1) * 256)
            s = dot_nt(block, xqr[4 * n : 4 * n + 4].reshape(256, DIM)) * SCALE2
            m = jnp.max(s, axis=0, keepdims=True)
            e = jnp.exp2(s - m)
            exps[b, :, cols] = e
            part[b, 0:1, cols] = m
            part[b, 1:2, cols] = jnp.sum(e, axis=0, keepdims=True)

    def value_block(b):
        block = vb[b].reshape(128, DIM)
        for n in range(4):
            cols = slice(n * 256, (n + 1) * 256)
            d = dot_nt(block, xgr[4 * n : 4 * n + 4].reshape(256, DIM)) * SCALE
            prods[b, :, cols] = d
            part[b, 2:3, cols] = jnp.sum(exps[b, :, cols] * d, axis=0, keepdims=True)

    near_first = y_others[1:] + y_others[:1]
    arrived(QUERY, xqr.at[pl.ds(0, 15)])
    key_block(y)
    for b in near_first:
        along_y(0, kb, b, b).wait_recv()
        key_block(b)
    arrived(OWN, str_.at[pl.ds(0, 15)])
    stats = jnp.concatenate([side_by_side(str_, t) for t in range(8)], axis=1)
    m = stats[0:1]
    for b in range(4):
        m = jnp.maximum(m, part[b, 0:1, :])
    fo = jnp.exp2(stats[0:1] - m)
    total = stats[1:2] * fo
    for b in range(4):
        f = jnp.exp2(part[b, 0:1, :] - m)
        total = total + part[b, 1:2, :] * f
        part[b, 3:4, :] = f
    inv = 1.0 / total
    weights = stats[3:4]

    def probabilities(b):
        coef = part[b, 3:4, :] * inv
        for n in range(4):
            cols = slice(n * 256, (n + 1) * 256)
            p = exps[b, :, cols] * coef[:, cols]
            exps[b, :, cols] = p
            pw[b, :, cols] = (p * weights[:, cols]).astype(BF16)

    arrived(GRAD, xgr.at[pl.ds(0, 15)])
    q_all = xqr[...].reshape(16 * SLOTS, DIM)
    g_all = xgr[...].reshape(16 * SLOTS, DIM)
    for b in y_others:
        probabilities(b)
        sbv[b] = dot_nn(pw[b], g_all).astype(BF16)
        remote(YSUM_V, sbv.at[b], rv.at[y], y_peer(b)).start()
    probabilities(y)

    value_block(y)
    for b in near_first:
        along_y(1, vb, b, b).wait_recv()
        value_block(b)
    inner = stats[2:3] * (fo * inv * SCALE)
    for b in range(4):
        inner = inner + part[b, 2:3, :]

    def finish(b):
        for n in range(4):
            cols = slice(n * 256, (n + 1) * 256)
            dscore = exps[b, :, cols] * (prods[b, :, cols] - inner[:, cols])
            ds[b, :, cols] = (dscore * weights[:, cols]).astype(BF16)

    for b in y_others:
        finish(b)
        sbk[b] = dot_nn(ds[b], q_all).astype(BF16)
        remote(YSUM_K, sbk.at[b], rk.at[y], y_peer(b)).start()
    finish(y)
    final = jnp.concatenate(
        [m, inv, inner * (1.0 / SCALE), jnp.zeros((5, 16 * SLOTS), F32)], axis=0
    )
    for t in range(8):
        fs[t] = final[:, t * DIM : (t + 1) * DIM]
    keys = kb[...].reshape(PROMPT, DIM)
    grad_v = dot_nn(pw[y], g_all)
    grad_k = dot_nn(ds[y], q_all)
    for b in a_others:
        remote(FIN, fs.at[lax.div(b, 2)], fr.at[a], a_peer(b)).start()
    fr[a] = fs[lax.div(a, 2)]
    for t in range(8):
        grad_q = dot_tn(ds[:, :, t * 128 : (t + 1) * 128].reshape(PROMPT, 2 * SLOTS), keys)
        dqs[2 * t] = grad_q[:SLOTS].astype(BF16)
        dqs[2 * t + 1] = grad_q[SLOTS:].astype(BF16)
    for b in a_others:
        remote(DQ, dqs.at[b], dqr.at[a], a_peer(b)).start()
    own_part = pltpu.make_async_copy(dqs.at[a], dqr.at[a], out_sem.at[4])
    own_part.start()

    def next_sum(total, kind_y, received, held, send, kind_z, target):
        arrived(kind_y, received.at[pl.ds(0, 3)])
        for b in y_others:
            total = total + received[b].astype(F32)
        held[...] = total.reshape(4, 32, DIM)
        send[...] = total.astype(BF16).reshape(4, 32, DIM)
        for b in z_others:
            remote(kind_z, send.at[b], target.at[z_hi], z_peer(b)).start()

    next_sum(grad_v, YSUM_V, rv, hv, szv, ZSUM_V, rzv)
    next_sum(grad_k, YSUM_K, rk, hk, szk, ZSUM_K, rzk)

    arrived(FIN, fr.at[pl.ds(0, 15)])
    for t in range(8):
        cols = slice(t * 256, (t + 1) * 256)
        fin = side_by_side(fr, t)
        m, inv, inner = fin[0:1], fin[1:2], fin[2:3]
        coef = jnp.exp2(st[t, 0:1, :] - m) * inv * weight
        e = own_e[t]
        p = (e * coef).astype(BF16)
        dsc = (e * (own_d[t] - inner) * (coef * SCALE)).astype(BF16)
        dvo[:, cols] = dot_nn(p, both(xg, t)).astype(BF16)
        dko[:, cols] = dot_nn(dsc, both(xq, t)).astype(BF16)
        grad_q = dot_tn(dsc, ck[:, cols])
        dqo[2 * t] = grad_q[:SLOTS, :DIM].astype(BF16)
        dqo[2 * t + 1] = grad_q[SLOTS:, DIM:].astype(BF16)
    stores = [
        pltpu.make_async_copy(src, dst, out_sem.at[n])
        for n, (src, dst) in enumerate(
            ((dqo, own_hbm), (dko, dk_hbm), (dvo, dv_hbm), (t3.at[a], gp_hbm.at[a]))
        )
    ]
    for store in stores[:3]:
        store.start()

    arrived(ZSUM_V, rzv.at[pl.ds(0, 3)])
    arrived(ZSUM_K, rzk.at[pl.ds(0, 3)])
    line = lax.broadcasted_iota(jnp.int32, (16, 8, DIM), 1)
    lines = jnp.zeros((16, 8, DIM), F32)
    for kv, (held, received) in enumerate(((hk, rzk), (hv, rzv))):
        part = held[z_hi]
        for b in z_others:
            part = part + received[b].astype(F32)
        for r in range(2):
            lines = jnp.where(line == kv * 2 + r, part[r * 16 : (r + 1) * 16][:, None, :], lines)
    t3[...] = lines
    for b in a_others:
        remote(OUT, t3.at[b], gp_hbm.at[a], a_peer(b)).start()
    stores[3].start()
    arrived(DQ, dqr.at[pl.ds(0, 15)])
    arrived(OUT, gp_hbm.at[pl.ds(0, 15)])

    sent(KV, kvs.at[pl.ds(0, 15)])
    sent(QUERY, xq.at[pl.ds(0, 15)])
    sent(GRAD, xg.at[pl.ds(0, 15)])
    sent(ZK, kb.at[0, pl.ds(0, 3)])
    sent(ZV, vb.at[0, pl.ds(0, 3)])
    sent(ZSUM, gsumr.at[pl.ds(0, 3)])
    sent(YK, kb.at[pl.ds(0, 3)])
    sent(YV, vb.at[pl.ds(0, 3)])
    sent(OWN, str_.at[pl.ds(0, 15)])
    sent(FIN, fr.at[pl.ds(0, 15)])
    sent(DQ, dqs.at[pl.ds(0, 15)])
    sent(YSUM_V, sbv.at[pl.ds(0, 3)])
    sent(YSUM_K, sbk.at[pl.ds(0, 3)])
    sent(ZSUM_V, szv.at[pl.ds(0, 3)])
    sent(ZSUM_K, szk.at[pl.ds(0, 3)])
    sent(OUT, t3.at[pl.ds(0, 15)])
    for store in stores + [own_part]:
        store.wait()


def store_all(own, other, dk, dv, gp, dq_out, dk_out, dv_out, gk_out, gv_out, *scratch):
    (
        own_held, other_held, dk_held, dv_held, gp_held, dq_held, gk_held, gv_held,
        in_sem, out_sem,
    ) = scratch
    pairs = [(own, own_held), (other, other_held), (gp, gp_held)]
    stores = []
    for source, held, target in ((dk, dk_held, dk_out), (dv, dv_held, dv_out)):
        for first in range(0, ROWS, SLOTS):
            span = pl.ds(first, SLOTS)
            pairs.append((source.at[span], held.at[span]))
            stores.append((held.at[span], target.at[span]))
    stores += [(dq_held, dq_out), (gk_held, gk_out), (gv_held, gv_out)]
    loads = [pltpu.make_async_copy(*pair, in_sem.at[n]) for n, pair in enumerate(pairs)]
    stores = [pltpu.make_async_copy(*pair, out_sem.at[n]) for n, pair in enumerate(stores)]
    for load in loads:
        load.start()
    loads[0].wait()
    loads[1].wait()
    for h in range(HEADS):
        cols = slice(h * DIM, (h + 1) * DIM)
        total = own_held[h].astype(F32) + other_held[h].astype(F32)
        dq_held[:, cols] = total.astype(BF16)
    stores[4].start()
    loads[2].wait()
    for h in range(HEADS):
        cols = slice(h * DIM, (h + 1) * DIM)
        gk_held[:, cols] = gp_held[h, 0:2, :].astype(BF16)
        gv_held[:, cols] = gp_held[h, 2:4, :].astype(BF16)
    stores[5].start()
    stores[6].start()
    for n in range(4):
        loads[3 + n].wait()
        stores[n].start()
    for store in stores:
        store.wait()


def shards(prompt_k, prompt_v, comp_q, comp_k, comp_v, grad_out, rewards, mask_pos):
    hbm = pl.BlockSpec(memory_space=pltpu.HBM)
    V = pltpu.VMEM
    grads = pl.pallas_call(
        kernel,
        out_shape=(
            jax.ShapeDtypeStruct((HEADS, SLOTS, DIM), BF16),
            jax.ShapeDtypeStruct((HEADS, SLOTS, DIM), BF16),
            jax.ShapeDtypeStruct((ROWS, WIDTH), BF16),
            jax.ShapeDtypeStruct((ROWS, WIDTH), BF16),
            jax.ShapeDtypeStruct((16, 8, DIM), F32),
        ),
        in_specs=[hbm] * 8,
        out_specs=(hbm,) * 5,
        scratch_shapes=[
            V((2, WIDTH), BF16),
            V((2, WIDTH), BF16),
            V((1, 1), F32),
            V((1, SLOTS), jnp.int32),
            V((ROWS, WIDTH), BF16),
            V((ROWS, WIDTH), BF16),
            V((ROWS, WIDTH), BF16),
            V((SLOTS, WIDTH), BF16),
            V((16, SLOTS, DIM), BF16),
            V((16, SLOTS, DIM), BF16),
            V((16, SLOTS, DIM), BF16),
            V((16, SLOTS, DIM), BF16),
            V((16, 8, DIM), F32),
            V((16, 8, DIM), F32),
            V((4, 4, 32, DIM), BF16),
            V((4, 4, 32, DIM), BF16),
            V((8, DIM), F32),
            V((4, 8, DIM), F32),
            V((8, 128, DIM), F32),
            V((8, 128, DIM), F32),
            V((8, 8, DIM), F32),
            V((16, 8, DIM), F32),
            V((8, 8, DIM), F32),
            V((16, 8, DIM), F32),
            V((4, 128, 16 * SLOTS), F32),
            V((4, 128, 16 * SLOTS), F32),
            V((4, 8, 16 * SLOTS), F32),
            V((4, 128, 16 * SLOTS), BF16),
            V((4, 128, 16 * SLOTS), BF16),
            V((4, 128, DIM), BF16),
            V((4, 128, DIM), BF16),
            V((4, 128, DIM), BF16),
            V((4, 128, DIM), BF16),
            V((4, 32, DIM), F32),
            V((4, 32, DIM), F32),
            V((4, 32, DIM), BF16),
            V((4, 32, DIM), BF16),
            V((4, 32, DIM), BF16),
            V((4, 32, DIM), BF16),
            V((16, 8, DIM), F32),
            V((16, SLOTS, DIM), BF16),
            V((16, SLOTS, DIM), BF16),
            V((ROWS, WIDTH), BF16),
            V((ROWS, WIDTH), BF16),
            pltpu.SemaphoreType.DMA((8,)),
            pltpu.SemaphoreType.DMA((5,)),
            pltpu.SemaphoreType.DMA((KINDS,)),
            pltpu.SemaphoreType.DMA((KINDS,)),
            pltpu.SemaphoreType.DMA((2, 4)),
        ],
        compiler_params=pltpu.CompilerParams(
            collective_id=0, has_side_effects=True, vmem_limit_bytes=60 * 1024 * 1024
        ),
    )(
        prompt_k, prompt_v, rewards, mask_pos[0], comp_q[0, 0], comp_k[0, 0], comp_v[0, 0],
        grad_out[0, 0],
    )
    shapes = [(SLOTS, WIDTH), (ROWS, WIDTH), (ROWS, WIDTH), (2, WIDTH), (2, WIDTH)]
    dq, dk, dv, gk, gv = pl.pallas_call(
        store_all,
        out_shape=[jax.ShapeDtypeStruct(shape, BF16) for shape in shapes],
        in_specs=[hbm] * 5,
        out_specs=[hbm] * 5,
        scratch_shapes=[V(grad.shape, grad.dtype) for grad in grads]
        + [
            V((SLOTS, WIDTH), BF16),
            V((2, WIDTH), BF16),
            V((2, WIDTH), BF16),
            pltpu.SemaphoreType.DMA((7,)),
            pltpu.SemaphoreType.DMA((7,)),
        ],
        compiler_params=pltpu.CompilerParams(vmem_limit_bytes=60 * 1024 * 1024),
    )(*grads)
    return dq[None, None], dk[None, None], dv[None, None], gk, gv


def solution(mesh):
    wide = P("grp", "ctx", None, None)
    rows = P(("grp", "ctx"), None)
    return jax.shard_map(
        shards,
        mesh=mesh,
        in_specs=(rows, rows, wide, wide, wide, wide, P("grp", "ctx"), P("grp", "ctx", None)),
        out_specs=(wide, wide, wide, rows, rows),
        check_vma=False,
    )
```

```python
import jax
import jax.numpy as jnp
from jax import lax
from jax.experimental import pallas as pl
from jax.experimental.pallas import tpu as pltpu
from jax.sharding import PartitionSpec as P

HEADS = 16
DIM = 128
SLOTS = 64
ROWS = 128
WIDTH = 2048
PROMPT = 512
F32 = jnp.float32
BF16 = jnp.bfloat16
SCALE = DIM ** -0.5
SCALE2 = SCALE * 1.4426950408889634
MESH = pl.DeviceIdType.MESH

(
    KV, QUERY, GRAD, ZK, ZV, ZSUM, YK, YV, OWN, FIN, DQ, YSUM_K, YSUM_V, ZSUM_K, ZSUM_V, OUT, KINDS
) = range(17)


def dot_nt(a, b):
    return lax.dot_general(a, b, (((1,), (1,)), ((), ())), preferred_element_type=F32)


def dot_nn(a, b):
    return lax.dot_general(a, b, (((1,), (0,)), ((), ())), preferred_element_type=F32)


def dot_tn(a, b):
    return lax.dot_general(a, b, (((0,), (0,)), ((), ())), preferred_element_type=F32)


def kernel(
    pk_hbm, pv_hbm, rw_hbm, mp_hbm, cq_hbm, ck_hbm, cv_hbm, go_hbm,
    own_hbm, dqr, dk_hbm, dv_hbm, gp_hbm,
    pk, pv, rw, mp, cq, ck, cv, go, xq, xqr, xg, xgr, kvs, kvr, kb, vb, gsum, gsumr, own_e, own_d, st, str_,
    fs, fr, exps, prods, part, pw, ds,
    sbk, sbv, rk, rv, hk, hv, szk, szv, rzk, rzv, t3, dqs, dqo, dko, dvo,
    in_sem, out_sem, ss, rs, ry,
):
    grp = lax.axis_index("grp")
    ctx = lax.axis_index("ctx")
    x_lo, y = lax.div(grp, 4), lax.rem(grp, 4)
    z = lax.div(ctx, 4)
    z_hi, z_lo, low = lax.div(z, 2), lax.rem(z, 2), lax.rem(ctx, 4)
    a = z_lo * 8 + x_lo * 4 + low

    def a_peer(b):
        return {
            "grp": lax.rem(lax.div(b, 4), 2) * 4 + y,
            "ctx": (z_hi * 2 + lax.div(b, 8)) * 4 + lax.rem(b, 4),
        }

    def z_peer(b):
        return {"grp": grp, "ctx": (b * 2 + z_lo) * 4 + low}

    def y_peer(b):
        return {"grp": x_lo * 4 + b, "ctx": ctx}

    flips = [(dz, 0, 1, dc) for dz in (1, 0) for dc in (1, 0)]
    flips += [(dz, 1, dx, dc) for dz in (1, 0) for dx in (1, 0) for dc in (1, 0)]
    flips += [(1, 0, 0, 1), (1, 0, 0, 0), (0, 0, 0, 1)]

    def flipped(bit, flip):
        return 1 - bit if flip else bit

    x_hi, core = lax.div(low, 2), lax.rem(low, 2)
    a_others = [
        flipped(z_lo, dz) * 8 + flipped(x_lo, dl) * 4 + flipped(x_hi, dh) * 2 + flipped(core, dc)
        for dz, dl, dh, dc in flips
    ]
    z_others = [lax.rem(z_hi + k, 4) for k in (2, 1, 3)]
    y_others = [lax.rem(y + k, 4) for k in (2, 1, 3)]

    def remote(kind, src, dst, device):
        return pltpu.make_async_remote_copy(
            src_ref=src, dst_ref=dst, send_sem=ss.at[kind], recv_sem=rs.at[kind],
            device_id=device, device_id_type=MESH,
        )

    def along_y(kv, ref, row, b):
        return pltpu.make_async_remote_copy(
            src_ref=ref.at[row], dst_ref=ref.at[row], send_sem=ss.at[YK + kv],
            recv_sem=ry.at[kv, row], device_id=y_peer(b), device_id_type=MESH,
        )

    def arrived(kind, dst):
        remote(kind, dst, dst, y_peer(y_others[0])).wait_recv()

    def sent(kind, src):
        remote(kind, src, src, y_peer(y_others[0])).wait_send()

    loads = [
        pltpu.make_async_copy(src, dst, in_sem.at[n])
        for n, (src, dst) in enumerate(
            (
                (pk_hbm, pk), (pv_hbm, pv), (rw_hbm, rw), (mp_hbm, mp),
                (cq_hbm, cq), (go_hbm, go), (ck_hbm, ck), (cv_hbm, cv),
            )
        )
    ]
    for load in loads[:4]:
        load.start()

    barrier = pltpu.get_barrier_semaphore()
    for b in z_others:
        pl.semaphore_signal(barrier, inc=1, device_id=z_peer(b), device_id_type=MESH)
    for b in y_others:
        pl.semaphore_signal(barrier, inc=1, device_id=y_peer(b), device_id_type=MESH)
    for b in a_others:
        pl.semaphore_signal(barrier, inc=1, device_id=a_peer(b), device_id_type=MESH)
    for load in loads[4:]:
        load.start()

    for load in loads[:4]:
        load.wait()
    pos = mp[...]
    pos2 = jnp.concatenate([pos, pos], axis=1)
    live = pos < ROWS
    count = jnp.sum(jnp.where(live, 1.0, 0.0), axis=1, keepdims=True)
    reward = rw[...]
    lines = jnp.concatenate(
        [
            pk[...].astype(F32),
            pv[...].astype(F32),
            jnp.broadcast_to(count, (1, WIDTH)),
            jnp.broadcast_to(reward, (1, WIDTH)),
            jnp.zeros((2, WIDTH), F32),
        ],
        axis=0,
    )
    for h in range(HEADS):
        kvs[h] = lines[:, h * DIM : (h + 1) * DIM]

    pl.semaphore_wait(barrier, 21)

    for b in a_others:
        remote(KV, kvs.at[b], kvr.at[a], a_peer(b)).start()
    kvr[a] = kvs[a]

    row = lax.broadcasted_iota(jnp.int32, (ROWS, 2 * SLOTS), 0)
    pick = jnp.where(row == jnp.minimum(pos2, ROWS - 1), 1.0, 0.0).astype(BF16)
    loads[4].wait()
    picked = dot_tn(pick, cq[...])[:SLOTS].astype(BF16)
    for h in range(HEADS):
        xq[h] = picked[:, h * DIM : (h + 1) * DIM]
    for b in a_others[:4]:
        remote(QUERY, xq.at[b], xqr.at[a], a_peer(b)).start()
    xqr[a] = xq[a]
    loads[5].wait()
    for h in range(HEADS):
        xg[h] = go[:, h * DIM : (h + 1) * DIM]

    nothing = jnp.zeros((SLOTS, DIM), BF16)

    def both(ref, t):
        return jnp.concatenate(
            [
                jnp.concatenate([ref[2 * t], nothing], axis=1),
                jnp.concatenate([nothing, ref[2 * t + 1]], axis=1),
            ],
            axis=0,
        )

    def own_scores(t):
        cols = slice(t * 256, (t + 1) * 256)
        s = dot_nt(ck[:, cols], both(xq, t)) * SCALE2
        d = dot_nt(cv[:, cols], both(xg, t))
        m = jnp.max(s, axis=0, keepdims=True)
        e = jnp.exp2(s - m)
        own_e[t] = e
        own_d[t] = d
        st[t] = jnp.concatenate(
            [
                m,
                jnp.sum(e, axis=0, keepdims=True),
                jnp.sum(e * d, axis=0, keepdims=True),
                jnp.zeros((5, DIM), F32),
            ],
            axis=0,
        )

    left = lax.broadcasted_iota(jnp.int32, (8, DIM), 1) < SLOTS
    odd = jnp.broadcast_to(lax.rem(a, 2), (8, DIM)) == 1

    def side_by_side(ref, t):
        one, two = ref[2 * t], ref[2 * t + 1]
        moved = pltpu.roll(jnp.where(odd, one, two), SLOTS, 1)
        return jnp.where(left != odd, jnp.where(left, one, two), moved)

    loads[6].wait()
    loads[7].wait()
    for t in range(4):
        own_scores(t)

    arrived(KV, kvr.at[pl.ds(0, 15)])
    blocks = kvr[...]
    kb[y, z_hi, 0:16, :] = blocks[:, 0, :].astype(BF16)
    kb[y, z_hi, 16:32, :] = blocks[:, 1, :].astype(BF16)
    for b in z_others:
        remote(ZK, kb.at[y, z_hi], kb.at[y, z_hi], z_peer(b)).start()
    vb[y, z_hi, 0:16, :] = blocks[:, 2, :].astype(BF16)
    vb[y, z_hi, 16:32, :] = blocks[:, 3, :].astype(BF16)
    for b in z_others:
        remote(ZV, vb.at[y, z_hi], vb.at[y, z_hi], z_peer(b)).start()
    mine = lax.broadcasted_iota(jnp.int32, (16, DIM), 0) // 4 % 2 == x_lo
    count16 = jnp.sum(jnp.where(mine, blocks[:, 4, :], 0.0), axis=0, keepdims=True)
    reward16 = jnp.sum(jnp.where(mine, blocks[:, 5, :], 0.0), axis=0, keepdims=True)
    gsum[...] = jnp.concatenate([count16, reward16, jnp.zeros((6, DIM), F32)], axis=0)
    for b in z_others:
        remote(ZSUM, gsum, gsumr.at[z_hi], z_peer(b)).start()
    for b in a_others[4:]:
        remote(QUERY, xq.at[b], xqr.at[a], a_peer(b)).start()
    for b in a_others:
        remote(GRAD, xg.at[b], xgr.at[a], a_peer(b)).start()
    xgr[a] = xg[a]

    for t in range(4, 8):
        own_scores(t)

    arrived(ZK, kb.at[0, pl.ds(0, 3)])
    for b in y_others:
        along_y(0, kb, y, b).start()
    arrived(ZV, vb.at[0, pl.ds(0, 3)])
    for b in y_others:
        along_y(1, vb, y, b).start()
    arrived(ZSUM, gsumr.at[pl.ds(0, 3)])
    total = gsum[...]
    for b in z_others:
        total = total + gsumr[b]
    weight = (reward - total[1:2] / 32.0) * (SLOTS * 32) / total[0:1]
    weight = jnp.where(pos2 < ROWS, weight, 0.0)
    for t in range(8):
        st[t, 3:4, :] = weight
    for b in a_others:
        remote(OWN, st.at[lax.div(b, 2)], str_.at[a], a_peer(b)).start()
    str_[a] = st[lax.div(a, 2)]

    def key_block(b):
        block = kb[b].reshape(128, DIM)
        for n in range(4):
            cols = slice(n * 256, (n + 1) * 256)
            s = dot_nt(block, xqr[4 * n : 4 * n + 4].reshape(256, DIM)) * SCALE2
            m = jnp.max(s, axis=0, keepdims=True)
            e = jnp.exp2(s - m)
            exps[b, :, cols] = e
            part[b, 0:1, cols] = m
            part[b, 1:2, cols] = jnp.sum(e, axis=0, keepdims=True)

    def value_block(b):
        block = vb[b].reshape(128, DIM)
        for n in range(4):
            cols = slice(n * 256, (n + 1) * 256)
            d = dot_nt(block, xgr[4 * n : 4 * n + 4].reshape(256, DIM)) * SCALE
            prods[b, :, cols] = d
            part[b, 2:3, cols] = jnp.sum(exps[b, :, cols] * d, axis=0, keepdims=True)

    near_first = y_others[1:] + y_others[:1]
    arrived(QUERY, xqr.at[pl.ds(0, 15)])
    key_block(y)
    for b in near_first:
        along_y(0, kb, b, b).wait_recv()
        key_block(b)
    arrived(OWN, str_.at[pl.ds(0, 15)])
    stats = jnp.concatenate([side_by_side(str_, t) for t in range(8)], axis=1)
    m = stats[0:1]
    for b in range(4):
        m = jnp.maximum(m, part[b, 0:1, :])
    fo = jnp.exp2(stats[0:1] - m)
    total = stats[1:2] * fo
    for b in range(4):
        f = jnp.exp2(part[b, 0:1, :] - m)
        total = total + part[b, 1:2, :] * f
        part[b, 3:4, :] = f
    inv = 1.0 / total
    weights = stats[3:4]

    def probabilities(b):
        coef = part[b, 3:4, :] * inv
        for n in range(4):
            cols = slice(n * 256, (n + 1) * 256)
            p = exps[b, :, cols] * coef[:, cols]
            exps[b, :, cols] = p
            pw[b, :, cols] = (p * weights[:, cols]).astype(BF16)

    for b in y_others + [y]:
        probabilities(b)
    arrived(GRAD, xgr.at[pl.ds(0, 15)])
    q_all = xqr[...].reshape(16 * SLOTS, DIM)
    g_all = xgr[...].reshape(16 * SLOTS, DIM)
    for b in y_others:
        sbv[b] = dot_nn(pw[b], g_all).astype(BF16)
        remote(YSUM_V, sbv.at[b], rv.at[y], y_peer(b)).start()
    value_block(y)
    for b in near_first:
        along_y(1, vb, b, b).wait_recv()
        value_block(b)
    inner = stats[2:3] * (fo * inv * SCALE)
    for b in range(4):
        inner = inner + part[b, 2:3, :]

    def finish(b):
        for n in range(4):
            cols = slice(n * 256, (n + 1) * 256)
            dscore = exps[b, :, cols] * (prods[b, :, cols] - inner[:, cols])
            ds[b, :, cols] = (dscore * weights[:, cols]).astype(BF16)

    for b in y_others:
        finish(b)
        sbk[b] = dot_nn(ds[b], q_all).astype(BF16)
        remote(YSUM_K, sbk.at[b], rk.at[y], y_peer(b)).start()
    finish(y)
    final = jnp.concatenate(
        [m, inv, inner * (1.0 / SCALE), jnp.zeros((5, 16 * SLOTS), F32)], axis=0
    )
    for t in range(8):
        fs[t] = final[:, t * DIM : (t + 1) * DIM]
    keys = kb[...].reshape(PROMPT, DIM)
    grad_v = dot_nn(pw[y], g_all)
    grad_k = dot_nn(ds[y], q_all)
    for b in a_others:
        remote(FIN, fs.at[lax.div(b, 2)], fr.at[a], a_peer(b)).start()
    fr[a] = fs[lax.div(a, 2)]
    for t in range(8):
        grad_q = dot_tn(ds[:, :, t * 128 : (t + 1) * 128].reshape(PROMPT, 2 * SLOTS), keys)
        dqs[2 * t] = grad_q[:SLOTS].astype(BF16)
        dqs[2 * t + 1] = grad_q[SLOTS:].astype(BF16)
    def next_sum(total, kind_y, received, held, send, kind_z, target):
        arrived(kind_y, received.at[pl.ds(0, 3)])
        for b in y_others:
            total = total + received[b].astype(F32)
        held[...] = total.reshape(4, 32, DIM)
        send[...] = total.astype(BF16).reshape(4, 32, DIM)
        for b in z_others:
            remote(kind_z, send.at[b], target.at[z_hi], z_peer(b)).start()

    next_sum(grad_v, YSUM_V, rv, hv, szv, ZSUM_V, rzv)
    for b in a_others:
        remote(DQ, dqs.at[b], dqr.at[a], a_peer(b)).start()
    own_part = pltpu.make_async_copy(dqs.at[a], dqr.at[a], out_sem.at[4])
    own_part.start()
    next_sum(grad_k, YSUM_K, rk, hk, szk, ZSUM_K, rzk)

    arrived(FIN, fr.at[pl.ds(0, 15)])
    for t in range(8):
        cols = slice(t * 256, (t + 1) * 256)
        fin = side_by_side(fr, t)
        m, inv, inner = fin[0:1], fin[1:2], fin[2:3]
        coef = jnp.exp2(st[t, 0:1, :] - m) * inv * weight
        e = own_e[t]
        p = (e * coef).astype(BF16)
        dsc = (e * (own_d[t] - inner) * (coef * SCALE)).astype(BF16)
        dvo[:, cols] = dot_nn(p, both(xg, t)).astype(BF16)
        dko[:, cols] = dot_nn(dsc, both(xq, t)).astype(BF16)
        grad_q = dot_tn(dsc, ck[:, cols])
        dqo[2 * t] = grad_q[:SLOTS, :DIM].astype(BF16)
        dqo[2 * t + 1] = grad_q[SLOTS:, DIM:].astype(BF16)
    stores = [
        pltpu.make_async_copy(src, dst, out_sem.at[n])
        for n, (src, dst) in enumerate(
            ((dqo, own_hbm), (dko, dk_hbm), (dvo, dv_hbm), (t3.at[a], gp_hbm.at[a]))
        )
    ]
    for store in stores[:3]:
        store.start()

    arrived(ZSUM_V, rzv.at[pl.ds(0, 3)])
    arrived(ZSUM_K, rzk.at[pl.ds(0, 3)])
    line = lax.broadcasted_iota(jnp.int32, (16, 8, DIM), 1)
    lines = jnp.zeros((16, 8, DIM), F32)
    for kv, (held, received) in enumerate(((hk, rzk), (hv, rzv))):
        part = held[z_hi]
        for b in z_others:
            part = part + received[b].astype(F32)
        for r in range(2):
            lines = jnp.where(line == kv * 2 + r, part[r * 16 : (r + 1) * 16][:, None, :], lines)
    t3[...] = lines
    for b in a_others:
        remote(OUT, t3.at[b], gp_hbm.at[a], a_peer(b)).start()
    stores[3].start()
    arrived(DQ, dqr.at[pl.ds(0, 15)])
    arrived(OUT, gp_hbm.at[pl.ds(0, 15)])

    sent(KV, kvs.at[pl.ds(0, 15)])
    sent(QUERY, xq.at[pl.ds(0, 15)])
    sent(GRAD, xg.at[pl.ds(0, 15)])
    sent(ZK, kb.at[0, pl.ds(0, 3)])
    sent(ZV, vb.at[0, pl.ds(0, 3)])
    sent(ZSUM, gsumr.at[pl.ds(0, 3)])
    sent(YK, kb.at[pl.ds(0, 3)])
    sent(YV, vb.at[pl.ds(0, 3)])
    sent(OWN, str_.at[pl.ds(0, 15)])
    sent(FIN, fr.at[pl.ds(0, 15)])
    sent(DQ, dqs.at[pl.ds(0, 15)])
    sent(YSUM_V, sbv.at[pl.ds(0, 3)])
    sent(YSUM_K, sbk.at[pl.ds(0, 3)])
    sent(ZSUM_V, szv.at[pl.ds(0, 3)])
    sent(ZSUM_K, szk.at[pl.ds(0, 3)])
    sent(OUT, t3.at[pl.ds(0, 15)])
    for store in stores + [own_part]:
        store.wait()


def store_all(own, other, dk, dv, gp, dq_out, dk_out, dv_out, gk_out, gv_out, *scratch):
    (
        own_held, other_held, dk_held, dv_held, gp_held, dq_held, gk_held, gv_held,
        in_sem, out_sem,
    ) = scratch
    pairs = [(own, own_held), (other, other_held), (gp, gp_held)]
    stores = []
    for source, held, target in ((dk, dk_held, dk_out), (dv, dv_held, dv_out)):
        for first in range(0, ROWS, SLOTS):
            span = pl.ds(first, SLOTS)
            pairs.append((source.at[span], held.at[span]))
            stores.append((held.at[span], target.at[span]))
    stores += [(dq_held, dq_out), (gk_held, gk_out), (gv_held, gv_out)]
    loads = [pltpu.make_async_copy(*pair, in_sem.at[n]) for n, pair in enumerate(pairs)]
    stores = [pltpu.make_async_copy(*pair, out_sem.at[n]) for n, pair in enumerate(stores)]
    for load in loads:
        load.start()
    loads[0].wait()
    loads[1].wait()
    for h in range(HEADS):
        cols = slice(h * DIM, (h + 1) * DIM)
        total = own_held[h].astype(F32) + other_held[h].astype(F32)
        dq_held[:, cols] = total.astype(BF16)
    stores[4].start()
    for n in range(4):
        loads[3 + n].wait()
        stores[n].start()
    loads[2].wait()
    for h in range(HEADS):
        cols = slice(h * DIM, (h + 1) * DIM)
        gk_held[:, cols] = gp_held[h, 0:2, :].astype(BF16)
        gv_held[:, cols] = gp_held[h, 2:4, :].astype(BF16)
    stores[5].start()
    stores[6].start()
    for store in stores:
        store.wait()


def shards(prompt_k, prompt_v, comp_q, comp_k, comp_v, grad_out, rewards, mask_pos):
    hbm = pl.BlockSpec(memory_space=pltpu.HBM)
    V = pltpu.VMEM
    grads = pl.pallas_call(
        kernel,
        out_shape=(
            jax.ShapeDtypeStruct((HEADS, SLOTS, DIM), BF16),
            jax.ShapeDtypeStruct((HEADS, SLOTS, DIM), BF16),
            jax.ShapeDtypeStruct((ROWS, WIDTH), BF16),
            jax.ShapeDtypeStruct((ROWS, WIDTH), BF16),
            jax.ShapeDtypeStruct((16, 8, DIM), F32),
        ),
        in_specs=[hbm] * 8,
        out_specs=(hbm,) * 5,
        scratch_shapes=[
            V((2, WIDTH), BF16),
            V((2, WIDTH), BF16),
            V((1, 1), F32),
            V((1, SLOTS), jnp.int32),
            V((ROWS, WIDTH), BF16),
            V((ROWS, WIDTH), BF16),
            V((ROWS, WIDTH), BF16),
            V((SLOTS, WIDTH), BF16),
            V((16, SLOTS, DIM), BF16),
            V((16, SLOTS, DIM), BF16),
            V((16, SLOTS, DIM), BF16),
            V((16, SLOTS, DIM), BF16),
            V((16, 8, DIM), F32),
            V((16, 8, DIM), F32),
            V((4, 4, 32, DIM), BF16),
            V((4, 4, 32, DIM), BF16),
            V((8, DIM), F32),
            V((4, 8, DIM), F32),
            V((8, 128, DIM), F32),
            V((8, 128, DIM), F32),
            V((8, 8, DIM), F32),
            V((16, 8, DIM), F32),
            V((8, 8, DIM), F32),
            V((16, 8, DIM), F32),
            V((4, 128, 16 * SLOTS), F32),
            V((4, 128, 16 * SLOTS), F32),
            V((4, 8, 16 * SLOTS), F32),
            V((4, 128, 16 * SLOTS), BF16),
            V((4, 128, 16 * SLOTS), BF16),
            V((4, 128, DIM), BF16),
            V((4, 128, DIM), BF16),
            V((4, 128, DIM), BF16),
            V((4, 128, DIM), BF16),
            V((4, 32, DIM), F32),
            V((4, 32, DIM), F32),
            V((4, 32, DIM), BF16),
            V((4, 32, DIM), BF16),
            V((4, 32, DIM), BF16),
            V((4, 32, DIM), BF16),
            V((16, 8, DIM), F32),
            V((16, SLOTS, DIM), BF16),
            V((16, SLOTS, DIM), BF16),
            V((ROWS, WIDTH), BF16),
            V((ROWS, WIDTH), BF16),
            pltpu.SemaphoreType.DMA((8,)),
            pltpu.SemaphoreType.DMA((5,)),
            pltpu.SemaphoreType.DMA((KINDS,)),
            pltpu.SemaphoreType.DMA((KINDS,)),
            pltpu.SemaphoreType.DMA((2, 4)),
        ],
        compiler_params=pltpu.CompilerParams(
            collective_id=0, has_side_effects=True, vmem_limit_bytes=60 * 1024 * 1024
        ),
    )(
        prompt_k, prompt_v, rewards, mask_pos[0], comp_q[0, 0], comp_k[0, 0], comp_v[0, 0],
        grad_out[0, 0],
    )
    shapes = [(SLOTS, WIDTH), (ROWS, WIDTH), (ROWS, WIDTH), (2, WIDTH), (2, WIDTH)]
    dq, dk, dv, gk, gv = pl.pallas_call(
        store_all,
        out_shape=[jax.ShapeDtypeStruct(shape, BF16) for shape in shapes],
        in_specs=[hbm] * 5,
        out_specs=[hbm] * 5,
        scratch_shapes=[V(grad.shape, grad.dtype) for grad in grads]
        + [
            V((SLOTS, WIDTH), BF16),
            V((2, WIDTH), BF16),
            V((2, WIDTH), BF16),
            pltpu.SemaphoreType.DMA((7,)),
            pltpu.SemaphoreType.DMA((7,)),
        ],
        compiler_params=pltpu.CompilerParams(vmem_limit_bytes=60 * 1024 * 1024),
    )(*grads)
    return dq[None, None], dk[None, None], dv[None, None], gk, gv


def solution(mesh):
    wide = P("grp", "ctx", None, None)
    rows = P(("grp", "ctx"), None)
    return jax.shard_map(
        shards,
        mesh=mesh,
        in_specs=(rows, rows, wide, wide, wide, wide, P("grp", "ctx"), P("grp", "ctx", None)),
        out_specs=(wide, wide, wide, rows, rows),
        check_vma=False,
    )
```

```python
import jax
import jax.numpy as jnp
from jax import lax
from jax.experimental import pallas as pl
from jax.experimental.pallas import tpu as pltpu
from jax.sharding import PartitionSpec as P

HEADS = 16
DIM = 128
SLOTS = 64
ROWS = 128
WIDTH = 2048
PROMPT = 512
F32 = jnp.float32
BF16 = jnp.bfloat16
SCALE = DIM ** -0.5
SCALE2 = SCALE * 1.4426950408889634
MESH = pl.DeviceIdType.MESH

(
    KV, QUERY, GRAD, ZK, ZV, ZSUM, YK, YV, OWN, FIN, DQ, YSUM_K, YSUM_V, ZSUM_K, ZSUM_V, OUT, KINDS
) = range(17)


def dot_nt(a, b):
    return lax.dot_general(a, b, (((1,), (1,)), ((), ())), preferred_element_type=F32)


def dot_nn(a, b):
    return lax.dot_general(a, b, (((1,), (0,)), ((), ())), preferred_element_type=F32)


def dot_tn(a, b):
    return lax.dot_general(a, b, (((0,), (0,)), ((), ())), preferred_element_type=F32)


def kernel(
    pk_hbm, pv_hbm, rw_hbm, mp_hbm, cq_hbm, ck_hbm, cv_hbm, go_hbm,
    own_hbm, dqr, dk_hbm, dv_hbm, gp_hbm,
    pk, pv, rw, mp, cq, ck, cv, go, xq, xqr, xg, xgr, kvs, kvr, kb, vb, gsum, gsumr, own_e, own_d, st, str_,
    fs, fr, exps, prods, part, pw, ds,
    sbk, sbv, rk, rv, hk, hv, szk, szv, rzk, rzv, t3, dqs, dqo, dko, dvo,
    in_sem, out_sem, ss, rs, ry,
):
    grp = lax.axis_index("grp")
    ctx = lax.axis_index("ctx")
    x_lo, y = lax.div(grp, 4), lax.rem(grp, 4)
    z = lax.div(ctx, 4)
    z_hi, z_lo, low = lax.div(z, 2), lax.rem(z, 2), lax.rem(ctx, 4)
    a = z_lo * 8 + x_lo * 4 + low

    def a_peer(b):
        return {
            "grp": lax.rem(lax.div(b, 4), 2) * 4 + y,
            "ctx": (z_hi * 2 + lax.div(b, 8)) * 4 + lax.rem(b, 4),
        }

    def z_peer(b):
        return {"grp": grp, "ctx": (b * 2 + z_lo) * 4 + low}

    def y_peer(b):
        return {"grp": x_lo * 4 + b, "ctx": ctx}

    flips = [(dz, 0, 1, dc) for dz in (1, 0) for dc in (1, 0)]
    flips += [(dz, 1, dx, dc) for dz in (1, 0) for dx in (1, 0) for dc in (1, 0)]
    flips += [(1, 0, 0, 1), (1, 0, 0, 0), (0, 0, 0, 1)]

    def flipped(bit, flip):
        return 1 - bit if flip else bit

    x_hi, core = lax.div(low, 2), lax.rem(low, 2)
    a_others = [
        flipped(z_lo, dz) * 8 + flipped(x_lo, dl) * 4 + flipped(x_hi, dh) * 2 + flipped(core, dc)
        for dz, dl, dh, dc in flips
    ]
    z_others = [lax.rem(z_hi + k, 4) for k in (2, 1, 3)]
    y_others = [lax.rem(y + k, 4) for k in (2, 1, 3)]

    def remote(kind, src, dst, device):
        return pltpu.make_async_remote_copy(
            src_ref=src, dst_ref=dst, send_sem=ss.at[kind], recv_sem=rs.at[kind],
            device_id=device, device_id_type=MESH,
        )

    def along_y(kv, ref, row, b):
        return pltpu.make_async_remote_copy(
            src_ref=ref.at[row], dst_ref=ref.at[row], send_sem=ss.at[YK + kv],
            recv_sem=ry.at[kv, row], device_id=y_peer(b), device_id_type=MESH,
        )

    def arrived(kind, dst):
        remote(kind, dst, dst, y_peer(y_others[0])).wait_recv()

    def sent(kind, src):
        remote(kind, src, src, y_peer(y_others[0])).wait_send()

    loads = [
        pltpu.make_async_copy(src, dst, in_sem.at[n])
        for n, (src, dst) in enumerate(
            (
                (pk_hbm, pk), (pv_hbm, pv), (rw_hbm, rw), (mp_hbm, mp),
                (cq_hbm, cq), (go_hbm, go), (ck_hbm, ck), (cv_hbm, cv),
            )
        )
    ]
    for load in loads[:4]:
        load.start()

    barrier = pltpu.get_barrier_semaphore()
    for b in z_others:
        pl.semaphore_signal(barrier, inc=1, device_id=z_peer(b), device_id_type=MESH)
    for b in y_others:
        pl.semaphore_signal(barrier, inc=1, device_id=y_peer(b), device_id_type=MESH)
    for b in a_others:
        pl.semaphore_signal(barrier, inc=1, device_id=a_peer(b), device_id_type=MESH)
    for load in loads[4:]:
        load.start()

    for load in loads[:4]:
        load.wait()
    pos = mp[...]
    pos2 = jnp.concatenate([pos, pos], axis=1)
    live = pos < ROWS
    count = jnp.sum(jnp.where(live, 1.0, 0.0), axis=1, keepdims=True)
    reward = rw[...]
    lines = jnp.concatenate(
        [
            pk[...].astype(F32),
            pv[...].astype(F32),
            jnp.broadcast_to(count, (1, WIDTH)),
            jnp.broadcast_to(reward, (1, WIDTH)),
            jnp.zeros((2, WIDTH), F32),
        ],
        axis=0,
    )
    for h in range(HEADS):
        kvs[h] = lines[:, h * DIM : (h + 1) * DIM]

    pl.semaphore_wait(barrier, 21)

    for b in a_others:
        remote(KV, kvs.at[b], kvr.at[a], a_peer(b)).start()
    kvr[a] = kvs[a]

    row = lax.broadcasted_iota(jnp.int32, (ROWS, 2 * SLOTS), 0)
    pick = jnp.where(row == jnp.minimum(pos2, ROWS - 1), 1.0, 0.0).astype(BF16)
    loads[4].wait()
    picked = dot_tn(pick, cq[...])[:SLOTS].astype(BF16)
    for h in range(HEADS):
        xq[h] = picked[:, h * DIM : (h + 1) * DIM]
    loads[5].wait()
    for h in range(HEADS):
        xg[h] = go[:, h * DIM : (h + 1) * DIM]

    nothing = jnp.zeros((SLOTS, DIM), BF16)

    def both(ref, t):
        return jnp.concatenate(
            [
                jnp.concatenate([ref[2 * t], nothing], axis=1),
                jnp.concatenate([nothing, ref[2 * t + 1]], axis=1),
            ],
            axis=0,
        )

    def own_scores(t):
        cols = slice(t * 256, (t + 1) * 256)
        s = dot_nt(ck[:, cols], both(xq, t)) * SCALE2
        d = dot_nt(cv[:, cols], both(xg, t))
        m = jnp.max(s, axis=0, keepdims=True)
        e = jnp.exp2(s - m)
        own_e[t] = e
        own_d[t] = d
        st[t] = jnp.concatenate(
            [
                m,
                jnp.sum(e, axis=0, keepdims=True),
                jnp.sum(e * d, axis=0, keepdims=True),
                jnp.zeros((5, DIM), F32),
            ],
            axis=0,
        )

    left = lax.broadcasted_iota(jnp.int32, (8, DIM), 1) < SLOTS
    odd = jnp.broadcast_to(lax.rem(a, 2), (8, DIM)) == 1

    def side_by_side(ref, t):
        one, two = ref[2 * t], ref[2 * t + 1]
        moved = pltpu.roll(jnp.where(odd, one, two), SLOTS, 1)
        return jnp.where(left != odd, jnp.where(left, one, two), moved)

    loads[6].wait()
    loads[7].wait()
    for t in range(4):
        own_scores(t)

    arrived(KV, kvr.at[pl.ds(0, 15)])
    blocks = kvr[...]
    kb[y, z_hi, 0:16, :] = blocks[:, 0, :].astype(BF16)
    kb[y, z_hi, 16:32, :] = blocks[:, 1, :].astype(BF16)
    for b in z_others:
        remote(ZK, kb.at[y, z_hi], kb.at[y, z_hi], z_peer(b)).start()
    vb[y, z_hi, 0:16, :] = blocks[:, 2, :].astype(BF16)
    vb[y, z_hi, 16:32, :] = blocks[:, 3, :].astype(BF16)
    for b in z_others:
        remote(ZV, vb.at[y, z_hi], vb.at[y, z_hi], z_peer(b)).start()
    mine = lax.broadcasted_iota(jnp.int32, (16, DIM), 0) // 4 % 2 == x_lo
    count16 = jnp.sum(jnp.where(mine, blocks[:, 4, :], 0.0), axis=0, keepdims=True)
    reward16 = jnp.sum(jnp.where(mine, blocks[:, 5, :], 0.0), axis=0, keepdims=True)
    gsum[...] = jnp.concatenate([count16, reward16, jnp.zeros((6, DIM), F32)], axis=0)
    for b in z_others:
        remote(ZSUM, gsum, gsumr.at[z_hi], z_peer(b)).start()
    for b in a_others:
        remote(QUERY, xq.at[b], xqr.at[a], a_peer(b)).start()
    xqr[a] = xq[a]
    for b in a_others:
        remote(GRAD, xg.at[b], xgr.at[a], a_peer(b)).start()
    xgr[a] = xg[a]

    for t in range(4, 8):
        own_scores(t)

    arrived(ZK, kb.at[0, pl.ds(0, 3)])
    for b in y_others:
        along_y(0, kb, y, b).start()
    arrived(ZV, vb.at[0, pl.ds(0, 3)])
    for b in y_others:
        along_y(1, vb, y, b).start()
    arrived(ZSUM, gsumr.at[pl.ds(0, 3)])
    total = gsum[...]
    for b in z_others:
        total = total + gsumr[b]
    weight = (reward - total[1:2] / 32.0) * (SLOTS * 32) / total[0:1]
    weight = jnp.where(pos2 < ROWS, weight, 0.0)
    for t in range(8):
        st[t, 3:4, :] = weight
    for b in a_others:
        remote(OWN, st.at[lax.div(b, 2)], str_.at[a], a_peer(b)).start()
    str_[a] = st[lax.div(a, 2)]

    def key_block(b):
        block = kb[b].reshape(128, DIM)
        for n in range(4):
            cols = slice(n * 256, (n + 1) * 256)
            s = dot_nt(block, xqr[4 * n : 4 * n + 4].reshape(256, DIM)) * SCALE2
            m = jnp.max(s, axis=0, keepdims=True)
            e = jnp.exp2(s - m)
            exps[b, :, cols] = e
            part[b, 0:1, cols] = m
            part[b, 1:2, cols] = jnp.sum(e, axis=0, keepdims=True)

    def value_block(b):
        block = vb[b].reshape(128, DIM)
        for n in range(4):
            cols = slice(n * 256, (n + 1) * 256)
            d = dot_nt(block, xgr[4 * n : 4 * n + 4].reshape(256, DIM)) * SCALE
            prods[b, :, cols] = d
            part[b, 2:3, cols] = jnp.sum(exps[b, :, cols] * d, axis=0, keepdims=True)

    near_first = y_others[1:] + y_others[:1]
    arrived(QUERY, xqr.at[pl.ds(0, 15)])
    key_block(y)
    for b in near_first:
        along_y(0, kb, b, b).wait_recv()
        key_block(b)
    arrived(OWN, str_.at[pl.ds(0, 15)])
    stats = jnp.concatenate([side_by_side(str_, t) for t in range(8)], axis=1)
    m = stats[0:1]
    for b in range(4):
        m = jnp.maximum(m, part[b, 0:1, :])
    fo = jnp.exp2(stats[0:1] - m)
    total = stats[1:2] * fo
    for b in range(4):
        f = jnp.exp2(part[b, 0:1, :] - m)
        total = total + part[b, 1:2, :] * f
        part[b, 3:4, :] = f
    inv = 1.0 / total
    weights = stats[3:4]

    def probabilities(b):
        coef = part[b, 3:4, :] * inv
        for n in range(4):
            cols = slice(n * 256, (n + 1) * 256)
            p = exps[b, :, cols] * coef[:, cols]
            exps[b, :, cols] = p
            pw[b, :, cols] = (p * weights[:, cols]).astype(BF16)

    for b in y_others + [y]:
        probabilities(b)
    arrived(GRAD, xgr.at[pl.ds(0, 15)])
    q_all = xqr[...].reshape(16 * SLOTS, DIM)
    g_all = xgr[...].reshape(16 * SLOTS, DIM)
    for b in y_others:
        sbv[b] = dot_nn(pw[b], g_all).astype(BF16)
        remote(YSUM_V, sbv.at[b], rv.at[y], y_peer(b)).start()
    value_block(y)
    for b in near_first:
        along_y(1, vb, b, b).wait_recv()
        value_block(b)
    inner = stats[2:3] * (fo * inv * SCALE)
    for b in range(4):
        inner = inner + part[b, 2:3, :]

    def finish(b):
        for n in range(4):
            cols = slice(n * 256, (n + 1) * 256)
            dscore = exps[b, :, cols] * (prods[b, :, cols] - inner[:, cols])
            ds[b, :, cols] = (dscore * weights[:, cols]).astype(BF16)

    for b in y_others:
        finish(b)
        sbk[b] = dot_nn(ds[b], q_all).astype(BF16)
        remote(YSUM_K, sbk.at[b], rk.at[y], y_peer(b)).start()
    finish(y)
    final = jnp.concatenate(
        [m, inv, inner * (1.0 / SCALE), jnp.zeros((5, 16 * SLOTS), F32)], axis=0
    )
    for t in range(8):
        fs[t] = final[:, t * DIM : (t + 1) * DIM]
    keys = kb[...].reshape(PROMPT, DIM)
    grad_v = dot_nn(pw[y], g_all)
    grad_k = dot_nn(ds[y], q_all)
    for b in a_others:
        remote(FIN, fs.at[lax.div(b, 2)], fr.at[a], a_peer(b)).start()
    fr[a] = fs[lax.div(a, 2)]
    for t in range(8):
        grad_q = dot_tn(ds[:, :, t * 128 : (t + 1) * 128].reshape(PROMPT, 2 * SLOTS), keys)
        dqs[2 * t] = grad_q[:SLOTS].astype(BF16)
        dqs[2 * t + 1] = grad_q[SLOTS:].astype(BF16)
    for b in a_others:
        remote(DQ, dqs.at[b], dqr.at[a], a_peer(b)).start()
    own_part = pltpu.make_async_copy(dqs.at[a], dqr.at[a], out_sem.at[4])
    own_part.start()

    def next_sum(total, kind_y, received, held, send, kind_z, target):
        arrived(kind_y, received.at[pl.ds(0, 3)])
        for b in y_others:
            total = total + received[b].astype(F32)
        held[...] = total.reshape(4, 32, DIM)
        send[...] = total.astype(BF16).reshape(4, 32, DIM)
        for b in z_others:
            remote(kind_z, send.at[b], target.at[z_hi], z_peer(b)).start()

    next_sum(grad_v, YSUM_V, rv, hv, szv, ZSUM_V, rzv)
    next_sum(grad_k, YSUM_K, rk, hk, szk, ZSUM_K, rzk)

    arrived(FIN, fr.at[pl.ds(0, 15)])
    for t in range(8):
        cols = slice(t * 256, (t + 1) * 256)
        fin = side_by_side(fr, t)
        m, inv, inner = fin[0:1], fin[1:2], fin[2:3]
        coef = jnp.exp2(st[t, 0:1, :] - m) * inv * weight
        e = own_e[t]
        p = (e * coef).astype(BF16)
        dsc = (e * (own_d[t] - inner) * (coef * SCALE)).astype(BF16)
        dvo[:, cols] = dot_nn(p, both(xg, t)).astype(BF16)
        dko[:, cols] = dot_nn(dsc, both(xq, t)).astype(BF16)
        grad_q = dot_tn(dsc, ck[:, cols])
        dqo[2 * t] = grad_q[:SLOTS, :DIM].astype(BF16)
        dqo[2 * t + 1] = grad_q[SLOTS:, DIM:].astype(BF16)
    stores = [
        pltpu.make_async_copy(src, dst, out_sem.at[n])
        for n, (src, dst) in enumerate(
            ((dqo, own_hbm), (dko, dk_hbm), (dvo, dv_hbm), (t3.at[a], gp_hbm.at[a]))
        )
    ]
    for store in stores[:3]:
        store.start()

    arrived(ZSUM_V, rzv.at[pl.ds(0, 3)])
    arrived(ZSUM_K, rzk.at[pl.ds(0, 3)])
    line = lax.broadcasted_iota(jnp.int32, (16, 8, DIM), 1)
    lines = jnp.zeros((16, 8, DIM), F32)
    for kv, (held, received) in enumerate(((hk, rzk), (hv, rzv))):
        part = held[z_hi]
        for b in z_others:
            part = part + received[b].astype(F32)
        for r in range(2):
            lines = jnp.where(line == kv * 2 + r, part[r * 16 : (r + 1) * 16][:, None, :], lines)
    t3[...] = lines
    for b in a_others:
        remote(OUT, t3.at[b], gp_hbm.at[a], a_peer(b)).start()
    stores[3].start()
    arrived(DQ, dqr.at[pl.ds(0, 15)])
    arrived(OUT, gp_hbm.at[pl.ds(0, 15)])

    sent(KV, kvs.at[pl.ds(0, 15)])
    sent(QUERY, xq.at[pl.ds(0, 15)])
    sent(GRAD, xg.at[pl.ds(0, 15)])
    sent(ZK, kb.at[0, pl.ds(0, 3)])
    sent(ZV, vb.at[0, pl.ds(0, 3)])
    sent(ZSUM, gsumr.at[pl.ds(0, 3)])
    sent(YK, kb.at[pl.ds(0, 3)])
    sent(YV, vb.at[pl.ds(0, 3)])
    sent(OWN, str_.at[pl.ds(0, 15)])
    sent(FIN, fr.at[pl.ds(0, 15)])
    sent(DQ, dqs.at[pl.ds(0, 15)])
    sent(YSUM_V, sbv.at[pl.ds(0, 3)])
    sent(YSUM_K, sbk.at[pl.ds(0, 3)])
    sent(ZSUM_V, szv.at[pl.ds(0, 3)])
    sent(ZSUM_K, szk.at[pl.ds(0, 3)])
    sent(OUT, t3.at[pl.ds(0, 15)])
    for store in stores + [own_part]:
        store.wait()


def store_all(own, other, dk, dv, gp, dq_out, dk_out, dv_out, gk_out, gv_out, *scratch):
    (
        own_held, other_held, dk_held, dv_held, gp_held, dq_held, gk_held, gv_held,
        in_sem, out_sem,
    ) = scratch
    pairs = [(own, own_held), (other, other_held), (gp, gp_held)]
    stores = []
    for source, held, target in ((dk, dk_held, dk_out), (dv, dv_held, dv_out)):
        for first in range(0, ROWS, SLOTS):
            span = pl.ds(first, SLOTS)
            pairs.append((source.at[span], held.at[span]))
            stores.append((held.at[span], target.at[span]))
    stores += [(dq_held, dq_out), (gk_held, gk_out), (gv_held, gv_out)]
    loads = [pltpu.make_async_copy(*pair, in_sem.at[n]) for n, pair in enumerate(pairs)]
    stores = [pltpu.make_async_copy(*pair, out_sem.at[n]) for n, pair in enumerate(stores)]
    for load in loads:
        load.start()
    loads[0].wait()
    loads[1].wait()
    for h in range(HEADS):
        cols = slice(h * DIM, (h + 1) * DIM)
        total = own_held[h].astype(F32) + other_held[h].astype(F32)
        dq_held[:, cols] = total.astype(BF16)
    stores[4].start()
    for n in range(4):
        loads[3 + n].wait()
        stores[n].start()
    loads[2].wait()
    for h in range(HEADS):
        cols = slice(h * DIM, (h + 1) * DIM)
        gk_held[:, cols] = gp_held[h, 0:2, :].astype(BF16)
        gv_held[:, cols] = gp_held[h, 2:4, :].astype(BF16)
    stores[5].start()
    stores[6].start()
    for store in stores:
        store.wait()


def shards(prompt_k, prompt_v, comp_q, comp_k, comp_v, grad_out, rewards, mask_pos):
    hbm = pl.BlockSpec(memory_space=pltpu.HBM)
    V = pltpu.VMEM
    grads = pl.pallas_call(
        kernel,
        out_shape=(
            jax.ShapeDtypeStruct((HEADS, SLOTS, DIM), BF16),
            jax.ShapeDtypeStruct((HEADS, SLOTS, DIM), BF16),
            jax.ShapeDtypeStruct((ROWS, WIDTH), BF16),
            jax.ShapeDtypeStruct((ROWS, WIDTH), BF16),
            jax.ShapeDtypeStruct((16, 8, DIM), F32),
        ),
        in_specs=[hbm] * 8,
        out_specs=(hbm,) * 5,
        scratch_shapes=[
            V((2, WIDTH), BF16),
            V((2, WIDTH), BF16),
            V((1, 1), F32),
            V((1, SLOTS), jnp.int32),
            V((ROWS, WIDTH), BF16),
            V((ROWS, WIDTH), BF16),
            V((ROWS, WIDTH), BF16),
            V((SLOTS, WIDTH), BF16),
            V((16, SLOTS, DIM), BF16),
            V((16, SLOTS, DIM), BF16),
            V((16, SLOTS, DIM), BF16),
            V((16, SLOTS, DIM), BF16),
            V((16, 8, DIM), F32),
            V((16, 8, DIM), F32),
            V((4, 4, 32, DIM), BF16),
            V((4, 4, 32, DIM), BF16),
            V((8, DIM), F32),
            V((4, 8, DIM), F32),
            V((8, 128, DIM), F32),
            V((8, 128, DIM), F32),
            V((8, 8, DIM), F32),
            V((16, 8, DIM), F32),
            V((8, 8, DIM), F32),
            V((16, 8, DIM), F32),
            V((4, 128, 16 * SLOTS), F32),
            V((4, 128, 16 * SLOTS), F32),
            V((4, 8, 16 * SLOTS), F32),
            V((4, 128, 16 * SLOTS), BF16),
            V((4, 128, 16 * SLOTS), BF16),
            V((4, 128, DIM), BF16),
            V((4, 128, DIM), BF16),
            V((4, 128, DIM), BF16),
            V((4, 128, DIM), BF16),
            V((4, 32, DIM), F32),
            V((4, 32, DIM), F32),
            V((4, 32, DIM), BF16),
            V((4, 32, DIM), BF16),
            V((4, 32, DIM), BF16),
            V((4, 32, DIM), BF16),
            V((16, 8, DIM), F32),
            V((16, SLOTS, DIM), BF16),
            V((16, SLOTS, DIM), BF16),
            V((ROWS, WIDTH), BF16),
            V((ROWS, WIDTH), BF16),
            pltpu.SemaphoreType.DMA((8,)),
            pltpu.SemaphoreType.DMA((5,)),
            pltpu.SemaphoreType.DMA((KINDS,)),
            pltpu.SemaphoreType.DMA((KINDS,)),
            pltpu.SemaphoreType.DMA((2, 4)),
        ],
        compiler_params=pltpu.CompilerParams(
            collective_id=0, has_side_effects=True, vmem_limit_bytes=60 * 1024 * 1024
        ),
    )(
        prompt_k, prompt_v, rewards, mask_pos[0], comp_q[0, 0], comp_k[0, 0], comp_v[0, 0],
        grad_out[0, 0],
    )
    shapes = [(SLOTS, WIDTH), (ROWS, WIDTH), (ROWS, WIDTH), (2, WIDTH), (2, WIDTH)]
    dq, dk, dv, gk, gv = pl.pallas_call(
        store_all,
        out_shape=[jax.ShapeDtypeStruct(shape, BF16) for shape in shapes],
        in_specs=[hbm] * 5,
        out_specs=[hbm] * 5,
        scratch_shapes=[V(grad.shape, grad.dtype) for grad in grads]
        + [
            V((SLOTS, WIDTH), BF16),
            V((2, WIDTH), BF16),
            V((2, WIDTH), BF16),
            pltpu.SemaphoreType.DMA((7,)),
            pltpu.SemaphoreType.DMA((7,)),
        ],
        compiler_params=pltpu.CompilerParams(vmem_limit_bytes=60 * 1024 * 1024),
    )(*grads)
    return dq[None, None], dk[None, None], dv[None, None], gk, gv


def solution(mesh):
    wide = P("grp", "ctx", None, None)
    rows = P(("grp", "ctx"), None)
    return jax.shard_map(
        shards,
        mesh=mesh,
        in_specs=(rows, rows, wide, wide, wide, wide, P("grp", "ctx"), P("grp", "ctx", None)),
        out_specs=(wide, wide, wide, rows, rows),
        check_vma=False,
    )
```

```python
import jax
import jax.numpy as jnp
from jax import lax
from jax.experimental import pallas as pl
from jax.experimental.pallas import tpu as pltpu
from jax.sharding import PartitionSpec as P

HEADS = 16
DIM = 128
SLOTS = 64
ROWS = 128
WIDTH = 2048
PROMPT = 512
F32 = jnp.float32
BF16 = jnp.bfloat16
SCALE = DIM ** -0.5
SCALE2 = SCALE * 1.4426950408889634
MESH = pl.DeviceIdType.MESH

(
    KV, QUERY, GRAD, ZK, ZV, ZSUM, YK, YV, OWN, FIN, DQ, YSUM_K, YSUM_V, ZSUM_K, ZSUM_V, OUT, KINDS
) = range(17)


def dot_nt(a, b):
    return lax.dot_general(a, b, (((1,), (1,)), ((), ())), preferred_element_type=F32)


def dot_nn(a, b):
    return lax.dot_general(a, b, (((1,), (0,)), ((), ())), preferred_element_type=F32)


def dot_tn(a, b):
    return lax.dot_general(a, b, (((0,), (0,)), ((), ())), preferred_element_type=F32)


def kernel(
    pk_hbm, pv_hbm, rw_hbm, mp_hbm, cq_hbm, ck_hbm, cv_hbm, go_hbm,
    own_hbm, dqr, dk_hbm, dv_hbm, gp_hbm,
    pk, pv, rw, mp, cq, ck, cv, go, xq, xqr, xg, xgr, kvs, kvr, kb, vb, gsum, gsumr, own_e, own_d, st, str_,
    fs, fr, exps, prods, part, pw, ds,
    sbk, sbv, rk, rv, hk, hv, szk, szv, rzk, rzv, t3, dqs, dqo, dko, dvo,
    in_sem, out_sem, ss, rs, ry,
):
    grp = lax.axis_index("grp")
    ctx = lax.axis_index("ctx")
    x_lo, y = lax.div(grp, 4), lax.rem(grp, 4)
    z = lax.div(ctx, 4)
    z_hi, z_lo, low = lax.div(z, 2), lax.rem(z, 2), lax.rem(ctx, 4)
    a = z_lo * 8 + x_lo * 4 + low

    def a_peer(b):
        return {
            "grp": lax.rem(lax.div(b, 4), 2) * 4 + y,
            "ctx": (z_hi * 2 + lax.div(b, 8)) * 4 + lax.rem(b, 4),
        }

    def z_peer(b):
        return {"grp": grp, "ctx": (b * 2 + z_lo) * 4 + low}

    def y_peer(b):
        return {"grp": x_lo * 4 + b, "ctx": ctx}

    flips = [(dz, 0, 1, dc) for dz in (1, 0) for dc in (1, 0)]
    flips += [(dz, 1, dx, dc) for dz in (1, 0) for dx in (1, 0) for dc in (1, 0)]
    flips += [(1, 0, 0, 1), (1, 0, 0, 0), (0, 0, 0, 1)]

    def flipped(bit, flip):
        return 1 - bit if flip else bit

    x_hi, core = lax.div(low, 2), lax.rem(low, 2)
    a_others = [
        flipped(z_lo, dz) * 8 + flipped(x_lo, dl) * 4 + flipped(x_hi, dh) * 2 + flipped(core, dc)
        for dz, dl, dh, dc in flips
    ]
    z_others = [lax.rem(z_hi + k, 4) for k in (2, 1, 3)]
    y_others = [lax.rem(y + k, 4) for k in (2, 1, 3)]

    def remote(kind, src, dst, device):
        return pltpu.make_async_remote_copy(
            src_ref=src, dst_ref=dst, send_sem=ss.at[kind], recv_sem=rs.at[kind],
            device_id=device, device_id_type=MESH,
        )

    def along_y(kv, ref, row, b):
        return pltpu.make_async_remote_copy(
            src_ref=ref.at[row], dst_ref=ref.at[row], send_sem=ss.at[YK + kv],
            recv_sem=ry.at[kv, row], device_id=y_peer(b), device_id_type=MESH,
        )

    def arrived(kind, dst):
        remote(kind, dst, dst, y_peer(y_others[0])).wait_recv()

    def sent(kind, src):
        remote(kind, src, src, y_peer(y_others[0])).wait_send()

    loads = [
        pltpu.make_async_copy(src, dst, in_sem.at[n])
        for n, (src, dst) in enumerate(
            (
                (pk_hbm, pk), (pv_hbm, pv), (rw_hbm, rw), (mp_hbm, mp),
                (cq_hbm, cq), (go_hbm, go), (ck_hbm, ck), (cv_hbm, cv),
            )
        )
    ]
    for load in loads[:4]:
        load.start()

    barrier = pltpu.get_barrier_semaphore()
    for b in z_others:
        pl.semaphore_signal(barrier, inc=1, device_id=z_peer(b), device_id_type=MESH)
    for b in y_others:
        pl.semaphore_signal(barrier, inc=1, device_id=y_peer(b), device_id_type=MESH)
    for b in a_others:
        pl.semaphore_signal(barrier, inc=1, device_id=a_peer(b), device_id_type=MESH)
    for load in loads[4:]:
        load.start()

    for load in loads[:4]:
        load.wait()
    pos = mp[...]
    pos2 = jnp.concatenate([pos, pos], axis=1)
    live = pos < ROWS
    count = jnp.sum(jnp.where(live, 1.0, 0.0), axis=1, keepdims=True)
    reward = rw[...]
    lines = jnp.concatenate(
        [
            pk[...].astype(F32),
            pv[...].astype(F32),
            jnp.broadcast_to(count, (1, WIDTH)),
            jnp.broadcast_to(reward, (1, WIDTH)),
            jnp.zeros((2, WIDTH), F32),
        ],
        axis=0,
    )
    for h in range(HEADS):
        kvs[h] = lines[:, h * DIM : (h + 1) * DIM]

    pl.semaphore_wait(barrier, 21)

    for b in a_others:
        remote(KV, kvs.at[b], kvr.at[a], a_peer(b)).start()
    kvr[a] = kvs[a]

    row = lax.broadcasted_iota(jnp.int32, (ROWS, 2 * SLOTS), 0)
    pick = jnp.where(row == jnp.minimum(pos2, ROWS - 1), 1.0, 0.0).astype(BF16)
    loads[4].wait()
    picked = dot_tn(pick, cq[...])[:SLOTS].astype(BF16)
    for h in range(HEADS):
        xq[h] = picked[:, h * DIM : (h + 1) * DIM]
    loads[5].wait()
    for h in range(HEADS):
        xg[h] = go[:, h * DIM : (h + 1) * DIM]

    nothing = jnp.zeros((SLOTS, DIM), BF16)

    def both(ref, t):
        return jnp.concatenate(
            [
                jnp.concatenate([ref[2 * t], nothing], axis=1),
                jnp.concatenate([nothing, ref[2 * t + 1]], axis=1),
            ],
            axis=0,
        )

    def own_scores(t):
        cols = slice(t * 256, (t + 1) * 256)
        s = dot_nt(ck[:, cols], both(xq, t)) * SCALE2
        d = dot_nt(cv[:, cols], both(xg, t))
        m = jnp.max(s, axis=0, keepdims=True)
        e = jnp.exp2(s - m)
        own_e[t] = e
        own_d[t] = d
        st[t] = jnp.concatenate(
            [
                m,
                jnp.sum(e, axis=0, keepdims=True),
                jnp.sum(e * d, axis=0, keepdims=True),
                jnp.zeros((5, DIM), F32),
            ],
            axis=0,
        )

    left = lax.broadcasted_iota(jnp.int32, (8, DIM), 1) < SLOTS
    odd = jnp.broadcast_to(lax.rem(a, 2), (8, DIM)) == 1

    def side_by_side(ref, t):
        one, two = ref[2 * t], ref[2 * t + 1]
        moved = pltpu.roll(jnp.where(odd, one, two), SLOTS, 1)
        return jnp.where(left != odd, jnp.where(left, one, two), moved)

    loads[6].wait()
    loads[7].wait()
    for t in range(4):
        own_scores(t)

    arrived(KV, kvr.at[pl.ds(0, 15)])
    blocks = kvr[...]
    kb[y, z_hi, 0:16, :] = blocks[:, 0, :].astype(BF16)
    kb[y, z_hi, 16:32, :] = blocks[:, 1, :].astype(BF16)
    for b in z_others:
        remote(ZK, kb.at[y, z_hi], kb.at[y, z_hi], z_peer(b)).start()
    vb[y, z_hi, 0:16, :] = blocks[:, 2, :].astype(BF16)
    vb[y, z_hi, 16:32, :] = blocks[:, 3, :].astype(BF16)
    for b in z_others:
        remote(ZV, vb.at[y, z_hi], vb.at[y, z_hi], z_peer(b)).start()
    mine = lax.broadcasted_iota(jnp.int32, (16, DIM), 0) // 4 % 2 == x_lo
    count16 = jnp.sum(jnp.where(mine, blocks[:, 4, :], 0.0), axis=0, keepdims=True)
    reward16 = jnp.sum(jnp.where(mine, blocks[:, 5, :], 0.0), axis=0, keepdims=True)
    gsum[...] = jnp.concatenate([count16, reward16, jnp.zeros((6, DIM), F32)], axis=0)
    for b in z_others:
        remote(ZSUM, gsum, gsumr.at[z_hi], z_peer(b)).start()
    for b in a_others:
        remote(QUERY, xq.at[b], xqr.at[a], a_peer(b)).start()
    xqr[a] = xq[a]
    for b in a_others:
        remote(GRAD, xg.at[b], xgr.at[a], a_peer(b)).start()
    xgr[a] = xg[a]

    for t in range(4, 8):
        own_scores(t)

    arrived(ZK, kb.at[0, pl.ds(0, 3)])
    for b in y_others:
        along_y(0, kb, y, b).start()
    arrived(ZV, vb.at[0, pl.ds(0, 3)])
    for b in y_others:
        along_y(1, vb, y, b).start()
    arrived(ZSUM, gsumr.at[pl.ds(0, 3)])
    total = gsum[...]
    for b in z_others:
        total = total + gsumr[b]
    weight = (reward - total[1:2] / 32.0) * (SLOTS * 32) / total[0:1]
    weight = jnp.where(pos2 < ROWS, weight, 0.0)
    for t in range(8):
        st[t, 3:4, :] = weight
    for b in a_others:
        remote(OWN, st.at[lax.div(b, 2)], str_.at[a], a_peer(b)).start()
    str_[a] = st[lax.div(a, 2)]

    def key_block(b):
        block = kb[b].reshape(128, DIM)
        for n in range(4):
            cols = slice(n * 256, (n + 1) * 256)
            s = dot_nt(block, xqr[4 * n : 4 * n + 4].reshape(256, DIM)) * SCALE2
            m = jnp.max(s, axis=0, keepdims=True)
            e = jnp.exp2(s - m)
            exps[b, :, cols] = e
            part[b, 0:1, cols] = m
            part[b, 1:2, cols] = jnp.sum(e, axis=0, keepdims=True)

    def value_blocks(b):
        block = vb[b : b + 2].reshape(256, DIM)
        for n in range(4):
            cols = slice(n * 256, (n + 1) * 256)
            d = dot_nt(block, xgr[4 * n : 4 * n + 4].reshape(256, DIM)) * SCALE
            prods[b : b + 2, :, cols] = d.reshape(2, 128, 256)
            p = exps[b : b + 2, :, cols].reshape(256, 256)
            part[b, 2:3, cols] = jnp.sum(p * d, axis=0, keepdims=True)

    near_first = y_others[1:] + y_others[:1]
    arrived(QUERY, xqr.at[pl.ds(0, 15)])
    key_block(y)
    for b in near_first:
        along_y(0, kb, b, b).wait_recv()
        key_block(b)
    arrived(OWN, str_.at[pl.ds(0, 15)])
    stats = jnp.concatenate([side_by_side(str_, t) for t in range(8)], axis=1)
    m = stats[0:1]
    for b in range(4):
        m = jnp.maximum(m, part[b, 0:1, :])
    fo = jnp.exp2(stats[0:1] - m)
    total = stats[1:2] * fo
    for b in range(4):
        f = jnp.exp2(part[b, 0:1, :] - m)
        total = total + part[b, 1:2, :] * f
        part[b, 3:4, :] = f
    inv = 1.0 / total
    weights = stats[3:4]

    def probabilities(b):
        coef = part[b, 3:4, :] * inv
        for n in range(4):
            cols = slice(n * 256, (n + 1) * 256)
            p = exps[b, :, cols] * coef[:, cols]
            exps[b, :, cols] = p
            pw[b, :, cols] = (p * weights[:, cols]).astype(BF16)

    for b in y_others + [y]:
        probabilities(b)
    arrived(GRAD, xgr.at[pl.ds(0, 15)])
    q_all = xqr[...].reshape(16 * SLOTS, DIM)
    g_all = xgr[...].reshape(16 * SLOTS, DIM)
    for b in y_others:
        sbv[b] = dot_nn(pw[b], g_all).astype(BF16)
        remote(YSUM_V, sbv.at[b], rv.at[y], y_peer(b)).start()
    for b in near_first:
        along_y(1, vb, b, b).wait_recv()
    value_blocks(0)
    value_blocks(2)
    inner = stats[2:3] * (fo * inv * SCALE)
    for b in (0, 2):
        inner = inner + part[b, 2:3, :]

    def finish(b):
        for n in range(4):
            cols = slice(n * 256, (n + 1) * 256)
            dscore = exps[b, :, cols] * (prods[b, :, cols] - inner[:, cols])
            ds[b, :, cols] = (dscore * weights[:, cols]).astype(BF16)

    for b in y_others:
        finish(b)
        sbk[b] = dot_nn(ds[b], q_all).astype(BF16)
        remote(YSUM_K, sbk.at[b], rk.at[y], y_peer(b)).start()
    finish(y)
    final = jnp.concatenate(
        [m, inv, inner * (1.0 / SCALE), jnp.zeros((5, 16 * SLOTS), F32)], axis=0
    )
    for t in range(8):
        fs[t] = final[:, t * DIM : (t + 1) * DIM]
    keys = kb[...].reshape(PROMPT, DIM)
    grad_v = dot_nn(pw[y], g_all)
    grad_k = dot_nn(ds[y], q_all)
    for b in a_others:
        remote(FIN, fs.at[lax.div(b, 2)], fr.at[a], a_peer(b)).start()
    fr[a] = fs[lax.div(a, 2)]
    for t in range(8):
        grad_q = dot_tn(ds[:, :, t * 128 : (t + 1) * 128].reshape(PROMPT, 2 * SLOTS), keys)
        dqs[2 * t] = grad_q[:SLOTS].astype(BF16)
        dqs[2 * t + 1] = grad_q[SLOTS:].astype(BF16)
    for b in a_others:
        remote(DQ, dqs.at[b], dqr.at[a], a_peer(b)).start()
    own_part = pltpu.make_async_copy(dqs.at[a], dqr.at[a], out_sem.at[4])
    own_part.start()

    def next_sum(total, kind_y, received, held, send, kind_z, target):
        arrived(kind_y, received.at[pl.ds(0, 3)])
        for b in y_others:
            total = total + received[b].astype(F32)
        held[...] = total.reshape(4, 32, DIM)
        send[...] = total.astype(BF16).reshape(4, 32, DIM)
        for b in z_others:
            remote(kind_z, send.at[b], target.at[z_hi], z_peer(b)).start()

    next_sum(grad_v, YSUM_V, rv, hv, szv, ZSUM_V, rzv)
    next_sum(grad_k, YSUM_K, rk, hk, szk, ZSUM_K, rzk)

    arrived(FIN, fr.at[pl.ds(0, 15)])
    for t in range(8):
        cols = slice(t * 256, (t + 1) * 256)
        fin = side_by_side(fr, t)
        m, inv, inner = fin[0:1], fin[1:2], fin[2:3]
        coef = jnp.exp2(st[t, 0:1, :] - m) * inv * weight
        e = own_e[t]
        p = (e * coef).astype(BF16)
        dsc = (e * (own_d[t] - inner) * (coef * SCALE)).astype(BF16)
        dvo[:, cols] = dot_nn(p, both(xg, t)).astype(BF16)
        dko[:, cols] = dot_nn(dsc, both(xq, t)).astype(BF16)
        grad_q = dot_tn(dsc, ck[:, cols])
        dqo[2 * t] = grad_q[:SLOTS, :DIM].astype(BF16)
        dqo[2 * t + 1] = grad_q[SLOTS:, DIM:].astype(BF16)
    stores = [
        pltpu.make_async_copy(src, dst, out_sem.at[n])
        for n, (src, dst) in enumerate(
            ((dqo, own_hbm), (dko, dk_hbm), (dvo, dv_hbm), (t3.at[a], gp_hbm.at[a]))
        )
    ]
    for store in stores[:3]:
        store.start()

    arrived(ZSUM_V, rzv.at[pl.ds(0, 3)])
    arrived(ZSUM_K, rzk.at[pl.ds(0, 3)])
    line = lax.broadcasted_iota(jnp.int32, (16, 8, DIM), 1)
    lines = jnp.zeros((16, 8, DIM), F32)
    for kv, (held, received) in enumerate(((hk, rzk), (hv, rzv))):
        part = held[z_hi]
        for b in z_others:
            part = part + received[b].astype(F32)
        for r in range(2):
            lines = jnp.where(line == kv * 2 + r, part[r * 16 : (r + 1) * 16][:, None, :], lines)
    t3[...] = lines
    for b in a_others:
        remote(OUT, t3.at[b], gp_hbm.at[a], a_peer(b)).start()
    stores[3].start()
    arrived(DQ, dqr.at[pl.ds(0, 15)])
    arrived(OUT, gp_hbm.at[pl.ds(0, 15)])

    sent(KV, kvs.at[pl.ds(0, 15)])
    sent(QUERY, xq.at[pl.ds(0, 15)])
    sent(GRAD, xg.at[pl.ds(0, 15)])
    sent(ZK, kb.at[0, pl.ds(0, 3)])
    sent(ZV, vb.at[0, pl.ds(0, 3)])
    sent(ZSUM, gsumr.at[pl.ds(0, 3)])
    sent(YK, kb.at[pl.ds(0, 3)])
    sent(YV, vb.at[pl.ds(0, 3)])
    sent(OWN, str_.at[pl.ds(0, 15)])
    sent(FIN, fr.at[pl.ds(0, 15)])
    sent(DQ, dqs.at[pl.ds(0, 15)])
    sent(YSUM_V, sbv.at[pl.ds(0, 3)])
    sent(YSUM_K, sbk.at[pl.ds(0, 3)])
    sent(ZSUM_V, szv.at[pl.ds(0, 3)])
    sent(ZSUM_K, szk.at[pl.ds(0, 3)])
    sent(OUT, t3.at[pl.ds(0, 15)])
    for store in stores + [own_part]:
        store.wait()


def store_all(own, other, dk, dv, gp, dq_out, dk_out, dv_out, gk_out, gv_out, *scratch):
    (
        own_held, other_held, dk_held, dv_held, gp_held, dq_held, gk_held, gv_held,
        in_sem, out_sem,
    ) = scratch
    pairs = [(own, own_held), (other, other_held), (gp, gp_held)]
    stores = []
    for source, held, target in ((dk, dk_held, dk_out), (dv, dv_held, dv_out)):
        for first in range(0, ROWS, SLOTS):
            span = pl.ds(first, SLOTS)
            pairs.append((source.at[span], held.at[span]))
            stores.append((held.at[span], target.at[span]))
    stores += [(dq_held, dq_out), (gk_held, gk_out), (gv_held, gv_out)]
    loads = [pltpu.make_async_copy(*pair, in_sem.at[n]) for n, pair in enumerate(pairs)]
    stores = [pltpu.make_async_copy(*pair, out_sem.at[n]) for n, pair in enumerate(stores)]
    for load in loads:
        load.start()
    loads[0].wait()
    loads[1].wait()
    for h in range(HEADS):
        cols = slice(h * DIM, (h + 1) * DIM)
        total = own_held[h].astype(F32) + other_held[h].astype(F32)
        dq_held[:, cols] = total.astype(BF16)
    stores[4].start()
    for n in range(4):
        loads[3 + n].wait()
        stores[n].start()
    loads[2].wait()
    for h in range(HEADS):
        cols = slice(h * DIM, (h + 1) * DIM)
        gk_held[:, cols] = gp_held[h, 0:2, :].astype(BF16)
        gv_held[:, cols] = gp_held[h, 2:4, :].astype(BF16)
    stores[5].start()
    stores[6].start()
    for store in stores:
        store.wait()


def shards(prompt_k, prompt_v, comp_q, comp_k, comp_v, grad_out, rewards, mask_pos):
    hbm = pl.BlockSpec(memory_space=pltpu.HBM)
    V = pltpu.VMEM
    grads = pl.pallas_call(
        kernel,
        out_shape=(
            jax.ShapeDtypeStruct((HEADS, SLOTS, DIM), BF16),
            jax.ShapeDtypeStruct((HEADS, SLOTS, DIM), BF16),
            jax.ShapeDtypeStruct((ROWS, WIDTH), BF16),
            jax.ShapeDtypeStruct((ROWS, WIDTH), BF16),
            jax.ShapeDtypeStruct((16, 8, DIM), F32),
        ),
        in_specs=[hbm] * 8,
        out_specs=(hbm,) * 5,
        scratch_shapes=[
            V((2, WIDTH), BF16),
            V((2, WIDTH), BF16),
            V((1, 1), F32),
            V((1, SLOTS), jnp.int32),
            V((ROWS, WIDTH), BF16),
            V((ROWS, WIDTH), BF16),
            V((ROWS, WIDTH), BF16),
            V((SLOTS, WIDTH), BF16),
            V((16, SLOTS, DIM), BF16),
            V((16, SLOTS, DIM), BF16),
            V((16, SLOTS, DIM), BF16),
            V((16, SLOTS, DIM), BF16),
            V((16, 8, DIM), F32),
            V((16, 8, DIM), F32),
            V((4, 4, 32, DIM), BF16),
            V((4, 4, 32, DIM), BF16),
            V((8, DIM), F32),
            V((4, 8, DIM), F32),
            V((8, 128, DIM), F32),
            V((8, 128, DIM), F32),
            V((8, 8, DIM), F32),
            V((16, 8, DIM), F32),
            V((8, 8, DIM), F32),
            V((16, 8, DIM), F32),
            V((4, 128, 16 * SLOTS), F32),
            V((4, 128, 16 * SLOTS), F32),
            V((4, 8, 16 * SLOTS), F32),
            V((4, 128, 16 * SLOTS), BF16),
            V((4, 128, 16 * SLOTS), BF16),
            V((4, 128, DIM), BF16),
            V((4, 128, DIM), BF16),
            V((4, 128, DIM), BF16),
            V((4, 128, DIM), BF16),
            V((4, 32, DIM), F32),
            V((4, 32, DIM), F32),
            V((4, 32, DIM), BF16),
            V((4, 32, DIM), BF16),
            V((4, 32, DIM), BF16),
            V((4, 32, DIM), BF16),
            V((16, 8, DIM), F32),
            V((16, SLOTS, DIM), BF16),
            V((16, SLOTS, DIM), BF16),
            V((ROWS, WIDTH), BF16),
            V((ROWS, WIDTH), BF16),
            pltpu.SemaphoreType.DMA((8,)),
            pltpu.SemaphoreType.DMA((5,)),
            pltpu.SemaphoreType.DMA((KINDS,)),
            pltpu.SemaphoreType.DMA((KINDS,)),
            pltpu.SemaphoreType.DMA((2, 4)),
        ],
        compiler_params=pltpu.CompilerParams(
            collective_id=0, has_side_effects=True, vmem_limit_bytes=60 * 1024 * 1024
        ),
    )(
        prompt_k, prompt_v, rewards, mask_pos[0], comp_q[0, 0], comp_k[0, 0], comp_v[0, 0],
        grad_out[0, 0],
    )
    shapes = [(SLOTS, WIDTH), (ROWS, WIDTH), (ROWS, WIDTH), (2, WIDTH), (2, WIDTH)]
    dq, dk, dv, gk, gv = pl.pallas_call(
        store_all,
        out_shape=[jax.ShapeDtypeStruct(shape, BF16) for shape in shapes],
        in_specs=[hbm] * 5,
        out_specs=[hbm] * 5,
        scratch_shapes=[V(grad.shape, grad.dtype) for grad in grads]
        + [
            V((SLOTS, WIDTH), BF16),
            V((2, WIDTH), BF16),
            V((2, WIDTH), BF16),
            pltpu.SemaphoreType.DMA((7,)),
            pltpu.SemaphoreType.DMA((7,)),
        ],
        compiler_params=pltpu.CompilerParams(vmem_limit_bytes=60 * 1024 * 1024),
    )(*grads)
    return dq[None, None], dk[None, None], dv[None, None], gk, gv


def solution(mesh):
    wide = P("grp", "ctx", None, None)
    rows = P(("grp", "ctx"), None)
    return jax.shard_map(
        shards,
        mesh=mesh,
        in_specs=(rows, rows, wide, wide, wide, wide, P("grp", "ctx"), P("grp", "ctx", None)),
        out_specs=(wide, wide, wide, rows, rows),
        check_vma=False,
    )
```

```python
import jax
import jax.numpy as jnp
from jax import lax
from jax.experimental import pallas as pl
from jax.experimental.pallas import tpu as pltpu
from jax.sharding import PartitionSpec as P

HEADS = 16
DIM = 128
SLOTS = 64
ROWS = 128
WIDTH = 2048
PROMPT = 512
F32 = jnp.float32
BF16 = jnp.bfloat16
SCALE = DIM ** -0.5
SCALE2 = SCALE * 1.4426950408889634
MESH = pl.DeviceIdType.MESH

(
    KV, QUERY, GRAD, ZK, ZV, ZSUM, YK, YV, OWN, FIN, DQ, YSUM_K, YSUM_V, ZSUM_K, ZSUM_V, OUT, KINDS
) = range(17)


def dot_nt(a, b):
    return lax.dot_general(a, b, (((1,), (1,)), ((), ())), preferred_element_type=F32)


def dot_nn(a, b):
    return lax.dot_general(a, b, (((1,), (0,)), ((), ())), preferred_element_type=F32)


def dot_tn(a, b):
    return lax.dot_general(a, b, (((0,), (0,)), ((), ())), preferred_element_type=F32)


def kernel(
    pk_hbm, pv_hbm, rw_hbm, mp_hbm, cq_hbm, ck_hbm, cv_hbm, go_hbm,
    own_hbm, dqr, dk_hbm, dv_hbm, gp_hbm,
    pk, pv, rw, mp, cq, ck, cv, go, xq, xqr, xg, xgr, kvs, kvr, kb, vb, gsum, gsumr, own_e, own_d, st, str_,
    fs, fr, exps, prods, part, pw, ds,
    sbk, sbv, rk, rv, hk, hv, szk, szv, rzk, rzv, t3, dqs, dqo, dko, dvo,
    in_sem, out_sem, ss, rs, ry,
):
    grp = lax.axis_index("grp")
    ctx = lax.axis_index("ctx")
    x_lo, y = lax.div(grp, 4), lax.rem(grp, 4)
    z = lax.div(ctx, 4)
    z_hi, z_lo, low = lax.div(z, 2), lax.rem(z, 2), lax.rem(ctx, 4)
    a = z_lo * 8 + x_lo * 4 + low

    def a_peer(b):
        return {
            "grp": lax.rem(lax.div(b, 4), 2) * 4 + y,
            "ctx": (z_hi * 2 + lax.div(b, 8)) * 4 + lax.rem(b, 4),
        }

    def z_peer(b):
        return {"grp": grp, "ctx": (b * 2 + z_lo) * 4 + low}

    def y_peer(b):
        return {"grp": x_lo * 4 + b, "ctx": ctx}

    flips = [(dz, 0, 1, dc) for dz in (1, 0) for dc in (1, 0)]
    flips += [(dz, 1, dx, dc) for dz in (1, 0) for dx in (1, 0) for dc in (1, 0)]
    flips += [(1, 0, 0, 1), (1, 0, 0, 0), (0, 0, 0, 1)]

    def flipped(bit, flip):
        return 1 - bit if flip else bit

    x_hi, core = lax.div(low, 2), lax.rem(low, 2)
    a_others = [
        flipped(z_lo, dz) * 8 + flipped(x_lo, dl) * 4 + flipped(x_hi, dh) * 2 + flipped(core, dc)
        for dz, dl, dh, dc in flips
    ]
    z_others = [lax.rem(z_hi + k, 4) for k in (2, 1, 3)]
    y_others = [lax.rem(y + k, 4) for k in (2, 1, 3)]

    def remote(kind, src, dst, device):
        return pltpu.make_async_remote_copy(
            src_ref=src, dst_ref=dst, send_sem=ss.at[kind], recv_sem=rs.at[kind],
            device_id=device, device_id_type=MESH,
        )

    def along_y(kv, ref, row, b):
        return pltpu.make_async_remote_copy(
            src_ref=ref.at[row], dst_ref=ref.at[row], send_sem=ss.at[YK + kv],
            recv_sem=ry.at[kv, row], device_id=y_peer(b), device_id_type=MESH,
        )

    def arrived(kind, dst):
        remote(kind, dst, dst, y_peer(y_others[0])).wait_recv()

    def sent(kind, src):
        remote(kind, src, src, y_peer(y_others[0])).wait_send()

    loads = [
        pltpu.make_async_copy(src, dst, in_sem.at[n])
        for n, (src, dst) in enumerate(
            (
                (pk_hbm, pk), (pv_hbm, pv), (rw_hbm, rw), (mp_hbm, mp),
                (cq_hbm, cq), (go_hbm, go), (ck_hbm, ck), (cv_hbm, cv),
            )
        )
    ]
    for load in loads[:4]:
        load.start()

    barrier = pltpu.get_barrier_semaphore()
    for b in z_others:
        pl.semaphore_signal(barrier, inc=1, device_id=z_peer(b), device_id_type=MESH)
    for b in y_others:
        pl.semaphore_signal(barrier, inc=1, device_id=y_peer(b), device_id_type=MESH)
    for b in a_others:
        pl.semaphore_signal(barrier, inc=1, device_id=a_peer(b), device_id_type=MESH)
    for load in loads[4:]:
        load.start()

    for load in loads[:4]:
        load.wait()
    pos = mp[...]
    pos2 = jnp.concatenate([pos, pos], axis=1)
    live = pos < ROWS
    count = jnp.sum(jnp.where(live, 1.0, 0.0), axis=1, keepdims=True)
    reward = rw[...]
    lines = jnp.concatenate(
        [
            pk[...].astype(F32),
            pv[...].astype(F32),
            jnp.broadcast_to(count, (1, WIDTH)),
            jnp.broadcast_to(reward, (1, WIDTH)),
            jnp.zeros((2, WIDTH), F32),
        ],
        axis=0,
    )
    for h in range(HEADS):
        kvs[h] = lines[:, h * DIM : (h + 1) * DIM]

    pl.semaphore_wait(barrier, 21)

    for b in a_others:
        remote(KV, kvs.at[b], kvr.at[a], a_peer(b)).start()
    kvr[a] = kvs[a]

    row = lax.broadcasted_iota(jnp.int32, (ROWS, 2 * SLOTS), 0)
    pick = jnp.where(row == jnp.minimum(pos2, ROWS - 1), 1.0, 0.0).astype(BF16)
    loads[4].wait()
    picked = dot_tn(pick, cq[...])[:SLOTS].astype(BF16)
    for h in range(HEADS):
        xq[h] = picked[:, h * DIM : (h + 1) * DIM]
    loads[5].wait()
    for h in range(HEADS):
        xg[h] = go[:, h * DIM : (h + 1) * DIM]

    nothing = jnp.zeros((SLOTS, DIM), BF16)

    def both(ref, t):
        return jnp.concatenate(
            [
                jnp.concatenate([ref[2 * t], nothing], axis=1),
                jnp.concatenate([nothing, ref[2 * t + 1]], axis=1),
            ],
            axis=0,
        )

    def own_scores(t):
        cols = slice(t * 256, (t + 1) * 256)
        s = dot_nt(ck[:, cols], both(xq, t)) * SCALE2
        d = dot_nt(cv[:, cols], both(xg, t))
        m = jnp.max(s, axis=0, keepdims=True)
        e = jnp.exp2(s - m)
        own_e[t] = e
        own_d[t] = d
        st[t] = jnp.concatenate(
            [
                m,
                jnp.sum(e, axis=0, keepdims=True),
                jnp.sum(e * d, axis=0, keepdims=True),
                jnp.zeros((5, DIM), F32),
            ],
            axis=0,
        )

    left = lax.broadcasted_iota(jnp.int32, (8, DIM), 1) < SLOTS
    odd = jnp.broadcast_to(lax.rem(a, 2), (8, DIM)) == 1

    def side_by_side(ref, t):
        one, two = ref[2 * t], ref[2 * t + 1]
        moved = pltpu.roll(jnp.where(odd, one, two), SLOTS, 1)
        return jnp.where(left != odd, jnp.where(left, one, two), moved)

    loads[6].wait()
    loads[7].wait()
    for t in range(4):
        own_scores(t)

    arrived(KV, kvr.at[pl.ds(0, 15)])
    blocks = kvr[...]
    kb[y, z_hi, 0:16, :] = blocks[:, 0, :].astype(BF16)
    kb[y, z_hi, 16:32, :] = blocks[:, 1, :].astype(BF16)
    for b in z_others:
        remote(ZK, kb.at[y, z_hi], kb.at[y, z_hi], z_peer(b)).start()
    vb[y, z_hi, 0:16, :] = blocks[:, 2, :].astype(BF16)
    vb[y, z_hi, 16:32, :] = blocks[:, 3, :].astype(BF16)
    for b in z_others:
        remote(ZV, vb.at[y, z_hi], vb.at[y, z_hi], z_peer(b)).start()
    mine = lax.broadcasted_iota(jnp.int32, (16, DIM), 0) // 4 % 2 == x_lo
    count16 = jnp.sum(jnp.where(mine, blocks[:, 4, :], 0.0), axis=0, keepdims=True)
    reward16 = jnp.sum(jnp.where(mine, blocks[:, 5, :], 0.0), axis=0, keepdims=True)
    gsum[...] = jnp.concatenate([count16, reward16, jnp.zeros((6, DIM), F32)], axis=0)
    for b in z_others:
        remote(ZSUM, gsum, gsumr.at[z_hi], z_peer(b)).start()
    for b in a_others:
        remote(QUERY, xq.at[b], xqr.at[a], a_peer(b)).start()
    xqr[a] = xq[a]
    for b in a_others:
        remote(GRAD, xg.at[b], xgr.at[a], a_peer(b)).start()
    xgr[a] = xg[a]

    for t in range(4, 8):
        own_scores(t)

    arrived(ZK, kb.at[0, pl.ds(0, 3)])
    for b in y_others:
        along_y(0, kb, y, b).start()
    arrived(ZV, vb.at[0, pl.ds(0, 3)])
    for b in y_others:
        along_y(1, vb, y, b).start()
    arrived(ZSUM, gsumr.at[pl.ds(0, 3)])
    total = gsum[...]
    for b in z_others:
        total = total + gsumr[b]
    weight = (reward - total[1:2] / 32.0) * (SLOTS * 32) / total[0:1]
    weight = jnp.where(pos2 < ROWS, weight, 0.0)
    for t in range(8):
        st[t, 3:4, :] = weight
    for b in a_others:
        remote(OWN, st.at[lax.div(b, 2)], str_.at[a], a_peer(b)).start()
    str_[a] = st[lax.div(a, 2)]

    def key_block(b):
        block = kb[b].reshape(128, DIM)
        for n in range(4):
            cols = slice(n * 256, (n + 1) * 256)
            s = dot_nt(block, xqr[4 * n : 4 * n + 4].reshape(256, DIM)) * SCALE2
            m = jnp.max(s, axis=0, keepdims=True)
            e = jnp.exp2(s - m)
            exps[b, :, cols] = e
            part[b, 0:1, cols] = m
            part[b, 1:2, cols] = jnp.sum(e, axis=0, keepdims=True)

    def value_blocks(b):
        block = vb[...].reshape(PROMPT, DIM)
        for n in range(4):
            cols = slice(n * 256, (n + 1) * 256)
            d = dot_nt(block, xgr[4 * n : 4 * n + 4].reshape(256, DIM)) * SCALE
            prods[:, :, cols] = d.reshape(4, 128, 256)
            p = exps[:, :, cols].reshape(PROMPT, 256)
            part[b, 2:3, cols] = jnp.sum(p * d, axis=0, keepdims=True)

    near_first = y_others[1:] + y_others[:1]
    arrived(QUERY, xqr.at[pl.ds(0, 15)])
    key_block(y)
    for b in near_first:
        along_y(0, kb, b, b).wait_recv()
        key_block(b)
    arrived(OWN, str_.at[pl.ds(0, 15)])
    stats = jnp.concatenate([side_by_side(str_, t) for t in range(8)], axis=1)
    m = stats[0:1]
    for b in range(4):
        m = jnp.maximum(m, part[b, 0:1, :])
    fo = jnp.exp2(stats[0:1] - m)
    total = stats[1:2] * fo
    for b in range(4):
        f = jnp.exp2(part[b, 0:1, :] - m)
        total = total + part[b, 1:2, :] * f
        part[b, 3:4, :] = f
    inv = 1.0 / total
    weights = stats[3:4]

    def probabilities(b):
        coef = part[b, 3:4, :] * inv
        for n in range(4):
            cols = slice(n * 256, (n + 1) * 256)
            p = exps[b, :, cols] * coef[:, cols]
            exps[b, :, cols] = p
            pw[b, :, cols] = (p * weights[:, cols]).astype(BF16)

    for b in y_others + [y]:
        probabilities(b)
    arrived(GRAD, xgr.at[pl.ds(0, 15)])
    q_all = xqr[...].reshape(16 * SLOTS, DIM)
    g_all = xgr[...].reshape(16 * SLOTS, DIM)
    for b in y_others:
        sbv[b] = dot_nn(pw[b], g_all).astype(BF16)
        remote(YSUM_V, sbv.at[b], rv.at[y], y_peer(b)).start()
    for b in near_first:
        along_y(1, vb, b, b).wait_recv()
    value_blocks(0)
    inner = stats[2:3] * (fo * inv * SCALE)
    for b in (0,):
        inner = inner + part[b, 2:3, :]

    def finish(b):
        for n in range(4):
            cols = slice(n * 256, (n + 1) * 256)
            dscore = exps[b, :, cols] * (prods[b, :, cols] - inner[:, cols])
            ds[b, :, cols] = (dscore * weights[:, cols]).astype(BF16)

    for b in y_others:
        finish(b)
        sbk[b] = dot_nn(ds[b], q_all).astype(BF16)
        remote(YSUM_K, sbk.at[b], rk.at[y], y_peer(b)).start()
    finish(y)
    final = jnp.concatenate(
        [m, inv, inner * (1.0 / SCALE), jnp.zeros((5, 16 * SLOTS), F32)], axis=0
    )
    for t in range(8):
        fs[t] = final[:, t * DIM : (t + 1) * DIM]
    keys = kb[...].reshape(PROMPT, DIM)
    grad_v = dot_nn(pw[y], g_all)
    grad_k = dot_nn(ds[y], q_all)
    for b in a_others:
        remote(FIN, fs.at[lax.div(b, 2)], fr.at[a], a_peer(b)).start()
    fr[a] = fs[lax.div(a, 2)]
    for t in range(8):
        grad_q = dot_tn(ds[:, :, t * 128 : (t + 1) * 128].reshape(PROMPT, 2 * SLOTS), keys)
        dqs[2 * t] = grad_q[:SLOTS].astype(BF16)
        dqs[2 * t + 1] = grad_q[SLOTS:].astype(BF16)
    for b in a_others:
        remote(DQ, dqs.at[b], dqr.at[a], a_peer(b)).start()
    own_part = pltpu.make_async_copy(dqs.at[a], dqr.at[a], out_sem.at[4])
    own_part.start()

    def next_sum(total, kind_y, received, held, send, kind_z, target):
        arrived(kind_y, received.at[pl.ds(0, 3)])
        for b in y_others:
            total = total + received[b].astype(F32)
        held[...] = total.reshape(4, 32, DIM)
        send[...] = total.astype(BF16).reshape(4, 32, DIM)
        for b in z_others:
            remote(kind_z, send.at[b], target.at[z_hi], z_peer(b)).start()

    next_sum(grad_v, YSUM_V, rv, hv, szv, ZSUM_V, rzv)
    next_sum(grad_k, YSUM_K, rk, hk, szk, ZSUM_K, rzk)

    arrived(FIN, fr.at[pl.ds(0, 15)])
    for t in range(8):
        cols = slice(t * 256, (t + 1) * 256)
        fin = side_by_side(fr, t)
        m, inv, inner = fin[0:1], fin[1:2], fin[2:3]
        coef = jnp.exp2(st[t, 0:1, :] - m) * inv * weight
        e = own_e[t]
        p = (e * coef).astype(BF16)
        dsc = (e * (own_d[t] - inner) * (coef * SCALE)).astype(BF16)
        dvo[:, cols] = dot_nn(p, both(xg, t)).astype(BF16)
        dko[:, cols] = dot_nn(dsc, both(xq, t)).astype(BF16)
        grad_q = dot_tn(dsc, ck[:, cols])
        dqo[2 * t] = grad_q[:SLOTS, :DIM].astype(BF16)
        dqo[2 * t + 1] = grad_q[SLOTS:, DIM:].astype(BF16)
    stores = [
        pltpu.make_async_copy(src, dst, out_sem.at[n])
        for n, (src, dst) in enumerate(
            ((dqo, own_hbm), (dko, dk_hbm), (dvo, dv_hbm), (t3.at[a], gp_hbm.at[a]))
        )
    ]
    for store in stores[:3]:
        store.start()

    arrived(ZSUM_V, rzv.at[pl.ds(0, 3)])
    arrived(ZSUM_K, rzk.at[pl.ds(0, 3)])
    line = lax.broadcasted_iota(jnp.int32, (16, 8, DIM), 1)
    lines = jnp.zeros((16, 8, DIM), F32)
    for kv, (held, received) in enumerate(((hk, rzk), (hv, rzv))):
        part = held[z_hi]
        for b in z_others:
            part = part + received[b].astype(F32)
        for r in range(2):
            lines = jnp.where(line == kv * 2 + r, part[r * 16 : (r + 1) * 16][:, None, :], lines)
    t3[...] = lines
    for b in a_others:
        remote(OUT, t3.at[b], gp_hbm.at[a], a_peer(b)).start()
    stores[3].start()
    arrived(DQ, dqr.at[pl.ds(0, 15)])
    arrived(OUT, gp_hbm.at[pl.ds(0, 15)])

    sent(KV, kvs.at[pl.ds(0, 15)])
    sent(QUERY, xq.at[pl.ds(0, 15)])
    sent(GRAD, xg.at[pl.ds(0, 15)])
    sent(ZK, kb.at[0, pl.ds(0, 3)])
    sent(ZV, vb.at[0, pl.ds(0, 3)])
    sent(ZSUM, gsumr.at[pl.ds(0, 3)])
    sent(YK, kb.at[pl.ds(0, 3)])
    sent(YV, vb.at[pl.ds(0, 3)])
    sent(OWN, str_.at[pl.ds(0, 15)])
    sent(FIN, fr.at[pl.ds(0, 15)])
    sent(DQ, dqs.at[pl.ds(0, 15)])
    sent(YSUM_V, sbv.at[pl.ds(0, 3)])
    sent(YSUM_K, sbk.at[pl.ds(0, 3)])
    sent(ZSUM_V, szv.at[pl.ds(0, 3)])
    sent(ZSUM_K, szk.at[pl.ds(0, 3)])
    sent(OUT, t3.at[pl.ds(0, 15)])
    for store in stores + [own_part]:
        store.wait()


def store_all(own, other, dk, dv, gp, dq_out, dk_out, dv_out, gk_out, gv_out, *scratch):
    (
        own_held, other_held, dk_held, dv_held, gp_held, dq_held, gk_held, gv_held,
        in_sem, out_sem,
    ) = scratch
    pairs = [(own, own_held), (other, other_held), (gp, gp_held)]
    stores = []
    for source, held, target in ((dk, dk_held, dk_out), (dv, dv_held, dv_out)):
        for first in range(0, ROWS, SLOTS):
            span = pl.ds(first, SLOTS)
            pairs.append((source.at[span], held.at[span]))
            stores.append((held.at[span], target.at[span]))
    stores += [(dq_held, dq_out), (gk_held, gk_out), (gv_held, gv_out)]
    loads = [pltpu.make_async_copy(*pair, in_sem.at[n]) for n, pair in enumerate(pairs)]
    stores = [pltpu.make_async_copy(*pair, out_sem.at[n]) for n, pair in enumerate(stores)]
    for load in loads:
        load.start()
    loads[0].wait()
    loads[1].wait()
    for h in range(HEADS):
        cols = slice(h * DIM, (h + 1) * DIM)
        total = own_held[h].astype(F32) + other_held[h].astype(F32)
        dq_held[:, cols] = total.astype(BF16)
    stores[4].start()
    for n in range(4):
        loads[3 + n].wait()
        stores[n].start()
    loads[2].wait()
    for h in range(HEADS):
        cols = slice(h * DIM, (h + 1) * DIM)
        gk_held[:, cols] = gp_held[h, 0:2, :].astype(BF16)
        gv_held[:, cols] = gp_held[h, 2:4, :].astype(BF16)
    stores[5].start()
    stores[6].start()
    for store in stores:
        store.wait()


def shards(prompt_k, prompt_v, comp_q, comp_k, comp_v, grad_out, rewards, mask_pos):
    hbm = pl.BlockSpec(memory_space=pltpu.HBM)
    V = pltpu.VMEM
    grads = pl.pallas_call(
        kernel,
        out_shape=(
            jax.ShapeDtypeStruct((HEADS, SLOTS, DIM), BF16),
            jax.ShapeDtypeStruct((HEADS, SLOTS, DIM), BF16),
            jax.ShapeDtypeStruct((ROWS, WIDTH), BF16),
            jax.ShapeDtypeStruct((ROWS, WIDTH), BF16),
            jax.ShapeDtypeStruct((16, 8, DIM), F32),
        ),
        in_specs=[hbm] * 8,
        out_specs=(hbm,) * 5,
        scratch_shapes=[
            V((2, WIDTH), BF16),
            V((2, WIDTH), BF16),
            V((1, 1), F32),
            V((1, SLOTS), jnp.int32),
            V((ROWS, WIDTH), BF16),
            V((ROWS, WIDTH), BF16),
            V((ROWS, WIDTH), BF16),
            V((SLOTS, WIDTH), BF16),
            V((16, SLOTS, DIM), BF16),
            V((16, SLOTS, DIM), BF16),
            V((16, SLOTS, DIM), BF16),
            V((16, SLOTS, DIM), BF16),
            V((16, 8, DIM), F32),
            V((16, 8, DIM), F32),
            V((4, 4, 32, DIM), BF16),
            V((4, 4, 32, DIM), BF16),
            V((8, DIM), F32),
            V((4, 8, DIM), F32),
            V((8, 128, DIM), F32),
            V((8, 128, DIM), F32),
            V((8, 8, DIM), F32),
            V((16, 8, DIM), F32),
            V((8, 8, DIM), F32),
            V((16, 8, DIM), F32),
            V((4, 128, 16 * SLOTS), F32),
            V((4, 128, 16 * SLOTS), F32),
            V((4, 8, 16 * SLOTS), F32),
            V((4, 128, 16 * SLOTS), BF16),
            V((4, 128, 16 * SLOTS), BF16),
            V((4, 128, DIM), BF16),
            V((4, 128, DIM), BF16),
            V((4, 128, DIM), BF16),
            V((4, 128, DIM), BF16),
            V((4, 32, DIM), F32),
            V((4, 32, DIM), F32),
            V((4, 32, DIM), BF16),
            V((4, 32, DIM), BF16),
            V((4, 32, DIM), BF16),
            V((4, 32, DIM), BF16),
            V((16, 8, DIM), F32),
            V((16, SLOTS, DIM), BF16),
            V((16, SLOTS, DIM), BF16),
            V((ROWS, WIDTH), BF16),
            V((ROWS, WIDTH), BF16),
            pltpu.SemaphoreType.DMA((8,)),
            pltpu.SemaphoreType.DMA((5,)),
            pltpu.SemaphoreType.DMA((KINDS,)),
            pltpu.SemaphoreType.DMA((KINDS,)),
            pltpu.SemaphoreType.DMA((2, 4)),
        ],
        compiler_params=pltpu.CompilerParams(
            collective_id=0, has_side_effects=True, vmem_limit_bytes=60 * 1024 * 1024
        ),
    )(
        prompt_k, prompt_v, rewards, mask_pos[0], comp_q[0, 0], comp_k[0, 0], comp_v[0, 0],
        grad_out[0, 0],
    )
    shapes = [(SLOTS, WIDTH), (ROWS, WIDTH), (ROWS, WIDTH), (2, WIDTH), (2, WIDTH)]
    dq, dk, dv, gk, gv = pl.pallas_call(
        store_all,
        out_shape=[jax.ShapeDtypeStruct(shape, BF16) for shape in shapes],
        in_specs=[hbm] * 5,
        out_specs=[hbm] * 5,
        scratch_shapes=[V(grad.shape, grad.dtype) for grad in grads]
        + [
            V((SLOTS, WIDTH), BF16),
            V((2, WIDTH), BF16),
            V((2, WIDTH), BF16),
            pltpu.SemaphoreType.DMA((7,)),
            pltpu.SemaphoreType.DMA((7,)),
        ],
        compiler_params=pltpu.CompilerParams(vmem_limit_bytes=60 * 1024 * 1024),
    )(*grads)
    return dq[None, None], dk[None, None], dv[None, None], gk, gv


def solution(mesh):
    wide = P("grp", "ctx", None, None)
    rows = P(("grp", "ctx"), None)
    return jax.shard_map(
        shards,
        mesh=mesh,
        in_specs=(rows, rows, wide, wide, wide, wide, P("grp", "ctx"), P("grp", "ctx", None)),
        out_specs=(wide, wide, wide, rows, rows),
        check_vma=False,
    )
```

```python
import jax
import jax.numpy as jnp
from jax import lax
from jax.experimental import pallas as pl
from jax.experimental.pallas import tpu as pltpu
from jax.sharding import PartitionSpec as P

HEADS = 16
DIM = 128
SLOTS = 64
ROWS = 128
WIDTH = 2048
PROMPT = 512
F32 = jnp.float32
BF16 = jnp.bfloat16
SCALE = DIM ** -0.5
SCALE2 = SCALE * 1.4426950408889634
MESH = pl.DeviceIdType.MESH

(
    KV, QUERY, GRAD, ZK, ZV, ZSUM, YK, YV, OWN, FIN, DQ, YSUM_K, YSUM_V, ZSUM_K, ZSUM_V, OUT, KINDS
) = range(17)


def dot_nt(a, b):
    return lax.dot_general(a, b, (((1,), (1,)), ((), ())), preferred_element_type=F32)


def dot_nn(a, b):
    return lax.dot_general(a, b, (((1,), (0,)), ((), ())), preferred_element_type=F32)


def dot_tn(a, b):
    return lax.dot_general(a, b, (((0,), (0,)), ((), ())), preferred_element_type=F32)


def kernel(
    pk_hbm, pv_hbm, rw_hbm, mp_hbm, cq_hbm, ck_hbm, cv_hbm, go_hbm,
    own_hbm, dqr, dk_hbm, dv_hbm, gp_hbm,
    pk, pv, rw, mp, cq, ck, cv, go, xq, xqr, xg, xgr, kvs, kvr, kb, vb, gsum, gsumr, own_e, own_d, st, str_,
    fs, fr, exps, prods, part, pw, ds,
    sbk, sbv, rk, rv, hk, hv, szk, szv, rzk, rzv, t3, dqs, dqo, dko, dvo,
    in_sem, out_sem, ss, rs, ry,
):
    grp = lax.axis_index("grp")
    ctx = lax.axis_index("ctx")
    x_lo, y = lax.div(grp, 4), lax.rem(grp, 4)
    z = lax.div(ctx, 4)
    z_hi, z_lo, low = lax.div(z, 2), lax.rem(z, 2), lax.rem(ctx, 4)
    a = z_lo * 8 + x_lo * 4 + low

    def a_peer(b):
        return {
            "grp": lax.rem(lax.div(b, 4), 2) * 4 + y,
            "ctx": (z_hi * 2 + lax.div(b, 8)) * 4 + lax.rem(b, 4),
        }

    def z_peer(b):
        return {"grp": grp, "ctx": (b * 2 + z_lo) * 4 + low}

    def y_peer(b):
        return {"grp": x_lo * 4 + b, "ctx": ctx}

    flips = [(dz, 0, 1, dc) for dz in (1, 0) for dc in (1, 0)]
    flips += [(dz, 1, dx, dc) for dz in (1, 0) for dx in (1, 0) for dc in (1, 0)]
    flips += [(1, 0, 0, 1), (1, 0, 0, 0), (0, 0, 0, 1)]

    def flipped(bit, flip):
        return 1 - bit if flip else bit

    x_hi, core = lax.div(low, 2), lax.rem(low, 2)
    a_others = [
        flipped(z_lo, dz) * 8 + flipped(x_lo, dl) * 4 + flipped(x_hi, dh) * 2 + flipped(core, dc)
        for dz, dl, dh, dc in flips
    ]
    z_others = [lax.rem(z_hi + k, 4) for k in (2, 1, 3)]
    y_others = [lax.rem(y + k, 4) for k in (2, 1, 3)]

    def remote(kind, src, dst, device):
        return pltpu.make_async_remote_copy(
            src_ref=src, dst_ref=dst, send_sem=ss.at[kind], recv_sem=rs.at[kind],
            device_id=device, device_id_type=MESH,
        )

    def along_y(kv, ref, row, b):
        return pltpu.make_async_remote_copy(
            src_ref=ref.at[row], dst_ref=ref.at[row], send_sem=ss.at[YK + kv],
            recv_sem=ry.at[kv, row], device_id=y_peer(b), device_id_type=MESH,
        )

    def arrived(kind, dst):
        remote(kind, dst, dst, y_peer(y_others[0])).wait_recv()

    def sent(kind, src):
        remote(kind, src, src, y_peer(y_others[0])).wait_send()

    loads = [
        pltpu.make_async_copy(src, dst, in_sem.at[n])
        for n, (src, dst) in enumerate(
            (
                (pk_hbm, pk), (pv_hbm, pv), (rw_hbm, rw), (mp_hbm, mp),
                (cq_hbm, cq), (go_hbm, go), (ck_hbm, ck), (cv_hbm, cv),
            )
        )
    ]
    for load in loads[:4]:
        load.start()

    barrier = pltpu.get_barrier_semaphore()
    for b in z_others:
        pl.semaphore_signal(barrier, inc=1, device_id=z_peer(b), device_id_type=MESH)
    for b in y_others:
        pl.semaphore_signal(barrier, inc=1, device_id=y_peer(b), device_id_type=MESH)
    for b in a_others:
        pl.semaphore_signal(barrier, inc=1, device_id=a_peer(b), device_id_type=MESH)
    for load in loads[4:]:
        load.start()

    for load in loads[:4]:
        load.wait()
    pos = mp[...]
    pos2 = jnp.concatenate([pos, pos], axis=1)
    live = pos < ROWS
    count = jnp.sum(jnp.where(live, 1.0, 0.0), axis=1, keepdims=True)
    reward = rw[...]
    lines = jnp.concatenate(
        [
            pk[...].astype(F32),
            pv[...].astype(F32),
            jnp.broadcast_to(count, (1, WIDTH)),
            jnp.broadcast_to(reward, (1, WIDTH)),
            jnp.zeros((2, WIDTH), F32),
        ],
        axis=0,
    )
    for h in range(HEADS):
        kvs[h] = lines[:, h * DIM : (h + 1) * DIM]

    pl.semaphore_wait(barrier, 21)

    for b in a_others:
        remote(KV, kvs.at[b], kvr.at[a], a_peer(b)).start()
    kvr[a] = kvs[a]

    row = lax.broadcasted_iota(jnp.int32, (ROWS, 2 * SLOTS), 0)
    pick = jnp.where(row == jnp.minimum(pos2, ROWS - 1), 1.0, 0.0).astype(BF16)
    loads[4].wait()
    picked = dot_tn(pick, cq[...])[:SLOTS].astype(BF16)
    for h in range(HEADS):
        xq[h] = picked[:, h * DIM : (h + 1) * DIM]
    loads[5].wait()
    for h in range(HEADS):
        xg[h] = go[:, h * DIM : (h + 1) * DIM]

    nothing = jnp.zeros((SLOTS, DIM), BF16)

    def both(ref, t):
        return jnp.concatenate(
            [
                jnp.concatenate([ref[2 * t], nothing], axis=1),
                jnp.concatenate([nothing, ref[2 * t + 1]], axis=1),
            ],
            axis=0,
        )

    def own_scores(t):
        cols = slice(t * 256, (t + 1) * 256)
        s = dot_nt(ck[:, cols], both(xq, t)) * SCALE2
        d = dot_nt(cv[:, cols], both(xg, t))
        m = jnp.max(s, axis=0, keepdims=True)
        e = jnp.exp2(s - m)
        own_e[t] = e
        own_d[t] = d
        st[t] = jnp.concatenate(
            [
                m,
                jnp.sum(e, axis=0, keepdims=True),
                jnp.sum(e * d, axis=0, keepdims=True),
                jnp.zeros((5, DIM), F32),
            ],
            axis=0,
        )

    left = lax.broadcasted_iota(jnp.int32, (8, DIM), 1) < SLOTS
    odd = jnp.broadcast_to(lax.rem(a, 2), (8, DIM)) == 1

    def side_by_side(ref, t):
        one, two = ref[2 * t], ref[2 * t + 1]
        moved = pltpu.roll(jnp.where(odd, one, two), SLOTS, 1)
        return jnp.where(left != odd, jnp.where(left, one, two), moved)

    loads[6].wait()
    loads[7].wait()
    for t in range(4):
        own_scores(t)

    arrived(KV, kvr.at[pl.ds(0, 15)])
    blocks = kvr[...]
    kb[y, z_hi, 0:16, :] = blocks[:, 0, :].astype(BF16)
    kb[y, z_hi, 16:32, :] = blocks[:, 1, :].astype(BF16)
    for b in z_others:
        remote(ZK, kb.at[y, z_hi], kb.at[y, z_hi], z_peer(b)).start()
    vb[y, z_hi, 0:16, :] = blocks[:, 2, :].astype(BF16)
    vb[y, z_hi, 16:32, :] = blocks[:, 3, :].astype(BF16)
    for b in z_others:
        remote(ZV, vb.at[y, z_hi], vb.at[y, z_hi], z_peer(b)).start()
    mine = lax.broadcasted_iota(jnp.int32, (16, DIM), 0) // 4 % 2 == x_lo
    count16 = jnp.sum(jnp.where(mine, blocks[:, 4, :], 0.0), axis=0, keepdims=True)
    reward16 = jnp.sum(jnp.where(mine, blocks[:, 5, :], 0.0), axis=0, keepdims=True)
    gsum[...] = jnp.concatenate([count16, reward16, jnp.zeros((6, DIM), F32)], axis=0)
    for b in z_others:
        remote(ZSUM, gsum, gsumr.at[z_hi], z_peer(b)).start()
    for b in a_others:
        remote(QUERY, xq.at[b], xqr.at[a], a_peer(b)).start()
    xqr[a] = xq[a]
    for b in a_others:
        remote(GRAD, xg.at[b], xgr.at[a], a_peer(b)).start()
    xgr[a] = xg[a]

    for t in range(4, 8):
        own_scores(t)

    arrived(ZK, kb.at[0, pl.ds(0, 3)])
    for b in y_others:
        along_y(0, kb, y, b).start()
    arrived(ZV, vb.at[0, pl.ds(0, 3)])
    for b in y_others:
        along_y(1, vb, y, b).start()
    arrived(ZSUM, gsumr.at[pl.ds(0, 3)])
    total = gsum[...]
    for b in z_others:
        total = total + gsumr[b]
    weight = (reward - total[1:2] / 32.0) * (SLOTS * 32) / total[0:1]
    weight = jnp.where(pos2 < ROWS, weight, 0.0)
    for t in range(8):
        st[t, 3:4, :] = weight
    for b in a_others:
        remote(OWN, st.at[lax.div(b, 2)], str_.at[a], a_peer(b)).start()
    str_[a] = st[lax.div(a, 2)]

    def key_block(b):
        block = kb[b].reshape(128, DIM)
        for n in range(4):
            cols = slice(n * 256, (n + 1) * 256)
            s = dot_nt(block, xqr[4 * n : 4 * n + 4].reshape(256, DIM)) * SCALE2
            m = jnp.max(s, axis=0, keepdims=True)
            e = jnp.exp2(s - m)
            exps[b, :, cols] = e
            part[b, 0:1, cols] = m
            part[b, 1:2, cols] = jnp.sum(e, axis=0, keepdims=True)

    def value_blocks(b):
        block = vb[b : b + 2].reshape(256, DIM)
        for n in range(4):
            cols = slice(n * 256, (n + 1) * 256)
            d = dot_nt(block, xgr[4 * n : 4 * n + 4].reshape(256, DIM)) * SCALE
            prods[b : b + 2, :, cols] = d.reshape(2, 128, 256)
            p = exps[b : b + 2, :, cols].reshape(256, 256)
            part[b, 2:3, cols] = jnp.sum(p * d, axis=0, keepdims=True)

    near_first = y_others[1:] + y_others[:1]
    arrived(QUERY, xqr.at[pl.ds(0, 15)])
    key_block(y)
    for b in near_first:
        along_y(0, kb, b, b).wait_recv()
        key_block(b)
    arrived(OWN, str_.at[pl.ds(0, 15)])
    stats = jnp.concatenate([side_by_side(str_, t) for t in range(8)], axis=1)
    m = stats[0:1]
    for b in range(4):
        m = jnp.maximum(m, part[b, 0:1, :])
    fo = jnp.exp2(stats[0:1] - m)
    total = stats[1:2] * fo
    for b in range(4):
        f = jnp.exp2(part[b, 0:1, :] - m)
        total = total + part[b, 1:2, :] * f
        part[b, 3:4, :] = f
    inv = 1.0 / total
    weights = stats[3:4]

    def probabilities(b):
        coef = part[b, 3:4, :] * inv
        for n in range(4):
            cols = slice(n * 256, (n + 1) * 256)
            p = exps[b, :, cols] * coef[:, cols]
            exps[b, :, cols] = p
            pw[b, :, cols] = (p * weights[:, cols]).astype(BF16)

    for b in y_others + [y]:
        probabilities(b)
    arrived(GRAD, xgr.at[pl.ds(0, 15)])
    q_all = xqr[...].reshape(16 * SLOTS, DIM)
    g_all = xgr[...].reshape(16 * SLOTS, DIM)
    for b in y_others:
        sbv[b] = dot_nn(pw[b], g_all).astype(BF16)
        remote(YSUM_V, sbv.at[b], rv.at[y], y_peer(b)).start()
    for b in near_first:
        along_y(1, vb, b, b).wait_recv()
    value_blocks(0)
    value_blocks(2)
    inner = stats[2:3] * (fo * inv * SCALE)
    for b in (0, 2):
        inner = inner + part[b, 2:3, :]

    def finish(b):
        for n in range(4):
            cols = slice(n * 256, (n + 1) * 256)
            dscore = exps[b, :, cols] * (prods[b, :, cols] - inner[:, cols])
            ds[b, :, cols] = (dscore * weights[:, cols]).astype(BF16)

    for b in y_others:
        finish(b)
        sbk[b] = dot_nn(ds[b], q_all).astype(BF16)
        remote(YSUM_K, sbk.at[b], rk.at[y], y_peer(b)).start()
    finish(y)
    final = jnp.concatenate(
        [m, inv, inner * (1.0 / SCALE), jnp.zeros((5, 16 * SLOTS), F32)], axis=0
    )
    for t in range(8):
        fs[t] = final[:, t * DIM : (t + 1) * DIM]
    keys = kb[...].reshape(PROMPT, DIM)
    grad_v = dot_nn(pw[y], g_all)
    grad_k = dot_nn(ds[y], q_all)
    for t in range(8):
        grad_q = dot_tn(ds[:, :, t * 128 : (t + 1) * 128].reshape(PROMPT, 2 * SLOTS), keys)
        dqs[2 * t] = grad_q[:SLOTS].astype(BF16)
        dqs[2 * t + 1] = grad_q[SLOTS:].astype(BF16)
    for b in a_others:
        remote(DQ, dqs.at[b], dqr.at[a], a_peer(b)).start()
    own_part = pltpu.make_async_copy(dqs.at[a], dqr.at[a], out_sem.at[4])
    own_part.start()
    for b in a_others:
        remote(FIN, fs.at[lax.div(b, 2)], fr.at[a], a_peer(b)).start()
    fr[a] = fs[lax.div(a, 2)]

    def next_sum(total, kind_y, received, held, send, kind_z, target):
        arrived(kind_y, received.at[pl.ds(0, 3)])
        for b in y_others:
            total = total + received[b].astype(F32)
        held[...] = total.reshape(4, 32, DIM)
        send[...] = total.astype(BF16).reshape(4, 32, DIM)
        for b in z_others:
            remote(kind_z, send.at[b], target.at[z_hi], z_peer(b)).start()

    next_sum(grad_v, YSUM_V, rv, hv, szv, ZSUM_V, rzv)
    next_sum(grad_k, YSUM_K, rk, hk, szk, ZSUM_K, rzk)

    arrived(FIN, fr.at[pl.ds(0, 15)])
    for t in range(8):
        cols = slice(t * 256, (t + 1) * 256)
        fin = side_by_side(fr, t)
        m, inv, inner = fin[0:1], fin[1:2], fin[2:3]
        coef = jnp.exp2(st[t, 0:1, :] - m) * inv * weight
        e = own_e[t]
        p = (e * coef).astype(BF16)
        dsc = (e * (own_d[t] - inner) * (coef * SCALE)).astype(BF16)
        dvo[:, cols] = dot_nn(p, both(xg, t)).astype(BF16)
        dko[:, cols] = dot_nn(dsc, both(xq, t)).astype(BF16)
        grad_q = dot_tn(dsc, ck[:, cols])
        dqo[2 * t] = grad_q[:SLOTS, :DIM].astype(BF16)
        dqo[2 * t + 1] = grad_q[SLOTS:, DIM:].astype(BF16)
    stores = [
        pltpu.make_async_copy(src, dst, out_sem.at[n])
        for n, (src, dst) in enumerate(
            ((dqo, own_hbm), (dko, dk_hbm), (dvo, dv_hbm), (t3.at[a], gp_hbm.at[a]))
        )
    ]
    for store in stores[:3]:
        store.start()

    arrived(ZSUM_V, rzv.at[pl.ds(0, 3)])
    arrived(ZSUM_K, rzk.at[pl.ds(0, 3)])
    line = lax.broadcasted_iota(jnp.int32, (16, 8, DIM), 1)
    lines = jnp.zeros((16, 8, DIM), F32)
    for kv, (held, received) in enumerate(((hk, rzk), (hv, rzv))):
        part = held[z_hi]
        for b in z_others:
            part = part + received[b].astype(F32)
        for r in range(2):
            lines = jnp.where(line == kv * 2 + r, part[r * 16 : (r + 1) * 16][:, None, :], lines)
    t3[...] = lines
    for b in a_others:
        remote(OUT, t3.at[b], gp_hbm.at[a], a_peer(b)).start()
    stores[3].start()
    arrived(DQ, dqr.at[pl.ds(0, 15)])
    arrived(OUT, gp_hbm.at[pl.ds(0, 15)])

    sent(KV, kvs.at[pl.ds(0, 15)])
    sent(QUERY, xq.at[pl.ds(0, 15)])
    sent(GRAD, xg.at[pl.ds(0, 15)])
    sent(ZK, kb.at[0, pl.ds(0, 3)])
    sent(ZV, vb.at[0, pl.ds(0, 3)])
    sent(ZSUM, gsumr.at[pl.ds(0, 3)])
    sent(YK, kb.at[pl.ds(0, 3)])
    sent(YV, vb.at[pl.ds(0, 3)])
    sent(OWN, str_.at[pl.ds(0, 15)])
    sent(FIN, fr.at[pl.ds(0, 15)])
    sent(DQ, dqs.at[pl.ds(0, 15)])
    sent(YSUM_V, sbv.at[pl.ds(0, 3)])
    sent(YSUM_K, sbk.at[pl.ds(0, 3)])
    sent(ZSUM_V, szv.at[pl.ds(0, 3)])
    sent(ZSUM_K, szk.at[pl.ds(0, 3)])
    sent(OUT, t3.at[pl.ds(0, 15)])
    for store in stores + [own_part]:
        store.wait()


def store_all(own, other, dk, dv, gp, dq_out, dk_out, dv_out, gk_out, gv_out, *scratch):
    (
        own_held, other_held, dk_held, dv_held, gp_held, dq_held, gk_held, gv_held,
        in_sem, out_sem,
    ) = scratch
    pairs = [(own, own_held), (other, other_held), (gp, gp_held)]
    stores = []
    for source, held, target in ((dk, dk_held, dk_out), (dv, dv_held, dv_out)):
        for first in range(0, ROWS, SLOTS):
            span = pl.ds(first, SLOTS)
            pairs.append((source.at[span], held.at[span]))
            stores.append((held.at[span], target.at[span]))
    stores += [(dq_held, dq_out), (gk_held, gk_out), (gv_held, gv_out)]
    loads = [pltpu.make_async_copy(*pair, in_sem.at[n]) for n, pair in enumerate(pairs)]
    stores = [pltpu.make_async_copy(*pair, out_sem.at[n]) for n, pair in enumerate(stores)]
    for load in loads:
        load.start()
    loads[0].wait()
    loads[1].wait()
    for h in range(HEADS):
        cols = slice(h * DIM, (h + 1) * DIM)
        total = own_held[h].astype(F32) + other_held[h].astype(F32)
        dq_held[:, cols] = total.astype(BF16)
    stores[4].start()
    for n in range(4):
        loads[3 + n].wait()
        stores[n].start()
    loads[2].wait()
    for h in range(HEADS):
        cols = slice(h * DIM, (h + 1) * DIM)
        gk_held[:, cols] = gp_held[h, 0:2, :].astype(BF16)
        gv_held[:, cols] = gp_held[h, 2:4, :].astype(BF16)
    stores[5].start()
    stores[6].start()
    for store in stores:
        store.wait()


def shards(prompt_k, prompt_v, comp_q, comp_k, comp_v, grad_out, rewards, mask_pos):
    hbm = pl.BlockSpec(memory_space=pltpu.HBM)
    V = pltpu.VMEM
    grads = pl.pallas_call(
        kernel,
        out_shape=(
            jax.ShapeDtypeStruct((HEADS, SLOTS, DIM), BF16),
            jax.ShapeDtypeStruct((HEADS, SLOTS, DIM), BF16),
            jax.ShapeDtypeStruct((ROWS, WIDTH), BF16),
            jax.ShapeDtypeStruct((ROWS, WIDTH), BF16),
            jax.ShapeDtypeStruct((16, 8, DIM), F32),
        ),
        in_specs=[hbm] * 8,
        out_specs=(hbm,) * 5,
        scratch_shapes=[
            V((2, WIDTH), BF16),
            V((2, WIDTH), BF16),
            V((1, 1), F32),
            V((1, SLOTS), jnp.int32),
            V((ROWS, WIDTH), BF16),
            V((ROWS, WIDTH), BF16),
            V((ROWS, WIDTH), BF16),
            V((SLOTS, WIDTH), BF16),
            V((16, SLOTS, DIM), BF16),
            V((16, SLOTS, DIM), BF16),
            V((16, SLOTS, DIM), BF16),
            V((16, SLOTS, DIM), BF16),
            V((16, 8, DIM), F32),
            V((16, 8, DIM), F32),
            V((4, 4, 32, DIM), BF16),
            V((4, 4, 32, DIM), BF16),
            V((8, DIM), F32),
            V((4, 8, DIM), F32),
            V((8, 128, DIM), F32),
            V((8, 128, DIM), F32),
            V((8, 8, DIM), F32),
            V((16, 8, DIM), F32),
            V((8, 8, DIM), F32),
            V((16, 8, DIM), F32),
            V((4, 128, 16 * SLOTS), F32),
            V((4, 128, 16 * SLOTS), F32),
            V((4, 8, 16 * SLOTS), F32),
            V((4, 128, 16 * SLOTS), BF16),
            V((4, 128, 16 * SLOTS), BF16),
            V((4, 128, DIM), BF16),
            V((4, 128, DIM), BF16),
            V((4, 128, DIM), BF16),
            V((4, 128, DIM), BF16),
            V((4, 32, DIM), F32),
            V((4, 32, DIM), F32),
            V((4, 32, DIM), BF16),
            V((4, 32, DIM), BF16),
            V((4, 32, DIM), BF16),
            V((4, 32, DIM), BF16),
            V((16, 8, DIM), F32),
            V((16, SLOTS, DIM), BF16),
            V((16, SLOTS, DIM), BF16),
            V((ROWS, WIDTH), BF16),
            V((ROWS, WIDTH), BF16),
            pltpu.SemaphoreType.DMA((8,)),
            pltpu.SemaphoreType.DMA((5,)),
            pltpu.SemaphoreType.DMA((KINDS,)),
            pltpu.SemaphoreType.DMA((KINDS,)),
            pltpu.SemaphoreType.DMA((2, 4)),
        ],
        compiler_params=pltpu.CompilerParams(
            collective_id=0, has_side_effects=True, vmem_limit_bytes=60 * 1024 * 1024
        ),
    )(
        prompt_k, prompt_v, rewards, mask_pos[0], comp_q[0, 0], comp_k[0, 0], comp_v[0, 0],
        grad_out[0, 0],
    )
    shapes = [(SLOTS, WIDTH), (ROWS, WIDTH), (ROWS, WIDTH), (2, WIDTH), (2, WIDTH)]
    dq, dk, dv, gk, gv = pl.pallas_call(
        store_all,
        out_shape=[jax.ShapeDtypeStruct(shape, BF16) for shape in shapes],
        in_specs=[hbm] * 5,
        out_specs=[hbm] * 5,
        scratch_shapes=[V(grad.shape, grad.dtype) for grad in grads]
        + [
            V((SLOTS, WIDTH), BF16),
            V((2, WIDTH), BF16),
            V((2, WIDTH), BF16),
            pltpu.SemaphoreType.DMA((7,)),
            pltpu.SemaphoreType.DMA((7,)),
        ],
        compiler_params=pltpu.CompilerParams(vmem_limit_bytes=60 * 1024 * 1024),
    )(*grads)
    return dq[None, None], dk[None, None], dv[None, None], gk, gv


def solution(mesh):
    wide = P("grp", "ctx", None, None)
    rows = P(("grp", "ctx"), None)
    return jax.shard_map(
        shards,
        mesh=mesh,
        in_specs=(rows, rows, wide, wide, wide, wide, P("grp", "ctx"), P("grp", "ctx", None)),
        out_specs=(wide, wide, wide, rows, rows),
        check_vma=False,
    )
```
